128 devices in a mesh: dev: 128 (over x, y, z, core).
Axes of the slice: x: 4, y: 4, z: 4, core: 2. Of those that a mesh axis runs over, the one named last changes fastest.
Arguments:
- stream: bfloat16 [16384, 1536], P('dev'), may hold values from -24 to 24
- attn_gain: bfloat16 [1536], P('dev'), may hold values from 0.5 to 1.5
- w_query: bfloat16 [1536, 1536], P('dev'), may hold values from -0.15625 to 0.15625
- w_key: bfloat16 [1536, 768], P('dev'), may hold values from -0.15625 to 0.15625
- w_value: bfloat16 [1536, 768], P('dev'), may hold values from -0.15625 to 0.15625
- w_out: bfloat16 [1536, 1536], P('dev'), may hold values from -0.625 to 0.625
- mlp_gain: bfloat16 [1536], P('dev'), may hold values from 0.5 to 1.5
- w_gate: bfloat16 [1536, 4096], P('dev'), may hold values from -0.15625 to 0.15625
- w_up: bfloat16 [1536, 4096], P('dev'), may hold values from -0.15625 to 0.15625
- w_down: bfloat16 [4096, 1536], P('dev'), may hold values from -0.09375 to 0.09375
- parent: int32 [128], replicated, may hold values from -1 to 127, as said below
- live_mask: int32 [16384], P('dev'), may hold values from 0 to 1, as said below
- cotangent: bfloat16 [16384, 1536], P('dev'), may hold values from -6 to 6
Outputs:
- mixed_out: bfloat16 [16384, 1536], P('dev')
- stream_grad: float32 [16384, 1536], P('dev')
- attn_gain_grad: float32 [1536], P('dev')
- w_query_grad: float32 [1536, 1536], P('dev')
- w_key_grad: float32 [1536, 768], P('dev')
- w_value_grad: float32 [1536, 768], P('dev')
- w_out_grad: float32 [1536, 1536], P('dev')
- mlp_gain_grad: float32 [1536], P('dev')
- w_gate_grad: float32 [1536, 4096], P('dev')
- w_up_grad: float32 [1536, 4096], P('dev')
- w_down_grad: float32 [4096, 1536], P('dev')
- stream_rms: float32 [16384], P('dev')
- branch_rms: float32 [16384], P('dev')
The draws below stay inside these ranges and needn't reach their ends.
Inputs may be any that keep to these rules, and one draw needn't show every extreme that they name: parent[b] is the block before b in its tree, or -1. There are 6 trees of 20 blocks: a chain of 8 trunk blocks, 4 branch blocks whose parent is the last trunk block, and 2 leaf blocks under each branch. All other blocks are padding, with parent -1 and no children. A tree's blocks may stand at any block indices. `live_mask`: every token of a trunk or branch block is 1, every token of a padding block 0; in a leaf block the 1s come first.
All inputs are finite; a program needn't handle non-finite values.
Results may differ from the reference program's by a relative error of at most 0.015.
Values may be sent and summed in bfloat16 or wider, within the bound.
A program may use at most 576 MiB of HBM per device.

```python
import jax
import jax.numpy as jnp
from jax import lax

D = 1536
FF = 4096
HEADS = 16
KV_HEADS = 8
HEAD_DIM = 96
QD = 1536
KVD = 768
BLOCK = 128
TRUNK = 8
BRANCHES = 4
LEAVES = 2
DEPTH = 10
NB = 128
TOKENS = 16384
TREES = 6


def tree_layout(key):
    tree_size = TRUNK + BRANCHES + BRANCHES * LEAVES
    logical = jnp.arange(NB, dtype=jnp.int32)
    tree_index = logical // tree_size
    tree_rank = logical % tree_size
    tree_start = tree_index * tree_size
    leaf_rank = tree_rank - TRUNK - BRANCHES
    upper_block = jnp.where(tree_rank < TRUNK, tree_start + tree_rank - 1, jnp.where(tree_rank < TRUNK + BRANCHES, tree_start + TRUNK - 1, tree_start + TRUNK + leaf_rank // LEAVES))
    padding = tree_index >= TREES
    upper_block = jnp.where(jnp.logical_or(tree_rank == 0, padding), -1, upper_block).astype(jnp.int32)
    arrangement = jax.random.permutation(jax.random.fold_in(key, 11), NB).astype(jnp.int32)
    chosen = jax.random.randint(jax.random.fold_in(key, 12), (), 0, TREES).astype(jnp.int32) * tree_size
    placements = ((0, chosen + TRUNK + BRANCHES), (NB // 2, chosen + TRUNK + BRANCHES + 1), (NB - 1, chosen + TRUNK))
    for slot_index, wanted in placements:
        found_at = jnp.argmax(arrangement == wanted)
        current = arrangement[slot_index]
        arrangement = arrangement.at[found_at].set(current).at[slot_index].set(wanted)
    storage = jnp.zeros((NB,), jnp.int32).at[arrangement].set(logical)
    logical_upper = upper_block[arrangement]
    parent = jnp.where(logical_upper >= 0, storage[jnp.maximum(logical_upper, 0)], -1).astype(jnp.int32)
    lengths = jax.random.randint(jax.random.fold_in(key, 13), (NB,), 1, BLOCK + 1)
    offsets = jnp.arange(BLOCK, dtype=jnp.int32)
    is_leaf = tree_rank[arrangement] >= TRUNK + BRANCHES
    is_padding = padding[arrangement]
    kept_rows = jnp.logical_or(jnp.logical_not(is_leaf[:, None]), offsets[None, :] < lengths[:, None])
    live_rows = jnp.logical_and(jnp.logical_not(is_padding[:, None]), kept_rows)
    return (parent, live_rows.astype(jnp.int32).reshape(NB * BLOCK))


def draw_parent(key, part):
    layout = tree_layout(key)
    return layout[0]


def draw_live_mask(key, part):
    layout = tree_layout(key)
    return layout[1]


def strengthened(array, key, source, target, blocks, factor):
    owner, partner = [(jnp.arange(array.shape[position]) // (array.shape[position] // blocks)).reshape([-1 if axis == position else 1 for axis in range(array.ndim)]) for position in (source, target)]
    chosen = jax.random.permutation(key, blocks)[partner]
    strong = (owner == chosen) | (owner == (partner + blocks // 2) % blocks)
    return jnp.where(strong, factor * array, array)


def steps_of(stream_key, shape, cuts, low, high):
    def one(position, shards_of):
        heights = jax.random.uniform(jax.random.fold_in(jax.random.fold_in(stream_key, 6), position), (shards_of,), jnp.float32, low / len(cuts), high / len(cuts))
        return jnp.repeat(jnp.exp(heights), shape[position] // shards_of).reshape((-1,) + (1,) * (len(shape) - position - 1))

    loudness = one(*cuts[0])
    for cut in cuts[1:]:
        loudness = loudness * one(*cut)
    return loudness


def gaussian(key, shape, width, most, split=(), kind=jnp.bfloat16):
    drawn = width * jax.random.normal(key, shape, jnp.float32)
    if split:
        drawn = drawn * steps_of(key, shape, split, -0.22, 0.18)
    return jnp.clip(drawn, -most, most).astype(kind)


def bell_draw_with(own_key, dims, deviation, bound, cuts, heavy, held_as=jnp.bfloat16):
    result = deviation * jax.random.normal(own_key, dims, jnp.float32)
    if cuts:
        result = result * steps_of(own_key, dims, cuts, -0.22, 0.18)
    return jnp.clip(strengthened(result, jax.random.fold_in(own_key, 3), *heavy), -bound, bound).astype(held_as)


def setup_inputs(seed: int = 0) -> dict:
    key_of = jax.random.split(jax.random.key(seed), 14)
    return {
        "stream": bell_draw_with(key_of[0], (TOKENS, D), 1.0, 24.0, ((0, 128),), (0, 1, 128, 5.5)),
        "attn_gain": jnp.clip(1.0 + 0.1 * jax.random.normal(key_of[1], (D,), jnp.float32), 0.5, 1.5).astype(jnp.bfloat16),
        "w_query": gaussian(key_of[2], (D, QD), D ** -0.5, 0.15625, ((0, 128),)),
        "w_key": gaussian(key_of[3], (D, KVD), D ** -0.5, 0.15625, ((0, 128),)),
        "w_value": gaussian(key_of[4], (D, KVD), D ** -0.5, 0.15625, ((0, 128),)),
        "w_out": gaussian(key_of[5], (QD, D), (QD // 16) ** -0.5, 0.625, ((0, 128),)),
        "mlp_gain": jnp.clip(1.0 + 0.1 * jax.random.normal(key_of[6], (D,), jnp.float32), 0.5, 1.5).astype(jnp.bfloat16),
        "w_gate": gaussian(key_of[7], (D, FF), D ** -0.5, 0.15625, ((0, 128),)),
        "w_up": gaussian(key_of[8], (D, FF), D ** -0.5, 0.15625, ((0, 128),)),
        "w_down": gaussian(key_of[9], (FF, D), FF ** -0.5, 0.09375, ((0, 128),)),
        "parent": draw_parent(jax.random.fold_in(key_of[13], 71), 0),
        "live_mask": draw_live_mask(jax.random.fold_in(key_of[13], 71), 0),
        "cotangent": gaussian(key_of[12], (TOKENS, D), 1.0, 6.0, ((0, 128),)),
    }


EPSILON = 1e-05
ROPE_BASE = 100000.0
NEGATIVE = -1e+30
HIGHEST = lax.Precision.HIGHEST

@jax.custom_vjp
def low(v):
    return lax.optimization_barrier(v.astype(jnp.bfloat16)).astype(jnp.float32)

@jax.custom_vjp
def low_back(v):
    return v

def low_keep(v):
    return (low(v), None)

def low_pass(kept, grad):
    return (grad,)

def back_keep(v):
    return (v, None)

def back_low(kept, grad):
    return (low(grad),)
low.defvjp(low_keep, low_pass)
low_back.defvjp(back_keep, back_low)

def matmul(left, right):
    return jnp.dot(left, right, precision=HIGHEST, preferred_element_type=jnp.float32)

def ancestry(parent, block_ids):
    columns = [block_ids]
    for hop_index in range(DEPTH - 1):
        previous = columns[-1]
        upward = jnp.take(parent, jnp.maximum(previous, 0), axis=0)
        columns.append(jnp.where(previous >= 0, upward, -1).astype(jnp.int32))
    return jnp.stack(columns, axis=1)

def rope_tables(places):
    half_size = HEAD_DIM // 2
    frequency = ROPE_BASE ** (-2.0 * jnp.arange(half_size, dtype=jnp.float32) / HEAD_DIM)
    angles = places.astype(jnp.float32)[:, None] * frequency[None, :]
    return (jnp.cos(angles), jnp.sin(angles))

def rotate(incoming, cosine_table, sine_table):
    token_count = incoming.shape[0]
    pieces = incoming.reshape(token_count, -1, HEAD_DIM)
    half_size = HEAD_DIM // 2
    front_half = pieces[:, :, :half_size]
    back_half = pieces[:, :, half_size:]
    cosine = cosine_table[:, None, :]
    sine_part = sine_table[:, None, :]
    turned = jnp.concatenate([front_half * cosine - back_half * sine_part, back_half * cosine + front_half * sine_part], axis=2)
    return turned.reshape(token_count, -1)

def permitted(present, key_flags):
    offsets = jnp.arange(BLOCK, dtype=jnp.int32)
    earlier = offsets[None, :] <= offsets[:, None]
    diagonal = offsets[None, :] == offsets[:, None]
    own_block = (jnp.arange(DEPTH) == 0)[:, None, None]
    causal = jnp.logical_or(jnp.logical_not(own_block), earlier[None])
    key_ok = jnp.logical_or(key_flags[:, :, None, :], jnp.logical_and(own_block, diagonal[None])[None])
    allowed = jnp.logical_and(jnp.logical_and(present[:, :, None, None], causal[None]), key_ok)
    return allowed.transpose(0, 2, 1, 3).reshape(present.shape[0], BLOCK, DEPTH * BLOCK)

def attend_block(block_query, context, block_allowed):
    key_width = KV_HEADS * HEAD_DIM
    grouped = block_query.reshape(BLOCK, KV_HEADS, HEADS // KV_HEADS, HEAD_DIM)
    key_rows = context[:, :key_width].reshape(DEPTH * BLOCK, KV_HEADS, HEAD_DIM)
    value_rows = context[:, key_width:].reshape(DEPTH * BLOCK, KV_HEADS, HEAD_DIM)
    scores = jnp.einsum('qkgd,tkd->kgqt', grouped, key_rows, precision=HIGHEST) * HEAD_DIM ** (-0.5)
    scores = low_back(scores)
    scores = jnp.where(block_allowed, scores, NEGATIVE)
    largest = lax.optimization_barrier(jnp.max(scores, axis=-1, keepdims=True))
    exp_terms = jnp.where(block_allowed, jnp.exp(scores - largest), 0.0)
    chances = exp_terms / lax.optimization_barrier(jnp.sum(exp_terms, axis=-1, keepdims=True))
    chances = low(chances)
    output = jnp.einsum('kgqt,tkd->qkgd', chances, value_rows, precision=HIGHEST)
    return output.reshape(BLOCK, HEADS * HEAD_DIM)

def reference(stream, attn_gain, w_query, w_key, w_value, w_out, mlp_gain, w_gate, w_up, w_down, parent, live_mask, cotangent):
    key_width = KV_HEADS * HEAD_DIM
    block_ids = jnp.arange(NB, dtype=jnp.int32)
    lineage = ancestry(parent, block_ids)
    depths = lax.optimization_barrier(jnp.sum(lineage >= 0, axis=1)) - 1
    places = (depths[:, None] * BLOCK + jnp.arange(BLOCK, dtype=jnp.int32)[None, :]).reshape(NB * BLOCK)
    cosine_table, sine_table = rope_tables(places)
    safe_ids = jnp.maximum(lineage, 0)
    key_flags = jnp.take(live_mask.reshape(NB, BLOCK), safe_ids, axis=0) > 0
    allowed = permitted(lineage >= 0, key_flags)

    def attention(rotated_query, context_local):
        context_blocks = context_local.reshape(NB, BLOCK, 2 * key_width)
        query_blocks = rotated_query.reshape(NB, BLOCK, HEADS * HEAD_DIM)

        def one_block(packed):
            block_query, block_lineage, block_allowed = packed
            context = jnp.take(context_blocks, block_lineage, axis=0).reshape(DEPTH * BLOCK, 2 * key_width)
            return attend_block(block_query, context, block_allowed)
        outputs = lax.map(jax.checkpoint(one_block), (query_blocks, safe_ids, allowed))
        return outputs.reshape(NB * BLOCK, HEADS * HEAD_DIM)

    def forward(stream_wide, gain_one, query_weight, key_weight, value_weight, out_weight, gain_two, gate_weight, up_weight, down_weight):
        stream_rms = jnp.sqrt(lax.optimization_barrier(jnp.mean(stream_wide * stream_wide, axis=1, keepdims=True)) + EPSILON)
        normed = low(stream_wide / stream_rms * gain_one)
        query_raw = low_back(matmul(normed, query_weight))
        key_raw = low_back(matmul(normed, key_weight))
        value_low = low(low_back(matmul(normed, value_weight)))
        rotated_query = low(rotate(query_raw, cosine_table, sine_table))
        rotated_key = low(rotate(key_raw, cosine_table, sine_table))
        attended = attention(rotated_query, jnp.concatenate([rotated_key, value_low], axis=1))
        attended_low = low(low_back(attended))
        branch = low_back(matmul(attended_low, out_weight))
        middle = stream_wide + branch
        branch_rms = jnp.sqrt(lax.optimization_barrier(jnp.mean(middle * middle, axis=1, keepdims=True)) + EPSILON)
        mid_normed = low(middle / branch_rms * gain_two)
        gate_value = low_back(matmul(mid_normed, gate_weight))
        up_value = low_back(matmul(mid_normed, up_weight))
        activated = low(jax.nn.silu(gate_value) * up_value)
        mixed_out = middle + low_back(matmul(activated, down_weight))
        return (mixed_out, (stream_rms[:, 0], branch_rms[:, 0]))
    arguments = tuple((argument.astype(jnp.float32) for argument in (stream, attn_gain, w_query, w_key, w_value, w_out, mlp_gain, w_gate, w_up, w_down)))
    mixed_out, pullback, statistics = jax.vjp(forward, *arguments, has_aux=True)
    gradients = pullback(cotangent.astype(jnp.float32))
    return (mixed_out.astype(jnp.bfloat16), gradients[0], gradients[1], gradients[2], gradients[3], gradients[4], gradients[5], gradients[6], gradients[7], gradients[8], gradients[9], statistics[0], statistics[1])
```

```python
import functools

import jax
import jax.numpy as jnp
import numpy as np
from jax import lax
from jax.experimental import pallas as pl
from jax.experimental.pallas import tpu as pltpu
from jax.sharding import PartitionSpec as P

HEADS = 16
KV_HEADS = 8
HEAD_DIM = 96
BLOCK = 128
DEPTH = 10
D = 1536
FF = 4096
MEMBERS = 8
LANES = 128

EPSILON = 1e-05
ROPE_BASE = 100000.0
NEGATIVE = -1e30
SCALE = HEAD_DIM ** (-0.5)
MESH = pl.DeviceIdType.MESH
BF16 = jnp.bfloat16
F32 = jnp.float32
VMEM_BYTES = 56 * 2**20


def spot():
    me = lax.axis_index("dev")
    return me // 32, (me // 8) % 4, (me // 2) % 4, me % 2


def device_of(x, y, z, c):
    return ((x % 4) * 4 + (y % 4)) * 8 + (z % 4) * 2 + c


def greet(peers):
    barrier = pltpu.get_barrier_semaphore()
    for peer in peers:
        pl.semaphore_signal(barrier, inc=1, device_id=(peer,), device_id_type=MESH)
    pl.semaphore_wait(barrier, len(peers))


def axis_peers(x, y, z, c, far):
    steps = (1, 2, 3) if far else (1, 3)
    return [device_of(x + k, y, z, c) for k in steps] + [device_of(x, y + k, z, c) for k in steps]


def group_peer(x, y, z, c, k):
    member = (z * 2 + c + k) % MEMBERS
    return (x * 4 + y) * MEMBERS + member


class Wire:
    def __init__(self, send_sems, recv_sems):
        self.send_sems = send_sems
        self.recv_sems = recv_sems
        self.sent = []

    def send(self, source, target, peer):
        slot = len(self.sent)
        copy = pltpu.make_async_remote_copy(
            src_ref=source,
            dst_ref=target,
            send_sem=self.send_sems.at[slot],
            recv_sem=self.recv_sems.at[slot],
            device_id=(peer,),
            device_id_type=MESH,
        )
        copy.start()
        self.sent.append(copy)
        return copy

    def close(self):
        for copy in self.sent:
            copy.wait_send()


class Ring:
    def __init__(self, wire, own, part, place, up, down):
        self.wire, self.own, self.part = wire, own, part
        self.place, self.up, self.down = place, up, down

    def begin(self):
        send, part, place = self.wire.send, self.part, self.place
        self.low_up = send(self.own(0), part(place, 0), self.up)
        self.high_down = send(self.own(1), part(place, 1), self.down)
        self.high_up = send(self.own(1), part(place, 1), self.up)
        self.low_down = send(self.own(0), part(place, 0), self.down)

    def relay(self):
        before, after = (self.place + 3) % 4, (self.place + 1) % 4
        self.low_up.wait_recv()
        self.far_up = self.wire.send(self.part(before, 0), self.part(before, 0), self.up)
        self.high_down.wait_recv()
        self.far_down = self.wire.send(self.part(after, 1), self.part(after, 1), self.down)

    def near(self):
        self.high_up.wait_recv()
        self.low_down.wait_recv()

    def far(self):
        self.far_up.wait_recv()
        self.far_down.wait_recv()


class PlaneGather:
    def __init__(self, wire, own, out, xyzc):
        self.wire, self.own, self.out = wire, own, out
        x, y, z, c = xyzc
        self.x, self.y = x, y
        self.x_up, self.x_down = device_of(x + 1, y, z, c), device_of(x + 3, y, z, c)
        self.y_up, self.y_down = device_of(x, y + 1, z, c), device_of(x, y + 3, z, c)
        self.half = out.shape[2] // 2
        self.width = out.shape[3] // 2

    def view(self, ref, lead, half, side):
        rows = pl.ds(half * self.half, self.half)
        cols = pl.ds(side * self.width, self.width)
        return ref.at[lead + (rows, cols)]

    def first(self):
        out, x, y = self.out, self.x, self.y
        self.one = Ring(
            self.wire,
            lambda side: self.view(self.own, (), 0, side),
            lambda place, side: self.view(out, (place, y), 0, side),
            x, self.x_up, self.x_down,
        )
        self.two = Ring(
            self.wire,
            lambda side: self.view(self.own, (), 1, side),
            lambda place, side: self.view(out, (x, place), 1, side),
            y, self.y_up, self.y_down,
        )
        self.one.begin()
        self.two.begin()

    def relay(self):
        self.one.relay()
        self.two.relay()

    def settle(self):
        for ring in (self.one, self.two):
            ring.near()
            ring.far()

    def second(self):
        out, x, y = self.out, self.x, self.y
        every = slice(None)
        self.one = Ring(
            self.wire,
            lambda side: self.view(out, (every, y), 0, side),
            lambda place, side: self.view(out, (every, place), 0, side),
            y, self.y_up, self.y_down,
        )
        self.two = Ring(
            self.wire,
            lambda side: self.view(out, (x, every), 1, side),
            lambda place, side: self.view(out, (place, every), 1, side),
            x, self.x_up, self.x_down,
        )
        self.one.begin()
        self.two.begin()


class GroupGather:
    def __init__(self, wire, own, out, xyzc):
        self.wire, self.own, self.out = wire, own, out
        x, y, z, c = xyzc
        self.z, self.c = z, c
        self.sibling = device_of(x, y, z, 1 - c)
        half = out.shape[2] // 2
        self.ring = Ring(
            wire,
            lambda side: own.at[pl.ds(side * half, half)],
            lambda place, side: out.at[place, c, pl.ds(side * half, half)],
            z, device_of(x, y, z + 1, c), device_of(x, y, z + 3, c),
        )
        self.crossed = []

    def begin(self):
        self.ring.begin()
        self.crossed.append(self.wire.send(self.own, self.out.at[self.z, self.c], self.sibling))

    def cross(self, k):
        piece = self.out.at[(self.z + k) % 4, self.c]
        self.crossed.append(self.wire.send(piece, piece, self.sibling))

    def relay(self):
        self.ring.relay()

    def near(self):
        self.ring.near()
        self.cross(1)
        self.cross(3)

    def far(self):
        self.ring.far()
        self.cross(2)

    def finish(self):
        for copy in self.crossed:
            copy.wait_recv()


class PlaneScatter:
    def __init__(self, wire, terms, mine, first_in, summed, second_in, local_sem, xyzc):
        self.wire, self.terms = wire, terms
        self.mine, self.first_in, self.summed, self.second_in = mine, first_in, summed, second_in
        self.x, self.y, self.z, self.c = xyzc
        self.half = terms.shape[2] // 2
        self.local_sem = local_sem

    def peer(self, along_x, k):
        if along_x:
            return device_of(self.x + k, self.y, self.z, self.c)
        return device_of(self.x, self.y + k, self.z, self.c)

    def line(self, half, place):
        rows = pl.ds(half * self.half, self.half)
        if half == 0:
            return self.terms.at[place, :, rows]
        return self.terms.at[:, place, rows]

    def first(self):
        self.copies = []
        self.locals = []
        for half, place in ((0, self.x), (1, self.y)):
            copy = pltpu.make_async_copy(
                self.line(half, place), self.mine.at[half], self.local_sem.at[half]
            )
            copy.start()
            self.locals.append(copy)
        for k in (2, 1, 3):
            for half, place in ((0, self.x), (1, self.y)):
                self.copies.append(
                    self.wire.send(
                        self.line(half, (place + k) % 4),
                        self.first_in.at[half, k - 1],
                        self.peer(half == 0, k),
                    )
                )

    def add_first(self):
        for copy in self.locals:
            copy.wait()
        for copy in self.copies:
            copy.wait_recv()

        def body(step, carry):
            half, line = step // 4, step % 4
            total = self.mine[half, line].astype(F32)
            for k in range(3):
                total = total + self.first_in[half, k, line].astype(F32)
            self.summed[half, line] = total.astype(BF16)
            return carry

        lax.fori_loop(0, 8, body, 0)

    def second(self):
        self.copies = []
        for k in (2, 1, 3):
            for half, place in ((0, self.y), (1, self.x)):
                self.copies.append(
                    self.wire.send(
                        self.summed.at[half, (place + k) % 4],
                        self.second_in.at[half, k - 1],
                        self.peer(half == 1, k),
                    )
                )

    def total(self, half):
        place = (self.y, self.x)[half]
        total = self.summed[half, place].astype(F32)
        for k in range(3):
            total = total + self.second_in[half, k].astype(F32)
        return total

    def arrive(self):
        for copy in self.copies:
            copy.wait_recv()


def scatter_scratch(rows, cols):
    half = rows // 2
    return [
        pltpu.VMEM((2, 4, half, cols), BF16),
        pltpu.VMEM((2, 3, 4, half, cols), BF16),
        pltpu.VMEM((2, 4, half, cols), BF16),
        pltpu.VMEM((2, 3, half, cols), BF16),
        pltpu.SemaphoreType.DMA((2,)),
    ]


class GroupScatter:
    def __init__(self, wire, terms, mine, crossed_in, summed, ring_in, local_sem, xyzc):
        self.wire, self.terms = wire, terms
        self.mine, self.crossed_in, self.summed, self.ring_in = mine, crossed_in, summed, ring_in
        self.x, self.y, self.z, self.c = xyzc
        self.local_sem = local_sem

    def begin(self):
        self.local = pltpu.make_async_copy(self.terms.at[:, self.c], self.mine, self.local_sem)
        self.local.start()
        sibling = device_of(self.x, self.y, self.z, 1 - self.c)
        self.crossed = {}
        for k in (2, 1, 3, 0):
            place = (self.z + k) % 4
            self.crossed[k] = self.wire.send(
                self.terms.at[place, 1 - self.c], self.crossed_in.at[place], sibling
            )

    def turn(self):
        self.local.wait()
        self.copies = []
        for k in (2, 1, 3):
            place = (self.z + k) % 4
            self.crossed[k].wait_recv()

            def body(step, carry):
                rows = pl.ds(pl.multiple_of(step * 32, 32), 32)
                total = self.mine[place, rows].astype(F32) + self.crossed_in[place, rows].astype(F32)
                self.summed[place, rows] = total.astype(BF16)
                return carry

            lax.fori_loop(0, 4, body, 0)
            self.copies.append(
                self.wire.send(
                    self.summed.at[place],
                    self.ring_in.at[k - 1],
                    device_of(self.x, self.y, self.z + k, self.c),
                )
            )

    def finish(self, out):
        self.crossed[0].wait_recv()
        for copy in self.copies:
            copy.wait_recv()

        def body(step, carry):
            rows = pl.ds(pl.multiple_of(step * 32, 32), 32)
            total = self.mine[self.z, rows].astype(F32) + self.crossed_in[self.z, rows].astype(F32)
            for k in range(3):
                total = total + self.ring_in[k, rows].astype(F32)
            out[rows] = total
            return carry

        lax.fori_loop(0, 4, body, 0)


def group_scatter_scratch(cols):
    return [
        pltpu.VMEM((4, BLOCK, cols), BF16),
        pltpu.VMEM((4, BLOCK, cols), BF16),
        pltpu.VMEM((4, BLOCK, cols), BF16),
        pltpu.VMEM((3, BLOCK, cols), BF16),
        pltpu.SemaphoreType.DMA,
    ]


def wire_scratch(count):
    return [pltpu.SemaphoreType.DMA((count,)), pltpu.SemaphoreType.DMA((count,))]


ANY = pl.BlockSpec(memory_space=pl.ANY)
INVMEM = pl.BlockSpec(memory_space=pltpu.VMEM)


def communicate(kernel, out_shapes, in_specs, out_specs, scratch, ident, name):
    return pl.pallas_call(
        kernel,
        out_shape=out_shapes,
        in_specs=in_specs,
        out_specs=out_specs,
        scratch_shapes=scratch,
        compiler_params=pltpu.CompilerParams(
            collective_id=ident, has_side_effects=True, vmem_limit_bytes=VMEM_BYTES
        ),
        name=name,
    )


def opening_kernel(
    stream, cotangent, packed, w_out, w_down, small,
    stream_all, cotangent_all, wide_all, out_all, down_all, gains_all, small_all,
    packed_in, out_in, small_in, wide_tall, out_tall, wide_own, out_own, gain_own,
    send_sems, recv_sems, local_sems,
):
    xyzc = x, y, z, c = spot()
    j = z * 2 + c
    wire = Wire(send_sems, recv_sems)
    group = [group_peer(x, y, z, c, k) for k in range(1, MEMBERS)]
    greet(group + axis_peers(x, y, z, c, True))

    locals_ = []

    def keep(source, target):
        copy = pltpu.make_async_copy(source, target, local_sems.at[len(locals_)])
        copy.start()
        locals_.append(copy)

    dealt = []
    for k in range(1, MEMBERS):
        member = (j + k) % MEMBERS
        half = pl.ds(pl.multiple_of((member % 2) * 768, 768), 768)
        dealt.append(wire.send(packed.at[member], packed_in.at[j], group[k - 1]))
        dealt.append(wire.send(w_out.at[:, half], out_in.at[j], group[k - 1]))
        dealt.append(wire.send(small, small_in.at[j], group[k - 1]))
    own_half = pl.ds(pl.multiple_of(c * 768, 768), 768)
    keep(packed.at[j], packed_in.at[j])
    keep(w_out.at[:, own_half], out_in.at[j])
    keep(small, small_in.at[j])
    keep(stream, stream_all.at[z, c])
    keep(cotangent, cotangent_all.at[z, c])
    keep(w_down, down_all.at[x, y])

    streams = GroupGather(wire, stream, stream_all, xyzc)
    streams.begin()

    for copy in dealt:
        copy.wait_recv()
    for copy in locals_[:3]:
        copy.wait()
    for member in range(MEMBERS):
        rows = pl.ds(member * 12, 12)
        wide_tall[rows] = packed_in[member].astype(F32)[:12]
        out_tall[rows] = out_in[member].astype(F32)[:12]
    wide_own[...] = wide_tall[...].astype(BF16)
    out_own[...] = out_tall[...].astype(BF16)
    gain = small_in[0].astype(F32)
    for member in range(1, MEMBERS):
        gain = gain + small_in[member].astype(F32)
    gain_own[...] = gain.astype(BF16)

    keep(wide_own, wide_all.at[x, y])
    keep(out_own, out_all.at[x, y, :, own_half])
    keep(gain_own, gains_all.at[x, y])
    keep(small_in, small_all)

    half_out = out_all.at[:, :, :, own_half]
    wide = PlaneGather(wire, wide_own, wide_all, xyzc)
    down = PlaneGather(wire, w_down, down_all, xyzc)
    outs = PlaneGather(wire, out_own, half_out, xyzc)
    planes = (wide, down, outs)
    tiny = [
        wire.send(gain_own, gains_all.at[x, y], device_of(x + k, y, z, c)) for k in range(1, 4)
    ]
    for plane in planes:
        plane.first()
    streams.relay()
    for plane in planes:
        plane.relay()
    for copy in locals_[3:]:
        copy.wait()
    for copy in tiny:
        copy.wait_recv()
    line = gains_all.at[:, y]
    tiny = [wire.send(line, line, device_of(x, y + k, z, c)) for k in range(1, 4)]
    for plane in planes:
        plane.settle()
    for plane in planes:
        plane.second()
    streams.near()
    streams.far()
    cotangents = GroupGather(wire, cotangent, cotangent_all, xyzc)
    cotangents.begin()
    for plane in planes:
        plane.relay()
    cotangents.relay()
    outs.settle()
    sibling = device_of(x, y, z, 1 - c)
    swapped = wire.send(half_out, half_out, sibling)
    wide.settle()
    down.settle()
    cotangents.near()
    cotangents.far()
    swapped.wait_recv()
    for copy in tiny:
        copy.wait_recv()
    streams.finish()
    cotangents.finish()
    wire.close()


def opening(stream, cotangent, packed, w_out, w_down, small):
    shape = jax.ShapeDtypeStruct
    return communicate(
        opening_kernel,
        (
            shape((4, 2, BLOCK, D), BF16),
            shape((4, 2, BLOCK, D), BF16),
            shape((4, 4, 96, 1536), BF16),
            shape((4, 4, 96, 1536), BF16),
            shape((4, 4, 32, 1536), BF16),
            shape((4, 4, 16, LANES), BF16),
            shape((MEMBERS, 16, LANES), BF16),
        ),
        [ANY] * 6,
        (ANY,) * 7,
        [
            pltpu.VMEM((MEMBERS, 16, 1536), BF16),
            pltpu.VMEM((MEMBERS, 16, 768), BF16),
            pltpu.VMEM((MEMBERS, 16, LANES), BF16),
            pltpu.VMEM((96, 1536), F32),
            pltpu.VMEM((96, 768), F32),
            pltpu.VMEM((96, 1536), BF16),
            pltpu.VMEM((96, 768), BF16),
            pltpu.VMEM((16, LANES), BF16),
        ]
        + wire_scratch(120)
        + [pltpu.SemaphoreType.DMA((10,))],
        1,
        "opening",
    )(stream, cotangent, packed, w_out, w_down, small)


def context_kernel(own, out, send_sems, recv_sems, local_sem):
    xyzc = x, y, z, c = spot()
    wire = Wire(send_sems, recv_sems)
    greet(axis_peers(x, y, z, c, False))
    local = pltpu.make_async_copy(own, out.at[x, y], local_sem)
    local.start()
    plane = PlaneGather(wire, own, out, xyzc)
    plane.first()
    plane.relay()
    local.wait()
    plane.settle()
    plane.second()
    plane.relay()
    plane.settle()
    wire.close()


def gather_context(own):
    return communicate(
        context_kernel,
        jax.ShapeDtypeStruct((4, 4) + own.shape, BF16),
        [ANY],
        ANY,
        wire_scratch(24) + [pltpu.SemaphoreType.DMA],
        2,
        "gather_context",
    )(own)


def deal_kernel(terms, out, send_sems, recv_sems, local_sem):
    x, y, z, c = spot()
    j = z * 2 + c
    wire = Wire(send_sems, recv_sems)
    group = [group_peer(x, y, z, c, k) for k in range(1, MEMBERS)]
    greet(group)
    local = pltpu.make_async_copy(terms.at[j], out.at[j], local_sem)
    local.start()
    copies = [
        wire.send(terms.at[(j + k) % MEMBERS], out.at[j], group[k - 1])
        for k in (4, 5, 3, 2, 6, 7, 1)
    ]
    local.wait()
    for copy in copies:
        copy.wait_recv()
    wire.close()


def deal(terms, ident):
    return communicate(
        deal_kernel,
        jax.ShapeDtypeStruct(terms.shape, terms.dtype),
        [ANY],
        ANY,
        wire_scratch(7) + [pltpu.SemaphoreType.DMA],
        ident,
        "deal",
    )(terms)


def group_gather_kernel(own, out, send_sems, recv_sems, local_sem):
    xyzc = x, y, z, c = spot()
    wire = Wire(send_sems, recv_sems)
    greet([device_of(x, y, z + 1, c), device_of(x, y, z + 3, c), device_of(x, y, z, 1 - c)])
    local = pltpu.make_async_copy(own, out.at[z, c], local_sem)
    local.start()
    gather = GroupGather(wire, own, out, xyzc)
    gather.begin()
    gather.relay()
    gather.near()
    gather.far()
    local.wait()
    gather.finish()
    wire.close()


def group_gather(own, ident):
    return communicate(
        group_gather_kernel,
        jax.ShapeDtypeStruct((4, 2) + own.shape, own.dtype),
        [ANY],
        ANY,
        wire_scratch(10) + [pltpu.SemaphoreType.DMA],
        ident,
        "group_gather",
    )(own)


def split_rows(tall, dealt):
    for member in range(MEMBERS):
        dealt[member] = tall[pl.ds(member * 12, 12)]


def feed_kernel(
    grad_terms, wide_terms, down_terms, grad_out, wide_out, down_out, *scratch
):
    xyzc = x, y, z, c = spot()
    j = z * 2 + c
    wide_tall, wide_dealt, *scratch = scratch
    group_scratch, wide_scratch, down_scratch = scratch[:5], scratch[5:10], scratch[10:15]
    send_sems, recv_sems = scratch[15:]
    wire = Wire(send_sems, recv_sems)
    group = [group_peer(x, y, z, c, k) for k in range(1, MEMBERS)]
    greet(group + axis_peers(x, y, z, c, True))
    rows = GroupScatter(wire, grad_terms, *group_scratch, xyzc)
    wide = PlaneScatter(wire, wide_terms, *wide_scratch, xyzc)
    down = PlaneScatter(wire, down_terms, *down_scratch, xyzc)
    rows.begin()
    wide.first()
    down.first()
    rows.turn()
    wide.add_first()
    wide.second()
    down.add_first()
    down.second()
    rows.finish(grad_out)
    wide.arrive()
    for half in range(2):
        wide_tall[pl.ds(half * 48, 48)] = wide.total(half)
    split_rows(wide_tall, wide_dealt)
    wide_out[j] = wide_dealt[j]
    dealt = [
        wire.send(wide_dealt.at[(j + k) % MEMBERS], wide_out.at[j], group[k - 1])
        for k in range(1, MEMBERS)
    ]
    down.arrive()
    for half in range(2):
        down_out[pl.ds(half * 16, 16)] = down.total(half)
    for copy in dealt:
        copy.wait_recv()
    wire.close()


def feed_exchange(grad_terms, wide_terms, down_terms):
    shape = jax.ShapeDtypeStruct
    return communicate(
        feed_kernel,
        (
            shape((BLOCK, D), F32),
            shape((MEMBERS, 12, 1024), F32),
            shape((32, D), F32),
        ),
        [ANY] * 3,
        (INVMEM,) * 3,
        [pltpu.VMEM((96, 1024), F32), pltpu.VMEM((MEMBERS, 12, 1024), F32)]
        + group_scatter_scratch(D)
        + scatter_scratch(96, 1024)
        + scatter_scratch(32, 1536)
        + wire_scratch(40),
        4,
        "feed_exchange",
    )(grad_terms, wide_terms, down_terms)


def context_back_kernel(terms, row_terms, out, row_out, *scratch):
    xyzc = x, y, z, c = spot()
    plane_scratch, group_scratch = scratch[:5], scratch[5:10]
    wire = Wire(*scratch[10:])
    greet(
        [device_of(x, y, z + k, c) for k in range(1, 4)]
        + [device_of(x, y, z, 1 - c)]
        + axis_peers(x, y, z, c, True)
    )
    rows = GroupScatter(wire, row_terms, *group_scratch, xyzc)
    plane = PlaneScatter(wire, terms, *plane_scratch, xyzc)
    plane.first()
    rows.begin()
    rows.turn()
    plane.add_first()
    plane.second()
    rows.finish(row_out)
    plane.arrive()
    for half in range(2):
        out[pl.ds(half * 512, 512)] = plane.total(half)
    wire.close()


def context_back(terms, row_terms):
    shape = jax.ShapeDtypeStruct
    return communicate(
        context_back_kernel,
        (shape((1024, 256), F32), shape((BLOCK, D), F32)),
        [ANY] * 2,
        (INVMEM,) * 2,
        scatter_scratch(1024, 256) + group_scatter_scratch(D) + wire_scratch(24),
        6,
        "context_back",
    )(terms, row_terms)


def closing_kernel(
    grad_terms, wide_terms, out_terms, gain_terms,
    grad_out, wide_out, out_out, gain_out, *scratch
):
    xyzc = x, y, z, c = spot()
    j = z * 2 + c
    (
        wide_tall, wide_dealt, out_tall, out_dealt, out_mine, out_crossed,
        gain_in, gain_line, gain_in_two, gain_in_three, *scratch
    ) = scratch
    group_scratch, wide_scratch, out_scratch = scratch[:5], scratch[5:10], scratch[10:15]
    send_sems, recv_sems, local_sem = scratch[15:]
    wire = Wire(send_sems, recv_sems)
    group = [group_peer(x, y, z, c, k) for k in range(1, MEMBERS)]
    greet(group + axis_peers(x, y, z, c, True))
    sibling = device_of(x, y, z, 1 - c)

    rows = GroupScatter(wire, grad_terms, *group_scratch, xyzc)
    wide = PlaneScatter(wire, wide_terms, *wide_scratch, xyzc)
    own_half = pl.ds(pl.multiple_of(c * 768, 768), 768)
    other_half = pl.ds(pl.multiple_of((1 - c) * 768, 768), 768)
    crossed = wire.send(out_terms.at[:, :, :, other_half], out_crossed, sibling)
    local = pltpu.make_async_copy(out_terms.at[:, :, :, own_half], out_mine, local_sem)
    local.start()
    rows.begin()
    wide.first()
    gains = [
        wire.send(gain_terms.at[(x + k) % 4], gain_in.at[k - 1], device_of(x + k, y, z, c))
        for k in range(1, 4)
    ]
    local.wait()
    crossed.wait_recv()

    def body(step, carry):
        a, b = step // 4, step % 4
        total = out_mine[a, b].astype(F32) + out_crossed[a, b].astype(F32)
        out_mine[a, b] = total.astype(BF16)
        return carry

    lax.fori_loop(0, 16, body, 0)
    outs = PlaneScatter(wire, out_mine, *out_scratch, xyzc)
    outs.first()
    rows.turn()
    for copy in gains:
        copy.wait_recv()
    gain_line[...] = gain_terms[x] + gain_in[0] + gain_in[1] + gain_in[2]
    gains = [
        wire.send(gain_line.at[(y + k) % 4], gain_in_two.at[k - 1], device_of(x, y + k, z, c))
        for k in range(1, 4)
    ]
    wide.add_first()
    wide.second()
    outs.add_first()
    outs.second()
    for copy in gains:
        copy.wait_recv()
    gain_in_three[j] = gain_line[y] + gain_in_two[0] + gain_in_two[1] + gain_in_two[2]
    gains = [
        wire.send(gain_in_three.at[j], gain_in_three.at[j], group[k - 1]) for k in range(1, MEMBERS)
    ]
    wide.arrive()
    for half in range(2):
        wide_tall[pl.ds(half * 48, 48)] = wide.total(half)
    split_rows(wide_tall, wide_dealt)
    wide_out[j] = wide_dealt[j]
    dealt = [
        wire.send(wide_dealt.at[(j + k) % MEMBERS], wide_out.at[j], group[k - 1])
        for k in range(1, MEMBERS)
    ]
    outs.arrive()
    for half in range(2):
        out_tall[pl.ds(half * 48, 48)] = outs.total(half)
    split_rows(out_tall, out_dealt)
    out_out[j] = out_dealt[j]
    dealt += [
        wire.send(out_dealt.at[(j + k) % MEMBERS], out_out.at[j], group[k - 1])
        for k in range(1, MEMBERS)
    ]
    rows.finish(grad_out)
    for copy in gains:
        copy.wait_recv()
    total = gain_in_three[0]
    for member in range(1, MEMBERS):
        total = total + gain_in_three[member]
    gain_out[...] = total
    for copy in dealt:
        copy.wait_recv()
    wire.close()


def closing(grad_terms, wide_terms, out_terms, gain_terms):
    shape = jax.ShapeDtypeStruct
    return communicate(
        closing_kernel,
        (
            shape((BLOCK, D), F32),
            shape((MEMBERS, 12, 512), F32),
            shape((MEMBERS, 12, 768), F32),
            shape((8, LANES), F32),
        ),
        [ANY, ANY, ANY, INVMEM],
        (INVMEM,) * 4,
        [
            pltpu.VMEM((96, 512), F32),
            pltpu.VMEM((MEMBERS, 12, 512), F32),
            pltpu.VMEM((96, 768), F32),
            pltpu.VMEM((MEMBERS, 12, 768), F32),
            pltpu.VMEM((4, 4, 96, 768), BF16),
            pltpu.VMEM((4, 4, 96, 768), BF16),
            pltpu.VMEM((3, 4, 8, LANES), F32),
            pltpu.VMEM((4, 8, LANES), F32),
            pltpu.VMEM((3, 8, LANES), F32),
            pltpu.VMEM((MEMBERS, 8, LANES), F32),
        ]
        + group_scatter_scratch(D)
        + scatter_scratch(96, 512)
        + scatter_scratch(96, 768)
        + wire_scratch(80)
        + [pltpu.SemaphoreType.DMA],
        7,
        "closing",
    )(grad_terms, wide_terms, out_terms, gain_terms)


def lineage_kernel(parent, first, lineage):
    def one(block, carry):
        def hop(step, node):
            lineage[block, step] = node
            above = parent[jnp.maximum(node, 0)]
            return jnp.where(node >= 0, above, -1)

        lax.fori_loop(0, DEPTH, hop, first[0] + block)
        return carry

    lax.fori_loop(0, MEMBERS, one, 0)


def group_lineage(parent, first):
    smem = pl.BlockSpec(memory_space=pltpu.SMEM)
    return pl.pallas_call(
        lineage_kernel,
        out_shape=jax.ShapeDtypeStruct((MEMBERS, DEPTH), jnp.int32),
        in_specs=[smem, smem],
        out_specs=smem,
        name="group_lineage",
    )(parent, first.reshape(1))


def rope_tables():
    half = HEAD_DIM // 2
    frequency = ROPE_BASE ** (-2.0 * np.arange(half, dtype=np.float64) / HEAD_DIM)
    frequency = frequency.astype(np.float32)
    places = np.arange(DEPTH * BLOCK, dtype=np.float32)
    angles = (places[:, None] * frequency[None, :]).astype(np.float64)
    cosine = np.zeros((DEPTH * BLOCK, LANES), np.float32)
    sine = np.zeros((DEPTH * BLOCK, LANES), np.float32)
    cosine[:, :half] = cosine[:, 64 : 64 + half] = np.cos(angles)
    sine[:, 64 : 64 + half] = np.sin(angles)
    sine[:, :half] = -sine[:, 64 : 64 + half]
    return (
        jnp.asarray(cosine.reshape(DEPTH, BLOCK, LANES)),
        jnp.asarray(sine.reshape(DEPTH, BLOCK, LANES)),
    )


def swap_halves(rows):
    return jnp.concatenate([rows[..., 64:], rows[..., :64]], axis=-1)


def load_context(lineage, block, kv, keys, values):
    for step in range(DEPTH):
        node = jnp.maximum(lineage[block, step], 0)
        rows = pl.ds(step * BLOCK, BLOCK)
        keys[rows] = kv[node, :, :LANES]
        values[rows] = kv[node, :, LANES:]


def count_ancestors(lineage, block):
    count = jnp.int32(0)
    for step in range(DEPTH):
        count = count + jnp.where(lineage[block, step] >= 0, 1, 0)
    return count


def attend_kernel(lineage, query, kv, live, out, keys, values):
    block = pl.program_id(0)
    load_context(lineage, block, kv, keys, values)
    scores = lax.dot_general(
        query[0], keys[...], (((1,), (1,)), ((), ())), preferred_element_type=F32
    ) * SCALE
    seen = lax.broadcasted_iota(jnp.int32, (1, DEPTH * BLOCK), 1) < count_ancestors(lineage, block) * BLOCK
    t = lax.broadcasted_iota(jnp.int32, (2 * BLOCK, BLOCK), 0) % BLOCK
    u = lax.broadcasted_iota(jnp.int32, (2 * BLOCK, BLOCK), 1)
    own = jnp.logical_and(u <= t, jnp.logical_or(live[0] > 0.5, u == t))
    scores = jnp.concatenate(
        [
            jnp.where(own, scores[:, :BLOCK], NEGATIVE),
            jnp.where(seen[:, BLOCK:], scores[:, BLOCK:], NEGATIVE),
        ],
        axis=1,
    )
    largest = jnp.max(scores, axis=1, keepdims=True)
    terms = jnp.exp(scores - largest)
    chances = (terms / jnp.sum(terms, axis=1, keepdims=True)).astype(BF16)
    attended = jnp.dot(chances, values[...], preferred_element_type=F32).astype(BF16)
    out[0, :, :LANES] = attended[:BLOCK]
    out[0, :, LANES:] = attended[BLOCK:]


def attend(lineage, query, kv, live):
    return pl.pallas_call(
        attend_kernel,
        grid_spec=pltpu.PrefetchScalarGridSpec(
            num_scalar_prefetch=1,
            grid=(MEMBERS,),
            in_specs=[
                pl.BlockSpec((1, 2 * BLOCK, LANES), lambda b, s: (b, 0, 0)),
                pl.BlockSpec((128, BLOCK, 2 * LANES), lambda b, s: (0, 0, 0)),
                pl.BlockSpec((1, 1, LANES), lambda b, s: (b, 0, 0)),
            ],
            out_specs=pl.BlockSpec((1, BLOCK, 2 * LANES), lambda b, s: (b, 0, 0)),
            scratch_shapes=[
                pltpu.VMEM((DEPTH * BLOCK, LANES), BF16),
                pltpu.VMEM((DEPTH * BLOCK, LANES), BF16),
            ],
        ),
        out_shape=jax.ShapeDtypeStruct((MEMBERS, BLOCK, 2 * LANES), BF16),
        compiler_params=pltpu.CompilerParams(vmem_limit_bytes=VMEM_BYTES),
        name="attend",
    )(lineage, query, kv, live)


def attend_back_kernel(lineage, query, kv, live, grad, grad_query, grad_kv, keys, values, sums):
    block = pl.program_id(0)

    @pl.when(block == 0)
    def _():
        def clear(step, carry):
            sums[step] = jnp.zeros((BLOCK, 2 * LANES), F32)
            return carry

        lax.fori_loop(0, 128, clear, 0)

    load_context(lineage, block, kv, keys, values)
    queries = query[0]
    grads = jnp.concatenate([grad[0, :, :LANES], grad[0, :, LANES:]], axis=0)
    across = (((1,), (1,)), ((), ()))
    scores = lax.dot_general(keys[...], queries, across, preferred_element_type=F32) * SCALE
    seen = lax.broadcasted_iota(jnp.int32, (DEPTH * BLOCK, 1), 0) < count_ancestors(lineage, block) * BLOCK
    u = lax.broadcasted_iota(jnp.int32, (BLOCK, 2 * BLOCK), 0)
    t = lax.broadcasted_iota(jnp.int32, (BLOCK, 2 * BLOCK), 1) % BLOCK
    alive = jnp.transpose(jnp.broadcast_to(live[0], (BLOCK, BLOCK)))
    alive = jnp.concatenate([alive, alive], axis=1)
    own = jnp.logical_and(u <= t, jnp.logical_or(alive > 0.5, u == t))
    scores = jnp.concatenate(
        [
            jnp.where(own, scores[:BLOCK], NEGATIVE),
            jnp.where(seen[BLOCK:], scores[BLOCK:], NEGATIVE),
        ],
        axis=0,
    )
    largest = jnp.max(scores, axis=0, keepdims=True)
    terms = jnp.exp(scores - largest)
    chances = terms / jnp.sum(terms, axis=0, keepdims=True)
    grad_chances = lax.dot_general(values[...], grads, across, preferred_element_type=F32)
    inner = jnp.sum(chances * grad_chances, axis=0, keepdims=True)
    grad_scores = (chances * (grad_chances - inner)).astype(BF16)
    grad_query[0] = (
        lax.dot_general(grad_scores, keys[...], (((0,), (0,)), ((), ())), preferred_element_type=F32) * SCALE
    )
    grad_keys = jnp.dot(grad_scores, queries, preferred_element_type=F32) * SCALE
    grad_values = jnp.dot(chances.astype(BF16), grads, preferred_element_type=F32)
    for step in range(DEPTH):
        node = lineage[block, step]
        rows = slice(step * BLOCK, (step + 1) * BLOCK)

        @pl.when(node >= 0)
        def _():
            sums[node, :, :LANES] += grad_keys[rows]
            sums[node, :, LANES:] += grad_values[rows]

    @pl.when(block == MEMBERS - 1)
    def _():
        def store(step, carry):
            grad_kv[step] = sums[step].astype(BF16)
            return carry

        lax.fori_loop(0, 128, store, 0)


def attend_back(lineage, query, kv, live, grad):
    whole = pl.BlockSpec((128, BLOCK, 2 * LANES), lambda b, s: (0, 0, 0), pipeline_mode=pl.Buffered(1))
    return pl.pallas_call(
        attend_back_kernel,
        grid_spec=pltpu.PrefetchScalarGridSpec(
            num_scalar_prefetch=1,
            grid=(MEMBERS,),
            in_specs=[
                pl.BlockSpec((1, 2 * BLOCK, LANES), lambda b, s: (b, 0, 0)),
                whole,
                pl.BlockSpec((1, 1, LANES), lambda b, s: (b, 0, 0)),
                pl.BlockSpec((1, BLOCK, 2 * LANES), lambda b, s: (b, 0, 0)),
            ],
            out_specs=[
                pl.BlockSpec((1, 2 * BLOCK, LANES), lambda b, s: (b, 0, 0)),
                whole,
            ],
            scratch_shapes=[
                pltpu.VMEM((DEPTH * BLOCK, LANES), BF16),
                pltpu.VMEM((DEPTH * BLOCK, LANES), BF16),
                pltpu.VMEM((128, BLOCK, 2 * LANES), F32),
            ],
        ),
        out_shape=(
            jax.ShapeDtypeStruct((MEMBERS, 2 * BLOCK, LANES), F32),
            jax.ShapeDtypeStruct((128, BLOCK, 2 * LANES), BF16),
        ),
        compiler_params=pltpu.CompilerParams(vmem_limit_bytes=VMEM_BYTES),
        name="attend_back",
    )(lineage, query, kv, live, grad)


def pack_columns(w_query, w_key, w_value, w_gate, w_up):
    rows = w_query.shape[0]
    lanes = ((0, 0),) * 4
    query = jnp.pad(w_query.reshape(rows, MEMBERS, 2, 2, 48), lanes + ((0, 16),)).reshape(rows, MEMBERS, 256)
    key = jnp.pad(w_key.reshape(rows, MEMBERS, 2, 48), lanes[:3] + ((0, 16),)).reshape(rows, MEMBERS, 128)
    value = jnp.pad(w_value.reshape(rows, MEMBERS, 96), lanes[:2] + ((0, 32),))
    gate, up = (
        w.reshape(rows, 16, MEMBERS, 32).transpose(0, 2, 1, 3).reshape(rows, MEMBERS, 512) for w in (w_gate, w_up)
    )
    packed = jnp.concatenate([query, key, value, gate, up], axis=2).transpose(1, 0, 2)
    return jnp.pad(packed, ((0, 0), (0, 4), (0, 0)))


def pack_small(attn_gain, mlp_gain, live, member):
    lane = jnp.arange(LANES)
    spread = lambda gain: jnp.where(
        lane // 12 == member, jnp.take(gain, lane % 12, axis=0), jnp.zeros((), BF16)
    )
    rows = jnp.stack([spread(attn_gain), spread(mlp_gain), live.astype(BF16)])
    return jnp.pad(rows, ((0, 13), (0, 0)))


def norm_back(grad_normed, scaled_rows, gain, rms_rows):
    weighted = grad_normed * gain.astype(F32)
    return (weighted - scaled_rows * jnp.mean(weighted * scaled_rows, axis=1, keepdims=True)) / rms_rows


def shards(
    stream, attn_gain, w_query, w_key, w_value, w_out, mlp_gain, w_gate, w_up, w_down, parent, live_mask, cotangent
):
    me = lax.axis_index("dev")
    member = me % MEMBERS
    lineage = group_lineage(parent, (me // MEMBERS) * MEMBERS)
    depths = jnp.sum(lineage >= 0, axis=1) - 1
    cosine_table, sine_table = rope_tables()
    cosine = jnp.take(cosine_table, depths, axis=0)
    sine = jnp.take(sine_table, depths, axis=0)

    packed = pack_columns(w_query, w_key, w_value, w_gate, w_up)
    small = pack_small(attn_gain, mlp_gain, live_mask, member)
    stream_all, cotangent_all, wide_all, out_all, down_all, gains_all, small_all = opening(
        stream, cotangent, packed, jnp.pad(w_out, ((0, 4), (0, 0))), w_down, small
    )
    stream_all = stream_all.reshape(MEMBERS * BLOCK, D)
    cotangent_all = cotangent_all.reshape(MEMBERS * BLOCK, D)
    wide_all = wide_all.reshape(D, 1536)
    w_attn, w_feed = wide_all[:, :512], wide_all[:, 512:]
    out_all = out_all.reshape(D, D)
    down_all = down_all.reshape(512, D)
    gains = gains_all.reshape(16, 16, LANES)[:, :2, :96].transpose(1, 0, 2).reshape(2, D)
    live = small_all[:, 2:3, :].astype(F32)

    wide = stream_all.astype(F32)
    rms_all = jnp.sqrt(jnp.mean(wide * wide, axis=1, keepdims=True) + EPSILON)
    scaled_all = wide / rms_all
    normed = (scaled_all * gains[0].astype(F32)).astype(BF16)
    raw = jnp.dot(normed, w_attn, preferred_element_type=F32).reshape(MEMBERS, BLOCK, 4, LANES)
    turning = raw[:, :, :3]
    turned = turning * cosine[:, :, None] + swap_halves(turning) * sine[:, :, None]
    query = turned[:, :, :2].astype(BF16).transpose(0, 2, 1, 3).reshape(MEMBERS, 2 * BLOCK, LANES)
    own_context = jnp.concatenate([turned[:, :, 2].astype(BF16), raw[:, :, 3].astype(BF16)], axis=2)
    context = gather_context(own_context.reshape(MEMBERS * BLOCK, 2 * LANES))
    context = context.reshape(128, BLOCK, 2 * LANES)

    attended = deal(attend(lineage, query, context, live), 3)
    attended = attended.reshape(MEMBERS, BLOCK, 2, LANES)[:, :, :, :HEAD_DIM]
    attended = attended.transpose(1, 0, 2, 3).reshape(BLOCK, D)
    stream_wide = stream.astype(F32)
    stream_rms = jnp.sqrt(jnp.mean(stream_wide * stream_wide, axis=1, keepdims=True) + EPSILON)
    middle = stream_wide + jnp.dot(attended, out_all, preferred_element_type=F32)
    branch_rms = jnp.sqrt(jnp.mean(middle * middle, axis=1, keepdims=True) + EPSILON)
    scaled_middle = middle / branch_rms
    mid_normed = (scaled_middle * gains[1].astype(F32)).astype(BF16)

    mid_all = group_gather(mid_normed, 8).reshape(MEMBERS * BLOCK, D)
    gate_up = jnp.dot(mid_all, w_feed, preferred_element_type=F32)
    gate_value, up_value = gate_up[:, :512], gate_up[:, 512:]
    sigmoid_gate = jax.nn.sigmoid(gate_value)
    silu_gate = gate_value * sigmoid_gate
    activated = (silu_gate * up_value).astype(BF16)
    down_terms = jnp.dot(activated, down_all, preferred_element_type=F32).astype(BF16)

    grad_act = jnp.einsum("td,fd->tf", cotangent_all, down_all, preferred_element_type=F32)
    grad_gate = (grad_act * up_value * sigmoid_gate * (1.0 + gate_value * (1.0 - sigmoid_gate))).astype(BF16)
    grad_up = (grad_act * silu_gate).astype(BF16)
    grad_feed = jnp.concatenate([grad_gate, grad_up], axis=1)
    grad_mid_terms = jnp.einsum("tf,df->td", grad_feed, w_feed, preferred_element_type=F32).astype(BF16)
    feed_terms = jnp.einsum("td,tf->df", mid_all, grad_feed, preferred_element_type=F32).astype(BF16)
    down_grad_terms = jnp.einsum("tf,td->fd", activated, cotangent_all, preferred_element_type=F32).astype(BF16)
    grad_mid_normed, feed_grad, down_grad = feed_exchange(
        grad_mid_terms.reshape(4, 2, BLOCK, D),
        feed_terms.reshape(4, 4, 96, 1024),
        down_grad_terms.reshape(4, 4, 32, D),
    )
    gate_grad, up_grad = (
        feed_grad[:, :, part : part + 512].reshape(MEMBERS, 12, 16, 32).transpose(1, 2, 0, 3).reshape(12, FF)
        for part in (0, 512)
    )

    gain_two_terms = jnp.sum(grad_mid_normed * scaled_middle, axis=0)
    grad_middle = cotangent.astype(F32) + norm_back(grad_mid_normed, scaled_middle, gains[1], branch_rms)
    grad_branch = grad_middle.astype(BF16)
    out_terms = jnp.einsum("tq,td->qd", attended, grad_branch, preferred_element_type=F32).astype(BF16)
    grad_attended = jnp.einsum("td,qd->tq", grad_branch, out_all, preferred_element_type=F32).astype(BF16)
    grad_attended = jnp.pad(
        grad_attended.reshape(BLOCK, MEMBERS, 2, HEAD_DIM).transpose(1, 0, 2, 3), ((0, 0), (0, 0), (0, 0), (0, 32))
    ).reshape(MEMBERS, BLOCK, 2 * LANES)
    grad_heads = deal(grad_attended, 5)
    grad_query, context_terms = attend_back(lineage, query, context, live, grad_heads)
    grad_context, down_sum = context_back(
        context_terms.reshape(4, 4, MEMBERS * BLOCK, 2 * LANES), down_terms.reshape(4, 2, BLOCK, D)
    )
    mixed_out = (middle + down_sum).astype(BF16)

    grad_context = grad_context.reshape(MEMBERS, BLOCK, 2, LANES)
    grad_turned = jnp.concatenate(
        [grad_query.reshape(MEMBERS, 2, BLOCK, LANES).transpose(0, 2, 1, 3), grad_context[:, :, :1]], axis=2
    )
    grad_turning = grad_turned * cosine[:, :, None] - swap_halves(grad_turned) * sine[:, :, None]
    grad_raw = jnp.concatenate([grad_turning.astype(BF16), grad_context[:, :, 1:].astype(BF16)], axis=2)
    grad_raw = grad_raw.reshape(MEMBERS * BLOCK, 512)
    attn_terms = jnp.einsum("td,tq->dq", normed, grad_raw, preferred_element_type=F32).astype(BF16)
    grad_normed_terms = jnp.einsum("tq,dq->td", grad_raw, w_attn, preferred_element_type=F32)
    gain_one_terms = jnp.sum(grad_normed_terms * scaled_all, axis=0)
    gain_terms = jnp.stack([gain_one_terms, gain_two_terms]).reshape(2, 16, 96).transpose(1, 0, 2)
    gain_terms = jnp.pad(gain_terms, ((0, 0), (0, 6), (0, 32))).reshape(4, 4, 8, LANES)
    grad_normed, attn_grad, out_grad, gain_grad = closing(
        grad_normed_terms.astype(BF16).reshape(4, 2, BLOCK, D),
        attn_terms.reshape(4, 4, 96, 512),
        out_terms.reshape(4, 4, 96, D),
        gain_terms,
    )
    stream_grad = grad_middle + norm_back(grad_normed, stream_wide / stream_rms, gains[0], stream_rms)
    query_grad = attn_grad[:, :, :256].reshape(MEMBERS, 12, 2, 2, 64)[..., :48]
    query_grad = query_grad.transpose(1, 0, 2, 3, 4).reshape(12, D)
    key_grad = attn_grad[:, :, 256:384].reshape(MEMBERS, 12, 2, 64)[..., :48]
    key_grad = key_grad.transpose(1, 0, 2, 3).reshape(12, 768)
    value_grad = attn_grad[:, :, 384:480].transpose(1, 0, 2).reshape(12, 768)
    out_grad = jnp.sum(out_grad.reshape(4, 2, 12, 768), axis=0).transpose(1, 0, 2).reshape(12, D)
    own_gains = lax.dynamic_slice(gain_grad, (0, member * 12), (2, 12))
    return (
        mixed_out, stream_grad, own_gains[0], query_grad, key_grad, value_grad, out_grad, own_gains[1],
        gate_grad, up_grad, down_grad, stream_rms[:, 0], branch_rms[:, 0],
    )


def solution(mesh):
    rows, line = P("dev", None), P("dev")
    return jax.shard_map(
        shards,
        mesh=mesh,
        in_specs=(rows, line, rows, rows, rows, rows, line, rows, rows, rows, P(), line, rows),
        out_specs=(rows, rows, line, rows, rows, rows, rows, line, rows, rows, rows, line, line),
        check_vma=False,
    )
```

```python
import functools

import jax
import jax.numpy as jnp
import numpy as np
from jax import lax
from jax.experimental import pallas as pl
from jax.experimental.pallas import tpu as pltpu
from jax.sharding import PartitionSpec as P

HEADS = 16
KV_HEADS = 8
HEAD_DIM = 96
BLOCK = 128
DEPTH = 10
D = 1536
FF = 4096
MEMBERS = 8
LANES = 128

EPSILON = 1e-05
ROPE_BASE = 100000.0
NEGATIVE = -1e30
SCALE = HEAD_DIM ** (-0.5)
MESH = pl.DeviceIdType.MESH
BF16 = jnp.bfloat16
F32 = jnp.float32
VMEM_BYTES = 56 * 2**20


def spot():
    me = lax.axis_index("dev")
    return me // 32, (me // 8) % 4, (me // 2) % 4, me % 2


def device_of(x, y, z, c):
    return ((x % 4) * 4 + (y % 4)) * 8 + (z % 4) * 2 + c


def greet(peers):
    barrier = pltpu.get_barrier_semaphore()
    for peer in peers:
        pl.semaphore_signal(barrier, inc=1, device_id=(peer,), device_id_type=MESH)
    pl.semaphore_wait(barrier, len(peers))


def axis_peers(x, y, z, c, far):
    steps = (1, 2, 3) if far else (1, 3)
    return [device_of(x + k, y, z, c) for k in steps] + [device_of(x, y + k, z, c) for k in steps]


def group_peer(x, y, z, c, k):
    member = (z * 2 + c + k) % MEMBERS
    return (x * 4 + y) * MEMBERS + member


class Wire:
    def __init__(self, send_sems, recv_sems):
        self.send_sems = send_sems
        self.recv_sems = recv_sems
        self.used = 0
        self.open = []

    def reserve(self, count):
        self.used += count
        return self.used - count

    def make(self, slot, source, target, peer):
        return pltpu.make_async_remote_copy(
            src_ref=source,
            dst_ref=target,
            send_sem=self.send_sems.at[slot],
            recv_sem=self.recv_sems.at[slot],
            device_id=(peer,),
            device_id_type=MESH,
        )

    def send(self, source, target, peer):
        copy = self.make(self.reserve(1), source, target, peer)
        copy.start()
        self.open.append(copy)
        return copy

    def close(self):
        for copy in self.open:
            copy.wait_send()
        self.open = []


class Ring:
    def __init__(self, wire, own, part, place, up, down):
        self.wire, self.own, self.part = wire, own, part
        self.place, self.up, self.down = place, up, down

    def begin(self):
        send, part, place = self.wire.send, self.part, self.place
        self.low_up = send(self.own(0), part(place, 0), self.up)
        self.high_down = send(self.own(1), part(place, 1), self.down)
        self.high_up = send(self.own(1), part(place, 1), self.up)
        self.low_down = send(self.own(0), part(place, 0), self.down)

    def relay(self):
        before, after = (self.place + 3) % 4, (self.place + 1) % 4
        self.low_up.wait_recv()
        self.far_up = self.wire.send(self.part(before, 0), self.part(before, 0), self.up)
        self.high_down.wait_recv()
        self.far_down = self.wire.send(self.part(after, 1), self.part(after, 1), self.down)

    def near(self):
        self.high_up.wait_recv()
        self.low_down.wait_recv()

    def far(self):
        self.far_up.wait_recv()
        self.far_down.wait_recv()


class PlaneGather:
    def __init__(self, wire, own, out, cut, xyzc):
        self.wire, self.own, self.out, self.cut = wire, own, out, cut
        x, y, z, c = xyzc
        self.x, self.y = x, y
        self.x_up, self.x_down = device_of(x + 1, y, z, c), device_of(x + 3, y, z, c)
        self.y_up, self.y_down = device_of(x, y + 1, z, c), device_of(x, y + 3, z, c)

    def pair(self, one_own, one_part, two_own, two_part, one_on_x):
        on_x = (self.x, self.x_up, self.x_down)
        on_y = (self.y, self.y_up, self.y_down)
        cut = self.cut
        self.one = Ring(
            self.wire,
            lambda side: one_own(cut(0, side)),
            lambda place, side: one_part(place, cut(0, side)),
            *(on_x if one_on_x else on_y),
        )
        self.two = Ring(
            self.wire,
            lambda side: two_own(cut(1, side)),
            lambda place, side: two_part(place, cut(1, side)),
            *(on_y if one_on_x else on_x),
        )
        self.one.begin()
        self.two.begin()

    def first(self):
        own, out, x, y = self.own, self.out, self.x, self.y
        self.pair(
            lambda q: own.at[q],
            lambda place, q: out.at[(place, y) + q],
            lambda q: own.at[q],
            lambda place, q: out.at[(x, place) + q],
            True,
        )

    def relay(self):
        self.one.relay()
        self.two.relay()

    def settle(self):
        for ring in (self.one, self.two):
            ring.near()
            ring.far()

    def second(self):
        out, x, y = self.out, self.x, self.y
        every = slice(None)
        self.pair(
            lambda q: out.at[(every, y) + q],
            lambda place, q: out.at[(every, place) + q],
            lambda q: out.at[(x, every) + q],
            lambda place, q: out.at[(place, every) + q],
            False,
        )


def quarter(rows, cols):
    return lambda half, side: (pl.ds(half * (rows // 2), rows // 2), pl.ds(side * (cols // 2), cols // 2))


def quarter_units(half, side):
    return (pl.ds(half * 6 + side * 3, 3),)


class GroupGather:
    def __init__(self, wire, own, out, xyzc):
        self.wire, self.own, self.out = wire, own, out
        x, y, z, c = xyzc
        self.z, self.c = z, c
        self.sibling = device_of(x, y, z, 1 - c)
        half = out.shape[2] // 2
        self.ring = Ring(
            wire,
            lambda side: own.at[pl.ds(side * half, half)],
            lambda place, side: out.at[place, c, pl.ds(side * half, half)],
            z, device_of(x, y, z + 1, c), device_of(x, y, z + 3, c),
        )
        self.crossed = []

    def begin(self):
        self.ring.begin()
        self.crossed.append(self.wire.send(self.own, self.out.at[self.z, self.c], self.sibling))

    def cross(self, k):
        piece = self.out.at[(self.z + k) % 4, self.c]
        self.crossed.append(self.wire.send(piece, piece, self.sibling))

    def relay(self):
        self.ring.relay()

    def near(self):
        self.ring.near()
        self.cross(1)
        self.cross(3)

    def far(self):
        self.ring.far()
        self.cross(2)

    def finish(self):
        for copy in self.crossed:
            copy.wait_recv()


class PlaneScatter:
    def __init__(self, wire, terms, scratch, xyzc):
        self.wire, self.terms = wire, terms
        *mine, self.first_in, self.summed, self.second_in, self.local_sem = scratch
        self.mine = mine[0] if mine else None
        self.x, self.y, self.z, self.c = xyzc
        self.half = terms.shape[2] // 2

    def peer(self, along_x, k):
        if along_x:
            return device_of(self.x + k, self.y, self.z, self.c)
        return device_of(self.x, self.y + k, self.z, self.c)

    def line(self, half, place):
        rows = pl.ds(half * self.half, self.half)
        if half == 0:
            return self.terms.at[place, :, rows]
        return self.terms.at[:, place, rows]

    def own(self, half, line):
        if self.mine is not None:
            return self.mine[half, line]
        rows = slice(half * self.half, (half + 1) * self.half)
        if half == 0:
            return self.terms[self.x, line, rows]
        return self.terms[line, self.y, rows]

    def first(self):
        self.copies = []
        self.locals = []
        if self.mine is not None:
            for half, place in ((0, self.x), (1, self.y)):
                copy = pltpu.make_async_copy(
                    self.line(half, place), self.mine.at[half], self.local_sem.at[half]
                )
                copy.start()
                self.locals.append(copy)
        for k in (2, 1, 3):
            for half, place in ((0, self.x), (1, self.y)):
                self.copies.append(
                    self.wire.send(
                        self.line(half, (place + k) % 4),
                        self.first_in.at[half, k - 1],
                        self.peer(half == 0, k),
                    )
                )

    def add_first(self):
        for copy in self.locals:
            copy.wait()
        for copy in self.copies:
            copy.wait_recv()
        for half in range(2):

            def body(line, carry):
                total = self.own(half, line).astype(F32)
                for k in range(3):
                    total = total + self.first_in[half, k, line].astype(F32)
                self.summed[half, line] = total.astype(BF16)
                return carry

            lax.fori_loop(0, 4, body, 0)

    def second(self):
        self.copies = []
        for k in (2, 1, 3):
            for half, place in ((0, self.y), (1, self.x)):
                self.copies.append(
                    self.wire.send(
                        self.summed.at[half, (place + k) % 4],
                        self.second_in.at[half, k - 1],
                        self.peer(half == 1, k),
                    )
                )

    def total(self, half):
        place = (self.y, self.x)[half]
        total = self.summed[half, place].astype(F32)
        for k in range(3):
            total = total + self.second_in[half, k].astype(F32)
        return total

    def arrive(self):
        for copy in self.copies:
            copy.wait_recv()


def scatter_scratch(rows, *rest, mine=True):
    piece = (rows // 2,) + rest
    own = [pltpu.VMEM((2, 4) + piece, BF16)] if mine else []
    return own + [
        pltpu.VMEM((2, 3, 4) + piece, BF16),
        pltpu.VMEM((2, 4) + piece, BF16),
        pltpu.VMEM((2, 3) + piece, BF16),
        pltpu.SemaphoreType.DMA((2,)),
    ]


class GroupScatter:
    def __init__(self, wire, terms, mine, crossed_in, summed, ring_in, local_sem, xyzc):
        self.wire, self.terms = wire, terms
        self.mine, self.crossed_in, self.summed, self.ring_in = mine, crossed_in, summed, ring_in
        self.x, self.y, self.z, self.c = xyzc
        self.local_sem = local_sem

    def begin(self):
        self.local = pltpu.make_async_copy(self.terms.at[:, self.c], self.mine, self.local_sem)
        self.local.start()
        sibling = device_of(self.x, self.y, self.z, 1 - self.c)
        self.crossed = {}
        for k in (2, 1, 3, 0):
            place = (self.z + k) % 4
            self.crossed[k] = self.wire.send(
                self.terms.at[place, 1 - self.c], self.crossed_in.at[place], sibling
            )

    def turn(self):
        self.local.wait()
        self.copies = []
        for k in (2, 1, 3):
            place = (self.z + k) % 4
            self.crossed[k].wait_recv()

            def body(tile, carry):
                total = self.mine[place, tile].astype(F32) + self.crossed_in[place, tile].astype(F32)
                self.summed[place, tile] = total.astype(BF16)
                return carry

            lax.fori_loop(0, 12, body, 0)
            self.copies.append(
                self.wire.send(
                    self.summed.at[place],
                    self.ring_in.at[k - 1],
                    device_of(self.x, self.y, self.z + k, self.c),
                )
            )

    def finish(self, out):
        self.crossed[0].wait_recv()
        for copy in self.copies:
            copy.wait_recv()
        for tile in range(12):
            total = self.mine[self.z, tile].astype(F32) + self.crossed_in[self.z, tile].astype(F32)
            for k in range(3):
                total = total + self.ring_in[k, tile].astype(F32)
            out[:, tile * LANES : (tile + 1) * LANES] = total


def group_scatter_scratch():
    return [
        pltpu.VMEM((4, 12, BLOCK, LANES), BF16),
        pltpu.VMEM((4, 12, BLOCK, LANES), BF16),
        pltpu.VMEM((4, 12, BLOCK, LANES), BF16),
        pltpu.VMEM((3, 12, BLOCK, LANES), BF16),
        pltpu.SemaphoreType.DMA,
    ]


def wire_scratch(count):
    return [pltpu.SemaphoreType.DMA((count,)), pltpu.SemaphoreType.DMA((count,))]


ANY = pl.BlockSpec(memory_space=pl.ANY)
INVMEM = pl.BlockSpec(memory_space=pltpu.VMEM)


def communicate(kernel, out_shapes, in_specs, out_specs, scratch, ident, name, vmem=VMEM_BYTES):
    return pl.pallas_call(
        kernel,
        out_shape=out_shapes,
        in_specs=in_specs,
        out_specs=out_specs,
        scratch_shapes=scratch,
        compiler_params=pltpu.CompilerParams(
            collective_id=ident, has_side_effects=True, vmem_limit_bytes=vmem
        ),
        name=name,
    )


def opening_kernel(
    stream, packed, w_out, small,
    stream_all, attn_all, feed_own, out_all, gains_all, small_all,
    packed_in, out_in, small_in, wide_tall, out_tall, wide_own, out_own, gain_own,
    send_sems, recv_sems, local_sems,
):
    xyzc = x, y, z, c = spot()
    j = z * 2 + c
    wire = Wire(send_sems, recv_sems)
    group = [group_peer(x, y, z, c, k) for k in range(1, MEMBERS)]
    greet(group + axis_peers(x, y, z, c, True))
    locals_ = []

    def keep(source, target):
        copy = pltpu.make_async_copy(source, target, local_sems.at[len(locals_)])
        copy.start()
        locals_.append(copy)

    dealt = []
    for k in range(1, MEMBERS):
        member = (j + k) % MEMBERS
        half = pl.ds(pl.multiple_of((member % 2) * 768, 768), 768)
        dealt.append(wire.send(packed.at[member], packed_in.at[j], group[k - 1]))
        dealt.append(wire.send(w_out.at[:, half], out_in.at[j], group[k - 1]))
        dealt.append(wire.send(small, small_in.at[j], group[k - 1]))
    own_half = pl.ds(pl.multiple_of(c * 768, 768), 768)
    keep(packed.at[j], packed_in.at[j])
    keep(w_out.at[:, own_half], out_in.at[j])
    keep(small, small_in.at[j])
    keep(stream, stream_all.at[z, c])
    streams = GroupGather(wire, stream, stream_all, xyzc)
    streams.begin()

    for copy in dealt:
        copy.wait_recv()
    for copy in locals_[:3]:
        copy.wait()
    for member in range(MEMBERS):
        rows = pl.ds(member * 12, 12)
        wide_tall[rows] = packed_in[member].astype(F32)[:12]
        out_tall[rows] = out_in[member].astype(F32)[:12]
    wide_own[...] = wide_tall[...].astype(BF16)
    out_own[...] = out_tall[...].astype(BF16)
    gain = small_in[0].astype(F32)
    for member in range(1, MEMBERS):
        gain = gain + small_in[member].astype(F32)
    gain_own[...] = gain.astype(BF16)

    attn_own = wide_own.at[:, pl.ds(0, 512)]
    keep(attn_own, attn_all.at[x, y])
    keep(out_own, out_all.at[x, y, :, own_half])
    keep(gain_own, gains_all.at[x, y])
    keep(small_in, small_all)
    keep(wide_own.at[:, pl.ds(512, 1024)], feed_own)

    half_out = out_all.at[:, :, :, own_half]
    attn = PlaneGather(wire, attn_own, attn_all, quarter(96, 512), xyzc)
    outs = PlaneGather(wire, out_own, half_out, quarter(96, 768), xyzc)
    planes = (attn, outs)
    tiny = [
        wire.send(gain_own, gains_all.at[x, y], device_of(x + k, y, z, c)) for k in range(1, 4)
    ]
    for plane in planes:
        plane.first()
    streams.relay()
    for plane in planes:
        plane.relay()
    for copy in locals_[3:]:
        copy.wait()
    for copy in tiny:
        copy.wait_recv()
    line = gains_all.at[:, y]
    tiny = [wire.send(line, line, device_of(x, y + k, z, c)) for k in range(1, 4)]
    for plane in planes:
        plane.settle()
        plane.second()
    streams.near()
    streams.far()
    for plane in planes:
        plane.relay()
    outs.settle()
    sibling = device_of(x, y, z, 1 - c)
    swapped = wire.send(half_out, half_out, sibling)
    attn.settle()
    streams.finish()
    for copy in tiny:
        copy.wait_recv()
    swapped.wait_recv()
    wire.close()


def opening(stream, packed, w_out, small):
    shape = jax.ShapeDtypeStruct
    return communicate(
        opening_kernel,
        (
            shape((4, 2, BLOCK, D), BF16),
            shape((4, 4, 96, 512), BF16),
            shape((96, 1024), BF16),
            shape((4, 4, 96, 1536), BF16),
            shape((4, 4, 16, LANES), BF16),
            shape((MEMBERS, 16, LANES), BF16),
        ),
        [ANY] * 4,
        (ANY,) * 6,
        [
            pltpu.VMEM((MEMBERS, 16, 1536), BF16),
            pltpu.VMEM((MEMBERS, 16, 768), BF16),
            pltpu.VMEM((MEMBERS, 16, LANES), BF16),
            pltpu.VMEM((96, 1536), F32),
            pltpu.VMEM((96, 768), F32),
            pltpu.VMEM((96, 1536), BF16),
            pltpu.VMEM((96, 768), BF16),
            pltpu.VMEM((16, LANES), BF16),
        ]
        + wire_scratch(86)
        + [pltpu.SemaphoreType.DMA((9,))],
        1,
        "opening",
    )(stream, packed, w_out, small)


def key_unit(member):
    return member + jnp.where(member >= 6, 6, 0) + jnp.where(member >= 7, 1, 0)


def value_unit(member):
    return member + 6 + jnp.where(member >= 6, 1, 0) + jnp.where(member >= 7, 1, 0)


def lane_of(shape):
    return lax.broadcasted_iota(jnp.int32, shape, len(shape) - 1)


def pack_tile(unit, extra, place):
    return jnp.where(lane_of(unit.shape) < HEAD_DIM, unit, pltpu.roll(extra, (96 - 32 * place) % LANES, 1))


def unpack_extra(tiles):
    lane = lane_of(tiles[0].shape)
    extra = jnp.where(lane < 32, pltpu.roll(tiles[0], 32, 1), 0.0)
    extra = jnp.where(jnp.logical_and(lane >= 32, lane < 64), pltpu.roll(tiles[1], 64, 1), extra)
    return jnp.where(jnp.logical_and(lane >= 64, lane < 96), pltpu.roll(tiles[2], 96, 1), extra)


def swap_halves(rows):
    lane = lane_of(rows.shape)
    return jnp.where(lane < HEAD_DIM // 2, pltpu.roll(rows, LANES - 48, 1), pltpu.roll(rows, 48, 1))


def rope_tables():
    half = HEAD_DIM // 2
    frequency = ROPE_BASE ** (-2.0 * np.arange(half, dtype=np.float64) / HEAD_DIM)
    frequency = frequency.astype(np.float32)
    places = np.arange(DEPTH * BLOCK, dtype=np.float32)
    angles = (places[:, None] * frequency[None, :]).astype(np.float64)
    cosine = np.zeros((DEPTH * BLOCK, LANES), np.float32)
    sine = np.zeros((DEPTH * BLOCK, LANES), np.float32)
    cosine[:, :half] = cosine[:, half:HEAD_DIM] = np.cos(angles)
    sine[:, half:HEAD_DIM] = np.sin(angles)
    sine[:, :half] = -sine[:, half:HEAD_DIM]
    return (
        jnp.asarray(cosine.reshape(DEPTH, BLOCK, LANES)),
        jnp.asarray(sine.reshape(DEPTH, BLOCK, LANES)),
    )


def count_ancestors(lineage, block):
    count = jnp.int32(0)
    for step in range(DEPTH):
        count = count + jnp.where(lineage[block, step] >= 0, 1, 0)
    return count


def write_lineage(parent, first, lineage):
    def one(block, carry):
        def hop(step, node):
            lineage[block, step] = node
            above = parent[jnp.maximum(node, 0)]
            return jnp.where(node >= 0, above, -1)

        lax.fori_loop(0, DEPTH, hop, first[0] + block)
        return carry

    lax.fori_loop(0, MEMBERS, one, 0)


def project_kernel(
    parent, first, stream, w_attn, gain, cosine, sine, lineage, normed, query, packed, units
):
    step = pl.program_id(0)

    @pl.when(step == 0)
    def _():
        write_lineage(parent, first, lineage)

    wide = stream[...].astype(F32)
    rms = jnp.sqrt(jnp.mean(wide * wide, axis=1, keepdims=True) + EPSILON)
    rows = (wide / rms * gain[...]).astype(BF16)
    normed[...] = rows
    raw = jnp.dot(rows, w_attn[...], preferred_element_type=F32)
    for part in range(2):
        block = step * 2 + part
        depth = count_ancestors(lineage, block) - 1
        cos, sin = cosine[depth], sine[depth]
        mine = raw[part * BLOCK : (part + 1) * BLOCK]

        def turn(head):
            v = mine[:, head * LANES : (head + 1) * LANES]
            return v * cos + swap_halves(v) * sin

        query[part, :BLOCK] = turn(0).astype(BF16)
        query[part, BLOCK:] = turn(1).astype(BF16)
        units[key_unit(block)] = turn(2)
        units[value_unit(block)] = mine[:, 3 * LANES :]

    @pl.when(step == 3)
    def _():
        for tile in range(12):
            packed[tile] = pack_tile(units[tile], units[12 + tile // 3], tile % 3).astype(BF16)


def project(parent, first, stream_all, w_attn, gain, cosine, sine):
    def whole(shape):
        return pl.BlockSpec(shape, lambda i, p, f: (0,) * len(shape))

    return pl.pallas_call(
        project_kernel,
        grid_spec=pltpu.PrefetchScalarGridSpec(
            num_scalar_prefetch=2,
            grid=(4,),
            in_specs=[
                pl.BlockSpec((2 * BLOCK, D), lambda i, p, f: (i, 0)),
                whole((D, 512)),
                whole((1, D)),
                whole((DEPTH, BLOCK, LANES)),
                whole((DEPTH, BLOCK, LANES)),
            ],
            out_specs=[
                pl.BlockSpec(memory_space=pltpu.SMEM),
                pl.BlockSpec((2 * BLOCK, D), lambda i, p, f: (i, 0)),
                pl.BlockSpec((2, 2 * BLOCK, LANES), lambda i, p, f: (i, 0, 0)),
                whole((12, BLOCK, LANES)),
            ],
            scratch_shapes=[pltpu.VMEM((16, BLOCK, LANES), F32)],
        ),
        out_shape=(
            jax.ShapeDtypeStruct((MEMBERS, DEPTH), jnp.int32),
            jax.ShapeDtypeStruct((MEMBERS * BLOCK, D), BF16),
            jax.ShapeDtypeStruct((MEMBERS, 2 * BLOCK, LANES), BF16),
            jax.ShapeDtypeStruct((12, BLOCK, LANES), BF16),
        ),
        compiler_params=pltpu.CompilerParams(vmem_limit_bytes=VMEM_BYTES),
        name="project",
    )(parent, first.reshape(1), stream_all, w_attn, gain, cosine, sine)


def attend_block(lineage, block, queries, alive, load, keys, values):
    for step in range(DEPTH):
        node = jnp.maximum(lineage[block, step], 0)
        rows = pl.ds(step * BLOCK, BLOCK)
        keys[rows] = load(node, key_unit(lax.rem(node, 8)))
        values[rows] = load(node, value_unit(lax.rem(node, 8)))
    scores = lax.dot_general(
        queries, keys[...], (((1,), (1,)), ((), ())), preferred_element_type=F32
    ) * SCALE
    limit = count_ancestors(lineage, block) * BLOCK
    seen = lax.broadcasted_iota(jnp.int32, (1, DEPTH * BLOCK), 1) < limit
    t = lax.broadcasted_iota(jnp.int32, (2 * BLOCK, BLOCK), 0) % BLOCK
    u = lax.broadcasted_iota(jnp.int32, (2 * BLOCK, BLOCK), 1)
    own = jnp.logical_and(u <= t, jnp.logical_or(alive > 0.5, u == t))
    scores = jnp.concatenate(
        [
            jnp.where(own, scores[:, :BLOCK], NEGATIVE),
            jnp.where(seen[:, BLOCK:], scores[:, BLOCK:], NEGATIVE),
        ],
        axis=1,
    )
    largest = jnp.max(scores, axis=1, keepdims=True)
    terms = jnp.exp(scores - largest)
    chances = (terms / jnp.sum(terms, axis=1, keepdims=True)).astype(BF16)
    return jnp.dot(chances, values[...], preferred_element_type=F32).astype(BF16)


def middle_kernel(
    lineage, live, gain, query, stream, cotangent, own_kv, w_out, own_feed, own_down,
    kv_out, middle, rms_out, grad_middle, grads_in, down_terms, feed_grad, down_grad, out_terms, gain_terms,
    kv, w_out_all, w_feed, w_down, mid_all, cot_all, acts, grad_feed, crossed_in, ring_in,
    feed_terms, feed_first, feed_summed, feed_second, feed_sem,
    wide_terms, wide_first, wide_summed, wide_second, wide_sem,
    keys, values, att_out, att_in, att_pad, grads_out, feed_tall, feed_dealt,
    send_sems, recv_sems, local_sems,
):
    xyzc = x, y, z, c = spot()
    j = z * 2 + c
    base = (x * 4 + y) * MEMBERS
    sibling = device_of(x, y, z, 1 - c)
    wire = Wire(send_sems, recv_sems)
    group = [group_peer(x, y, z, c, k) for k in range(1, MEMBERS)]
    greet(group + axis_peers(x, y, z, c, True))
    across, down_first = (((1,), (1,)), ((), ())), (((0,), (0,)), ((), ()))
    locals_ = []

    def keep(source, target):
        copy = pltpu.make_async_copy(source, target, local_sems.at[len(locals_)])
        copy.start()
        locals_.append(copy)
        return copy

    kept = keep(own_kv, kv.at[x, y, pl.ds(0, 12)])
    pairs = PlaneGather(wire, own_kv, kv, quarter_units, xyzc)
    pairs.first()
    cot_kept = keep(cotangent, cot_all.at[z, c])
    cotangents = GroupGather(wire, cotangent, cot_all, xyzc)
    cotangents.begin()
    out_kept = keep(w_out, w_out_all.at[:, pl.ds(0, 96)])
    feed_kept = keep(own_feed, w_feed.at[x, y])
    down_kept = keep(own_down, w_down.at[x, y])
    w_out_all[:, 96:, :] = jnp.zeros((16, 32, D), BF16)
    pairs.relay()
    kept.wait()
    pairs.settle()
    pairs.second()
    cotangents.relay()
    cotangents.near()
    cotangents.far()
    pairs.relay()
    feed = PlaneGather(wire, own_feed, w_feed, quarter(96, 1024), xyzc)
    down = PlaneGather(wire, own_down, w_down, quarter(32, 1536), xyzc)
    feed.first()
    down.first()
    pairs.settle()

    def unpack(line, carry):
        a, b = line // 4, line % 4
        for extra in range(4):
            tiles = [kv[a, b, extra * 3 + k].astype(F32) for k in range(3)]
            kv[a, b, 12 + extra] = unpack_extra(tiles).astype(BF16)
        return carry

    lax.fori_loop(0, 16, unpack, 0)
    kv_copied = keep(kv, kv_out)

    att_slot = wire.reserve(MEMBERS - 1)

    def load(node, unit):
        return kv[lax.div(node, 32), lax.rem(lax.div(node, 8), 4), unit]

    def att_copy(k):
        block = (j + 1 + k) % MEMBERS
        return wire.make(att_slot + k, att_out.at[block], att_in.at[j], base + block)

    def attend(k, carry):
        block = (j + 1 + k) % MEMBERS
        attended = attend_block(lineage, block, query[block], live[block], load, keys, values)
        att_out[block, :, :LANES] = attended[:BLOCK]
        att_out[block, :, LANES:] = attended[BLOCK:]

        @pl.when(k < MEMBERS - 1)
        def _():
            att_copy(k).start()

        return carry

    lax.fori_loop(0, 3, attend, 0)
    feed.relay()
    down.relay()
    lax.fori_loop(3, 6, attend, 0)
    feed.settle()
    down.settle()
    feed_kept.wait()
    down_kept.wait()
    feed.second()
    down.second()
    lax.fori_loop(6, MEMBERS, attend, 0)
    feed.relay()
    down.relay()
    att_in[j] = att_out[j]
    for k in range(MEMBERS - 1):
        att_copy(k).wait_recv()

    for member in range(MEMBERS):
        att_pad[:, member * 256 : (member + 1) * 256] = att_in[member]
    out_kept.wait()

    def project_out(step, carry):
        cols = pl.ds(pl.multiple_of(step * 512, 512), 512)
        weights = w_out_all[:, :, cols].reshape(16 * LANES, 512)
        branch = jnp.dot(att_pad[...], weights, preferred_element_type=F32)
        middle[:, cols] = stream[:, cols].astype(F32) + branch
        return carry

    lax.fori_loop(0, 3, project_out, 0)
    rms = jnp.sqrt(jnp.mean(middle[...] * middle[...], axis=1, keepdims=True) + EPSILON)
    rms_out[...] = jnp.broadcast_to(rms, (BLOCK, LANES))
    mid_all[z, c] = (middle[...] / rms * gain[...]).astype(BF16)
    mids = GroupGather(wire, mid_all.at[z, c], mid_all, xyzc)
    mids.begin()
    mids.relay()
    mids.near()
    mids.far()
    feed.settle()
    down.settle()
    kv_copied.wait()
    cot_kept.wait()
    cotangents.finish()
    mids.finish()
    wire.close()
    for k in range(MEMBERS - 1):
        att_copy(k).wait_send()

    crossed_slot, ring_slot = wire.reserve(4), wire.reserve(3)

    def crossed_copy(step):
        place = (z + 1 + step) % 4
        return wire.make(
            crossed_slot + step, kv.at[place, 2 + 1 - c, pl.ds(0, 12)], crossed_in.at[place], sibling
        )

    def ring_copy(step):
        place = (z + 1 + step) % 4
        return wire.make(
            ring_slot + step, kv.at[place, 2 + c, pl.ds(0, 12)], ring_in.at[step], device_of(x, y, z + 1 + step, c)
        )

    def turn(step):
        place = (z + 1 + step) % 4
        crossed_copy(step).wait_recv()

        def add(tile, carry):
            total = kv[place, 2 + c, tile].astype(F32) + crossed_in[place, tile].astype(F32)
            kv[place, 2 + c, tile] = total.astype(BF16)
            return carry

        lax.fori_loop(0, 12, add, 0)
        ring_copy(step).start()

    def feed_forward(step, carry):
        place = (z + 1 + step) % 4
        rows = mid_all[place].reshape(2 * BLOCK, D)
        weights = w_feed[...].reshape(D, 1024)
        both = jnp.dot(rows, weights, preferred_element_type=F32)
        gate, up = both[:, :512], both[:, 512:]
        sigmoid = 1.0 / (1.0 + jnp.exp(-gate))
        silu = gate * sigmoid
        activated = (silu * up).astype(BF16)
        acts[place] = activated
        cot = cot_all[place].reshape(2 * BLOCK, D)
        down_rows = w_down[...].reshape(512, D)
        grad_act = lax.dot_general(cot, down_rows, across, preferred_element_type=F32)
        grad_gate = (grad_act * up * sigmoid * (1.0 + gate * (1.0 - sigmoid))).astype(BF16)
        grad_up = (grad_act * silu).astype(BF16)
        grad_feed[place, :, :512] = grad_gate
        grad_feed[place, :, 512:] = grad_up
        grads = lax.dot_general(grad_feed[place], weights, across, preferred_element_type=F32).astype(BF16)
        for core in range(2):
            for tile in range(12):
                kv[place, 2 + core, tile] = grads[
                    core * BLOCK : (core + 1) * BLOCK, tile * LANES : (tile + 1) * LANES
                ]
        crossed_copy(step).start()
        outs = jnp.dot(activated, down_rows, preferred_element_type=F32).astype(BF16)
        for core in range(2):
            for tile in range(12):
                kv[place, core, tile] = outs[
                    core * BLOCK : (core + 1) * BLOCK, tile * LANES : (tile + 1) * LANES
                ]

        @pl.when(step > 0)
        def _():
            turn(step - 1)

        return carry

    lax.fori_loop(0, 4, feed_forward, 0)
    down_copied = keep(kv.at[:, pl.ds(0, 2), pl.ds(0, 12)], down_terms)

    def feed_weights(step, carry):
        cols = pl.ds(pl.multiple_of(step * 384, 384), 384)
        left = mid_all[:, :, :, cols].reshape(MEMBERS * BLOCK, 384)
        right = grad_feed[...].reshape(MEMBERS * BLOCK, 1024)
        total = lax.dot_general(left, right, down_first, preferred_element_type=F32)
        feed_terms[step] = total.astype(BF16).reshape(4, 96, 1024)
        return carry

    lax.fori_loop(0, 4, feed_weights, 0)
    feeds = PlaneScatter(wire, feed_terms, (feed_first, feed_summed, feed_second, feed_sem), xyzc)
    feeds.first()

    def down_weights(step, carry):
        cols = pl.ds(pl.multiple_of(step * 128, 128), 128)
        left = acts[:, :, cols].reshape(MEMBERS * BLOCK, 128)
        right = cot_all[...].reshape(MEMBERS * BLOCK, D)
        total = lax.dot_general(left, right, down_first, preferred_element_type=F32)
        wide_terms[step] = total.astype(BF16).reshape(4, 32, D)
        return carry

    lax.fori_loop(0, 4, down_weights, 0)
    wides = PlaneScatter(wire, wide_terms, (wide_first, wide_summed, wide_second, wide_sem), xyzc)
    wides.first()

    crossed_copy(3).wait_recv()
    for step in range(3):
        ring_copy(step).wait_recv()
    tiles = []
    for tile in range(12):
        total = kv[z, 2 + c, tile].astype(F32) + crossed_in[z, tile].astype(F32)
        for step in range(3):
            total = total + ring_in[step, tile].astype(F32)
        tiles.append(total)
    grad_mid = jnp.concatenate(tiles, axis=1)
    rms = rms_out[:, :1]
    scaled = middle[...] / rms
    gain_terms[...] = jnp.sum(grad_mid * scaled, axis=0, keepdims=True)
    weighted = grad_mid * gain[...]
    back = (weighted - scaled * jnp.mean(weighted * scaled, axis=1, keepdims=True)) / rms
    grad_middle[...] = cot_all[z, c].astype(F32) + back
    branch_grad = grad_middle[...].astype(BF16)

    def spread(step, carry):
        weights = w_out_all[pl.ds(step * 4, 4)].reshape(4 * LANES, D)
        grads = lax.dot_general(branch_grad, weights, across, preferred_element_type=F32).astype(BF16)
        for part in range(2):
            grads_out[step * 2 + part] = grads[:, part * 256 : (part + 1) * 256]
        return carry

    lax.fori_loop(0, 4, spread, 0)
    kept = keep(grads_out.at[j], grads_in.at[j])
    dealt = [
        wire.send(grads_out.at[(j + k) % MEMBERS], grads_in.at[j], group[k - 1]) for k in (4, 5, 3, 2, 6, 7, 1)
    ]

    def out_weights(step, carry):
        cols = pl.ds(pl.multiple_of(step * 512, 512), 512)
        total = lax.dot_general(att_pad[:, cols], branch_grad, down_first, preferred_element_type=F32)
        w_out_all[pl.ds(step * 4, 4)] = total.astype(BF16).reshape(4, LANES, D)
        return carry

    lax.fori_loop(0, 4, out_weights, 0)
    out_copied = keep(w_out_all.at[:, pl.ds(0, 96)], out_terms)

    feeds.add_first()
    feeds.second()
    wides.add_first()
    wides.second()
    feeds.arrive()
    for half in range(2):
        feed_tall[pl.ds(half * 48, 48)] = feeds.total(half)
    split_rows(feed_tall, feed_dealt)
    feed_grad[j] = feed_dealt[j]
    dealt += [
        wire.send(feed_dealt.at[(j + k) % MEMBERS], feed_grad.at[j], group[k - 1]) for k in range(1, MEMBERS)
    ]
    wides.arrive()
    for half in range(2):
        down_grad[pl.ds(half * 16, 16)] = wides.total(half)
    for copy in dealt:
        copy.wait_recv()
    for copy in (kept, down_copied, out_copied):
        copy.wait()
    wire.close()
    for step in range(4):
        crossed_copy(step).wait_send()
    for step in range(3):
        ring_copy(step).wait_send()


def middle_part(lineage, live, gain, query, stream, cotangent, own_kv, w_out, own_feed, own_down):
    shape = jax.ShapeDtypeStruct
    vmem = pltpu.VMEM
    smem = pl.BlockSpec(memory_space=pltpu.SMEM)
    return communicate(
        middle_kernel,
        (
            shape((4, 4, 16, BLOCK, LANES), BF16),
            shape((BLOCK, D), F32),
            shape((BLOCK, LANES), F32),
            shape((BLOCK, D), F32),
            shape((MEMBERS, BLOCK, 2 * LANES), BF16),
            shape((4, 2, 12, BLOCK, LANES), BF16),
            shape((MEMBERS, 12, 1024), F32),
            shape((32, D), F32),
            shape((16, 96, D), BF16),
            shape((1, D), F32),
        ),
        [smem] + [INVMEM] * 4 + [ANY] * 5,
        (ANY, INVMEM, INVMEM, INVMEM, ANY, ANY, INVMEM, INVMEM, ANY, INVMEM),
        [
            vmem((4, 4, 16, BLOCK, LANES), BF16),
            vmem((16, LANES, D), BF16),
            vmem((4, 4, 96, 1024), BF16),
            vmem((4, 4, 32, D), BF16),
            vmem((4, 2, BLOCK, D), BF16),
            vmem((4, 2, BLOCK, D), BF16),
            vmem((4, 2 * BLOCK, 512), BF16),
            vmem((4, 2 * BLOCK, 1024), BF16),
            vmem((4, 12, BLOCK, LANES), BF16),
            vmem((3, 12, BLOCK, LANES), BF16),
            vmem((4, 4, 96, 1024), BF16),
        ]
        + scatter_scratch(96, 1024, mine=False)
        + [vmem((4, 4, 32, D), BF16)]
        + scatter_scratch(32, D, mine=False)
        + [
            vmem((DEPTH * BLOCK, LANES), BF16),
            vmem((DEPTH * BLOCK, LANES), BF16),
            vmem((MEMBERS, BLOCK, 2 * LANES), BF16),
            vmem((MEMBERS, BLOCK, 2 * LANES), BF16),
            vmem((BLOCK, 2048), BF16),
            vmem((MEMBERS, BLOCK, 2 * LANES), BF16),
            vmem((96, 1024), F32),
            vmem((MEMBERS, 12, 1024), F32),
        ]
        + wire_scratch(144)
        + [pltpu.SemaphoreType.DMA((12,))],
        2,
        "middle_part",
        62 * 2**20,
    )(lineage, live, gain, query, stream, cotangent, own_kv, w_out, own_feed, own_down)


def split_rows(tall, dealt):
    for member in range(MEMBERS):
        dealt[member] = tall[pl.ds(member * 12, 12)]


def attend_back_kernel(lineage, query, kv, live, grad, grad_query, grad_kv, keys, values, sums):
    block = pl.program_id(0)

    @pl.when(block == 0)
    def _():
        def clear(step, carry):
            sums[step] = jnp.zeros((BLOCK, LANES), F32)
            return carry

        lax.fori_loop(0, 256, clear, 0)

    for step in range(DEPTH):
        node = jnp.maximum(lineage[block, step], 0)
        rows = pl.ds(step * BLOCK, BLOCK)
        at = lax.div(node, 8) * 16
        keys[rows] = kv[at + key_unit(lax.rem(node, 8))]
        values[rows] = kv[at + value_unit(lax.rem(node, 8))]
    queries = query[0]
    grads = jnp.concatenate([grad[0, :, :LANES], grad[0, :, LANES:]], axis=0)
    across = (((1,), (1,)), ((), ()))
    scores = lax.dot_general(keys[...], queries, across, preferred_element_type=F32) * SCALE
    limit = count_ancestors(lineage, block) * BLOCK
    seen = lax.broadcasted_iota(jnp.int32, (DEPTH * BLOCK, 1), 0) < limit
    u = lax.broadcasted_iota(jnp.int32, (BLOCK, 2 * BLOCK), 0)
    t = lax.broadcasted_iota(jnp.int32, (BLOCK, 2 * BLOCK), 1) % BLOCK
    alive = jnp.transpose(jnp.broadcast_to(live[0], (BLOCK, BLOCK)))
    alive = jnp.concatenate([alive, alive], axis=1)
    own = jnp.logical_and(u <= t, jnp.logical_or(alive > 0.5, u == t))
    scores = jnp.concatenate(
        [
            jnp.where(own, scores[:BLOCK], NEGATIVE),
            jnp.where(seen[BLOCK:], scores[BLOCK:], NEGATIVE),
        ],
        axis=0,
    )
    largest = jnp.max(scores, axis=0, keepdims=True)
    terms = jnp.exp(scores - largest)
    chances = terms / jnp.sum(terms, axis=0, keepdims=True)
    grad_chances = lax.dot_general(values[...], grads, across, preferred_element_type=F32)
    inner = jnp.sum(chances * grad_chances, axis=0, keepdims=True)
    grad_scores = (chances * (grad_chances - inner)).astype(BF16)
    grad_query[0] = (
        lax.dot_general(grad_scores, keys[...], (((0,), (0,)), ((), ())), preferred_element_type=F32) * SCALE
    )
    grad_keys = jnp.dot(grad_scores, queries, preferred_element_type=F32) * SCALE
    grad_values = jnp.dot(chances.astype(BF16), grads, preferred_element_type=F32)
    for step in range(DEPTH):
        node = lineage[block, step]
        rows = slice(step * BLOCK, (step + 1) * BLOCK)

        @pl.when(node >= 0)
        def _():
            at = lax.div(node, 8) * 16
            sums[at + key_unit(lax.rem(node, 8))] += grad_keys[rows]
            sums[at + value_unit(lax.rem(node, 8))] += grad_values[rows]

    @pl.when(block == MEMBERS - 1)
    def _():
        def store(line, carry):
            for tile in range(12):
                packed = pack_tile(sums[line * 16 + tile], sums[line * 16 + 12 + tile // 3], tile % 3)
                grad_kv[line * 12 + tile] = packed.astype(BF16)
            return carry

        lax.fori_loop(0, 16, store, 0)


def attend_back(lineage, query, kv, live, grad):
    def whole(count):
        return pl.BlockSpec((count, BLOCK, LANES), lambda b, s: (0, 0, 0), pipeline_mode=pl.Buffered(1))

    return pl.pallas_call(
        attend_back_kernel,
        grid_spec=pltpu.PrefetchScalarGridSpec(
            num_scalar_prefetch=1,
            grid=(MEMBERS,),
            in_specs=[
                pl.BlockSpec((1, 2 * BLOCK, LANES), lambda b, s: (b, 0, 0)),
                whole(256),
                pl.BlockSpec((1, 1, LANES), lambda b, s: (b, 0, 0)),
                pl.BlockSpec((1, BLOCK, 2 * LANES), lambda b, s: (b, 0, 0)),
            ],
            out_specs=[
                pl.BlockSpec((1, 2 * BLOCK, LANES), lambda b, s: (b, 0, 0)),
                whole(192),
            ],
            scratch_shapes=[
                pltpu.VMEM((DEPTH * BLOCK, LANES), BF16),
                pltpu.VMEM((DEPTH * BLOCK, LANES), BF16),
                pltpu.VMEM((256, BLOCK, LANES), F32),
            ],
        ),
        out_shape=(
            jax.ShapeDtypeStruct((MEMBERS, 2 * BLOCK, LANES), F32),
            jax.ShapeDtypeStruct((192, BLOCK, LANES), BF16),
        ),
        compiler_params=pltpu.CompilerParams(vmem_limit_bytes=VMEM_BYTES),
        name="attend_back",
    )(lineage, query, kv, live, grad)


def context_back_kernel(terms, row_terms, out, row_out, *scratch):
    xyzc = x, y, z, c = spot()
    plane_scratch, group_scratch = scratch[:5], scratch[5:10]
    wire = Wire(*scratch[10:])
    greet(
        [device_of(x, y, z + k, c) for k in range(1, 4)]
        + [device_of(x, y, z, 1 - c)]
        + axis_peers(x, y, z, c, True)
    )
    rows = GroupScatter(wire, row_terms, *group_scratch, xyzc)
    plane = PlaneScatter(wire, terms, plane_scratch, xyzc)
    plane.first()
    rows.begin()
    rows.turn()
    plane.add_first()
    plane.second()
    rows.finish(row_out)
    plane.arrive()
    for half in range(2):
        out[pl.ds(half * 6, 6)] = plane.total(half)
    wire.close()


def context_back(terms, row_terms):
    shape = jax.ShapeDtypeStruct
    return communicate(
        context_back_kernel,
        (shape((12, BLOCK, LANES), F32), shape((BLOCK, D), F32)),
        [ANY] * 2,
        (INVMEM,) * 2,
        scatter_scratch(12, BLOCK, LANES) + group_scatter_scratch() + wire_scratch(24),
        6,
        "context_back",
    )(terms, row_terms)


def unproject_kernel(
    lineage, grad_query, context, cosine, sine, normed, stream, w_attn, grad_terms, attn_terms, gain_terms, raw
):
    for block in range(MEMBERS):
        depth = count_ancestors(lineage, block) - 1
        cos, sin = cosine[depth], sine[depth]
        rows = slice(block * BLOCK, (block + 1) * BLOCK)

        def unit(index):
            if index < 12:
                return context[index]
            tile = (index - 12) * 3
            return unpack_extra([context[tile + k] for k in range(3)])

        def turn(v):
            return (v * cos - swap_halves(v) * sin).astype(BF16)

        key = block if block < 6 else 12 + 2 * (block - 6)
        value = block + 6 if block < 6 else 13 + 2 * (block - 6)
        raw[rows, :128] = turn(grad_query[block, :BLOCK])
        raw[rows, 128:256] = turn(grad_query[block, BLOCK:])
        raw[rows, 256:384] = turn(unit(key))
        raw[rows, 384:] = jnp.where(lane_of((BLOCK, LANES)) < HEAD_DIM, unit(value), 0.0).astype(BF16)

    gain_terms[...] = jnp.zeros((1, D), F32)

    def rows_back(step, carry):
        rows = pl.ds(pl.multiple_of(step * 256, 256), 256)
        grads = lax.dot_general(
            raw[rows], w_attn[...], (((1,), (1,)), ((), ())), preferred_element_type=F32
        )
        low = grads.astype(BF16)
        for core in range(2):
            for tile in range(12):
                grad_terms[step, core, tile] = low[
                    core * BLOCK : (core + 1) * BLOCK, tile * LANES : (tile + 1) * LANES
                ]
        wide = stream[rows].astype(F32)
        rms = jnp.sqrt(jnp.mean(wide * wide, axis=1, keepdims=True) + EPSILON)
        gain_terms[...] += jnp.sum(grads * (wide / rms), axis=0, keepdims=True)
        return carry

    lax.fori_loop(0, 4, rows_back, 0)

    def weights_back(step, carry):
        cols = pl.ds(pl.multiple_of(step * 384, 384), 384)
        total = lax.dot_general(
            normed[:, cols], raw[...], (((0,), (0,)), ((), ())), preferred_element_type=F32
        )
        attn_terms[step] = total.astype(BF16).reshape(4, 96, 512)
        return carry

    lax.fori_loop(0, 4, weights_back, 0)


def unproject(lineage, grad_query, context, cosine, sine, normed, stream, w_attn):
    smem = pl.BlockSpec(memory_space=pltpu.SMEM)
    shape = jax.ShapeDtypeStruct
    return pl.pallas_call(
        unproject_kernel,
        out_shape=(
            shape((4, 2, 12, BLOCK, LANES), BF16),
            shape((4, 4, 96, 512), BF16),
            shape((1, D), F32),
        ),
        in_specs=[smem] + [INVMEM] * 7,
        out_specs=(INVMEM,) * 3,
        scratch_shapes=[pltpu.VMEM((MEMBERS * BLOCK, 512), BF16)],
        compiler_params=pltpu.CompilerParams(vmem_limit_bytes=VMEM_BYTES),
        name="unproject",
    )(lineage, grad_query, context, cosine, sine, normed, stream, w_attn)


def closing_kernel(
    grad_terms, wide_terms, out_terms, gain_terms,
    grad_out, wide_out, out_out, gain_out, *scratch
):
    xyzc = x, y, z, c = spot()
    j = z * 2 + c
    (
        wide_tall, wide_dealt, out_tall, out_dealt, out_mine, out_crossed,
        gain_in, gain_line, gain_in_two, gain_in_three, *scratch
    ) = scratch
    group_scratch, wide_scratch, out_scratch = scratch[:5], scratch[5:10], scratch[10:15]
    send_sems, recv_sems, local_sem = scratch[15:]
    wire = Wire(send_sems, recv_sems)
    group = [group_peer(x, y, z, c, k) for k in range(1, MEMBERS)]
    greet(group + axis_peers(x, y, z, c, True))
    sibling = device_of(x, y, z, 1 - c)

    rows = GroupScatter(wire, grad_terms, *group_scratch, xyzc)
    wide = PlaneScatter(wire, wide_terms, wide_scratch, xyzc)
    own_half = pl.ds(pl.multiple_of(c * 768, 768), 768)
    other_half = pl.ds(pl.multiple_of((1 - c) * 768, 768), 768)
    crossed = wire.send(out_terms.at[:, :, :, other_half], out_crossed, sibling)
    local = pltpu.make_async_copy(out_terms.at[:, :, :, own_half], out_mine, local_sem)
    local.start()
    rows.begin()
    wide.first()
    gains = [
        wire.send(gain_terms.at[(x + k) % 4], gain_in.at[k - 1], device_of(x + k, y, z, c))
        for k in range(1, 4)
    ]
    local.wait()
    crossed.wait_recv()

    def body(step, carry):
        a, b = step // 4, step % 4
        total = out_mine[a, b].astype(F32) + out_crossed[a, b].astype(F32)
        out_mine[a, b] = total.astype(BF16)
        return carry

    lax.fori_loop(0, 16, body, 0)
    outs = PlaneScatter(wire, out_mine, out_scratch, xyzc)
    outs.first()
    rows.turn()
    for copy in gains:
        copy.wait_recv()
    gain_line[...] = gain_terms[x] + gain_in[0] + gain_in[1] + gain_in[2]
    gains = [
        wire.send(gain_line.at[(y + k) % 4], gain_in_two.at[k - 1], device_of(x, y + k, z, c))
        for k in range(1, 4)
    ]
    wide.add_first()
    wide.second()
    outs.add_first()
    outs.second()
    for copy in gains:
        copy.wait_recv()
    gain_in_three[j] = gain_line[y] + gain_in_two[0] + gain_in_two[1] + gain_in_two[2]
    gains = [
        wire.send(gain_in_three.at[j], gain_in_three.at[j], group[k - 1]) for k in range(1, MEMBERS)
    ]
    wide.arrive()
    for half in range(2):
        wide_tall[pl.ds(half * 48, 48)] = wide.total(half)
    split_rows(wide_tall, wide_dealt)
    wide_out[j] = wide_dealt[j]
    dealt = [
        wire.send(wide_dealt.at[(j + k) % MEMBERS], wide_out.at[j], group[k - 1])
        for k in range(1, MEMBERS)
    ]
    outs.arrive()
    for half in range(2):
        out_tall[pl.ds(half * 48, 48)] = outs.total(half)
    split_rows(out_tall, out_dealt)
    out_out[j] = out_dealt[j]
    dealt += [
        wire.send(out_dealt.at[(j + k) % MEMBERS], out_out.at[j], group[k - 1])
        for k in range(1, MEMBERS)
    ]
    rows.finish(grad_out)
    for copy in gains:
        copy.wait_recv()
    total = gain_in_three[0]
    for member in range(1, MEMBERS):
        total = total + gain_in_three[member]
    gain_out[...] = total
    for copy in dealt:
        copy.wait_recv()
    wire.close()


def closing(grad_terms, wide_terms, out_terms, gain_terms):
    shape = jax.ShapeDtypeStruct
    return communicate(
        closing_kernel,
        (
            shape((BLOCK, D), F32),
            shape((MEMBERS, 12, 512), F32),
            shape((MEMBERS, 12, 768), F32),
            shape((8, LANES), F32),
        ),
        [ANY, ANY, ANY, INVMEM],
        (INVMEM,) * 4,
        [
            pltpu.VMEM((96, 512), F32),
            pltpu.VMEM((MEMBERS, 12, 512), F32),
            pltpu.VMEM((96, 768), F32),
            pltpu.VMEM((MEMBERS, 12, 768), F32),
            pltpu.VMEM((4, 4, 96, 768), BF16),
            pltpu.VMEM((4, 4, 96, 768), BF16),
            pltpu.VMEM((3, 4, 8, LANES), F32),
            pltpu.VMEM((4, 8, LANES), F32),
            pltpu.VMEM((3, 8, LANES), F32),
            pltpu.VMEM((MEMBERS, 8, LANES), F32),
        ]
        + group_scatter_scratch()
        + scatter_scratch(96, 512)
        + scatter_scratch(96, 768)
        + wire_scratch(80)
        + [pltpu.SemaphoreType.DMA],
        7,
        "closing",
    )(grad_terms, wide_terms, out_terms, gain_terms)


def pack_columns(w_query, w_key, w_value, w_gate, w_up):
    rows = w_query.shape[0]
    query = jnp.pad(w_query.reshape(rows, MEMBERS, 2, 96), ((0, 0), (0, 0), (0, 0), (0, 32))).reshape(rows, MEMBERS, 256)
    key, value = (jnp.pad(w.reshape(rows, MEMBERS, 96), ((0, 0), (0, 0), (0, 32))) for w in (w_key, w_value))
    gate, up = (
        w.reshape(rows, 16, MEMBERS, 32).transpose(0, 2, 1, 3).reshape(rows, MEMBERS, 512) for w in (w_gate, w_up)
    )
    packed = jnp.concatenate([query, key, value, gate, up], axis=2).transpose(1, 0, 2)
    return jnp.pad(packed, ((0, 0), (0, 4), (0, 0)))


def pack_small(attn_gain, mlp_gain, live, member):
    gains = jnp.stack([attn_gain, mlp_gain]).astype(F32)
    place = lax.broadcasted_iota(jnp.int32, (12, LANES), 1) == member * 12 + lax.broadcasted_iota(jnp.int32, (12, LANES), 0)
    spread = jnp.sum(jnp.where(place[None], gains[:, :, None], 0.0), axis=1)
    rows = jnp.concatenate([spread.astype(BF16), live.astype(BF16)[None]])
    return jnp.pad(rows, ((0, 13), (0, 0)))


def norm_back(grad_normed, scaled_rows, gain, rms_rows):
    weighted = grad_normed * gain.astype(F32)
    return (weighted - scaled_rows * jnp.mean(weighted * scaled_rows, axis=1, keepdims=True)) / rms_rows


def shards(
    stream, attn_gain, w_query, w_key, w_value, w_out, mlp_gain, w_gate, w_up, w_down, parent, live_mask, cotangent
):
    me = lax.axis_index("dev")
    member = me % MEMBERS
    cosine, sine = rope_tables()
    packed = pack_columns(w_query, w_key, w_value, w_gate, w_up)
    small = pack_small(attn_gain, mlp_gain, live_mask, member)
    stream_all, w_attn, feed_own, out_all, gains_all, small_all = opening(
        stream, packed, jnp.pad(w_out, ((0, 4), (0, 0))), small
    )
    stream_all = stream_all.reshape(MEMBERS * BLOCK, D)
    w_attn = w_attn.reshape(D, 512)
    gains = gains_all.reshape(16, 16, LANES)[:, :2, :96].transpose(1, 0, 2).reshape(2, 1, D).astype(F32)
    live = small_all[:, 2:3, :].astype(F32)
    lineage, normed, query, own_context = project(
        parent, (me // MEMBERS) * MEMBERS, stream_all, w_attn, gains[0], cosine, sine
    )
    (
        context, middle, branch_rms, grad_middle, grad_heads, down_terms, feed_grad, down_grad, out_terms, gain_two_terms
    ) = middle_part(
        lineage, live, gains[1], query, stream, cotangent, own_context, out_all.reshape(16, 96, D), feed_own, w_down
    )
    gate_grad, up_grad = (
        feed_grad[:, :, part : part + 512].reshape(MEMBERS, 12, 16, 32).transpose(1, 2, 0, 3).reshape(12, FF)
        for part in (0, 512)
    )
    grad_query, context_terms = attend_back(
        lineage, query, context.reshape(256, BLOCK, LANES), live, grad_heads
    )
    grad_context, down_sum = context_back(context_terms.reshape(4, 4, 12, BLOCK, LANES), down_terms)
    mixed_out = (middle + down_sum).astype(BF16)
    grad_normed_terms, attn_terms, gain_one_terms = unproject(
        lineage, grad_query, grad_context, cosine, sine, normed, stream_all, w_attn
    )
    gain_terms = jnp.concatenate([gain_one_terms, gain_two_terms]).reshape(2, 16, 96).transpose(1, 0, 2)
    gain_terms = jnp.pad(gain_terms, ((0, 0), (0, 6), (0, 32))).reshape(4, 4, 8, LANES)
    grad_normed, attn_grad, out_grad, gain_grad = closing(
        grad_normed_terms, attn_terms, out_terms.reshape(4, 4, 96, D), gain_terms
    )
    stream_wide = stream.astype(F32)
    stream_rms = jnp.sqrt(jnp.mean(stream_wide * stream_wide, axis=1, keepdims=True) + EPSILON)
    stream_grad = grad_middle + norm_back(grad_normed, stream_wide / stream_rms, gains[0], stream_rms)
    query_grad = attn_grad[:, :, :256].reshape(MEMBERS, 12, 2, LANES)[..., :96]
    query_grad = query_grad.transpose(1, 0, 2, 3).reshape(12, D)
    key_grad = attn_grad[:, :, 256:352].transpose(1, 0, 2).reshape(12, 768)
    value_grad = attn_grad[:, :, 384:480].transpose(1, 0, 2).reshape(12, 768)
    out_grad = jnp.sum(out_grad.reshape(4, 2, 12, 768), axis=0).transpose(1, 0, 2).reshape(12, D)
    own_gains = lax.dynamic_slice(gain_grad, (0, member * 12), (2, 12))
    return (
        mixed_out, stream_grad, own_gains[0], query_grad, key_grad, value_grad, out_grad, own_gains[1],
        gate_grad, up_grad, down_grad, stream_rms[:, 0], branch_rms[:, 0],
    )


def solution(mesh):
    rows, line = P("dev", None), P("dev")
    return jax.shard_map(
        shards,
        mesh=mesh,
        in_specs=(rows, line, rows, rows, rows, rows, line, rows, rows, rows, P(), line, rows),
        out_specs=(rows, rows, line, rows, rows, rows, rows, line, rows, rows, rows, line, line),
        check_vma=False,
    )
```

```python
import functools

import jax
import jax.numpy as jnp
import numpy as np
from jax import lax
from jax.experimental import pallas as pl
from jax.experimental.pallas import tpu as pltpu
from jax.sharding import PartitionSpec as P

HEADS = 16
KV_HEADS = 8
HEAD_DIM = 96
BLOCK = 128
DEPTH = 10
D = 1536
FF = 4096
MEMBERS = 8
LANES = 128

EPSILON = 1e-05
ROPE_BASE = 100000.0
NEGATIVE = -1e30
SCALE = HEAD_DIM ** (-0.5)
MESH = pl.DeviceIdType.MESH
BF16 = jnp.bfloat16
F32 = jnp.float32
VMEM_BYTES = 56 * 2**20


def spot():
    me = lax.axis_index("dev")
    return me // 32, (me // 8) % 4, (me // 2) % 4, me % 2


def device_of(x, y, z, c):
    return ((x % 4) * 4 + (y % 4)) * 8 + (z % 4) * 2 + c


def greet(peers):
    barrier = pltpu.get_barrier_semaphore()
    for peer in peers:
        pl.semaphore_signal(barrier, inc=1, device_id=(peer,), device_id_type=MESH)
    pl.semaphore_wait(barrier, len(peers))


def axis_peers(x, y, z, c, far):
    steps = (1, 2, 3) if far else (1, 3)
    return [device_of(x + k, y, z, c) for k in steps] + [device_of(x, y + k, z, c) for k in steps]


def group_peer(x, y, z, c, k):
    member = (z * 2 + c + k) % MEMBERS
    return (x * 4 + y) * MEMBERS + member


class Wire:
    def __init__(self, send_sems, recv_sems):
        self.send_sems = send_sems
        self.recv_sems = recv_sems
        self.used = 0
        self.open = []

    def reserve(self, count):
        self.used += count
        return self.used - count

    def make(self, slot, source, target, peer):
        return pltpu.make_async_remote_copy(
            src_ref=source,
            dst_ref=target,
            send_sem=self.send_sems.at[slot],
            recv_sem=self.recv_sems.at[slot],
            device_id=(peer,),
            device_id_type=MESH,
        )

    def send(self, source, target, peer):
        copy = self.make(self.reserve(1), source, target, peer)
        copy.start()
        self.open.append(copy)
        return copy

    def close(self):
        for copy in self.open:
            copy.wait_send()
        self.open = []


class Ring:
    def __init__(self, wire, own, part, place, up, down):
        self.wire, self.own, self.part = wire, own, part
        self.place, self.up, self.down = place, up, down

    def begin(self):
        send, part, place = self.wire.send, self.part, self.place
        self.low_up = send(self.own(0), part(place, 0), self.up)
        self.high_down = send(self.own(1), part(place, 1), self.down)
        self.high_up = send(self.own(1), part(place, 1), self.up)
        self.low_down = send(self.own(0), part(place, 0), self.down)

    def relay(self):
        before, after = (self.place + 3) % 4, (self.place + 1) % 4
        self.low_up.wait_recv()
        self.far_up = self.wire.send(self.part(before, 0), self.part(before, 0), self.up)
        self.high_down.wait_recv()
        self.far_down = self.wire.send(self.part(after, 1), self.part(after, 1), self.down)

    def near(self):
        self.high_up.wait_recv()
        self.low_down.wait_recv()

    def far(self):
        self.far_up.wait_recv()
        self.far_down.wait_recv()


class PlaneGather:
    def __init__(self, wire, own, out, cut, xyzc):
        self.wire, self.own, self.out, self.cut = wire, own, out, cut
        x, y, z, c = xyzc
        self.x, self.y = x, y
        self.x_up, self.x_down = device_of(x + 1, y, z, c), device_of(x + 3, y, z, c)
        self.y_up, self.y_down = device_of(x, y + 1, z, c), device_of(x, y + 3, z, c)

    def pair(self, one_own, one_part, two_own, two_part, one_on_x):
        on_x = (self.x, self.x_up, self.x_down)
        on_y = (self.y, self.y_up, self.y_down)
        cut = self.cut
        self.one = Ring(
            self.wire,
            lambda side: one_own(cut(0, side)),
            lambda place, side: one_part(place, cut(0, side)),
            *(on_x if one_on_x else on_y),
        )
        self.two = Ring(
            self.wire,
            lambda side: two_own(cut(1, side)),
            lambda place, side: two_part(place, cut(1, side)),
            *(on_y if one_on_x else on_x),
        )
        self.one.begin()
        self.two.begin()

    def first(self):
        own, out, x, y = self.own, self.out, self.x, self.y
        self.pair(
            lambda q: own.at[q],
            lambda place, q: out.at[(place, y) + q],
            lambda q: own.at[q],
            lambda place, q: out.at[(x, place) + q],
            True,
        )

    def relay(self):
        self.one.relay()
        self.two.relay()

    def settle(self):
        for ring in (self.one, self.two):
            ring.near()
            ring.far()

    def second(self):
        out, x, y = self.out, self.x, self.y
        every = slice(None)
        self.pair(
            lambda q: out.at[(every, y) + q],
            lambda place, q: out.at[(every, place) + q],
            lambda q: out.at[(x, every) + q],
            lambda place, q: out.at[(place, every) + q],
            False,
        )


def quarter(rows, cols):
    return lambda half, side: (pl.ds(half * (rows // 2), rows // 2), pl.ds(side * (cols // 2), cols // 2))


def quarter_units(half, side):
    return (pl.ds(half * 6 + side * 3, 3),)


class GroupGather:
    def __init__(self, wire, own, out, xyzc):
        self.wire, self.own, self.out = wire, own, out
        x, y, z, c = xyzc
        self.z, self.c = z, c
        self.sibling = device_of(x, y, z, 1 - c)
        half = out.shape[2] // 2
        self.ring = Ring(
            wire,
            lambda side: own.at[pl.ds(side * half, half)],
            lambda place, side: out.at[place, c, pl.ds(side * half, half)],
            z, device_of(x, y, z + 1, c), device_of(x, y, z + 3, c),
        )
        self.crossed = []

    def begin(self):
        self.ring.begin()
        self.crossed.append(self.wire.send(self.own, self.out.at[self.z, self.c], self.sibling))

    def cross(self, k):
        piece = self.out.at[(self.z + k) % 4, self.c]
        self.crossed.append(self.wire.send(piece, piece, self.sibling))

    def relay(self):
        self.ring.relay()

    def near(self):
        self.ring.near()
        self.cross(1)
        self.cross(3)

    def far(self):
        self.ring.far()
        self.cross(2)

    def finish(self):
        for copy in self.crossed:
            copy.wait_recv()


class PlaneScatter:
    def __init__(self, wire, terms, scratch, xyzc):
        self.wire, self.terms = wire, terms
        *mine, self.first_in, self.summed, self.second_in, self.local_sem = scratch
        self.mine = mine[0] if mine else None
        self.x, self.y, self.z, self.c = xyzc
        self.half = terms.shape[2] // 2

    def peer(self, along_x, k):
        if along_x:
            return device_of(self.x + k, self.y, self.z, self.c)
        return device_of(self.x, self.y + k, self.z, self.c)

    def line(self, half, place):
        rows = pl.ds(half * self.half, self.half)
        if half == 0:
            return self.terms.at[place, :, rows]
        return self.terms.at[:, place, rows]

    def own(self, half, line):
        if self.mine is not None:
            return self.mine[half, line]
        rows = slice(half * self.half, (half + 1) * self.half)
        if half == 0:
            return self.terms[self.x, line, rows]
        return self.terms[line, self.y, rows]

    def first(self):
        self.copies = []
        self.locals = []
        if self.mine is not None:
            for half, place in ((0, self.x), (1, self.y)):
                copy = pltpu.make_async_copy(
                    self.line(half, place), self.mine.at[half], self.local_sem.at[half]
                )
                copy.start()
                self.locals.append(copy)
        for k in (2, 1, 3):
            for half, place in ((0, self.x), (1, self.y)):
                self.copies.append(
                    self.wire.send(
                        self.line(half, (place + k) % 4),
                        self.first_in.at[half, k - 1],
                        self.peer(half == 0, k),
                    )
                )

    def add_first(self):
        for copy in self.locals:
            copy.wait()
        for copy in self.copies:
            copy.wait_recv()
        for half in range(2):

            def body(line, carry):
                total = self.own(half, line).astype(F32)
                for k in range(3):
                    total = total + self.first_in[half, k, line].astype(F32)
                self.summed[half, line] = total.astype(BF16)
                return carry

            lax.fori_loop(0, 4, body, 0)

    def second(self):
        self.copies = []
        for k in (2, 1, 3):
            for half, place in ((0, self.y), (1, self.x)):
                self.copies.append(
                    self.wire.send(
                        self.summed.at[half, (place + k) % 4],
                        self.second_in.at[half, k - 1],
                        self.peer(half == 1, k),
                    )
                )

    def total(self, half):
        place = (self.y, self.x)[half]
        total = self.summed[half, place].astype(F32)
        for k in range(3):
            total = total + self.second_in[half, k].astype(F32)
        return total

    def arrive(self):
        for copy in self.copies:
            copy.wait_recv()


def scatter_scratch(rows, *rest, mine=True):
    piece = (rows // 2,) + rest
    own = [pltpu.VMEM((2, 4) + piece, BF16)] if mine else []
    return own + [
        pltpu.VMEM((2, 3, 4) + piece, BF16),
        pltpu.VMEM((2, 4) + piece, BF16),
        pltpu.VMEM((2, 3) + piece, BF16),
        pltpu.SemaphoreType.DMA((2,)),
    ]


class GroupScatter:
    def __init__(self, wire, terms, mine, crossed_in, summed, ring_in, local_sem, xyzc):
        self.wire, self.terms = wire, terms
        self.mine, self.crossed_in, self.summed, self.ring_in = mine, crossed_in, summed, ring_in
        self.x, self.y, self.z, self.c = xyzc
        self.local_sem = local_sem

    def begin(self):
        self.local = pltpu.make_async_copy(self.terms.at[:, self.c], self.mine, self.local_sem)
        self.local.start()
        sibling = device_of(self.x, self.y, self.z, 1 - self.c)
        self.crossed = {}
        for k in (2, 1, 3, 0):
            place = (self.z + k) % 4
            self.crossed[k] = self.wire.send(
                self.terms.at[place, 1 - self.c], self.crossed_in.at[place], sibling
            )

    def turn(self):
        self.local.wait()
        self.copies = []
        for k in (2, 1, 3):
            place = (self.z + k) % 4
            self.crossed[k].wait_recv()

            def body(tile, carry):
                total = self.mine[place, tile].astype(F32) + self.crossed_in[place, tile].astype(F32)
                self.summed[place, tile] = total.astype(BF16)
                return carry

            lax.fori_loop(0, 12, body, 0)
            self.copies.append(
                self.wire.send(
                    self.summed.at[place],
                    self.ring_in.at[k - 1],
                    device_of(self.x, self.y, self.z + k, self.c),
                )
            )

    def finish(self, out):
        self.crossed[0].wait_recv()
        for copy in self.copies:
            copy.wait_recv()
        for tile in range(12):
            total = self.mine[self.z, tile].astype(F32) + self.crossed_in[self.z, tile].astype(F32)
            for k in range(3):
                total = total + self.ring_in[k, tile].astype(F32)
            out[:, tile * LANES : (tile + 1) * LANES] = total


class ChipScatter:
    def __init__(self, wire, terms, at, crossed_in, ring_in, xyzc):
        self.wire, self.terms, self.at = wire, terms, at
        self.crossed_in, self.ring_in = crossed_in, ring_in
        self.x, self.y, self.z, self.c = xyzc
        self.crossed_slot, self.ring_slot = wire.reserve(4), wire.reserve(3)
        self.all_tiles = pl.ds(0, 12)

    def place(self, step):
        return (self.z + 1 + step) % 4

    def crossed(self, step):
        place = self.place(step)
        return self.wire.make(
            self.crossed_slot + step,
            self.terms.at[place, self.at + 1 - self.c, self.all_tiles],
            self.crossed_in.at[place],
            device_of(self.x, self.y, self.z, 1 - self.c),
        )

    def ring(self, step):
        return self.wire.make(
            self.ring_slot + step,
            self.terms.at[self.place(step), self.at + self.c, self.all_tiles],
            self.ring_in.at[step],
            device_of(self.x, self.y, self.z + 1 + step, self.c),
        )

    def put(self, step, grads):
        place = self.place(step)
        for core in range(2):
            for tile in range(12):
                self.terms[place, self.at + core, tile] = grads[
                    core * BLOCK : (core + 1) * BLOCK, tile * LANES : (tile + 1) * LANES
                ]
        self.crossed(step).start()

    def turn(self, step):
        place, line = self.place(step), self.at + self.c
        self.crossed(step).wait_recv()

        def add(tile, carry):
            total = self.terms[place, line, tile].astype(F32) + self.crossed_in[place, tile].astype(F32)
            self.terms[place, line, tile] = total.astype(BF16)
            return carry

        lax.fori_loop(0, 12, add, 0)
        self.ring(step).start()

    def total(self):
        self.crossed(3).wait_recv()
        for step in range(3):
            self.ring(step).wait_recv()
        tiles = []
        for tile in range(12):
            total = self.terms[self.z, self.at + self.c, tile].astype(F32)
            total = total + self.crossed_in[self.z, tile].astype(F32)
            for step in range(3):
                total = total + self.ring_in[step, tile].astype(F32)
            tiles.append(total)
        return jnp.concatenate(tiles, axis=1)

    def close(self):
        for step in range(4):
            self.crossed(step).wait_send()
        for step in range(3):
            self.ring(step).wait_send()


def group_scatter_scratch():
    return [
        pltpu.VMEM((4, 12, BLOCK, LANES), BF16),
        pltpu.VMEM((4, 12, BLOCK, LANES), BF16),
        pltpu.VMEM((4, 12, BLOCK, LANES), BF16),
        pltpu.VMEM((3, 12, BLOCK, LANES), BF16),
        pltpu.SemaphoreType.DMA,
    ]


def chip_scatter_scratch():
    return [pltpu.VMEM((4, 12, BLOCK, LANES), BF16), pltpu.VMEM((3, 12, BLOCK, LANES), BF16)]


def wire_scratch(count):
    return [pltpu.SemaphoreType.DMA((count,)), pltpu.SemaphoreType.DMA((count,))]


ANY = pl.BlockSpec(memory_space=pl.ANY)
INVMEM = pl.BlockSpec(memory_space=pltpu.VMEM)


def communicate(kernel, out_shapes, in_specs, out_specs, scratch, ident, name, vmem=VMEM_BYTES):
    return pl.pallas_call(
        kernel,
        out_shape=out_shapes,
        in_specs=in_specs,
        out_specs=out_specs,
        scratch_shapes=scratch,
        compiler_params=pltpu.CompilerParams(
            collective_id=ident, has_side_effects=True, vmem_limit_bytes=vmem
        ),
        name=name,
    )


def opening_kernel(
    stream, packed, w_out, small,
    stream_all, attn_all, feed_own, out_all, gains_all, small_all,
    packed_in, out_in, small_in, wide_tall, out_tall, wide_own, out_own, gain_own,
    send_sems, recv_sems, local_sems,
):
    xyzc = x, y, z, c = spot()
    j = z * 2 + c
    wire = Wire(send_sems, recv_sems)
    group = [group_peer(x, y, z, c, k) for k in range(1, MEMBERS)]
    greet(group + axis_peers(x, y, z, c, True))
    locals_ = []

    def keep(source, target):
        copy = pltpu.make_async_copy(source, target, local_sems.at[len(locals_)])
        copy.start()
        locals_.append(copy)

    dealt = []
    for k in range(1, MEMBERS):
        member = (j + k) % MEMBERS
        half = pl.ds(pl.multiple_of((member % 2) * 768, 768), 768)
        dealt.append(wire.send(packed.at[member], packed_in.at[j], group[k - 1]))
        dealt.append(wire.send(w_out.at[:, half], out_in.at[j], group[k - 1]))
        dealt.append(wire.send(small, small_in.at[j], group[k - 1]))
    own_half = pl.ds(pl.multiple_of(c * 768, 768), 768)
    keep(packed.at[j], packed_in.at[j])
    keep(w_out.at[:, own_half], out_in.at[j])
    keep(small, small_in.at[j])
    keep(stream, stream_all.at[z, c])
    streams = GroupGather(wire, stream, stream_all, xyzc)
    streams.begin()

    for copy in dealt:
        copy.wait_recv()
    for copy in locals_[:3]:
        copy.wait()
    for member in range(MEMBERS):
        rows = pl.ds(member * 12, 12)
        wide_tall[rows] = packed_in[member].astype(F32)[:12]
        out_tall[rows] = out_in[member].astype(F32)[:12]
    wide_own[...] = wide_tall[...].astype(BF16)
    out_own[...] = out_tall[...].astype(BF16)
    gain = small_in[0].astype(F32)
    for member in range(1, MEMBERS):
        gain = gain + small_in[member].astype(F32)
    gain_own[...] = gain.astype(BF16)

    attn_own = wide_own.at[:, pl.ds(0, 512)]
    keep(attn_own, attn_all.at[x, y])
    keep(out_own, out_all.at[x, y, :, own_half])
    keep(gain_own, gains_all.at[x, y])
    keep(small_in, small_all)
    keep(wide_own.at[:, pl.ds(512, 1024)], feed_own)

    half_out = out_all.at[:, :, :, own_half]
    attn = PlaneGather(wire, attn_own, attn_all, quarter(96, 512), xyzc)
    outs = PlaneGather(wire, out_own, half_out, quarter(96, 768), xyzc)
    planes = (attn, outs)
    tiny = [
        wire.send(gain_own, gains_all.at[x, y], device_of(x + k, y, z, c)) for k in range(1, 4)
    ]
    for plane in planes:
        plane.first()
    streams.relay()
    for plane in planes:
        plane.relay()
    for copy in locals_[3:]:
        copy.wait()
    for copy in tiny:
        copy.wait_recv()
    line = gains_all.at[:, y]
    tiny = [wire.send(line, line, device_of(x, y + k, z, c)) for k in range(1, 4)]
    for plane in planes:
        plane.settle()
        plane.second()
    streams.near()
    streams.far()
    for plane in planes:
        plane.relay()
    outs.settle()
    sibling = device_of(x, y, z, 1 - c)
    swapped = wire.send(half_out, half_out, sibling)
    attn.settle()
    streams.finish()
    for copy in tiny:
        copy.wait_recv()
    swapped.wait_recv()
    wire.close()


def opening(stream, packed, w_out, small):
    shape = jax.ShapeDtypeStruct
    return communicate(
        opening_kernel,
        (
            shape((4, 2, BLOCK, D), BF16),
            shape((4, 4, 96, 512), BF16),
            shape((96, 1024), BF16),
            shape((4, 4, 96, 1536), BF16),
            shape((4, 4, 16, LANES), BF16),
            shape((MEMBERS, 16, LANES), BF16),
        ),
        [ANY] * 4,
        (ANY,) * 6,
        [
            pltpu.VMEM((MEMBERS, 16, 1536), BF16),
            pltpu.VMEM((MEMBERS, 16, 768), BF16),
            pltpu.VMEM((MEMBERS, 16, LANES), BF16),
            pltpu.VMEM((96, 1536), F32),
            pltpu.VMEM((96, 768), F32),
            pltpu.VMEM((96, 1536), BF16),
            pltpu.VMEM((96, 768), BF16),
            pltpu.VMEM((16, LANES), BF16),
        ]
        + wire_scratch(86)
        + [pltpu.SemaphoreType.DMA((9,))],
        1,
        "opening",
    )(stream, packed, w_out, small)


def key_unit(member):
    return member + jnp.where(member >= 6, 6, 0) + jnp.where(member >= 7, 1, 0)


def value_unit(member):
    return member + 6 + jnp.where(member >= 6, 1, 0) + jnp.where(member >= 7, 1, 0)


def lane_of(shape):
    return lax.broadcasted_iota(jnp.int32, shape, len(shape) - 1)


def pack_tile(unit, extra, place):
    return jnp.where(lane_of(unit.shape) < HEAD_DIM, unit, pltpu.roll(extra, (96 - 32 * place) % LANES, 1))


def unpack_extra(tiles):
    lane = lane_of(tiles[0].shape)
    extra = jnp.where(lane < 32, pltpu.roll(tiles[0], 32, 1), 0.0)
    extra = jnp.where(jnp.logical_and(lane >= 32, lane < 64), pltpu.roll(tiles[1], 64, 1), extra)
    return jnp.where(jnp.logical_and(lane >= 64, lane < 96), pltpu.roll(tiles[2], 96, 1), extra)


def swap_halves(rows):
    lane = lane_of(rows.shape)
    return jnp.where(lane < HEAD_DIM // 2, pltpu.roll(rows, LANES - 48, 1), pltpu.roll(rows, 48, 1))


def rope_tables():
    half = HEAD_DIM // 2
    frequency = ROPE_BASE ** (-2.0 * np.arange(half, dtype=np.float64) / HEAD_DIM)
    frequency = frequency.astype(np.float32)
    places = np.arange(DEPTH * BLOCK, dtype=np.float32)
    angles = (places[:, None] * frequency[None, :]).astype(np.float64)
    cosine = np.zeros((DEPTH * BLOCK, LANES), np.float32)
    sine = np.zeros((DEPTH * BLOCK, LANES), np.float32)
    cosine[:, :half] = cosine[:, half:HEAD_DIM] = np.cos(angles)
    sine[:, half:HEAD_DIM] = np.sin(angles)
    sine[:, :half] = -sine[:, half:HEAD_DIM]
    return (
        jnp.asarray(cosine.reshape(DEPTH, BLOCK, LANES)),
        jnp.asarray(sine.reshape(DEPTH, BLOCK, LANES)),
    )


def count_ancestors(lineage, block):
    count = jnp.int32(0)
    for step in range(DEPTH):
        count = count + jnp.where(lineage[block, step] >= 0, 1, 0)
    return count


def write_lineage(parent, first, lineage):
    def one(block, carry):
        def hop(step, node):
            lineage[block, step] = node
            above = parent[jnp.maximum(node, 0)]
            return jnp.where(node >= 0, above, -1)

        lax.fori_loop(0, DEPTH, hop, first[0] + block)
        return carry

    lax.fori_loop(0, MEMBERS, one, 0)


def project_kernel(
    parent, first, stream, w_attn, gain, cosine, sine, lineage, query, packed, units
):
    step = pl.program_id(0)

    @pl.when(step == 0)
    def _():
        write_lineage(parent, first, lineage)

    wide = stream[...].astype(F32)
    rms = jnp.sqrt(jnp.mean(wide * wide, axis=1, keepdims=True) + EPSILON)
    rows = (wide / rms * gain[...]).astype(BF16)
    raw = jnp.dot(rows, w_attn[...], preferred_element_type=F32)
    for part in range(2):
        block = step * 2 + part
        depth = count_ancestors(lineage, block) - 1
        cos, sin = cosine[depth], sine[depth]
        mine = raw[part * BLOCK : (part + 1) * BLOCK]

        def turn(head):
            v = mine[:, head * LANES : (head + 1) * LANES]
            return v * cos + swap_halves(v) * sin

        query[part, :BLOCK] = turn(0).astype(BF16)
        query[part, BLOCK:] = turn(1).astype(BF16)
        units[key_unit(block)] = turn(2)
        units[value_unit(block)] = mine[:, 3 * LANES :]

    @pl.when(step == 3)
    def _():
        for tile in range(12):
            packed[tile] = pack_tile(units[tile], units[12 + tile // 3], tile % 3).astype(BF16)


def project(parent, first, stream_all, w_attn, gain, cosine, sine):
    def whole(shape):
        return pl.BlockSpec(shape, lambda i, p, f: (0,) * len(shape))

    return pl.pallas_call(
        project_kernel,
        grid_spec=pltpu.PrefetchScalarGridSpec(
            num_scalar_prefetch=2,
            grid=(4,),
            in_specs=[
                pl.BlockSpec((2 * BLOCK, D), lambda i, p, f: (i, 0)),
                whole((D, 512)),
                whole((1, D)),
                whole((DEPTH, BLOCK, LANES)),
                whole((DEPTH, BLOCK, LANES)),
            ],
            out_specs=[
                pl.BlockSpec(memory_space=pltpu.SMEM),
                pl.BlockSpec((2, 2 * BLOCK, LANES), lambda i, p, f: (i, 0, 0)),
                whole((12, BLOCK, LANES)),
            ],
            scratch_shapes=[pltpu.VMEM((16, BLOCK, LANES), F32)],
        ),
        out_shape=(
            jax.ShapeDtypeStruct((MEMBERS, DEPTH), jnp.int32),
            jax.ShapeDtypeStruct((MEMBERS, 2 * BLOCK, LANES), BF16),
            jax.ShapeDtypeStruct((12, BLOCK, LANES), BF16),
        ),
        compiler_params=pltpu.CompilerParams(vmem_limit_bytes=VMEM_BYTES),
        name="project",
    )(parent, first.reshape(1), stream_all, w_attn, gain, cosine, sine)


def attend_block(lineage, block, queries, alive, load, keys, values):
    for step in range(DEPTH):
        node = jnp.maximum(lineage[block, step], 0)
        rows = pl.ds(step * BLOCK, BLOCK)
        keys[rows] = load(node, key_unit(lax.rem(node, 8)))
        values[rows] = load(node, value_unit(lax.rem(node, 8)))
    scores = lax.dot_general(
        queries, keys[...], (((1,), (1,)), ((), ())), preferred_element_type=F32
    ) * SCALE
    limit = count_ancestors(lineage, block) * BLOCK
    seen = lax.broadcasted_iota(jnp.int32, (1, DEPTH * BLOCK), 1) < limit
    t = lax.broadcasted_iota(jnp.int32, (2 * BLOCK, BLOCK), 0) % BLOCK
    u = lax.broadcasted_iota(jnp.int32, (2 * BLOCK, BLOCK), 1)
    own = jnp.logical_and(u <= t, jnp.logical_or(alive > 0.5, u == t))
    scores = jnp.concatenate(
        [
            jnp.where(own, scores[:, :BLOCK], NEGATIVE),
            jnp.where(seen[:, BLOCK:], scores[:, BLOCK:], NEGATIVE),
        ],
        axis=1,
    )
    largest = jnp.max(scores, axis=1, keepdims=True)
    terms = jnp.exp(scores - largest)
    chances = (terms / jnp.sum(terms, axis=1, keepdims=True)).astype(BF16)
    return jnp.dot(chances, values[...], preferred_element_type=F32).astype(BF16)


def middle_kernel(
    lineage, live, gain, query, stream, cotangent, own_kv, w_out, own_feed, own_down,
    kv_out, middle, rms_out, grad_middle, grads_in, down_terms, feed_grad, down_grad, out_terms, gain_terms,
    kv, w_out_all, w_feed, w_down, mid_all, cot_all, acts, grad_feed, crossed_in, ring_in,
    feed_terms, feed_first, feed_summed, feed_second, feed_sem,
    wide_terms, wide_first, wide_summed, wide_second, wide_sem,
    keys, values, att_out, att_in, att_pad, grads_out, feed_tall, feed_dealt,
    send_sems, recv_sems, local_sems,
):
    xyzc = x, y, z, c = spot()
    j = z * 2 + c
    base = (x * 4 + y) * MEMBERS
    sibling = device_of(x, y, z, 1 - c)
    wire = Wire(send_sems, recv_sems)
    group = [group_peer(x, y, z, c, k) for k in range(1, MEMBERS)]
    greet(group + axis_peers(x, y, z, c, True))
    across, down_first = (((1,), (1,)), ((), ())), (((0,), (0,)), ((), ()))
    locals_ = []

    def keep(source, target):
        copy = pltpu.make_async_copy(source, target, local_sems.at[len(locals_)])
        copy.start()
        locals_.append(copy)
        return copy

    kept = keep(own_kv, kv.at[x, y, pl.ds(0, 12)])
    pairs = PlaneGather(wire, own_kv, kv, quarter_units, xyzc)
    pairs.first()
    cot_kept = keep(cotangent, cot_all.at[z, c])
    cotangents = GroupGather(wire, cotangent, cot_all, xyzc)
    cotangents.begin()
    out_kept = keep(w_out, w_out_all.at[:, pl.ds(0, 96)])
    feed_kept = keep(own_feed, w_feed.at[x, y])
    down_kept = keep(own_down, w_down.at[x, y])
    w_out_all[:, 96:, :] = jnp.zeros((16, 32, D), BF16)
    pairs.relay()
    kept.wait()
    pairs.settle()
    pairs.second()
    cotangents.relay()
    cotangents.near()
    cotangents.far()
    pairs.relay()
    feed = PlaneGather(wire, own_feed, w_feed, quarter(96, 1024), xyzc)
    down = PlaneGather(wire, own_down, w_down, quarter(32, 1536), xyzc)
    feed.first()
    down.first()
    pairs.settle()

    def unpack(line, carry):
        a, b = line // 4, line % 4
        for extra in range(4):
            tiles = [kv[a, b, extra * 3 + k].astype(F32) for k in range(3)]
            kv[a, b, 12 + extra] = unpack_extra(tiles).astype(BF16)
        return carry

    lax.fori_loop(0, 16, unpack, 0)
    kv_copied = keep(kv, kv_out)

    att_slot = wire.reserve(MEMBERS - 1)

    def load(node, unit):
        return kv[lax.div(node, 32), lax.rem(lax.div(node, 8), 4), unit]

    def att_copy(k):
        block = (j + 1 + k) % MEMBERS
        return wire.make(att_slot + k, att_out.at[block], att_in.at[j], base + block)

    def attend(k, carry):
        block = (j + 1 + k) % MEMBERS
        attended = attend_block(lineage, block, query[block], live[block], load, keys, values)
        att_out[block, :, :LANES] = attended[:BLOCK]
        att_out[block, :, LANES:] = attended[BLOCK:]

        @pl.when(k < MEMBERS - 1)
        def _():
            att_copy(k).start()

        return carry

    lax.fori_loop(0, 3, attend, 0)
    feed.relay()
    down.relay()
    lax.fori_loop(3, 6, attend, 0)
    feed.settle()
    down.settle()
    feed_kept.wait()
    down_kept.wait()
    feed.second()
    down.second()
    lax.fori_loop(6, MEMBERS, attend, 0)
    feed.relay()
    down.relay()
    att_in[j] = att_out[j]
    for k in range(MEMBERS - 1):
        att_copy(k).wait_recv()

    for member in range(MEMBERS):
        att_pad[:, member * 256 : (member + 1) * 256] = att_in[member]
    out_kept.wait()

    def project_out(step, carry):
        cols = pl.ds(pl.multiple_of(step * 512, 512), 512)
        weights = w_out_all[:, :, cols].reshape(16 * LANES, 512)
        branch = jnp.dot(att_pad[...], weights, preferred_element_type=F32)
        middle[:, cols] = stream[:, cols].astype(F32) + branch
        return carry

    lax.fori_loop(0, 3, project_out, 0)
    rms = jnp.sqrt(jnp.mean(middle[...] * middle[...], axis=1, keepdims=True) + EPSILON)
    rms_out[...] = jnp.broadcast_to(rms, (BLOCK, LANES))
    mid_all[z, c] = (middle[...] / rms * gain[...]).astype(BF16)
    mids = GroupGather(wire, mid_all.at[z, c], mid_all, xyzc)
    mids.begin()
    mids.relay()
    mids.near()
    mids.far()
    feed.settle()
    down.settle()
    kv_copied.wait()
    cot_kept.wait()
    cotangents.finish()
    mids.finish()
    wire.close()
    for k in range(MEMBERS - 1):
        att_copy(k).wait_send()

    grad_rows = ChipScatter(wire, kv, 2, crossed_in, ring_in, xyzc)

    def feed_forward(step, carry):
        place = (z + 1 + step) % 4
        rows = mid_all[place].reshape(2 * BLOCK, D)
        weights = w_feed[...].reshape(D, 1024)
        both = jnp.dot(rows, weights, preferred_element_type=F32)
        gate, up = both[:, :512], both[:, 512:]
        sigmoid = 1.0 / (1.0 + jnp.exp(-gate))
        silu = gate * sigmoid
        activated = (silu * up).astype(BF16)
        acts[place] = activated
        cot = cot_all[place].reshape(2 * BLOCK, D)
        down_rows = w_down[...].reshape(512, D)
        grad_act = lax.dot_general(cot, down_rows, across, preferred_element_type=F32)
        grad_gate = (grad_act * up * sigmoid * (1.0 + gate * (1.0 - sigmoid))).astype(BF16)
        grad_up = (grad_act * silu).astype(BF16)
        grad_feed[place, :, :512] = grad_gate
        grad_feed[place, :, 512:] = grad_up
        grads = lax.dot_general(grad_feed[place], weights, across, preferred_element_type=F32).astype(BF16)
        grad_rows.put(step, grads)
        outs = jnp.dot(activated, down_rows, preferred_element_type=F32).astype(BF16)
        for core in range(2):
            for tile in range(12):
                kv[place, core, tile] = outs[
                    core * BLOCK : (core + 1) * BLOCK, tile * LANES : (tile + 1) * LANES
                ]

        @pl.when(step > 0)
        def _():
            grad_rows.turn(step - 1)

        return carry

    lax.fori_loop(0, 4, feed_forward, 0)
    down_copied = keep(kv.at[:, pl.ds(0, 2), pl.ds(0, 12)], down_terms)

    def feed_weights(step, carry):
        cols = pl.ds(pl.multiple_of(step * 384, 384), 384)
        left = mid_all[:, :, :, cols].reshape(MEMBERS * BLOCK, 384)
        right = grad_feed[...].reshape(MEMBERS * BLOCK, 1024)
        total = lax.dot_general(left, right, down_first, preferred_element_type=F32)
        feed_terms[step] = total.astype(BF16).reshape(4, 96, 1024)
        return carry

    lax.fori_loop(0, 4, feed_weights, 0)
    feeds = PlaneScatter(wire, feed_terms, (feed_first, feed_summed, feed_second, feed_sem), xyzc)
    feeds.first()

    def down_weights(step, carry):
        cols = pl.ds(pl.multiple_of(step * 128, 128), 128)
        left = acts[:, :, cols].reshape(MEMBERS * BLOCK, 128)
        right = cot_all[...].reshape(MEMBERS * BLOCK, D)
        total = lax.dot_general(left, right, down_first, preferred_element_type=F32)
        wide_terms[step] = total.astype(BF16).reshape(4, 32, D)
        return carry

    lax.fori_loop(0, 4, down_weights, 0)
    wides = PlaneScatter(wire, wide_terms, (wide_first, wide_summed, wide_second, wide_sem), xyzc)
    wides.first()

    grad_mid = grad_rows.total()
    rms = rms_out[:, :1]
    scaled = middle[...] / rms
    gain_terms[...] = jnp.sum(grad_mid * scaled, axis=0, keepdims=True)
    weighted = grad_mid * gain[...]
    back = (weighted - scaled * jnp.mean(weighted * scaled, axis=1, keepdims=True)) / rms
    grad_middle[...] = cot_all[z, c].astype(F32) + back
    branch_grad = grad_middle[...].astype(BF16)

    def spread(step, carry):
        weights = w_out_all[pl.ds(step * 4, 4)].reshape(4 * LANES, D)
        grads = lax.dot_general(branch_grad, weights, across, preferred_element_type=F32).astype(BF16)
        for part in range(2):
            grads_out[step * 2 + part] = grads[:, part * 256 : (part + 1) * 256]
        return carry

    lax.fori_loop(0, 4, spread, 0)
    kept = keep(grads_out.at[j], grads_in.at[j])
    dealt = [
        wire.send(grads_out.at[(j + k) % MEMBERS], grads_in.at[j], group[k - 1]) for k in (4, 5, 3, 2, 6, 7, 1)
    ]

    def out_weights(step, carry):
        cols = pl.ds(pl.multiple_of(step * 512, 512), 512)
        total = lax.dot_general(att_pad[:, cols], branch_grad, down_first, preferred_element_type=F32)
        w_out_all[pl.ds(step * 4, 4)] = total.astype(BF16).reshape(4, LANES, D)
        return carry

    lax.fori_loop(0, 4, out_weights, 0)
    out_copied = keep(w_out_all.at[:, pl.ds(0, 96)], out_terms)

    feeds.add_first()
    feeds.second()
    wides.add_first()
    wides.second()
    feeds.arrive()
    for half in range(2):
        feed_tall[pl.ds(half * 48, 48)] = feeds.total(half)
    split_rows(feed_tall, feed_dealt)
    feed_grad[j] = feed_dealt[j]
    dealt += [
        wire.send(feed_dealt.at[(j + k) % MEMBERS], feed_grad.at[j], group[k - 1]) for k in range(1, MEMBERS)
    ]
    wides.arrive()
    for half in range(2):
        down_grad[pl.ds(half * 16, 16)] = wides.total(half)
    for copy in dealt:
        copy.wait_recv()
    for copy in (kept, down_copied, out_copied):
        copy.wait()
    wire.close()
    grad_rows.close()


def middle_part(lineage, live, gain, query, stream, cotangent, own_kv, w_out, own_feed, own_down):
    shape = jax.ShapeDtypeStruct
    vmem = pltpu.VMEM
    smem = pl.BlockSpec(memory_space=pltpu.SMEM)
    return communicate(
        middle_kernel,
        (
            shape((4, 4, 16, BLOCK, LANES), BF16),
            shape((BLOCK, D), F32),
            shape((BLOCK, LANES), F32),
            shape((BLOCK, D), F32),
            shape((MEMBERS, BLOCK, 2 * LANES), BF16),
            shape((4, 2, 12, BLOCK, LANES), BF16),
            shape((MEMBERS, 12, 1024), F32),
            shape((32, D), F32),
            shape((16, 96, D), BF16),
            shape((1, D), F32),
        ),
        [smem] + [INVMEM] * 4 + [ANY] * 5,
        (ANY, INVMEM, INVMEM, INVMEM, ANY, ANY, INVMEM, INVMEM, ANY, INVMEM),
        [
            vmem((4, 4, 16, BLOCK, LANES), BF16),
            vmem((16, LANES, D), BF16),
            vmem((4, 4, 96, 1024), BF16),
            vmem((4, 4, 32, D), BF16),
            vmem((4, 2, BLOCK, D), BF16),
            vmem((4, 2, BLOCK, D), BF16),
            vmem((4, 2 * BLOCK, 512), BF16),
            vmem((4, 2 * BLOCK, 1024), BF16),
        ]
        + chip_scatter_scratch()
        + [vmem((4, 4, 96, 1024), BF16)]
        + scatter_scratch(96, 1024, mine=False)
        + [vmem((4, 4, 32, D), BF16)]
        + scatter_scratch(32, D, mine=False)
        + [
            vmem((DEPTH * BLOCK, LANES), BF16),
            vmem((DEPTH * BLOCK, LANES), BF16),
            vmem((MEMBERS, BLOCK, 2 * LANES), BF16),
            vmem((MEMBERS, BLOCK, 2 * LANES), BF16),
            vmem((BLOCK, 2048), BF16),
            vmem((MEMBERS, BLOCK, 2 * LANES), BF16),
            vmem((96, 1024), F32),
            vmem((MEMBERS, 12, 1024), F32),
        ]
        + wire_scratch(144)
        + [pltpu.SemaphoreType.DMA((12,))],
        2,
        "middle_part",
        62 * 2**20,
    )(lineage, live, gain, query, stream, cotangent, own_kv, w_out, own_feed, own_down)


def split_rows(tall, dealt):
    for member in range(MEMBERS):
        dealt[member] = tall[pl.ds(member * 12, 12)]


def attend_back_kernel(lineage, query, kv, live, grad, grad_query, grad_kv, keys, values, sums):
    block = pl.program_id(0)

    @pl.when(block == 0)
    def _():
        def clear(step, carry):
            sums[step] = jnp.zeros((BLOCK, LANES), F32)
            return carry

        lax.fori_loop(0, 256, clear, 0)

    for step in range(DEPTH):
        node = jnp.maximum(lineage[block, step], 0)
        rows = pl.ds(step * BLOCK, BLOCK)
        at = lax.div(node, 8) * 16
        keys[rows] = kv[at + key_unit(lax.rem(node, 8))]
        values[rows] = kv[at + value_unit(lax.rem(node, 8))]
    queries = query[0]
    grads = jnp.concatenate([grad[0, :, :LANES], grad[0, :, LANES:]], axis=0)
    across = (((1,), (1,)), ((), ()))
    scores = lax.dot_general(keys[...], queries, across, preferred_element_type=F32) * SCALE
    limit = count_ancestors(lineage, block) * BLOCK
    seen = lax.broadcasted_iota(jnp.int32, (DEPTH * BLOCK, 1), 0) < limit
    u = lax.broadcasted_iota(jnp.int32, (BLOCK, 2 * BLOCK), 0)
    t = lax.broadcasted_iota(jnp.int32, (BLOCK, 2 * BLOCK), 1) % BLOCK
    alive = jnp.transpose(jnp.broadcast_to(live[0], (BLOCK, BLOCK)))
    alive = jnp.concatenate([alive, alive], axis=1)
    own = jnp.logical_and(u <= t, jnp.logical_or(alive > 0.5, u == t))
    scores = jnp.concatenate(
        [
            jnp.where(own, scores[:BLOCK], NEGATIVE),
            jnp.where(seen[BLOCK:], scores[BLOCK:], NEGATIVE),
        ],
        axis=0,
    )
    largest = jnp.max(scores, axis=0, keepdims=True)
    terms = jnp.exp(scores - largest)
    chances = terms / jnp.sum(terms, axis=0, keepdims=True)
    grad_chances = lax.dot_general(values[...], grads, across, preferred_element_type=F32)
    inner = jnp.sum(chances * grad_chances, axis=0, keepdims=True)
    grad_scores = (chances * (grad_chances - inner)).astype(BF16)
    grad_query[0] = (
        lax.dot_general(grad_scores, keys[...], (((0,), (0,)), ((), ())), preferred_element_type=F32) * SCALE
    )
    grad_keys = jnp.dot(grad_scores, queries, preferred_element_type=F32) * SCALE
    grad_values = jnp.dot(chances.astype(BF16), grads, preferred_element_type=F32)
    for step in range(DEPTH):
        node = lineage[block, step]
        rows = slice(step * BLOCK, (step + 1) * BLOCK)

        @pl.when(node >= 0)
        def _():
            at = lax.div(node, 8) * 16
            sums[at + key_unit(lax.rem(node, 8))] += grad_keys[rows]
            sums[at + value_unit(lax.rem(node, 8))] += grad_values[rows]

    @pl.when(block == MEMBERS - 1)
    def _():
        def store(line, carry):
            for tile in range(12):
                packed = pack_tile(sums[line * 16 + tile], sums[line * 16 + 12 + tile // 3], tile % 3)
                grad_kv[line * 12 + tile] = packed.astype(BF16)
            return carry

        lax.fori_loop(0, 16, store, 0)


def attend_back(lineage, query, kv, live, grad):
    def whole(count):
        return pl.BlockSpec((count, BLOCK, LANES), lambda b, s: (0, 0, 0), pipeline_mode=pl.Buffered(1))

    return pl.pallas_call(
        attend_back_kernel,
        grid_spec=pltpu.PrefetchScalarGridSpec(
            num_scalar_prefetch=1,
            grid=(MEMBERS,),
            in_specs=[
                pl.BlockSpec((1, 2 * BLOCK, LANES), lambda b, s: (b, 0, 0)),
                whole(256),
                pl.BlockSpec((1, 1, LANES), lambda b, s: (b, 0, 0)),
                pl.BlockSpec((1, BLOCK, 2 * LANES), lambda b, s: (b, 0, 0)),
            ],
            out_specs=[
                pl.BlockSpec((1, 2 * BLOCK, LANES), lambda b, s: (b, 0, 0)),
                whole(192),
            ],
            scratch_shapes=[
                pltpu.VMEM((DEPTH * BLOCK, LANES), BF16),
                pltpu.VMEM((DEPTH * BLOCK, LANES), BF16),
                pltpu.VMEM((256, BLOCK, LANES), F32),
            ],
        ),
        out_shape=(
            jax.ShapeDtypeStruct((MEMBERS, 2 * BLOCK, LANES), F32),
            jax.ShapeDtypeStruct((192, BLOCK, LANES), BF16),
        ),
        compiler_params=pltpu.CompilerParams(vmem_limit_bytes=VMEM_BYTES),
        name="attend_back",
    )(lineage, query, kv, live, grad)


def gain_tiles(rows):
    lane = lane_of((8, LANES))
    tiles = [rows[:, tile * LANES : (tile + 1) * LANES] for tile in range(12)]
    pieces = []
    for piece in range(16):
        tile, skip = divmod(piece * 96, LANES)
        low = pltpu.roll(tiles[tile], (LANES - skip) % LANES, 1)
        high = pltpu.roll(tiles[min(tile + 1, 11)], (LANES - skip) % LANES, 1)
        pieces.append(jnp.where(lane < LANES - skip, low, high))
    return pieces


def ending_kernel(
    lineage, grad_query, cosine, sine, stream_all, w_attn, gain, gain_two, stream, middle, grad_middle,
    kv_terms, down_terms, out_terms,
    mixed_out, stream_grad, attn_grad, out_grad, gain_grad, rms_out,
    normed, raw, units, grad_terms, crossed_in, ring_in, attn_terms, attn_tall, attn_dealt,
    out_tall, out_dealt, out_mine, out_crossed, gain_terms, gain_in, gain_line, gain_in_two, gain_in_three,
    *scratch,
):
    xyzc = x, y, z, c = spot()
    j = z * 2 + c
    down_scratch, kv_scratch, attn_scratch, out_scratch = scratch[:5], scratch[5:10], scratch[10:14], scratch[14:18]
    send_sems, recv_sems, local_sem = scratch[18:]
    wire = Wire(send_sems, recv_sems)
    group = [group_peer(x, y, z, c, k) for k in range(1, MEMBERS)]
    greet(group + axis_peers(x, y, z, c, True))
    sibling = device_of(x, y, z, 1 - c)
    pairs = PlaneScatter(wire, kv_terms, kv_scratch, xyzc)
    pairs.first()
    downs = GroupScatter(wire, down_terms, *down_scratch, xyzc)
    downs.begin()
    own_half = pl.ds(pl.multiple_of(c * 768, 768), 768)
    other_half = pl.ds(pl.multiple_of((1 - c) * 768, 768), 768)
    crossed = wire.send(out_terms.at[:, :, :, other_half], out_crossed, sibling)
    local = pltpu.make_async_copy(out_terms.at[:, :, :, own_half], out_mine, local_sem)
    local.start()

    def norm_rows(step, carry):
        rows = pl.ds(pl.multiple_of(step * BLOCK, BLOCK), BLOCK)
        wide = stream_all[rows].astype(F32)
        rms = jnp.sqrt(jnp.mean(wide * wide, axis=1, keepdims=True) + EPSILON)
        normed[rows] = (wide / rms * gain[...]).astype(BF16)
        return carry

    lax.fori_loop(0, MEMBERS, norm_rows, 0)

    def turn(block, v):
        depth = count_ancestors(lineage, block) - 1
        return (v * cosine[depth] - swap_halves(v) * sine[depth]).astype(BF16)

    def query_rows(block, carry):
        rows = pl.ds(pl.multiple_of(block * BLOCK, BLOCK), BLOCK)
        raw[rows, :128] = turn(block, grad_query[block, :BLOCK])
        raw[rows, 128:256] = turn(block, grad_query[block, BLOCK:])
        return carry

    lax.fori_loop(0, MEMBERS, query_rows, 0)
    local.wait()
    crossed.wait_recv()

    def add_halves(step, carry):
        a, b = step // 4, step % 4
        total = out_mine[a, b].astype(F32) + out_crossed[a, b].astype(F32)
        out_mine[a, b] = total.astype(BF16)
        return carry

    lax.fori_loop(0, 16, add_halves, 0)
    outs = PlaneScatter(wire, out_mine, out_scratch, xyzc)
    downs.turn()
    pairs.add_first()
    pairs.second()
    downs.finish(stream_grad)
    mixed_out[...] = (middle[...] + stream_grad[...]).astype(BF16)
    pairs.arrive()
    outs.first()
    for half in range(2):
        units[pl.ds(half * 6, 6)] = pairs.total(half)
    for extra in range(4):
        units[12 + extra] = unpack_extra([units[extra * 3 + k] for k in range(3)])

    def pair_rows(block, carry):
        rows = pl.ds(pl.multiple_of(block * BLOCK, BLOCK), BLOCK)
        raw[rows, 256:384] = turn(block, units[key_unit(block)])
        value = units[value_unit(block)]
        raw[rows, 384:] = jnp.where(lane_of((BLOCK, LANES)) < HEAD_DIM, value, 0.0).astype(BF16)
        return carry

    lax.fori_loop(0, MEMBERS, pair_rows, 0)

    grad_rows = ChipScatter(wire, grad_terms, 0, crossed_in, ring_in, xyzc)
    gain_terms[...] = jnp.zeros((1, D), F32)

    def rows_back(step, carry):
        rows = pl.ds(pl.multiple_of(grad_rows.place(step) * 256, 256), 256)
        grads = lax.dot_general(raw[rows], w_attn[...], (((1,), (1,)), ((), ())), preferred_element_type=F32)
        grad_rows.put(step, grads.astype(BF16))
        wide = stream_all[rows].astype(F32)
        rms = jnp.sqrt(jnp.mean(wide * wide, axis=1, keepdims=True) + EPSILON)
        gain_terms[...] += jnp.sum(grads * (wide / rms), axis=0, keepdims=True)

        @pl.when(step > 0)
        def _():
            grad_rows.turn(step - 1)

        return carry

    lax.fori_loop(0, 4, rows_back, 0)
    rows = jnp.concatenate([gain_terms[...], gain_two[...], jnp.zeros((6, D), F32)], axis=0)
    for piece, part in enumerate(gain_tiles(rows)):
        gain_in[piece // 4, piece % 4] = part
    gains = [
        wire.send(gain_in.at[(x + k) % 4], gain_line.at[k], device_of(x + k, y, z, c)) for k in range(1, 4)
    ]

    def weights_back(step, carry):
        cols = pl.ds(pl.multiple_of(step * 384, 384), 384)
        total = lax.dot_general(
            normed[:, cols], raw[...], (((0,), (0,)), ((), ())), preferred_element_type=F32
        )
        attn_terms[step] = total.astype(BF16).reshape(4, 96, 512)
        return carry

    lax.fori_loop(0, 4, weights_back, 0)
    attns = PlaneScatter(wire, attn_terms, attn_scratch, xyzc)
    attns.first()
    for copy in gains:
        copy.wait_recv()
    gain_line[0] = gain_in[x] + gain_line[1] + gain_line[2] + gain_line[3]
    gains = [
        wire.send(gain_line.at[0, (y + k) % 4], gain_in_two.at[k], device_of(x, y + k, z, c)) for k in range(1, 4)
    ]
    outs.add_first()
    outs.second()

    wide = stream[...].astype(F32)
    rms = jnp.sqrt(jnp.mean(wide * wide, axis=1, keepdims=True) + EPSILON)
    rms_out[...] = jnp.broadcast_to(rms, (BLOCK, LANES))
    scaled = wide / rms
    weighted = grad_rows.total() * gain[...]
    back = (weighted - scaled * jnp.mean(weighted * scaled, axis=1, keepdims=True)) / rms
    stream_grad[...] = grad_middle[...] + back

    for copy in gains:
        copy.wait_recv()
    gain_in_three[j] = gain_line[0, y] + gain_in_two[1] + gain_in_two[2] + gain_in_two[3]
    gains = [
        wire.send(gain_in_three.at[j], gain_in_three.at[j], group[k - 1]) for k in range(1, MEMBERS)
    ]
    attns.add_first()
    attns.second()
    outs.arrive()
    for half in range(2):
        out_tall[pl.ds(half * 48, 48)] = outs.total(half)
    split_rows(out_tall, out_dealt)
    out_grad[j] = out_dealt[j]
    dealt = [
        wire.send(out_dealt.at[(j + k) % MEMBERS], out_grad.at[j], group[k - 1]) for k in range(1, MEMBERS)
    ]
    attns.arrive()
    for half in range(2):
        attn_tall[pl.ds(half * 48, 48)] = attns.total(half)
    split_rows(attn_tall, attn_dealt)
    attn_grad[j] = attn_dealt[j]
    dealt += [
        wire.send(attn_dealt.at[(j + k) % MEMBERS], attn_grad.at[j], group[k - 1]) for k in range(1, MEMBERS)
    ]
    for copy in gains:
        copy.wait_recv()
    total = gain_in_three[0]
    for member in range(1, MEMBERS):
        total = total + gain_in_three[member]
    gain_grad[...] = total
    for copy in dealt:
        copy.wait_recv()
    wire.close()
    grad_rows.close()


def ending(
    lineage, grad_query, cosine, sine, stream_all, w_attn, gain, gain_two, stream, middle, grad_middle,
    kv_terms, down_terms, out_terms,
):
    shape, vmem = jax.ShapeDtypeStruct, pltpu.VMEM
    smem = pl.BlockSpec(memory_space=pltpu.SMEM)
    return communicate(
        ending_kernel,
        (
            shape((BLOCK, D), BF16),
            shape((BLOCK, D), F32),
            shape((MEMBERS, 12, 512), F32),
            shape((MEMBERS, 12, 768), F32),
            shape((8, LANES), F32),
            shape((BLOCK, LANES), F32),
        ),
        [smem] + [INVMEM] * 10 + [ANY] * 3,
        (INVMEM,) * 6,
        [
            vmem((MEMBERS * BLOCK, D), BF16),
            vmem((MEMBERS * BLOCK, 512), BF16),
            vmem((16, BLOCK, LANES), F32),
            vmem((4, 2, 12, BLOCK, LANES), BF16),
        ]
        + chip_scatter_scratch()
        + [
            vmem((4, 4, 96, 512), BF16),
            vmem((96, 512), F32),
            vmem((MEMBERS, 12, 512), F32),
            vmem((96, 768), F32),
            vmem((MEMBERS, 12, 768), F32),
            vmem((4, 4, 96, 768), BF16),
            vmem((4, 4, 96, 768), BF16),
            vmem((1, D), F32),
            vmem((4, 4, 8, LANES), F32),
            vmem((4, 4, 8, LANES), F32),
            vmem((4, 8, LANES), F32),
            vmem((MEMBERS, 8, LANES), F32),
        ]
        + group_scatter_scratch()
        + scatter_scratch(12, BLOCK, LANES)
        + scatter_scratch(96, 512, mine=False)
        + scatter_scratch(96, 768, mine=False)
        + wire_scratch(80)
        + [pltpu.SemaphoreType.DMA],
        7,
        "ending",
        62 * 2**20,
    )(
        lineage, grad_query, cosine, sine, stream_all, w_attn, gain, gain_two, stream, middle, grad_middle,
        kv_terms, down_terms, out_terms,
    )


def pack_columns(w_query, w_key, w_value, w_gate, w_up):
    rows = w_query.shape[0]
    query = jnp.pad(w_query.reshape(rows, MEMBERS, 2, 96), ((0, 0), (0, 0), (0, 0), (0, 32))).reshape(rows, MEMBERS, 256)
    key, value = (jnp.pad(w.reshape(rows, MEMBERS, 96), ((0, 0), (0, 0), (0, 32))) for w in (w_key, w_value))
    gate, up = (
        w.reshape(rows, 16, MEMBERS, 32).transpose(0, 2, 1, 3).reshape(rows, MEMBERS, 512) for w in (w_gate, w_up)
    )
    packed = jnp.concatenate([query, key, value, gate, up], axis=2).transpose(1, 0, 2)
    return jnp.pad(packed, ((0, 0), (0, 4), (0, 0)))


def pack_small(attn_gain, mlp_gain, live, member):
    gains = jnp.stack([attn_gain, mlp_gain]).astype(F32)
    place = lax.broadcasted_iota(jnp.int32, (12, LANES), 1) == member * 12 + lax.broadcasted_iota(jnp.int32, (12, LANES), 0)
    spread = jnp.sum(jnp.where(place[None], gains[:, :, None], 0.0), axis=1)
    rows = jnp.concatenate([spread.astype(BF16), live.astype(BF16)[None]])
    return jnp.pad(rows, ((0, 13), (0, 0)))


def shards(
    stream, attn_gain, w_query, w_key, w_value, w_out, mlp_gain, w_gate, w_up, w_down, parent, live_mask, cotangent
):
    me = lax.axis_index("dev")
    member = me % MEMBERS
    cosine, sine = rope_tables()
    packed = pack_columns(w_query, w_key, w_value, w_gate, w_up)
    small = pack_small(attn_gain, mlp_gain, live_mask, member)
    stream_all, w_attn, feed_own, out_all, gains_all, small_all = opening(
        stream, packed, jnp.pad(w_out, ((0, 4), (0, 0))), small
    )
    stream_all = stream_all.reshape(MEMBERS * BLOCK, D)
    w_attn = w_attn.reshape(D, 512)
    gains = gains_all.reshape(16, 16, LANES)[:, :2, :96].transpose(1, 0, 2).reshape(2, 1, D).astype(F32)
    live = small_all[:, 2:3, :].astype(F32)
    lineage, query, own_context = project(
        parent, (me // MEMBERS) * MEMBERS, stream_all, w_attn, gains[0], cosine, sine
    )
    (
        context, middle, branch_rms, grad_middle, grad_heads, down_terms, feed_grad, down_grad, out_terms, gain_two_terms
    ) = middle_part(
        lineage, live, gains[1], query, stream, cotangent, own_context, out_all.reshape(16, 96, D), feed_own, w_down
    )
    gate_grad, up_grad = (
        feed_grad[:, :, part : part + 512].reshape(MEMBERS, 12, 16, 32).transpose(1, 2, 0, 3).reshape(12, FF)
        for part in (0, 512)
    )
    grad_query, context_terms = attend_back(
        lineage, query, context.reshape(256, BLOCK, LANES), live, grad_heads
    )
    mixed_out, stream_grad, attn_grad, out_grad, gain_grad, stream_rms = ending(
        lineage, grad_query, cosine, sine, stream_all, w_attn, gains[0], gain_two_terms, stream, middle, grad_middle,
        context_terms.reshape(4, 4, 12, BLOCK, LANES), down_terms, out_terms.reshape(4, 4, 96, D),
    )
    query_grad = attn_grad[:, :, :256].reshape(MEMBERS, 12, 2, LANES)[..., :96]
    query_grad = query_grad.transpose(1, 0, 2, 3).reshape(12, D)
    key_grad = attn_grad[:, :, 256:352].transpose(1, 0, 2).reshape(12, 768)
    value_grad = attn_grad[:, :, 384:480].transpose(1, 0, 2).reshape(12, 768)
    out_grad = jnp.sum(out_grad.reshape(4, 2, 12, 768), axis=0).transpose(1, 0, 2).reshape(12, D)
    own_gains = lax.dynamic_slice(gain_grad, (0, member * 12), (2, 12))
    return (
        mixed_out, stream_grad, own_gains[0], query_grad, key_grad, value_grad, out_grad, own_gains[1],
        gate_grad, up_grad, down_grad, stream_rms[:, 0], branch_rms[:, 0],
    )


def solution(mesh):
    rows, line = P("dev", None), P("dev")
    return jax.shard_map(
        shards,
        mesh=mesh,
        in_specs=(rows, line, rows, rows, rows, rows, line, rows, rows, rows, P(), line, rows),
        out_specs=(rows, rows, line, rows, rows, rows, rows, line, rows, rows, rows, line, line),
        check_vma=False,
    )
```

```python
import functools

import jax
import jax.numpy as jnp
import numpy as np
from jax import lax
from jax.experimental import pallas as pl
from jax.experimental.pallas import tpu as pltpu
from jax.sharding import PartitionSpec as P

HEADS = 16
KV_HEADS = 8
HEAD_DIM = 96
BLOCK = 128
DEPTH = 10
D = 1536
FF = 4096
MEMBERS = 8
LANES = 128

EPSILON = 1e-05
ROPE_BASE = 100000.0
NEGATIVE = -1e30
SCALE = HEAD_DIM ** (-0.5)
MESH = pl.DeviceIdType.MESH
BF16 = jnp.bfloat16
F32 = jnp.float32
VMEM_BYTES = 56 * 2**20


def spot():
    me = lax.axis_index("dev")
    return me // 32, (me // 8) % 4, (me // 2) % 4, me % 2


def device_of(x, y, z, c):
    return ((x % 4) * 4 + (y % 4)) * 8 + (z % 4) * 2 + c


def announce(peers):
    barrier = pltpu.get_barrier_semaphore()
    for peer in peers:
        pl.semaphore_signal(barrier, inc=1, device_id=(peer,), device_id_type=MESH)


def await_peers(peers):
    pl.semaphore_wait(pltpu.get_barrier_semaphore(), len(peers))


def axis_peers(x, y, z, c, far):
    steps = (1, 2, 3) if far else (1, 3)
    return [device_of(x + k, y, z, c) for k in steps] + [device_of(x, y + k, z, c) for k in steps]


def group_peer(x, y, z, c, k):
    member = (z * 2 + c + k) % MEMBERS
    return (x * 4 + y) * MEMBERS + member


class Wire:
    def __init__(self, send_sems, recv_sems):
        self.send_sems = send_sems
        self.recv_sems = recv_sems
        self.used = 0
        self.open = []

    def reserve(self, count):
        self.used += count
        return self.used - count

    def make(self, slot, source, target, peer):
        return pltpu.make_async_remote_copy(
            src_ref=source,
            dst_ref=target,
            send_sem=self.send_sems.at[slot],
            recv_sem=self.recv_sems.at[slot],
            device_id=(peer,),
            device_id_type=MESH,
        )

    def send(self, source, target, peer):
        copy = self.make(self.reserve(1), source, target, peer)
        copy.start()
        self.open.append(copy)
        return copy

    def close(self):
        for copy in self.open:
            copy.wait_send()
        self.open = []


class Ring:
    def __init__(self, wire, own, part, place, up, down):
        self.wire, self.own, self.part = wire, own, part
        self.place, self.up, self.down = place, up, down

    def begin(self):
        send, part, place = self.wire.send, self.part, self.place
        self.low_up = send(self.own(0), part(place, 0), self.up)
        self.high_down = send(self.own(1), part(place, 1), self.down)
        self.high_up = send(self.own(1), part(place, 1), self.up)
        self.low_down = send(self.own(0), part(place, 0), self.down)

    def relay(self):
        before, after = (self.place + 3) % 4, (self.place + 1) % 4
        self.low_up.wait_recv()
        self.far_up = self.wire.send(self.part(before, 0), self.part(before, 0), self.up)
        self.high_down.wait_recv()
        self.far_down = self.wire.send(self.part(after, 1), self.part(after, 1), self.down)

    def near(self):
        self.high_up.wait_recv()
        self.low_down.wait_recv()

    def far(self):
        self.far_up.wait_recv()
        self.far_down.wait_recv()


class PlaneGather:
    def __init__(self, wire, own, out, cut, xyzc):
        self.wire, self.own, self.out, self.cut = wire, own, out, cut
        x, y, z, c = xyzc
        self.x, self.y = x, y
        self.x_up, self.x_down = device_of(x + 1, y, z, c), device_of(x + 3, y, z, c)
        self.y_up, self.y_down = device_of(x, y + 1, z, c), device_of(x, y + 3, z, c)

    def pair(self, one_own, one_part, two_own, two_part, one_on_x):
        on_x = (self.x, self.x_up, self.x_down)
        on_y = (self.y, self.y_up, self.y_down)
        cut = self.cut.quarter
        self.one = Ring(
            self.wire,
            lambda side: one_own(cut(0, side)),
            lambda place, side: one_part(place, cut(0, side)),
            *(on_x if one_on_x else on_y),
        )
        self.two = Ring(
            self.wire,
            lambda side: two_own(cut(1, side)),
            lambda place, side: two_part(place, cut(1, side)),
            *(on_y if one_on_x else on_x),
        )
        self.one.begin()
        self.two.begin()

    def first(self):
        own, out, x, y = self.own, self.out, self.x, self.y
        self.pair(
            lambda q: own.at[q],
            lambda place, q: out.at[(place, y) + q],
            lambda q: own.at[q],
            lambda place, q: out.at[(x, place) + q],
            True,
        )

    def relay(self):
        self.one.relay()
        self.two.relay()

    def settle(self):
        for ring in (self.one, self.two):
            ring.near()
            ring.far()

    def second(self):
        out, x, y = self.out, self.x, self.y
        every = slice(None)
        self.pair(
            lambda q: out.at[(every, y) + q],
            lambda place, q: out.at[(every, place) + q],
            lambda q: out.at[(x, every) + q],
            lambda place, q: out.at[(place, every) + q],
            False,
        )


class Rows:
    def __init__(self, rows, cols, start=0):
        self.rows, self.cols, self.start = rows // 2, cols // 2, start

    def half(self, half):
        return (pl.ds(half * self.rows, self.rows),)

    def side(self, side):
        return (slice(None), pl.ds(side * self.cols, self.cols))

    def quarter(self, half, side):
        first = self.start + side * self.cols
        if not isinstance(first, int):
            first = pl.multiple_of(first, LANES)
        return self.half(half) + (pl.ds(first, self.cols),)

    def shapes(self):
        return (self.rows, 2 * self.cols), (self.rows, self.cols)


class Units:
    def half(self, half):
        return (pl.ds(half * 6, 6),)

    def side(self, side):
        return (pl.ds(side * 3, 3),)

    def quarter(self, half, side):
        return (pl.ds(half * 6 + side * 3, 3),)

    def shapes(self):
        return (6, BLOCK, LANES), (3, BLOCK, LANES)


class GroupGather:
    def __init__(self, wire, own, out, xyzc):
        self.wire, self.own, self.out = wire, own, out
        x, y, z, c = xyzc
        self.z, self.c = z, c
        self.sibling = device_of(x, y, z, 1 - c)
        half = out.shape[2] // 2
        self.ring = Ring(
            wire,
            lambda side: own.at[pl.ds(side * half, half)],
            lambda place, side: out.at[place, c, pl.ds(side * half, half)],
            z, device_of(x, y, z + 1, c), device_of(x, y, z + 3, c),
        )
        self.crossed = []

    def begin(self):
        self.ring.begin()
        self.crossed.append(self.wire.send(self.own, self.out.at[self.z, self.c], self.sibling))

    def cross(self, k):
        piece = self.out.at[(self.z + k) % 4, self.c]
        self.crossed.append(self.wire.send(piece, piece, self.sibling))

    def relay(self):
        self.ring.relay()

    def near(self):
        self.ring.near()
        self.cross(1)
        self.cross(3)

    def far(self):
        self.ring.far()
        self.cross(2)

    def finish(self, after=0):
        for copy in self.crossed[after:]:
            copy.wait_recv()


class PlaneScatter:
    def __init__(self, wire, terms, cut, scratch, xyzc):
        self.wire, self.terms, self.cut = wire, terms, cut
        *room, self.near_in, self.far_in, self.passed, self.summed, self.second_in = scratch
        self.room = room
        self.x, self.y, self.z, self.c = xyzc

    def peer(self, along_x, k):
        if along_x:
            return device_of(self.x + k, self.y, self.z, self.c)
        return device_of(self.x, self.y + k, self.z, self.c)

    def place(self, half, k):
        return ((self.x, self.y)[half] + k) % 4

    def lead(self, half, k, line=slice(None)):
        place = self.place(half, k)
        return (place, line) if half == 0 else (line, place)

    def part(self, half, k, side):
        return self.terms.at[self.lead(half, k) + self.cut.quarter(half, side)]

    def own(self, half, line):
        if self.room:
            return self.room[0][half, line]
        return self.terms[self.lead(half, 0, line) + self.cut.half(half)]

    def edge(self, half, way, line):
        if self.room:
            return self.room[1][half, way, line]
        return self.terms[self.lead(half, (1, 3)[way], line) + self.cut.quarter(half, way)]

    def first(self):
        send = self.wire.send
        self.far, self.plain, self.locals = [], [], []
        if self.room:
            sems = self.room[2]
            for half in range(2):
                pairs = [(self.terms.at[self.lead(half, 0) + self.cut.half(half)], self.room[0].at[half])]
                pairs += [(self.part(half, (1, 3)[way], way), self.room[1].at[half, way]) for way in range(2)]
                for slot, (source, target) in enumerate(pairs):
                    copy = pltpu.make_async_copy(source, target, sems.at[half, slot])
                    copy.start()
                    self.locals.append(copy)
        for half in range(2):
            for way in range(2):
                self.far.append(
                    send(self.part(half, 2, way), self.far_in.at[half, way], self.peer(half == 0, (1, 3)[way]))
                )
        for half in range(2):
            for way in range(2):
                k = (1, 3)[way]
                landing = self.near_in.at[(half, way, slice(None)) + self.cut.side(1 - way)]
                self.plain.append(send(self.part(half, k, 1 - way), landing, self.peer(half == 0, k)))

    def relay(self):
        for copy in self.locals:
            copy.wait()
        self.relayed = []
        for half in range(2):
            for way in range(2):
                self.far[half * 2 + way].wait_recv()

                def add(line, carry):
                    total = self.edge(half, way, line).astype(F32) + self.far_in[half, way, line].astype(F32)
                    self.passed[half, way, line] = total.astype(BF16)
                    return carry

                lax.fori_loop(0, 4, add, 0)
                landing = self.near_in.at[(half, way, slice(None)) + self.cut.side(way)]
                self.relayed.append(
                    self.wire.send(self.passed.at[half, way], landing, self.peer(half == 0, (1, 3)[way]))
                )

    def add_first(self):
        for copy in self.plain + self.relayed:
            copy.wait_recv()
        for half in range(2):

            def body(line, carry):
                total = self.own(half, line).astype(F32)
                for way in range(2):
                    total = total + self.near_in[half, way, line].astype(F32)
                self.summed[half, line] = total.astype(BF16)
                return carry

            lax.fori_loop(0, 4, body, 0)

    def second(self):
        self.copies = []
        for k in (2, 1, 3):
            for half in range(2):
                self.copies.append(
                    self.wire.send(
                        self.summed.at[half, self.place(1 - half, k)],
                        self.second_in.at[half, k - 1],
                        self.peer(half == 1, k),
                    )
                )

    def total(self, half):
        total = self.summed[half, self.place(1 - half, 0)].astype(F32)
        for k in range(3):
            total = total + self.second_in[half, k].astype(F32)
        return total

    def arrive(self):
        for copy in self.copies:
            copy.wait_recv()


def scatter_scratch(cut, room=False):
    half, part = cut.shapes()
    vmem = pltpu.VMEM
    held = [vmem((2, 4) + half, BF16), vmem((2, 2, 4) + part, BF16), pltpu.SemaphoreType.DMA((2, 3))]
    return (held if room else []) + [
        vmem((2, 2, 4) + half, BF16),
        vmem((2, 2, 4) + part, BF16),
        vmem((2, 2, 4) + part, BF16),
        vmem((2, 4) + half, BF16),
        vmem((2, 3) + half, BF16),
    ]


class GroupScatter:
    def __init__(self, wire, terms, mine, crossed_in, summed, ring_in, local_sem, xyzc):
        self.wire, self.terms = wire, terms
        self.mine, self.crossed_in, self.summed, self.ring_in = mine, crossed_in, summed, ring_in
        self.x, self.y, self.z, self.c = xyzc
        self.local_sem = local_sem

    def begin(self):
        self.local = pltpu.make_async_copy(self.terms.at[:, self.c], self.mine, self.local_sem)
        self.local.start()
        sibling = device_of(self.x, self.y, self.z, 1 - self.c)
        self.crossed = {}
        for k in (2, 1, 3, 0):
            place = (self.z + k) % 4
            self.crossed[k] = self.wire.send(
                self.terms.at[place, 1 - self.c], self.crossed_in.at[place], sibling
            )

    def turn(self):
        self.local.wait()
        self.copies = []
        for k in (2, 1, 3):
            place = (self.z + k) % 4
            self.crossed[k].wait_recv()

            def body(tile, carry):
                total = self.mine[place, tile].astype(F32) + self.crossed_in[place, tile].astype(F32)
                self.summed[place, tile] = total.astype(BF16)
                return carry

            lax.fori_loop(0, 12, body, 0)
            self.copies.append(
                self.wire.send(
                    self.summed.at[place],
                    self.ring_in.at[k - 1],
                    device_of(self.x, self.y, self.z + k, self.c),
                )
            )

    def finish(self, out):
        self.crossed[0].wait_recv()
        for copy in self.copies:
            copy.wait_recv()
        for tile in range(12):
            total = self.mine[self.z, tile].astype(F32) + self.crossed_in[self.z, tile].astype(F32)
            for k in range(3):
                total = total + self.ring_in[k, tile].astype(F32)
            out[:, tile * LANES : (tile + 1) * LANES] = total


class ChipScatter:
    def __init__(self, wire, terms, at, crossed_in, ring_in, xyzc):
        self.wire, self.terms, self.at = wire, terms, at
        self.crossed_in, self.ring_in = crossed_in, ring_in
        self.x, self.y, self.z, self.c = xyzc
        self.crossed_slot, self.ring_slot = wire.reserve(4), wire.reserve(3)
        self.all_tiles = pl.ds(0, 12)

    def place(self, step):
        return (self.z + step) % 4

    def crossed(self, step):
        place = self.place(step)
        return self.wire.make(
            self.crossed_slot + step,
            self.terms.at[place, self.at + 1 - self.c, self.all_tiles],
            self.crossed_in.at[place],
            device_of(self.x, self.y, self.z, 1 - self.c),
        )

    def ring(self, step):
        return self.wire.make(
            self.ring_slot + step - 1,
            self.terms.at[self.place(step), self.at + self.c, self.all_tiles],
            self.ring_in.at[step - 1],
            device_of(self.x, self.y, self.z + step, self.c),
        )

    def put(self, step, grads):
        place = self.place(step)
        for core in range(2):
            for tile in range(12):
                self.terms[place, self.at + core, tile] = grads[
                    core * BLOCK : (core + 1) * BLOCK, tile * LANES : (tile + 1) * LANES
                ]
        self.crossed(step).start()

    def turn(self, step):
        place, line = self.place(step), self.at + self.c
        self.crossed(step).wait_recv()

        def add(tile, carry):
            total = self.terms[place, line, tile].astype(F32) + self.crossed_in[place, tile].astype(F32)
            self.terms[place, line, tile] = total.astype(BF16)
            return carry

        lax.fori_loop(0, 12, add, 0)
        self.ring(step).start()

    def total(self):
        self.crossed(0).wait_recv()
        for step in range(1, 4):
            self.ring(step).wait_recv()
        tiles = []
        for tile in range(12):
            total = self.terms[self.z, self.at + self.c, tile].astype(F32)
            total = total + self.crossed_in[self.z, tile].astype(F32)
            for step in range(3):
                total = total + self.ring_in[step, tile].astype(F32)
            tiles.append(total)
        return jnp.concatenate(tiles, axis=1)

    def close(self):
        for step in range(4):
            self.crossed(step).wait_send()
        for step in range(1, 4):
            self.ring(step).wait_send()


def group_scatter_scratch():
    return [
        pltpu.VMEM((4, 12, BLOCK, LANES), BF16),
        pltpu.VMEM((4, 12, BLOCK, LANES), BF16),
        pltpu.VMEM((4, 12, BLOCK, LANES), BF16),
        pltpu.VMEM((3, 12, BLOCK, LANES), BF16),
        pltpu.SemaphoreType.DMA,
    ]


def chip_scatter_scratch():
    return [pltpu.VMEM((4, 12, BLOCK, LANES), BF16), pltpu.VMEM((3, 12, BLOCK, LANES), BF16)]


def wire_scratch(count):
    return [pltpu.SemaphoreType.DMA((count,)), pltpu.SemaphoreType.DMA((count,))]


ANY = pl.BlockSpec(memory_space=pl.ANY)
INVMEM = pl.BlockSpec(memory_space=pltpu.VMEM)


def communicate(kernel, out_shapes, in_specs, out_specs, scratch, ident, name, vmem=VMEM_BYTES):
    return pl.pallas_call(
        kernel,
        out_shape=out_shapes,
        in_specs=in_specs,
        out_specs=out_specs,
        scratch_shapes=scratch,
        compiler_params=pltpu.CompilerParams(
            collective_id=ident, has_side_effects=True, vmem_limit_bytes=vmem
        ),
        name=name,
    )


def key_unit(member):
    return member + jnp.where(member >= 6, 6, 0) + jnp.where(member >= 7, 1, 0)


def value_unit(member):
    return member + 6 + jnp.where(member >= 6, 1, 0) + jnp.where(member >= 7, 1, 0)


def gain_rows(pieces):
    return jnp.concatenate(join_heads(pieces), axis=1)


def head_window(tiles, head):
    tile, skip = divmod(head * HEAD_DIM, LANES)
    lane = lane_of(tiles[0].shape)
    window = pltpu.roll(tiles[tile], (LANES - skip) % LANES, 1)
    if skip + HEAD_DIM > LANES:
        window = jnp.where(lane < LANES - skip, window, pltpu.roll(tiles[tile + 1], LANES - skip, 1))
    return jnp.where(lane < HEAD_DIM, window, 0.0)


def join_heads(pieces):
    lane = lane_of(pieces[0].shape)
    tiles = []
    for tile in range(len(pieces) * 3 // 4):
        piece, skip = divmod(tile * LANES, HEAD_DIM)
        low = pltpu.roll(pieces[piece], (LANES - skip) % LANES, 1)
        high = pltpu.roll(pieces[piece + 1], HEAD_DIM - skip, 1)
        tiles.append(jnp.where(lane < HEAD_DIM - skip, low, high))
    return tiles


def mix_groups(parts):
    group = lane_of(parts[0][0].shape) // 32
    mixed = None
    for i, (tile, g) in enumerate(parts):
        turned = pltpu.roll(tile, (32 * (i - g)) % LANES, 1)
        mixed = turned if mixed is None else jnp.where(group == i, turned, mixed)
    return mixed


def lane_of(shape):
    return lax.broadcasted_iota(jnp.int32, shape, len(shape) - 1)


def pack_tile(unit, extra, place):
    return jnp.where(lane_of(unit.shape) < HEAD_DIM, unit, pltpu.roll(extra, (96 - 32 * place) % LANES, 1))


def unpack_extra(tiles):
    lane = lane_of(tiles[0].shape)
    extra = jnp.where(lane < 32, pltpu.roll(tiles[0], 32, 1), 0.0)
    extra = jnp.where(jnp.logical_and(lane >= 32, lane < 64), pltpu.roll(tiles[1], 64, 1), extra)
    return jnp.where(jnp.logical_and(lane >= 64, lane < 96), pltpu.roll(tiles[2], 96, 1), extra)


def swap_halves(rows):
    lane = lane_of(rows.shape)
    return jnp.where(lane < HEAD_DIM // 2, pltpu.roll(rows, LANES - 48, 1), pltpu.roll(rows, 48, 1))


def rope_table():
    half = HEAD_DIM // 2
    frequency = ROPE_BASE ** (-2.0 * np.arange(half, dtype=np.float64) / HEAD_DIM)
    frequency = frequency.astype(np.float32)
    places = np.arange(DEPTH * BLOCK, dtype=np.float32)
    angles = (places[:, None] * frequency[None, :]).astype(np.float64)
    table = np.zeros((DEPTH * BLOCK, LANES), np.float32)
    table[:, :half] = np.cos(angles)
    table[:, half:HEAD_DIM] = np.sin(angles)
    return jnp.asarray(table.reshape(DEPTH, BLOCK, LANES))


def turning(table):
    lane = lane_of(table.shape)
    cosine = jnp.where(lane < 48, table, pltpu.roll(table, 48, 1))
    sine = jnp.where(lane < 48, -pltpu.roll(table, LANES - 48, 1), jnp.where(lane < HEAD_DIM, table, 0.0))
    return cosine, sine


def count_ancestors(lineage, block):
    count = jnp.int32(0)
    for step in range(DEPTH):
        count = count + jnp.where(lineage[block, step] >= 0, 1, 0)
    return count


def write_lineage(parent, first, lineage):
    def one(block, carry):
        def hop(step, node):
            lineage[block, step] = node
            above = parent[jnp.maximum(node, 0)]
            return jnp.where(node >= 0, above, -1)

        lax.fori_loop(0, DEPTH, hop, first + block)
        return carry

    lax.fori_loop(0, MEMBERS, one, 0)


def attend_block(lineage, block, queries, alive, load, scores):
    limit = count_ancestors(lineage, block)
    t = lax.broadcasted_iota(jnp.int32, (2 * BLOCK, BLOCK), 0) % BLOCK
    u = lax.broadcasted_iota(jnp.int32, (2 * BLOCK, BLOCK), 1)
    own = jnp.logical_and(u <= t, jnp.logical_or(alive > 0.5, u == t))
    nodes = [jnp.maximum(lineage[block, step], 0) for step in range(DEPTH)]
    pairs = range(0, DEPTH, 2)
    highest = None
    for step in pairs:
        keys = jnp.concatenate([load(node, key_unit(lax.rem(node, 8))) for node in nodes[step : step + 2]], axis=0)
        part = lax.dot_general(queries, keys, (((1,), (1,)), ((), ())), preferred_element_type=F32) * SCALE
        near = part[:, :BLOCK]
        if step == 0:
            near = jnp.where(own, near, NEGATIVE)
        else:
            near = near + jnp.where(step < limit, 0.0, NEGATIVE)
        far = part[:, BLOCK:] + jnp.where(step + 1 < limit, 0.0, NEGATIVE)
        scores[step] = near
        scores[step + 1] = far
        both = jnp.maximum(near, far)
        highest = both if step == 0 else jnp.maximum(highest, both)
    largest = jnp.max(highest, axis=1, keepdims=True)
    totals = jnp.zeros((2 * BLOCK, BLOCK), F32)
    attended = jnp.zeros((2 * BLOCK, LANES), F32)
    for step in pairs:
        near, far = jnp.exp(scores[step] - largest), jnp.exp(scores[step + 1] - largest)
        totals = totals + near + far
        values = jnp.concatenate(
            [load(node, value_unit(lax.rem(node, 8))) for node in nodes[step : step + 2]], axis=0
        )
        terms = jnp.concatenate([near.astype(BF16), far.astype(BF16)], axis=1)
        attended = attended + jnp.dot(terms, values, preferred_element_type=F32)
    total = jnp.sum(totals, axis=1, keepdims=True)
    return (attended / total).astype(BF16), largest + jnp.log(total)


def start_kernel(
    parent, table, stream, w_query, w_key, w_value, w_gate, w_up, w_out, small_rows, live_row, cotangent, own_down,
    lineage, live, gains, query, stream_all, attn_all,
    kv_out, middle, rms_out, grad_middle, grads_in, down_terms, gate_grad, up_grad, down_grad, out_terms, gain_terms,
    attended_out, log_rows,
    packed, out_low, small, stage, packed_in, out_in, small_in, wide_tall, wide_own, out_own, gain_own, gains_all,
    w_attn, own_kv, kv, w_out_all, w_feed, w_down, mid_all, cot_all, crossed_in, ring_in,
    att_out, att_in, att_pad, grads_out, feed_dealt, feed_in, *scratch,
):
    feed_scratch, wide_scratch = scratch[:5], scratch[5:10]
    send_sems, recv_sems, local_sems = scratch[10:]
    xyzc = x, y, z, c = spot()
    j = z * 2 + c
    base = (x * 4 + y) * MEMBERS
    sibling = device_of(x, y, z, 1 - c)
    wire = Wire(send_sems, recv_sems)
    group = [group_peer(x, y, z, c, k) for k in range(1, MEMBERS)]
    across, down_first = (((1,), (1,)), ((), ())), (((0,), (0,)), ((), ()))
    locals_ = []

    peers = group + axis_peers(x, y, z, c, True)
    announce(peers)

    stage[...] = jnp.zeros((16, FF), F32)

    def staged(weights):
        width = weights.shape[1]
        stage[:12, :width] = weights[...].astype(F32)
        return [stage[:, tile * LANES : (tile + 1) * LANES] for tile in range(width // LANES)]

    def put_packed(member, tile, value):
        packed[member, :, tile * LANES : (tile + 1) * LANES] = value.astype(BF16)

    tiles = staged(w_query)
    for head in range(HEADS):
        put_packed(head // 2, head % 2, head_window(tiles, head))
    for place, weights in ((2, w_key), (3, w_value)):
        tiles = staged(weights)
        for member in range(MEMBERS):
            put_packed(member, place, head_window(tiles, member))
    for place, weights in ((4, w_gate), (8, w_up)):
        tiles = staged(weights)
        for member in range(MEMBERS):
            for tile in range(4):
                parts = [(tiles[2 * (4 * tile + i) + member // 4], member % 4) for i in range(4)]
                put_packed(member, place + tile, mix_groups(parts))
    out_low[...] = jnp.concatenate(staged(w_out), axis=1).astype(BF16)
    rows = pltpu.roll(small_rows[...], 12 * j, 1)
    live_rows = jnp.broadcast_to(live_row[...].astype(F32), (8, LANES))
    rows = jnp.where(lax.broadcasted_iota(jnp.int32, (8, LANES), 0) == 2, live_rows, rows)
    small[...] = jnp.concatenate([rows, jnp.zeros((8, LANES), F32)], axis=0).astype(BF16)
    await_peers(peers)

    def keep(source, target):
        copy = pltpu.make_async_copy(source, target, local_sems.at[len(locals_)])
        copy.start()
        locals_.append(copy)
        return copy

    def to_members(source, target):
        return [wire.send(source((j + k) % MEMBERS), target.at[j], group[k - 1]) for k in range(1, MEMBERS)]

    def half_of(member):
        return pl.ds(pl.multiple_of((member % 2) * 768, 768), 768)

    own_half = half_of(c)
    packed_dealt = to_members(lambda member: packed.at[member], packed_in)
    small_dealt = to_members(lambda member: small, small_in)
    first_kept = (keep(packed.at[j], packed_in.at[j]), keep(small, small_in.at[j]))
    out_kept = keep(out_low.at[:, own_half], out_in.at[j])
    streams = GroupGather(wire, stream, mid_all, xyzc)
    streams.begin()
    stream_kept = keep(stream, mid_all.at[z, c])
    write_lineage(parent, base, lineage)
    for line in range(16):
        w_out_all[line // 4, line % 4, 96:] = jnp.zeros((32, D), BF16)

    for copy in packed_dealt + small_dealt:
        copy.wait_recv()
    out_dealt = to_members(lambda member: out_low.at[:, half_of(member)], out_in)
    for copy in first_kept:
        copy.wait()
    for member in range(MEMBERS):
        wide_tall[pl.ds(member * 12, 12)] = packed_in[member].astype(F32)[:12]
    wide_own[...] = wide_tall[...].astype(BF16)
    gain = small_in[0].astype(F32)
    for member in range(MEMBERS):
        row = small_in[member].astype(F32)
        live[member] = row[2:3]
        if member:
            gain = gain + row
    gain_own[...] = gain.astype(BF16)
    own_attn, own_feed = wide_own.at[:, pl.ds(0, 512)], wide_own.at[:, pl.ds(512, 1024)]
    attn = PlaneGather(wire, own_attn, w_attn, Rows(96, 512), xyzc)
    attn.first()
    tiny = [wire.send(gain_own, gains_all.at[x, y], device_of(x + k, y, z, c)) for k in range(1, 4)]
    attn_kept = keep(own_attn, w_attn.at[x, y])
    gain_kept = keep(gain_own, gains_all.at[x, y])
    feed_kept = keep(own_feed, w_feed.at[x, y])
    down_kept = keep(own_down, w_down.at[x, y])

    streams.relay()
    attn.relay()
    gain_kept.wait()
    for copy in tiny:
        copy.wait_recv()
    line = gains_all.at[:, y]
    tiny = [wire.send(line, line, device_of(x, y + k, z, c)) for k in range(1, 4)]
    attn_kept.wait()
    attn.settle()
    attn.second()
    feed = PlaneGather(wire, own_feed, w_feed, Rows(96, 1024), xyzc)
    down = PlaneGather(wire, own_down, w_down, Rows(32, D), xyzc)
    feed.first()
    down.first()
    for copy in out_dealt:
        copy.wait_recv()
    out_kept.wait()
    for member in range(MEMBERS):
        wide_tall[pl.ds(member * 12, 12), :768] = out_in[member].astype(F32)[:12]
    out_own[...] = wide_tall[:, :768].astype(BF16)
    out_kept = keep(out_own, w_out_all.at[x, y, pl.ds(0, 96), own_half])
    streams.near()
    streams.far()
    attn.relay()
    feed.relay()
    down.relay()
    for copy in tiny:
        copy.wait_recv()
    pieces = [gains_all[piece // 4, piece % 4].astype(F32)[:8] for piece in range(16)]
    gains[...] = gain_rows(pieces)
    attn.settle()
    stream_kept.wait()
    streams.finish()
    attn_copied = keep(w_attn, attn_all)
    stream_copied = keep(mid_all, stream_all)

    def project(step, carry):
        wide = mid_all[step].reshape(2 * BLOCK, D).astype(F32)
        rms = jnp.sqrt(jnp.mean(wide * wide, axis=1, keepdims=True) + EPSILON)
        rows = (wide * (1.0 / rms) * gains[0:1]).astype(BF16)
        raw = jnp.dot(rows, w_attn[...].reshape(D, 512), preferred_element_type=F32)
        for part in range(2):
            block = step * 2 + part
            depth = count_ancestors(lineage, block) - 1
            cos, sin = turning(table[depth])

            def turn(head):
                v = raw[part * BLOCK : (part + 1) * BLOCK, head * LANES : (head + 1) * LANES]
                return (v * cos + swap_halves(v) * sin).astype(BF16)

            query[block, :BLOCK] = turn(0)
            query[block, BLOCK:] = turn(1)
            kv[x, y, key_unit(block)] = turn(2)
            kv[x, y, value_unit(block)] = raw[part * BLOCK : (part + 1) * BLOCK, 3 * LANES :].astype(BF16)
        return carry

    lax.fori_loop(0, 2, project, 0)
    feed_kept.wait()
    down_kept.wait()
    feed.settle()
    feed.second()
    down.settle()
    down.second()
    lax.fori_loop(2, 4, project, 0)
    for tile in range(12):
        extra = kv[x, y, 12 + tile // 3].astype(F32)
        own_kv[tile] = pack_tile(kv[x, y, tile].astype(F32), extra, tile % 3).astype(BF16)

    pairs = PlaneGather(wire, own_kv, kv, Units(), xyzc)
    pairs.first()
    kept = keep(own_kv, kv.at[x, y, pl.ds(0, 12)])
    cotangents = GroupGather(wire, cotangent, cot_all, xyzc)
    cotangents.begin()
    cot_kept = keep(cotangent, cot_all.at[z, c])
    feed.relay()
    down.relay()
    pairs.relay()
    kept.wait()
    pairs.settle()
    pairs.second()
    cotangents.relay()
    cotangents.near()
    cotangents.far()
    pairs.relay()
    early, wire.open = wire.open, []
    out_kept.wait()
    outs = PlaneGather(wire, w_out_all.at[x, y], w_out_all, Rows(96, 768, c * 768), xyzc)
    outs.first()
    pairs.settle()
    feed.settle()
    down.settle()
    for copy in early:
        copy.wait_send()
    stream_copied.wait()
    attn_copied.wait()

    def unpack(line, carry):
        a, b = line // 4, line % 4
        for extra in range(4):
            tiles = [kv[a, b, extra * 3 + k].astype(F32) for k in range(3)]
            kv[a, b, 12 + extra] = unpack_extra(tiles).astype(BF16)
        return carry

    lax.fori_loop(0, 16, unpack, 0)
    kv_copied = keep(kv, kv_out)

    att_slot = wire.reserve(MEMBERS - 1)

    def load(node, unit):
        return kv[lax.div(node, 32), lax.rem(lax.div(node, 8), 4), unit]

    def att_copy(k):
        block = (j + 1 + k) % MEMBERS
        return wire.make(att_slot + k, att_out.at[block], att_in.at[j], base + block)

    def attend(k, scores):
        block = (j + 1 + k) % MEMBERS
        attended, logs = attend_block(lineage, block, query[block], live[block], load, scores)
        log_rows[block] = jnp.transpose(jnp.broadcast_to(logs, (2 * BLOCK, LANES)))[:8]
        att_out[block, :, :LANES] = attended[:BLOCK]
        att_out[block, :, LANES:] = attended[BLOCK:]

        @pl.when(k < MEMBERS - 1)
        def _():
            att_copy(k).start()

        return 0

    def attend_some(first, last):
        def some(scores):
            lax.fori_loop(first, last, lambda k, carry: attend(k, scores), 0)

        pl.run_scoped(some, pltpu.VMEM((DEPTH, 2 * BLOCK, LANES), F32))

    attend_some(0, 1)
    outs.relay()
    attend_some(1, 3)
    outs.settle()
    outs.second()
    attend_some(3, 5)
    outs.relay()
    attend_some(5, 7)
    outs.settle()
    swap_part = w_out_all.at[:, :, pl.ds(0, 96), own_half]
    swapped = wire.send(swap_part, swap_part, sibling)
    attend_some(7, MEMBERS)
    att_in[j] = att_out[j]
    att_copied = keep(att_out, attended_out)
    att_recv = [att_copy(k) for k in range(MEMBERS - 1)]

    for copy in att_recv:
        copy.wait_recv()
    for member in range(MEMBERS):
        att_pad[:, member * 256 : (member + 1) * 256] = att_in[member]
    swapped.wait_recv()

    def project_out(step, carry):
        cols = pl.ds(pl.multiple_of(step * 512, 512), 512)
        weights = w_out_all[:, :, :, cols].reshape(16 * LANES, 512)
        branch = jnp.dot(att_pad[...], weights, preferred_element_type=F32)
        middle[:, cols] = stream[:, cols].astype(F32) + branch
        return carry

    lax.fori_loop(0, 3, project_out, 0)
    rms = jnp.sqrt(jnp.mean(middle[...] * middle[...], axis=1, keepdims=True) + EPSILON)
    rms_out[...] = jnp.transpose(jnp.broadcast_to(rms, (BLOCK, LANES)))[:1]
    mid_all[z, c] = (middle[...] / rms * gains[1:2]).astype(BF16)
    late, wire.open = wire.open, []
    mids = GroupGather(wire, mid_all.at[z, c], mid_all, xyzc)
    mids.begin()
    mids.relay()
    for copy in late:
        copy.wait_send()
    kv_copied.wait()
    cot_kept.wait()
    cotangents.finish()
    for k in range(MEMBERS - 1):
        att_copy(k).wait_send()

    grad_rows = ChipScatter(wire, kv, 2, crossed_in, ring_in, xyzc)

    def rest(acts, grad_feed, feed_terms, wide_terms):
        feed_back_half(
            xyzc, wire, group, keep, mids, grad_rows, mid_all, cot_all, w_feed, w_down, w_out_all, kv, middle, gains,
            att_pad, att_copied, grads_out, feed_dealt, feed_in, wide_tall, feed_scratch, wide_scratch,
            acts, grad_feed, feed_terms, wide_terms,
            grad_middle, grads_in, down_terms, gate_grad, up_grad, down_grad, out_terms, gain_terms,
        )

    pl.run_scoped(
        rest,
        pltpu.VMEM((4, 2 * BLOCK, 512), BF16),
        pltpu.VMEM((4, 2 * BLOCK, 1024), BF16),
        pltpu.VMEM((4, 4, 96, 1024), BF16),
        pltpu.VMEM((4, 4, 32, D), BF16),
    )


def feed_back_half(
    xyzc, wire, group, keep, mids, grad_rows, mid_all, cot_all, w_feed, w_down, w_out_all, kv, middle, gains,
    att_pad, att_copied, grads_out, feed_dealt, feed_in, wide_tall, feed_scratch, wide_scratch,
    acts, grad_feed, feed_terms, wide_terms,
    grad_middle, grads_in, down_terms, gate_grad, up_grad, down_grad, out_terms, gain_terms,
):
    x, y, z, c = xyzc
    j = z * 2 + c
    across, down_first = (((1,), (1,)), ((), ())), (((0,), (0,)), ((), ()))

    def feed_forward(step):
        place = grad_rows.place(step)
        rows = mid_all[place].reshape(2 * BLOCK, D)
        weights = w_feed[...].reshape(D, 1024)
        both = jnp.dot(rows, weights, preferred_element_type=F32)
        gate, up = both[:, :512], both[:, 512:]
        sigmoid = 0.5 * jnp.tanh(0.5 * gate) + 0.5
        silu = gate * sigmoid
        acts[place] = (silu * up).astype(BF16)
        cot = cot_all[place].reshape(2 * BLOCK, D)
        grad_act = lax.dot_general(cot, w_down[...].reshape(512, D), across, preferred_element_type=F32)
        grad_gate = grad_act * up * sigmoid * (1.0 + gate * (1.0 - sigmoid))
        grad_feed[place, :, :512] = grad_gate.astype(BF16)
        grad_feed[place, :, 512:] = (grad_act * silu).astype(BF16)
        grads = lax.dot_general(grad_feed[place], weights, across, preferred_element_type=F32)
        grad_rows.put(step, grads.astype(BF16))

    mids.crossed[0].wait_recv()
    feed_forward(0)
    mids.near()
    mids.crossed[1].wait_recv()
    feed_forward(1)
    mids.far()
    mids.crossed[2].wait_recv()
    grad_rows.turn(1)
    feed_forward(3)
    mids.crossed[3].wait_recv()
    grad_rows.turn(3)
    feed_forward(2)
    grad_rows.turn(2)

    def feed_weights(step, carry):
        cols = pl.ds(pl.multiple_of(step * 384, 384), 384)
        left = mid_all[:, :, :, cols].reshape(MEMBERS * BLOCK, 384)
        right = grad_feed[...].reshape(MEMBERS * BLOCK, 1024)
        total = lax.dot_general(left, right, down_first, preferred_element_type=F32)
        feed_terms[step] = total.astype(BF16).reshape(4, 96, 1024)
        return carry

    lax.fori_loop(0, 4, feed_weights, 0)
    feeds = PlaneScatter(wire, feed_terms, Rows(96, 1024), feed_scratch, xyzc)
    feeds.first()

    def down_weights(step, carry):
        cols = pl.ds(pl.multiple_of(step * 128, 128), 128)
        left = acts[:, :, cols].reshape(MEMBERS * BLOCK, 128)
        right = cot_all[...].reshape(MEMBERS * BLOCK, D)
        total = lax.dot_general(left, right, down_first, preferred_element_type=F32)
        wide_terms[step] = total.astype(BF16).reshape(4, 32, D)
        return carry

    lax.fori_loop(0, 4, down_weights, 0)
    wides = PlaneScatter(wire, wide_terms, Rows(32, D), wide_scratch, xyzc)
    wides.first()

    def down_rows(place, carry):
        outs = jnp.dot(acts[place], w_down[...].reshape(512, D), preferred_element_type=F32).astype(BF16)
        for core in range(2):
            for tile in range(12):
                kv[place, core, tile] = outs[
                    core * BLOCK : (core + 1) * BLOCK, tile * LANES : (tile + 1) * LANES
                ]
        return carry

    lax.fori_loop(0, 4, down_rows, 0)
    down_copied = keep(kv.at[:, pl.ds(0, 2), pl.ds(0, 12)], down_terms)
    feeds.relay()

    grad_mid = grad_rows.total()
    rms = jnp.sqrt(jnp.mean(middle[...] * middle[...], axis=1, keepdims=True) + EPSILON)
    scaled = middle[...] / rms
    gain_terms[...] = jnp.sum(grad_mid * scaled, axis=0, keepdims=True)
    weighted = grad_mid * gains[1:2]
    back = (weighted - scaled * jnp.mean(weighted * scaled, axis=1, keepdims=True)) / rms
    grad_middle[...] = cot_all[z, c].astype(F32) + back
    branch_grad = grad_middle[...].astype(BF16)

    def spread(step, carry):
        weights = w_out_all[step].reshape(4 * LANES, D)
        grads = lax.dot_general(branch_grad, weights, across, preferred_element_type=F32).astype(BF16)
        for part in range(2):
            grads_out[step * 2 + part] = grads[:, part * 256 : (part + 1) * 256]
        return carry

    lax.fori_loop(0, 4, spread, 0)
    kept = keep(grads_out.at[j], grads_in.at[j])
    dealt = [
        wire.send(grads_out.at[(j + k) % MEMBERS], grads_in.at[j], group[k - 1]) for k in (4, 5, 3, 2, 6, 7, 1)
    ]
    wides.relay()

    def out_weights(step, carry):
        cols = pl.ds(pl.multiple_of(step * 512, 512), 512)
        total = lax.dot_general(att_pad[:, cols], branch_grad, down_first, preferred_element_type=F32)
        w_out_all[step] = total.astype(BF16).reshape(4, LANES, D)
        return carry

    lax.fori_loop(0, 4, out_weights, 0)
    out_copied = keep(w_out_all.at[:, :, pl.ds(0, 96)], out_terms)

    feeds.add_first()
    feeds.second()
    wides.add_first()
    wides.second()
    feeds.arrive()
    for half in range(2):
        wide_tall[pl.ds(half * 48, 48), :1024] = feeds.total(half)
    for member in range(MEMBERS):
        feed_dealt[member, :12] = wide_tall[pl.ds(member * 12, 12), :1024]
    feed_in[j] = feed_dealt[j]
    feed_dealt_copies = [
        wire.send(feed_dealt.at[(j + k) % MEMBERS], feed_in.at[j], group[k - 1]) for k in range(1, MEMBERS)
    ]
    wides.arrive()
    for half in range(2):
        down_grad[pl.ds(half * 16, 16)] = wides.total(half)
    for copy in feed_dealt_copies:
        copy.wait_recv()
    for grad, first in ((gate_grad, 0), (up_grad, 4)):
        for tile in range(32):
            line = tile // 2
            cols = slice((first + line // 4) * LANES, (first + line // 4 + 1) * LANES)
            parts = [(feed_in[4 * (tile % 2) + i][:, cols], line % 4) for i in range(4)]
            grad[:, tile * LANES : (tile + 1) * LANES] = mix_groups(parts)[:12]
    for copy in dealt:
        copy.wait_recv()
    for copy in (kept, down_copied, out_copied, att_copied):
        copy.wait()
    wire.close()
    grad_rows.close()


def start(
    parent, table, stream, w_query, w_key, w_value, w_gate, w_up, w_out, small_rows, live_row, cotangent, own_down
):
    shape, vmem = jax.ShapeDtypeStruct, pltpu.VMEM
    smem = pl.BlockSpec(memory_space=pltpu.SMEM)
    return communicate(
        start_kernel,
        (
            shape((MEMBERS, DEPTH), jnp.int32),
            shape((MEMBERS, 1, LANES), F32),
            shape((8, D), F32),
            shape((MEMBERS, 2 * BLOCK, LANES), BF16),
            shape((4, 2, BLOCK, D), BF16),
            shape((4, 4, 96, 512), BF16),
            shape((4, 4, 16, BLOCK, LANES), BF16),
            shape((BLOCK, D), F32),
            shape((1, LANES), F32),
            shape((BLOCK, D), F32),
            shape((MEMBERS, BLOCK, 2 * LANES), BF16),
            shape((4, 2, 12, BLOCK, LANES), BF16),
            shape((12, FF), F32),
            shape((12, FF), F32),
            shape((32, D), F32),
            shape((4, 4, 96, D), BF16),
            shape((1, D), F32),
            shape((MEMBERS, BLOCK, 2 * LANES), BF16),
            shape((MEMBERS, 8, 2 * BLOCK), F32),
        ),
        [smem] + [INVMEM] * 10 + [ANY] * 2,
        (smem,) + (INVMEM,) * 3 + (ANY,) * 3 + (INVMEM,) * 3 + (ANY,) * 2 + (INVMEM,) * 3 + (ANY, INVMEM, ANY, INVMEM),
        [
            vmem((MEMBERS, 16, 1536), BF16),
            vmem((16, 1536), BF16),
            vmem((16, LANES), BF16),
            vmem((16, FF), F32),
            vmem((MEMBERS, 16, 1536), BF16),
            vmem((MEMBERS, 16, 768), BF16),
            vmem((MEMBERS, 16, LANES), BF16),
            vmem((96, 1536), F32),
            vmem((96, 1536), BF16),
            vmem((96, 768), BF16),
            vmem((16, LANES), BF16),
            vmem((4, 4, 16, LANES), BF16),
            vmem((4, 4, 96, 512), BF16),
            vmem((12, BLOCK, LANES), BF16),
            vmem((4, 4, 16, BLOCK, LANES), BF16),
            vmem((4, 4, LANES, D), BF16),
            vmem((4, 4, 96, 1024), BF16),
            vmem((4, 4, 32, D), BF16),
            vmem((4, 2, BLOCK, D), BF16),
            vmem((4, 2, BLOCK, D), BF16),
        ]
        + chip_scatter_scratch()
        + [
            vmem((MEMBERS, BLOCK, 2 * LANES), BF16),
            vmem((MEMBERS, BLOCK, 2 * LANES), BF16),
            vmem((BLOCK, 2048), BF16),
            vmem((MEMBERS, BLOCK, 2 * LANES), BF16),
            vmem((MEMBERS, 16, 1024), F32),
            vmem((MEMBERS, 16, 1024), F32),
        ]
        + scatter_scratch(Rows(96, 1024))
        + scatter_scratch(Rows(32, D))
        + wire_scratch(242)
        + [pltpu.SemaphoreType.DMA((20,))],
        2,
        "start",
        63 * 2**20,
    )(parent, table, stream, w_query, w_key, w_value, w_gate, w_up, w_out, small_rows, live_row, cotangent, own_down)


def split_rows(tall, dealt):
    for member in range(MEMBERS):
        dealt[member, :12] = tall[pl.ds(member * 12, 12)]


def attend_back_kernel(
    lineage, query, live, grad, attended, log_rows, kv_in, grad_query, grad_kv, kv, sums, packed, sems
):
    loaded = pltpu.make_async_copy(kv_in, kv, sems.at[16])
    loaded.start()

    def clear(step, carry):
        sums[step] = jnp.zeros((BLOCK, LANES), F32)
        return carry

    lax.fori_loop(0, 256, clear, 0)
    loaded.wait()

    def one(block, carry):
        attend_back_block(block, lineage, query, live, grad, attended, log_rows, grad_query, kv, sums)
        return carry

    lax.fori_loop(0, MEMBERS, one, 0)

    def stored(line):
        rows = pl.ds(line * 12, 12)
        return pltpu.make_async_copy(packed.at[rows], grad_kv.at[rows], sems.at[line])

    def store(line, carry):
        for tile in range(12):
            total = pack_tile(sums[line * 16 + tile], sums[line * 16 + 12 + tile // 3], tile % 3)
            packed[line * 12 + tile] = total.astype(BF16)
        stored(line).start()
        return carry

    lax.fori_loop(0, 16, store, 0)
    for line in range(16):
        stored(line).wait()


def attend_back_block(block, lineage, query, live, grad, attended, log_rows, grad_query, kv, sums):
    across, down_first = (((1,), (1,)), ((), ())), (((0,), (0,)), ((), ()))
    queries = query[block]
    grads = jnp.concatenate([grad[block, :, :LANES], grad[block, :, LANES:]], axis=0)
    outs = jnp.concatenate([attended[block, :, :LANES], attended[block, :, LANES:]], axis=0)
    product = grads.astype(F32) * outs.astype(F32)
    high = product.astype(BF16)
    low = (product - high.astype(F32)).astype(BF16)
    ones = jnp.ones((8, LANES), BF16)
    inner = lax.dot_general(ones, high, across, preferred_element_type=F32)
    inner = (inner + lax.dot_general(ones, low, across, preferred_element_type=F32))[:1]
    logs = log_rows[block, :1]
    limit = count_ancestors(lineage, block)
    u = lax.broadcasted_iota(jnp.int32, (BLOCK, 2 * BLOCK), 0)
    t = lax.broadcasted_iota(jnp.int32, (BLOCK, 2 * BLOCK), 1) % BLOCK
    alive = jnp.transpose(jnp.broadcast_to(live[block], (BLOCK, BLOCK)))
    alive = jnp.concatenate([alive, alive], axis=1)
    own = jnp.logical_and(u <= t, jnp.logical_or(alive > 0.5, u == t))
    turned = jnp.zeros((LANES, 2 * BLOCK), F32)
    for step in range(0, DEPTH, 2):
        units = []
        for node in (lineage[block, step], lineage[block, step + 1]):
            safe = jnp.maximum(node, 0)
            at, member = lax.div(safe, 8) * 16, lax.rem(safe, 8)
            units.append((node, at + key_unit(member), at + value_unit(member)))
        keys = jnp.concatenate([kv[unit[1]] for unit in units], axis=0)
        values = jnp.concatenate([kv[unit[2]] for unit in units], axis=0)
        scores = lax.dot_general(keys, queries, across, preferred_element_type=F32) * SCALE
        near, far = scores[:BLOCK], scores[BLOCK:]
        if step == 0:
            near = jnp.where(own, jnp.exp(jnp.where(own, near - logs, NEGATIVE)), 0.0)
        else:
            near = jnp.exp(near + (jnp.where(step < limit, 0.0, NEGATIVE) - logs))
        far = jnp.exp(far + (jnp.where(step + 1 < limit, 0.0, NEGATIVE) - logs))
        chances = jnp.concatenate([near, far], axis=0)
        grad_chances = lax.dot_general(values, grads, across, preferred_element_type=F32)
        grad_scores = (chances * (grad_chances - inner)).astype(BF16)
        grad_keys = jnp.dot(grad_scores, queries, preferred_element_type=F32) * SCALE
        grad_values = jnp.dot(chances.astype(BF16), grads, preferred_element_type=F32)
        for part, (node, at_key, at_value) in enumerate(units):
            rows = slice(part * BLOCK, (part + 1) * BLOCK)
            sums[jnp.where(node >= 0, at_key, 256)] += grad_keys[rows]
            sums[jnp.where(node >= 0, at_value, 256)] += grad_values[rows]
        turned = turned + lax.dot_general(keys, grad_scores, down_first, preferred_element_type=F32)
    grad_query[block] = jnp.transpose(turned) * SCALE


def attend_back(lineage, query, kv, live, grad, attended, log_rows):
    vmem = pltpu.VMEM
    return pl.pallas_call(
        attend_back_kernel,
        in_specs=[pl.BlockSpec(memory_space=pltpu.SMEM)] + [INVMEM] * 5 + [ANY],
        out_specs=(INVMEM, ANY),
        out_shape=(
            jax.ShapeDtypeStruct((MEMBERS, 2 * BLOCK, LANES), F32),
            jax.ShapeDtypeStruct((192, BLOCK, LANES), BF16),
        ),
        scratch_shapes=[
            vmem((256, BLOCK, LANES), BF16),
            vmem((257, BLOCK, LANES), F32),
            vmem((192, BLOCK, LANES), BF16),
            pltpu.SemaphoreType.DMA((17,)),
        ],
        compiler_params=pltpu.CompilerParams(vmem_limit_bytes=VMEM_BYTES),
        name="attend_back",
    )(lineage, query, live, grad, attended, log_rows, kv)


def gain_tiles(rows):
    lane = lane_of((8, LANES))
    tiles = [rows[:, tile * LANES : (tile + 1) * LANES] for tile in range(12)]
    pieces = []
    for piece in range(16):
        tile, skip = divmod(piece * 96, LANES)
        low = pltpu.roll(tiles[tile], (LANES - skip) % LANES, 1)
        high = pltpu.roll(tiles[min(tile + 1, 11)], (LANES - skip) % LANES, 1)
        pieces.append(jnp.where(lane < LANES - skip, low, high))
    return pieces


def ending_kernel(
    lineage, grad_query, table, stream_all, w_attn, gain, gain_two, stream, middle, grad_middle,
    kv_terms, down_terms, out_terms,
    mixed_out, stream_grad, query_grad, key_grad, value_grad, out_grad, gain_one, gain_two_out, rms_out,
    attn_grad, out_in, normed, raw, units, grad_terms, crossed_in, ring_in, attn_terms, attn_tall, attn_dealt,
    out_tall, out_dealt, out_mine, out_crossed, gain_terms, gain_in, gain_line, gain_in_two, gain_in_three,
    *scratch,
):
    xyzc = x, y, z, c = spot()
    j = z * 2 + c
    down_scratch, kv_scratch, attn_scratch, out_scratch = scratch[:5], scratch[5:13], scratch[13:18], scratch[18:23]
    send_sems, recv_sems, local_sem = scratch[23:]
    wire = Wire(send_sems, recv_sems)
    group = [group_peer(x, y, z, c, k) for k in range(1, MEMBERS)]
    peers = group + axis_peers(x, y, z, c, True)
    announce(peers)
    await_peers(peers)
    sibling = device_of(x, y, z, 1 - c)
    pairs = PlaneScatter(wire, kv_terms, Units(), kv_scratch, xyzc)
    pairs.first()
    downs = GroupScatter(wire, down_terms, *down_scratch, xyzc)
    downs.begin()
    own_half = pl.ds(pl.multiple_of(c * 768, 768), 768)
    other_half = pl.ds(pl.multiple_of((1 - c) * 768, 768), 768)
    crossed = wire.send(out_terms.at[:, :, :, other_half], out_crossed, sibling)
    local = pltpu.make_async_copy(out_terms.at[:, :, :, own_half], out_mine, local_sem)
    local.start()

    def norm_rows(step, carry):
        rows = pl.ds(pl.multiple_of(step * BLOCK, BLOCK), BLOCK)
        wide = stream_all[rows].astype(F32)
        rms = jnp.sqrt(jnp.mean(wide * wide, axis=1, keepdims=True) + EPSILON)
        normed[rows] = (wide * (1.0 / rms) * gain[...]).astype(BF16)
        return carry

    lax.fori_loop(0, MEMBERS, norm_rows, 0)

    def turn(block, v):
        depth = count_ancestors(lineage, block) - 1
        cos, sin = turning(table[depth])
        return (v * cos - swap_halves(v) * sin).astype(BF16)

    def query_rows(block, carry):
        rows = pl.ds(pl.multiple_of(block * BLOCK, BLOCK), BLOCK)
        raw[rows, :128] = turn(block, grad_query[block, :BLOCK])
        raw[rows, 128:256] = turn(block, grad_query[block, BLOCK:])
        return carry

    lax.fori_loop(0, MEMBERS, query_rows, 0)
    pairs.relay()
    local.wait()
    crossed.wait_recv()

    def add_halves(step, carry):
        a, b = step // 4, step % 4
        total = out_mine[a, b].astype(F32) + out_crossed[a, b].astype(F32)
        out_mine[a, b] = total.astype(BF16)
        return carry

    lax.fori_loop(0, 16, add_halves, 0)
    outs = PlaneScatter(wire, out_mine, Rows(96, 768), out_scratch, xyzc)
    downs.turn()
    pairs.add_first()
    pairs.second()
    downs.finish(stream_grad)
    mixed_out[...] = (middle[...] + stream_grad[...]).astype(BF16)
    pairs.arrive()
    outs.first()
    for half in range(2):
        units[pl.ds(half * 6, 6)] = pairs.total(half)
    for extra in range(4):
        units[12 + extra] = unpack_extra([units[extra * 3 + k] for k in range(3)])

    def pair_rows(block, carry):
        rows = pl.ds(pl.multiple_of(block * BLOCK, BLOCK), BLOCK)
        raw[rows, 256:384] = turn(block, units[key_unit(block)])
        value = units[value_unit(block)]
        raw[rows, 384:] = jnp.where(lane_of((BLOCK, LANES)) < HEAD_DIM, value, 0.0).astype(BF16)
        return carry

    lax.fori_loop(0, MEMBERS, pair_rows, 0)

    grad_rows = ChipScatter(wire, grad_terms, 0, crossed_in, ring_in, xyzc)
    gain_terms[...] = jnp.zeros((1, D), F32)

    def rows_back(index, carry):
        step = (index + 1) % 4
        rows = pl.ds(pl.multiple_of(grad_rows.place(step) * 256, 256), 256)
        grads = lax.dot_general(raw[rows], w_attn[...], (((1,), (1,)), ((), ())), preferred_element_type=F32)
        grad_rows.put(step, grads.astype(BF16))
        wide = stream_all[rows].astype(F32)
        rms = jnp.sqrt(jnp.mean(wide * wide, axis=1, keepdims=True) + EPSILON)
        gain_terms[...] += jnp.sum(grads * (wide * (1.0 / rms)), axis=0, keepdims=True)

        @pl.when(index > 0)
        def _():
            grad_rows.turn(index)

        return carry

    lax.fori_loop(0, 4, rows_back, 0)
    outs.relay()
    rows = jnp.concatenate([gain_terms[...], gain_two[...], jnp.zeros((6, D), F32)], axis=0)
    for piece, part in enumerate(gain_tiles(rows)):
        gain_in[piece // 4, piece % 4] = part
    gains = [
        wire.send(gain_in.at[(x + k) % 4], gain_line.at[k], device_of(x + k, y, z, c)) for k in range(1, 4)
    ]

    def weights_back(step, carry):
        cols = pl.ds(pl.multiple_of(step * 384, 384), 384)
        total = lax.dot_general(
            normed[:, cols], raw[...], (((0,), (0,)), ((), ())), preferred_element_type=F32
        )
        attn_terms[step] = total.astype(BF16).reshape(4, 96, 512)
        return carry

    lax.fori_loop(0, 4, weights_back, 0)
    attns = PlaneScatter(wire, attn_terms, Rows(96, 512), attn_scratch, xyzc)
    attns.first()
    for copy in gains:
        copy.wait_recv()
    gain_line[0] = gain_in[x] + gain_line[1] + gain_line[2] + gain_line[3]
    gains = [
        wire.send(gain_line.at[0, (y + k) % 4], gain_in_two.at[k], device_of(x, y + k, z, c)) for k in range(1, 4)
    ]
    outs.add_first()
    outs.second()
    attns.relay()

    wide = stream[...].astype(F32)
    rms = jnp.sqrt(jnp.mean(wide * wide, axis=1, keepdims=True) + EPSILON)
    rms_out[...] = jnp.transpose(jnp.broadcast_to(rms, (BLOCK, LANES)))[:1]
    scaled = wide / rms
    weighted = grad_rows.total() * gain[...]
    back = (weighted - scaled * jnp.mean(weighted * scaled, axis=1, keepdims=True)) / rms
    stream_grad[...] = grad_middle[...] + back

    for copy in gains:
        copy.wait_recv()
    gain_in_three[j] = gain_line[0, y] + gain_in_two[1] + gain_in_two[2] + gain_in_two[3]
    gains = [
        wire.send(gain_in_three.at[j], gain_in_three.at[j], group[k - 1]) for k in range(1, MEMBERS)
    ]
    attns.add_first()
    attns.second()
    outs.arrive()
    for half in range(2):
        out_tall[pl.ds(half * 48, 48)] = outs.total(half)
    split_rows(out_tall, out_dealt)
    out_in[j] = out_dealt[j]
    dealt = [
        wire.send(out_dealt.at[(j + k) % MEMBERS], out_in.at[j], group[k - 1]) for k in range(1, MEMBERS)
    ]
    attns.arrive()
    for half in range(2):
        attn_tall[pl.ds(half * 48, 48)] = attns.total(half)
    split_rows(attn_tall, attn_dealt)
    attn_grad[j] = attn_dealt[j]
    dealt += [
        wire.send(attn_dealt.at[(j + k) % MEMBERS], attn_grad.at[j], group[k - 1]) for k in range(1, MEMBERS)
    ]
    for copy in gains:
        copy.wait_recv()
    total = gain_in_three[0]
    for member in range(1, MEMBERS):
        total = total + gain_in_three[member]
    own = pltpu.roll(total, (LANES - 12 * j) % LANES, 1)
    gain_one[...] = own[:1, :12]
    gain_two_out[...] = own[1:2, :12]
    for copy in dealt:
        copy.wait_recv()
    for core in range(2):
        total = out_in[core]
        for place in range(1, 4):
            total = total + out_in[place * 2 + core]
        out_grad[:, core * 768 : (core + 1) * 768] = total[:12]

    def tile_of(member, tile):
        return attn_grad[member, :, tile * LANES : (tile + 1) * LANES]

    for grad, pieces in (
        (query_grad, [tile_of(head // 2, head % 2) for head in range(HEADS)]),
        (key_grad, [tile_of(member, 2) for member in range(MEMBERS)]),
        (value_grad, [tile_of(member, 3) for member in range(MEMBERS)]),
    ):
        for tile, value in enumerate(join_heads(pieces)):
            grad[:, tile * LANES : (tile + 1) * LANES] = value[:12]
    wire.close()
    grad_rows.close()


def ending(
    lineage, grad_query, table, stream_all, w_attn, gain, gain_two, stream, middle, grad_middle,
    kv_terms, down_terms, out_terms,
):
    shape, vmem = jax.ShapeDtypeStruct, pltpu.VMEM
    smem = pl.BlockSpec(memory_space=pltpu.SMEM)
    return communicate(
        ending_kernel,
        (
            shape((BLOCK, D), BF16),
            shape((BLOCK, D), F32),
            shape((12, D), F32),
            shape((12, 768), F32),
            shape((12, 768), F32),
            shape((12, D), F32),
            shape((1, 12), F32),
            shape((1, 12), F32),
            shape((1, LANES), F32),
        ),
        [smem] + [INVMEM] * 9 + [ANY] * 3,
        (INVMEM,) * 9,
        [
            vmem((MEMBERS, 16, 512), F32),
            vmem((MEMBERS, 16, 768), F32),
            vmem((MEMBERS * BLOCK, D), BF16),
            vmem((MEMBERS * BLOCK, 512), BF16),
            vmem((16, BLOCK, LANES), F32),
            vmem((4, 2, 12, BLOCK, LANES), BF16),
        ]
        + chip_scatter_scratch()
        + [
            vmem((4, 4, 96, 512), BF16),
            vmem((96, 512), F32),
            vmem((MEMBERS, 16, 512), F32),
            vmem((96, 768), F32),
            vmem((MEMBERS, 16, 768), F32),
            vmem((4, 4, 96, 768), BF16),
            vmem((4, 4, 96, 768), BF16),
            vmem((1, D), F32),
            vmem((4, 4, 8, LANES), F32),
            vmem((4, 4, 8, LANES), F32),
            vmem((4, 8, LANES), F32),
            vmem((MEMBERS, 8, LANES), F32),
        ]
        + group_scatter_scratch()
        + scatter_scratch(Units(), room=True)
        + scatter_scratch(Rows(96, 512))
        + scatter_scratch(Rows(96, 768))
        + wire_scratch(96)
        + [pltpu.SemaphoreType.DMA],
        7,
        "ending",
        62 * 2**20,
    )(
        lineage, grad_query, table, stream_all, w_attn, gain, gain_two, stream, middle, grad_middle,
        kv_terms, down_terms, out_terms,
    )


def hand_over_kernel(*refs):
    count = len(refs) // 2
    for source, target in zip(refs[:count], refs[count:]):
        target[...] = source[...]


def hand_over(*arrays):
    return pl.pallas_call(
        hand_over_kernel,
        out_shape=tuple(jax.ShapeDtypeStruct(array.shape, array.dtype) for array in arrays),
        in_specs=[INVMEM] * len(arrays),
        out_specs=(INVMEM,) * len(arrays),
        compiler_params=pltpu.CompilerParams(vmem_limit_bytes=VMEM_BYTES),
        name="hand_over",
    )(*arrays)


def shards(
    stream, attn_gain, w_query, w_key, w_value, w_out, mlp_gain, w_gate, w_up, w_down, parent, live_mask, cotangent
):
    table = rope_table()
    small_rows = jnp.pad(jnp.stack([attn_gain, mlp_gain]).astype(F32), ((0, 6), (0, LANES - attn_gain.shape[0])))
    (
        lineage, live, gains, query, stream_all, w_attn, context, middle, branch_rms, grad_middle, grad_heads,
        down_terms, gate_grad, up_grad, down_grad, out_terms, gain_two_terms, attended, log_rows,
    ) = start(
        parent, table, stream, w_query, w_key, w_value, w_gate, w_up, w_out, small_rows,
        live_mask.reshape(1, BLOCK), cotangent, w_down,
    )
    grad_query, context_terms = attend_back(
        lineage, query, context.reshape(256, BLOCK, LANES), live, grad_heads, attended, log_rows
    )
    mixed_out, stream_grad, query_grad, key_grad, value_grad, out_grad, gain_one, gain_two, stream_rms = ending(
        lineage, grad_query, table, stream_all.reshape(MEMBERS * BLOCK, D), w_attn.reshape(D, 512), gains[:1],
        gain_two_terms, stream, middle, grad_middle,
        context_terms.reshape(4, 4, 12, BLOCK, LANES), down_terms, out_terms,
    )
    (
        mixed_out, stream_grad, gain_one, query_grad, key_grad, value_grad, out_grad, gain_two,
        gate_grad, up_grad, down_grad, stream_rms, branch_rms,
    ) = hand_over(
        mixed_out, stream_grad, gain_one, query_grad, key_grad, value_grad, out_grad, gain_two,
        gate_grad, up_grad, down_grad, stream_rms, branch_rms,
    )
    return (
        mixed_out, stream_grad, gain_one[0], query_grad, key_grad, value_grad, out_grad, gain_two[0],
        gate_grad, up_grad, down_grad, stream_rms[0], branch_rms[0],
    )


def solution(mesh):
    rows, line = P("dev", None), P("dev")
    return jax.shard_map(
        shards,
        mesh=mesh,
        in_specs=(rows, line, rows, rows, rows, rows, line, rows, rows, rows, P(), line, rows),
        out_specs=(rows, rows, line, rows, rows, rows, rows, line, rows, rows, rows, line, line),
        check_vma=False,
    )
```

```python
import functools

import jax
import jax.numpy as jnp
import numpy as np
from jax import lax
from jax.experimental import pallas as pl
from jax.experimental.pallas import tpu as pltpu
from jax.sharding import PartitionSpec as P

HEADS = 16
KV_HEADS = 8
HEAD_DIM = 96
BLOCK = 128
DEPTH = 10
D = 1536
FF = 4096
MEMBERS = 8
LANES = 128

EPSILON = 1e-05
ROPE_BASE = 100000.0
NEGATIVE = -1e30
SCALE = HEAD_DIM ** (-0.5)
MESH = pl.DeviceIdType.MESH
BF16 = jnp.bfloat16
F32 = jnp.float32
VMEM_BYTES = 56 * 2**20


def spot():
    me = lax.axis_index("dev")
    return me // 32, (me // 8) % 4, (me // 2) % 4, me % 2


def device_of(x, y, z, c):
    return ((x % 4) * 4 + (y % 4)) * 8 + (z % 4) * 2 + c


def announce(peers):
    barrier = pltpu.get_barrier_semaphore()
    for peer in peers:
        pl.semaphore_signal(barrier, inc=1, device_id=(peer,), device_id_type=MESH)


def await_peers(peers):
    pl.semaphore_wait(pltpu.get_barrier_semaphore(), len(peers))


def axis_peers(x, y, z, c, far):
    steps = (1, 2, 3) if far else (1, 3)
    return [device_of(x + k, y, z, c) for k in steps] + [device_of(x, y + k, z, c) for k in steps]


def group_peer(x, y, z, c, k):
    member = (z * 2 + c + k) % MEMBERS
    return (x * 4 + y) * MEMBERS + member


class Wire:
    def __init__(self, send_sems, recv_sems):
        self.send_sems = send_sems
        self.recv_sems = recv_sems
        self.used = 0
        self.open = []

    def reserve(self, count):
        self.used += count
        return self.used - count

    def make(self, slot, source, target, peer):
        return pltpu.make_async_remote_copy(
            src_ref=source,
            dst_ref=target,
            send_sem=self.send_sems.at[slot],
            recv_sem=self.recv_sems.at[slot],
            device_id=(peer,),
            device_id_type=MESH,
        )

    def send(self, source, target, peer):
        copy = self.make(self.reserve(1), source, target, peer)
        copy.start()
        self.open.append(copy)
        return copy

    def close(self):
        for copy in self.open:
            copy.wait_send()
        self.open = []


class Ring:
    def __init__(self, wire, own, part, place, up, down):
        self.wire, self.own, self.part = wire, own, part
        self.place, self.up, self.down = place, up, down

    def begin(self):
        send, part, place = self.wire.send, self.part, self.place
        self.low_up = send(self.own(0), part(place, 0), self.up)
        self.high_down = send(self.own(1), part(place, 1), self.down)
        self.high_up = send(self.own(1), part(place, 1), self.up)
        self.low_down = send(self.own(0), part(place, 0), self.down)

    def relay(self):
        before, after = (self.place + 3) % 4, (self.place + 1) % 4
        self.low_up.wait_recv()
        self.far_up = self.wire.send(self.part(before, 0), self.part(before, 0), self.up)
        self.high_down.wait_recv()
        self.far_down = self.wire.send(self.part(after, 1), self.part(after, 1), self.down)

    def near(self):
        self.high_up.wait_recv()
        self.low_down.wait_recv()

    def far(self):
        self.far_up.wait_recv()
        self.far_down.wait_recv()


class PlaneGather:
    def __init__(self, wire, own, out, cut, xyzc):
        self.wire, self.own, self.out, self.cut = wire, own, out, cut
        x, y, z, c = xyzc
        self.x, self.y = x, y
        self.x_up, self.x_down = device_of(x + 1, y, z, c), device_of(x + 3, y, z, c)
        self.y_up, self.y_down = device_of(x, y + 1, z, c), device_of(x, y + 3, z, c)

    def pair(self, one_own, one_part, two_own, two_part, one_on_x):
        on_x = (self.x, self.x_up, self.x_down)
        on_y = (self.y, self.y_up, self.y_down)
        cut = self.cut.quarter
        self.one = Ring(
            self.wire,
            lambda side: one_own(cut(0, side)),
            lambda place, side: one_part(place, cut(0, side)),
            *(on_x if one_on_x else on_y),
        )
        self.two = Ring(
            self.wire,
            lambda side: two_own(cut(1, side)),
            lambda place, side: two_part(place, cut(1, side)),
            *(on_y if one_on_x else on_x),
        )
        self.one.begin()
        self.two.begin()

    def first(self):
        own, out, x, y = self.own, self.out, self.x, self.y
        self.pair(
            lambda q: own.at[q],
            lambda place, q: out.at[(place, y) + q],
            lambda q: own.at[q],
            lambda place, q: out.at[(x, place) + q],
            True,
        )

    def relay(self):
        self.one.relay()
        self.two.relay()

    def settle(self):
        for ring in (self.one, self.two):
            ring.near()
            ring.far()

    def second(self):
        out, x, y = self.out, self.x, self.y
        every = slice(None)
        self.pair(
            lambda q: out.at[(every, y) + q],
            lambda place, q: out.at[(every, place) + q],
            lambda q: out.at[(x, every) + q],
            lambda place, q: out.at[(place, every) + q],
            False,
        )


class Rows:
    def __init__(self, rows, cols, start=0):
        self.rows, self.cols, self.start = rows // 2, cols // 2, start

    def half(self, half):
        return (pl.ds(half * self.rows, self.rows),)

    def side(self, side):
        return (slice(None), pl.ds(side * self.cols, self.cols))

    def quarter(self, half, side):
        first = self.start + side * self.cols
        if not isinstance(first, int):
            first = pl.multiple_of(first, LANES)
        return self.half(half) + (pl.ds(first, self.cols),)

    def shapes(self):
        return (self.rows, 2 * self.cols), (self.rows, self.cols)


class Units:
    def half(self, half):
        return (pl.ds(half * 6, 6),)

    def side(self, side):
        return (pl.ds(side * 3, 3),)

    def quarter(self, half, side):
        return (pl.ds(half * 6 + side * 3, 3),)

    def shapes(self):
        return (6, BLOCK, LANES), (3, BLOCK, LANES)


class GroupGather:
    def __init__(self, wire, own, out, xyzc):
        self.wire, self.own, self.out = wire, own, out
        x, y, z, c = xyzc
        self.z, self.c = z, c
        self.sibling = device_of(x, y, z, 1 - c)
        half = out.shape[2] // 2
        self.ring = Ring(
            wire,
            lambda side: own.at[pl.ds(side * half, half)],
            lambda place, side: out.at[place, c, pl.ds(side * half, half)],
            z, device_of(x, y, z + 1, c), device_of(x, y, z + 3, c),
        )
        self.crossed = []

    def begin(self):
        self.ring.begin()
        self.crossed.append(self.wire.send(self.own, self.out.at[self.z, self.c], self.sibling))

    def cross(self, k):
        piece = self.out.at[(self.z + k) % 4, self.c]
        self.crossed.append(self.wire.send(piece, piece, self.sibling))

    def relay(self):
        self.ring.relay()

    def near(self):
        self.ring.near()
        self.cross(1)
        self.cross(3)

    def far(self):
        self.ring.far()
        self.cross(2)

    def finish(self, after=0):
        for copy in self.crossed[after:]:
            copy.wait_recv()


class PlaneScatter:
    def __init__(self, wire, terms, cut, scratch, xyzc):
        self.wire, self.terms, self.cut = wire, terms, cut
        *room, self.near_in, self.far_in, self.passed, self.summed, self.second_in = scratch
        self.room = room
        self.x, self.y, self.z, self.c = xyzc

    def peer(self, along_x, k):
        if along_x:
            return device_of(self.x + k, self.y, self.z, self.c)
        return device_of(self.x, self.y + k, self.z, self.c)

    def place(self, half, k):
        return ((self.x, self.y)[half] + k) % 4

    def lead(self, half, k, line=slice(None)):
        place = self.place(half, k)
        return (place, line) if half == 0 else (line, place)

    def part(self, half, k, side):
        return self.terms.at[self.lead(half, k) + self.cut.quarter(half, side)]

    def own(self, half, line):
        if self.room:
            return self.room[0][half, line]
        return self.terms[self.lead(half, 0, line) + self.cut.half(half)]

    def edge(self, half, way, line):
        if self.room:
            return self.room[1][half, way, line]
        return self.terms[self.lead(half, (1, 3)[way], line) + self.cut.quarter(half, way)]

    def first(self):
        send = self.wire.send
        self.far, self.plain, self.locals = [], [], []
        if self.room:
            sems = self.room[2]
            for half in range(2):
                pairs = [(self.terms.at[self.lead(half, 0) + self.cut.half(half)], self.room[0].at[half])]
                pairs += [(self.part(half, (1, 3)[way], way), self.room[1].at[half, way]) for way in range(2)]
                for slot, (source, target) in enumerate(pairs):
                    copy = pltpu.make_async_copy(source, target, sems.at[half, slot])
                    copy.start()
                    self.locals.append(copy)
        for half in range(2):
            for way in range(2):
                self.far.append(
                    send(self.part(half, 2, way), self.far_in.at[half, way], self.peer(half == 0, (1, 3)[way]))
                )
        for half in range(2):
            for way in range(2):
                k = (1, 3)[way]
                landing = self.near_in.at[(half, way, slice(None)) + self.cut.side(1 - way)]
                self.plain.append(send(self.part(half, k, 1 - way), landing, self.peer(half == 0, k)))

    def relay(self):
        for copy in self.locals:
            copy.wait()
        self.relayed = []
        for half in range(2):
            for way in range(2):
                self.far[half * 2 + way].wait_recv()

                def add(line, carry):
                    total = self.edge(half, way, line).astype(F32) + self.far_in[half, way, line].astype(F32)
                    self.passed[half, way, line] = total.astype(BF16)
                    return carry

                lax.fori_loop(0, 4, add, 0)
                landing = self.near_in.at[(half, way, slice(None)) + self.cut.side(way)]
                self.relayed.append(
                    self.wire.send(self.passed.at[half, way], landing, self.peer(half == 0, (1, 3)[way]))
                )

    def add_first(self):
        for copy in self.plain + self.relayed:
            copy.wait_recv()
        for half in range(2):

            def body(line, carry):
                total = self.own(half, line).astype(F32)
                for way in range(2):
                    total = total + self.near_in[half, way, line].astype(F32)
                self.summed[half, line] = total.astype(BF16)
                return carry

            lax.fori_loop(0, 4, body, 0)

    def second(self):
        self.copies = []
        for k in (2, 1, 3):
            for half in range(2):
                self.copies.append(
                    self.wire.send(
                        self.summed.at[half, self.place(1 - half, k)],
                        self.second_in.at[half, k - 1],
                        self.peer(half == 1, k),
                    )
                )

    def total(self, half):
        total = self.summed[half, self.place(1 - half, 0)].astype(F32)
        for k in range(3):
            total = total + self.second_in[half, k].astype(F32)
        return total

    def arrive(self):
        for copy in self.copies:
            copy.wait_recv()


def scatter_scratch(cut, room=False):
    half, part = cut.shapes()
    vmem = pltpu.VMEM
    held = [vmem((2, 4) + half, BF16), vmem((2, 2, 4) + part, BF16), pltpu.SemaphoreType.DMA((2, 3))]
    return (held if room else []) + [
        vmem((2, 2, 4) + half, BF16),
        vmem((2, 2, 4) + part, BF16),
        vmem((2, 2, 4) + part, BF16),
        vmem((2, 4) + half, BF16),
        vmem((2, 3) + half, BF16),
    ]


class GroupScatter:
    def __init__(self, wire, terms, mine, crossed_in, summed, ring_in, local_sem, xyzc):
        self.wire, self.terms = wire, terms
        self.mine, self.crossed_in, self.summed, self.ring_in = mine, crossed_in, summed, ring_in
        self.x, self.y, self.z, self.c = xyzc
        self.local_sem = local_sem

    def begin(self):
        self.local = pltpu.make_async_copy(self.terms.at[:, self.c], self.mine, self.local_sem)
        self.local.start()
        sibling = device_of(self.x, self.y, self.z, 1 - self.c)
        self.crossed = {}
        for k in (2, 1, 3, 0):
            place = (self.z + k) % 4
            self.crossed[k] = self.wire.send(
                self.terms.at[place, 1 - self.c], self.crossed_in.at[place], sibling
            )

    def turn(self):
        self.local.wait()
        self.copies = []
        for k in (2, 1, 3):
            place = (self.z + k) % 4
            self.crossed[k].wait_recv()

            def body(tile, carry):
                total = self.mine[place, tile].astype(F32) + self.crossed_in[place, tile].astype(F32)
                self.summed[place, tile] = total.astype(BF16)
                return carry

            lax.fori_loop(0, 12, body, 0)
            self.copies.append(
                self.wire.send(
                    self.summed.at[place],
                    self.ring_in.at[k - 1],
                    device_of(self.x, self.y, self.z + k, self.c),
                )
            )

    def finish(self, out):
        self.crossed[0].wait_recv()
        for copy in self.copies:
            copy.wait_recv()
        for tile in range(12):
            total = self.mine[self.z, tile].astype(F32) + self.crossed_in[self.z, tile].astype(F32)
            for k in range(3):
                total = total + self.ring_in[k, tile].astype(F32)
            out[:, tile * LANES : (tile + 1) * LANES] = total


class ChipScatter:
    def __init__(self, wire, terms, at, crossed_in, ring_in, xyzc):
        self.wire, self.terms, self.at = wire, terms, at
        self.crossed_in, self.ring_in = crossed_in, ring_in
        self.x, self.y, self.z, self.c = xyzc
        self.crossed_slot, self.ring_slot = wire.reserve(4), wire.reserve(3)
        self.all_tiles = pl.ds(0, 12)

    def place(self, step):
        return (self.z + step) % 4

    def crossed(self, step):
        place = self.place(step)
        return self.wire.make(
            self.crossed_slot + step,
            self.terms.at[place, self.at + 1 - self.c, self.all_tiles],
            self.crossed_in.at[place],
            device_of(self.x, self.y, self.z, 1 - self.c),
        )

    def ring(self, step):
        return self.wire.make(
            self.ring_slot + step - 1,
            self.terms.at[self.place(step), self.at + self.c, self.all_tiles],
            self.ring_in.at[step - 1],
            device_of(self.x, self.y, self.z + step, self.c),
        )

    def put(self, step, grads):
        place = self.place(step)
        for core in range(2):
            for tile in range(12):
                self.terms[place, self.at + core, tile] = grads[
                    core * BLOCK : (core + 1) * BLOCK, tile * LANES : (tile + 1) * LANES
                ]
        self.crossed(step).start()

    def turn(self, step):
        place, line = self.place(step), self.at + self.c
        self.crossed(step).wait_recv()

        def add(tile, carry):
            total = self.terms[place, line, tile].astype(F32) + self.crossed_in[place, tile].astype(F32)
            self.terms[place, line, tile] = total.astype(BF16)
            return carry

        lax.fori_loop(0, 12, add, 0)
        self.ring(step).start()

    def total(self):
        self.crossed(0).wait_recv()
        for step in range(1, 4):
            self.ring(step).wait_recv()
        tiles = []
        for tile in range(12):
            total = self.terms[self.z, self.at + self.c, tile].astype(F32)
            total = total + self.crossed_in[self.z, tile].astype(F32)
            for step in range(3):
                total = total + self.ring_in[step, tile].astype(F32)
            tiles.append(total)
        return jnp.concatenate(tiles, axis=1)

    def close(self):
        for step in range(4):
            self.crossed(step).wait_send()
        for step in range(1, 4):
            self.ring(step).wait_send()


class RingScatter(ChipScatter):
    def __init__(self, wire, terms, crossed_in, near_in, far_in, xyzc):
        super().__init__(wire, terms, 0, crossed_in, None, xyzc)
        self.near_in, self.far_in = near_in, far_in
        self.moved = []

    def sum_tiles(self, place, tiles, extra=None):
        def add(tile, carry):
            total = self.terms[place, self.c, tile].astype(F32)
            if extra is None:
                total = total + self.crossed_in[place, tile].astype(F32)
            else:
                total = total + self.far_in[extra, tile - extra * 6].astype(F32)
            self.terms[place, self.c, tile] = total.astype(BF16)
            return carry

        lax.fori_loop(*tiles, add, 0)

    def move(self, place, first, landing, k):
        source = self.terms.at[place, self.c, pl.ds(first, 6)]
        copy = self.wire.send(source, landing, device_of(self.x, self.y, self.z + k, self.c))
        self.moved.append(copy)
        return copy

    def turn(self, step):
        place = self.place(step)
        self.crossed(step).wait_recv()
        self.sum_tiles(place, (0, 12))
        if step == 2:
            self.far = [self.move(place, 6 * way, self.far_in.at[way], (1, 3)[way]) for way in range(2)]
        else:
            way = (1, 3).index(step)
            plain = 6 * (1 - way)
            self.move(place, plain, self.near_in.at[way, pl.ds(plain, 6)], step)

    def pass_on(self, step):
        way = (1, 3).index(step)
        place = self.place(step)
        self.far[way].wait_recv()
        self.sum_tiles(place, (6 * way, 6 * way + 6), way)
        self.move(place, 6 * way, self.near_in.at[way, pl.ds(6 * way, 6)], step)

    def total(self):
        self.crossed(0).wait_recv()
        for copy in self.moved[2:]:
            copy.wait_recv()
        tiles = []
        for tile in range(12):
            total = self.terms[self.z, self.c, tile].astype(F32) + self.crossed_in[self.z, tile].astype(F32)
            for way in range(2):
                total = total + self.near_in[way, tile].astype(F32)
            tiles.append(total)
        return jnp.concatenate(tiles, axis=1)

    def close(self):
        for step in range(4):
            self.crossed(step).wait_send()


def group_scatter_scratch():
    return [
        pltpu.VMEM((4, 12, BLOCK, LANES), BF16),
        pltpu.VMEM((4, 12, BLOCK, LANES), BF16),
        pltpu.VMEM((4, 12, BLOCK, LANES), BF16),
        pltpu.VMEM((3, 12, BLOCK, LANES), BF16),
        pltpu.SemaphoreType.DMA,
    ]


def chip_scatter_scratch():
    return [pltpu.VMEM((4, 12, BLOCK, LANES), BF16), pltpu.VMEM((3, 12, BLOCK, LANES), BF16)]


def wire_scratch(count):
    return [pltpu.SemaphoreType.DMA((count,)), pltpu.SemaphoreType.DMA((count,))]


ANY = pl.BlockSpec(memory_space=pl.ANY)
INVMEM = pl.BlockSpec(memory_space=pltpu.VMEM)


def communicate(kernel, out_shapes, in_specs, out_specs, scratch, ident, name, vmem=VMEM_BYTES):
    return pl.pallas_call(
        kernel,
        out_shape=out_shapes,
        in_specs=in_specs,
        out_specs=out_specs,
        scratch_shapes=scratch,
        compiler_params=pltpu.CompilerParams(
            collective_id=ident, has_side_effects=True, vmem_limit_bytes=vmem
        ),
        name=name,
    )


def key_unit(member):
    return member + jnp.where(member >= 6, 6, 0) + jnp.where(member >= 7, 1, 0)


def value_unit(member):
    return member + 6 + jnp.where(member >= 6, 1, 0) + jnp.where(member >= 7, 1, 0)


def gain_rows(pieces):
    return jnp.concatenate(join_heads(pieces), axis=1)


def head_window(tiles, head):
    tile, skip = divmod(head * HEAD_DIM, LANES)
    lane = lane_of(tiles[0].shape)
    window = pltpu.roll(tiles[tile], (LANES - skip) % LANES, 1)
    if skip + HEAD_DIM > LANES:
        window = jnp.where(lane < LANES - skip, window, pltpu.roll(tiles[tile + 1], LANES - skip, 1))
    return jnp.where(lane < HEAD_DIM, window, 0.0)


def join_heads(pieces):
    lane = lane_of(pieces[0].shape)
    tiles = []
    for tile in range(len(pieces) * 3 // 4):
        piece, skip = divmod(tile * LANES, HEAD_DIM)
        low = pltpu.roll(pieces[piece], (LANES - skip) % LANES, 1)
        high = pltpu.roll(pieces[piece + 1], HEAD_DIM - skip, 1)
        tiles.append(jnp.where(lane < HEAD_DIM - skip, low, high))
    return tiles


def mix_groups(parts):
    group = lane_of(parts[0][0].shape) // 32
    mixed = None
    for i, (tile, g) in enumerate(parts):
        turned = pltpu.roll(tile, (32 * (i - g)) % LANES, 1)
        mixed = turned if mixed is None else jnp.where(group == i, turned, mixed)
    return mixed


def lane_of(shape):
    return lax.broadcasted_iota(jnp.int32, shape, len(shape) - 1)


def pack_tile(unit, extra, place):
    return jnp.where(lane_of(unit.shape) < HEAD_DIM, unit, pltpu.roll(extra, (96 - 32 * place) % LANES, 1))


def unpack_extra(tiles):
    lane = lane_of(tiles[0].shape)
    extra = jnp.where(lane < 32, pltpu.roll(tiles[0], 32, 1), 0.0)
    extra = jnp.where(jnp.logical_and(lane >= 32, lane < 64), pltpu.roll(tiles[1], 64, 1), extra)
    return jnp.where(jnp.logical_and(lane >= 64, lane < 96), pltpu.roll(tiles[2], 96, 1), extra)


def swap_halves(rows):
    lane = lane_of(rows.shape)
    return jnp.where(lane < HEAD_DIM // 2, pltpu.roll(rows, LANES - 48, 1), pltpu.roll(rows, 48, 1))


def rope_table():
    half = HEAD_DIM // 2
    frequency = ROPE_BASE ** (-2.0 * np.arange(half, dtype=np.float64) / HEAD_DIM)
    frequency = frequency.astype(np.float32)
    places = np.arange(DEPTH * BLOCK, dtype=np.float32)
    angles = (places[:, None] * frequency[None, :]).astype(np.float64)
    table = np.zeros((DEPTH * BLOCK, LANES), np.float32)
    table[:, :half] = np.cos(angles)
    table[:, half:HEAD_DIM] = np.sin(angles)
    return jnp.asarray(table.reshape(DEPTH, BLOCK, LANES))


def turning(table):
    lane = lane_of(table.shape)
    cosine = jnp.where(lane < 48, table, pltpu.roll(table, 48, 1))
    sine = jnp.where(lane < 48, -pltpu.roll(table, LANES - 48, 1), jnp.where(lane < HEAD_DIM, table, 0.0))
    return cosine, sine


def count_ancestors(lineage, block):
    count = jnp.int32(0)
    for step in range(DEPTH):
        count = count + jnp.where(lineage[block, step] >= 0, 1, 0)
    return count


def write_lineage(parent, first, lineage):
    def one(block, carry):
        def hop(step, node):
            lineage[block, step] = node
            above = parent[jnp.maximum(node, 0)]
            return jnp.where(node >= 0, above, -1)

        lax.fori_loop(0, DEPTH, hop, first + block)
        return carry

    lax.fori_loop(0, MEMBERS, one, 0)


def attend_block(lineage, block, queries, alive, load, scores):
    limit = count_ancestors(lineage, block)
    t = lax.broadcasted_iota(jnp.int32, (2 * BLOCK, BLOCK), 0) % BLOCK
    u = lax.broadcasted_iota(jnp.int32, (2 * BLOCK, BLOCK), 1)
    own = jnp.logical_and(u <= t, jnp.logical_or(alive > 0.5, u == t))
    nodes = [jnp.maximum(lineage[block, step], 0) for step in range(DEPTH)]
    pairs = range(0, DEPTH, 2)
    highest = None
    for step in pairs:
        keys = jnp.concatenate([load(node, key_unit(lax.rem(node, 8))) for node in nodes[step : step + 2]], axis=0)
        part = lax.dot_general(queries, keys, (((1,), (1,)), ((), ())), preferred_element_type=F32) * SCALE
        near = part[:, :BLOCK]
        if step == 0:
            near = jnp.where(own, near, NEGATIVE)
        else:
            near = near + jnp.where(step < limit, 0.0, NEGATIVE)
        far = part[:, BLOCK:] + jnp.where(step + 1 < limit, 0.0, NEGATIVE)
        scores[step] = near
        scores[step + 1] = far
        both = jnp.maximum(near, far)
        highest = both if step == 0 else jnp.maximum(highest, both)
    largest = jnp.max(highest, axis=1, keepdims=True)
    totals = jnp.zeros((2 * BLOCK, BLOCK), F32)
    attended = jnp.zeros((2 * BLOCK, LANES), F32)
    for step in pairs:
        near, far = jnp.exp(scores[step] - largest), jnp.exp(scores[step + 1] - largest)
        totals = totals + near + far
        values = jnp.concatenate(
            [load(node, value_unit(lax.rem(node, 8))) for node in nodes[step : step + 2]], axis=0
        )
        terms = jnp.concatenate([near.astype(BF16), far.astype(BF16)], axis=1)
        attended = attended + jnp.dot(terms, values, preferred_element_type=F32)
    total = jnp.sum(totals, axis=1, keepdims=True)
    return (attended / total).astype(BF16), largest + jnp.log(total)


def start_kernel(
    parent, table, stream, w_query, w_key, w_value, w_gate, w_up, w_out, small_rows, live_row, cotangent, own_down,
    lineage, live, gains, query, stream_all, attn_all,
    kv_out, middle, rms_out, grad_middle, grads_in, down_terms, gate_grad, up_grad, down_grad, out_terms, gain_terms,
    attended_out, log_rows,
    packed, out_low, small, stage, packed_in, out_in, small_in, wide_tall, wide_own, out_own, gain_own, gains_all,
    w_attn, own_kv, kv, w_out_all, w_feed, w_down, mid_all, cot_all, crossed_in, ring_in,
    att_out, att_in, att_pad, grads_out, feed_dealt, feed_in, *scratch,
):
    feed_scratch, wide_scratch = scratch[:5], scratch[5:10]
    send_sems, recv_sems, local_sems = scratch[10:]
    xyzc = x, y, z, c = spot()
    j = z * 2 + c
    base = (x * 4 + y) * MEMBERS
    sibling = device_of(x, y, z, 1 - c)
    wire = Wire(send_sems, recv_sems)
    group = [group_peer(x, y, z, c, k) for k in range(1, MEMBERS)]
    across, down_first = (((1,), (1,)), ((), ())), (((0,), (0,)), ((), ()))
    locals_ = []

    peers = group + axis_peers(x, y, z, c, True)
    announce(peers)

    stage[...] = jnp.zeros((16, FF), F32)
    wide_tall[96:] = jnp.zeros((8, 1536), F32)

    def staged(weights):
        width = weights.shape[1]
        stage[:12, :width] = weights[...].astype(F32)
        return [stage[:, tile * LANES : (tile + 1) * LANES] for tile in range(width // LANES)]

    def put_packed(member, tile, value):
        packed[member, :, tile * LANES : (tile + 1) * LANES] = value.astype(BF16)

    tiles = staged(w_query)
    for head in range(HEADS):
        put_packed(head // 2, head % 2, head_window(tiles, head))
    for place, weights in ((2, w_key), (3, w_value)):
        tiles = staged(weights)
        for member in range(MEMBERS):
            put_packed(member, place, head_window(tiles, member))
    for place, weights in ((4, w_gate), (8, w_up)):
        tiles = staged(weights)
        for member in range(MEMBERS):
            for tile in range(4):
                parts = [(tiles[2 * (4 * tile + i) + member // 4], member % 4) for i in range(4)]
                put_packed(member, place + tile, mix_groups(parts))
    out_low[...] = jnp.concatenate(staged(w_out), axis=1).astype(BF16)
    rows = pltpu.roll(small_rows[...], 12 * j, 1)
    live_rows = jnp.broadcast_to(live_row[...].astype(F32), (8, LANES))
    rows = jnp.where(lax.broadcasted_iota(jnp.int32, (8, LANES), 0) == 2, live_rows, rows)
    small[...] = jnp.concatenate([rows, jnp.zeros((8, LANES), F32)], axis=0).astype(BF16)
    await_peers(peers)

    def keep(source, target):
        copy = pltpu.make_async_copy(source, target, local_sems.at[len(locals_)])
        copy.start()
        locals_.append(copy)
        return copy

    def to_members(source, target):
        return [wire.send(source((j + k) % MEMBERS), target.at[j], group[k - 1]) for k in range(1, MEMBERS)]

    def half_of(member):
        return pl.ds(pl.multiple_of((member % 2) * 768, 768), 768)

    own_half = half_of(c)
    packed_dealt = to_members(lambda member: packed.at[member], packed_in)
    small_dealt = to_members(lambda member: small, small_in)
    first_kept = (keep(packed.at[j], packed_in.at[j]), keep(small, small_in.at[j]))
    out_kept = keep(out_low.at[:, own_half], out_in.at[j])
    streams = GroupGather(wire, stream, mid_all, xyzc)
    streams.begin()
    stream_kept = keep(stream, mid_all.at[z, c])
    write_lineage(parent, base, lineage)
    for line in range(16):
        w_out_all[line // 4, line % 4, 96:] = jnp.zeros((32, D), BF16)

    for copy in packed_dealt + small_dealt:
        copy.wait_recv()
    out_dealt = to_members(lambda member: out_low.at[:, half_of(member)], out_in)
    for copy in first_kept:
        copy.wait()
    for member in range(MEMBERS):
        wide_tall[pl.ds(member * 12, 12)] = packed_in[member].astype(F32)[:12]
    wide_own[...] = wide_tall[:96].astype(BF16)
    gain = small_in[0].astype(F32)
    for member in range(MEMBERS):
        row = small_in[member].astype(F32)
        live[member] = row[2:3]
        if member:
            gain = gain + row
    gain_own[...] = gain.astype(BF16)
    own_attn, own_feed = wide_own.at[:, pl.ds(0, 512)], wide_own.at[:, pl.ds(512, 1024)]
    attn = PlaneGather(wire, own_attn, w_attn, Rows(96, 512), xyzc)
    attn.first()
    tiny = [wire.send(gain_own, gains_all.at[x, y], device_of(x + k, y, z, c)) for k in range(1, 4)]
    attn_kept = keep(own_attn, w_attn.at[x, y])
    gain_kept = keep(gain_own, gains_all.at[x, y])
    feed_kept = keep(own_feed, w_feed.at[x, y])
    down_kept = keep(own_down, w_down.at[x, y])

    feed = PlaneGather(wire, own_feed, w_feed, Rows(96, 1024), xyzc)
    down = PlaneGather(wire, own_down, w_down, Rows(32, D), xyzc)
    feed.first()
    down.first()
    attn.relay()
    streams.relay()
    gain_kept.wait()
    for copy in tiny:
        copy.wait_recv()
    line = gains_all.at[:, y]
    tiny = [wire.send(line, line, device_of(x, y + k, z, c)) for k in range(1, 4)]
    attn_kept.wait()
    attn.settle()
    attn.second()
    feed.relay()
    down.relay()
    for copy in out_dealt:
        copy.wait_recv()
    out_kept.wait()
    for member in range(MEMBERS):
        wide_tall[pl.ds(member * 12, 12), :768] = out_in[member].astype(F32)[:12]
    out_own[...] = wide_tall[:96, :768].astype(BF16)
    out_kept = keep(out_own, w_out_all.at[x, y, pl.ds(0, 96), own_half])
    streams.near()
    streams.far()
    attn.relay()
    for copy in tiny:
        copy.wait_recv()
    pieces = [gains_all[piece // 4, piece % 4].astype(F32)[:8] for piece in range(16)]
    gains[...] = gain_rows(pieces)
    attn.settle()
    stream_kept.wait()
    streams.finish()
    attn_copied = keep(w_attn, attn_all)
    stream_copied = keep(mid_all, stream_all)

    def project(step, carry):
        wide = mid_all[step].reshape(2 * BLOCK, D).astype(F32)
        rms = jnp.sqrt(jnp.mean(wide * wide, axis=1, keepdims=True) + EPSILON)
        rows = (wide * (1.0 / rms) * gains[0:1]).astype(BF16)
        raw = jnp.dot(rows, w_attn[...].reshape(D, 512), preferred_element_type=F32)
        for part in range(2):
            block = step * 2 + part
            depth = count_ancestors(lineage, block) - 1
            cos, sin = turning(table[depth])

            def turn(head):
                v = raw[part * BLOCK : (part + 1) * BLOCK, head * LANES : (head + 1) * LANES]
                return (v * cos + swap_halves(v) * sin).astype(BF16)

            query[block, :BLOCK] = turn(0)
            query[block, BLOCK:] = turn(1)
            kv[x, y, key_unit(block)] = turn(2)
            kv[x, y, value_unit(block)] = raw[part * BLOCK : (part + 1) * BLOCK, 3 * LANES :].astype(BF16)
        return carry

    feed_kept.wait()
    down_kept.wait()
    feed.settle()
    feed.second()
    down.settle()
    down.second()
    lax.fori_loop(0, 2, project, 0)
    feed.relay()
    down.relay()
    lax.fori_loop(2, 4, project, 0)
    for tile in range(12):
        extra = kv[x, y, 12 + tile // 3].astype(F32)
        own_kv[tile] = pack_tile(kv[x, y, tile].astype(F32), extra, tile % 3).astype(BF16)

    pairs = PlaneGather(wire, own_kv, kv, Units(), xyzc)
    pairs.first()
    kept = keep(own_kv, kv.at[x, y, pl.ds(0, 12)])
    cotangents = GroupGather(wire, cotangent, cot_all, xyzc)
    cotangents.begin()
    cot_kept = keep(cotangent, cot_all.at[z, c])
    pairs.relay()
    kept.wait()
    pairs.settle()
    pairs.second()
    cotangents.relay()
    cotangents.near()
    cotangents.far()
    pairs.relay()
    early, wire.open = wire.open, []
    out_kept.wait()
    outs = PlaneGather(wire, w_out_all.at[x, y], w_out_all, Rows(96, 768, c * 768), xyzc)
    outs.first()
    pairs.settle()
    feed.settle()
    down.settle()
    for copy in early:
        copy.wait_send()
    stream_copied.wait()
    attn_copied.wait()

    def unpack(line, carry):
        a, b = line // 4, line % 4
        for extra in range(4):
            tiles = [kv[a, b, extra * 3 + k].astype(F32) for k in range(3)]
            kv[a, b, 12 + extra] = unpack_extra(tiles).astype(BF16)
        return carry

    lax.fori_loop(0, 16, unpack, 0)
    kv_copied = keep(kv, kv_out)

    att_slot = wire.reserve(MEMBERS - 1)

    def load(node, unit):
        return kv[lax.div(node, 32), lax.rem(lax.div(node, 8), 4), unit]

    def att_copy(k):
        block = (j + 1 + k) % MEMBERS
        return wire.make(att_slot + k, att_out.at[block], att_in.at[j], base + block)

    def attend(k, scores):
        block = (j + 1 + k) % MEMBERS
        attended, logs = attend_block(lineage, block, query[block], live[block], load, scores)
        log_rows[block] = jnp.transpose(jnp.broadcast_to(logs, (2 * BLOCK, LANES)))[:8]
        att_out[block, :, :LANES] = attended[:BLOCK]
        att_out[block, :, LANES:] = attended[BLOCK:]

        @pl.when(k < MEMBERS - 1)
        def _():
            att_copy(k).start()

        return 0

    def attend_some(first, last):
        def some(scores):
            lax.fori_loop(first, last, lambda k, carry: attend(k, scores), 0)

        pl.run_scoped(some, pltpu.VMEM((DEPTH, 2 * BLOCK, LANES), F32))

    attend_some(0, 1)
    outs.relay()
    attend_some(1, 3)
    outs.settle()
    outs.second()
    attend_some(3, 5)
    outs.relay()
    attend_some(5, 7)
    outs.settle()
    swap_part = w_out_all.at[:, :, pl.ds(0, 96), own_half]
    swapped = wire.send(swap_part, swap_part, sibling)
    attend_some(7, MEMBERS)
    att_in[j] = att_out[j]
    att_copied = keep(att_out, attended_out)
    att_recv = [att_copy(k) for k in range(MEMBERS - 1)]

    for copy in att_recv:
        copy.wait_recv()
    for member in range(MEMBERS):
        att_pad[:, member * 256 : (member + 1) * 256] = att_in[member]
    swapped.wait_recv()

    def project_out(step, carry):
        cols = pl.ds(pl.multiple_of(step * 512, 512), 512)
        weights = w_out_all[:, :, :, cols].reshape(16 * LANES, 512)
        branch = jnp.dot(att_pad[...], weights, preferred_element_type=F32)
        middle[:, cols] = stream[:, cols].astype(F32) + branch
        return carry

    lax.fori_loop(0, 3, project_out, 0)
    rms = jnp.sqrt(jnp.mean(middle[...] * middle[...], axis=1, keepdims=True) + EPSILON)
    rms_out[...] = jnp.transpose(jnp.broadcast_to(rms, (BLOCK, LANES)))[:1]
    mid_all[z, c] = (middle[...] / rms * gains[1:2]).astype(BF16)
    late, wire.open = wire.open, []
    mids = GroupGather(wire, mid_all.at[z, c], mid_all, xyzc)
    mids.begin()
    mids.relay()
    for copy in late:
        copy.wait_send()
    kv_copied.wait()
    cot_kept.wait()
    cotangents.finish()
    for k in range(MEMBERS - 1):
        att_copy(k).wait_send()

    grad_rows = ChipScatter(wire, kv, 2, crossed_in, ring_in, xyzc)

    def rest(acts, grad_feed, feed_terms, wide_terms):
        feed_back_half(
            xyzc, wire, group, keep, mids, grad_rows, mid_all, cot_all, w_feed, w_down, w_out_all, kv, middle, gains,
            att_pad, att_copied, grads_out, feed_dealt, feed_in, wide_tall, feed_scratch, wide_scratch,
            acts, grad_feed, feed_terms, wide_terms,
            grad_middle, grads_in, down_terms, gate_grad, up_grad, down_grad, out_terms, gain_terms,
        )

    pl.run_scoped(
        rest,
        pltpu.VMEM((4, 2 * BLOCK, 512), BF16),
        pltpu.VMEM((4, 2 * BLOCK, 1024), BF16),
        pltpu.VMEM((4, 4, 96, 1024), BF16),
        pltpu.VMEM((4, 4, 32, D), BF16),
    )


def feed_back_half(
    xyzc, wire, group, keep, mids, grad_rows, mid_all, cot_all, w_feed, w_down, w_out_all, kv, middle, gains,
    att_pad, att_copied, grads_out, feed_dealt, feed_in, wide_tall, feed_scratch, wide_scratch,
    acts, grad_feed, feed_terms, wide_terms,
    grad_middle, grads_in, down_terms, gate_grad, up_grad, down_grad, out_terms, gain_terms,
):
    x, y, z, c = xyzc
    j = z * 2 + c
    across, down_first = (((1,), (1,)), ((), ())), (((0,), (0,)), ((), ()))

    def feed_forward(step):
        place = grad_rows.place(step)
        rows = mid_all[place].reshape(2 * BLOCK, D)
        weights = w_feed[...].reshape(D, 1024)
        both = jnp.dot(rows, weights, preferred_element_type=F32)
        gate, up = both[:, :512], both[:, 512:]
        sigmoid = 0.5 * jnp.tanh(0.5 * gate) + 0.5
        silu = gate * sigmoid
        acts[place] = (silu * up).astype(BF16)
        cot = cot_all[place].reshape(2 * BLOCK, D)
        grad_act = lax.dot_general(cot, w_down[...].reshape(512, D), across, preferred_element_type=F32)
        grad_gate = grad_act * up * sigmoid * (1.0 + gate * (1.0 - sigmoid))
        grad_feed[place, :, :512] = grad_gate.astype(BF16)
        grad_feed[place, :, 512:] = (grad_act * silu).astype(BF16)

    def feed_back(step):
        place = grad_rows.place(step)
        weights = w_feed[...].reshape(D, 1024)
        grads = lax.dot_general(grad_feed[place], weights, across, preferred_element_type=F32)
        grad_rows.put(step, grads.astype(BF16))

    mids.crossed[0].wait_recv()
    feed_forward(0)
    feed_back(0)
    mids.near()
    mids.crossed[1].wait_recv()
    feed_forward(1)
    feed_back(1)
    mids.far()
    mids.crossed[2].wait_recv()
    grad_rows.turn(1)
    feed_forward(3)
    feed_back(3)
    mids.crossed[3].wait_recv()
    grad_rows.turn(3)
    feed_forward(2)

    def down_weights(step, carry):
        cols = pl.ds(pl.multiple_of(step * 128, 128), 128)
        left = acts[:, :, cols].reshape(MEMBERS * BLOCK, 128)
        right = cot_all[...].reshape(MEMBERS * BLOCK, D)
        total = lax.dot_general(left, right, down_first, preferred_element_type=F32)
        wide_terms[step] = total.astype(BF16).reshape(4, 32, D)
        return carry

    lax.fori_loop(0, 4, down_weights, 0)
    wides = PlaneScatter(wire, wide_terms, Rows(32, D), wide_scratch, xyzc)
    wides.first()
    feed_back(2)

    def feed_weights(step, carry):
        cols = pl.ds(pl.multiple_of(step * 384, 384), 384)
        left = mid_all[:, :, :, cols].reshape(MEMBERS * BLOCK, 384)
        right = grad_feed[...].reshape(MEMBERS * BLOCK, 1024)
        total = lax.dot_general(left, right, down_first, preferred_element_type=F32)
        feed_terms[step] = total.astype(BF16).reshape(4, 96, 1024)
        return carry

    lax.fori_loop(0, 2, feed_weights, 0)
    grad_rows.turn(2)
    lax.fori_loop(2, 4, feed_weights, 0)
    feeds = PlaneScatter(wire, feed_terms, Rows(96, 1024), feed_scratch, xyzc)
    feeds.first()
    wides.relay()

    def down_rows(place, carry):
        outs = jnp.dot(acts[place], w_down[...].reshape(512, D), preferred_element_type=F32).astype(BF16)
        for core in range(2):
            for tile in range(12):
                kv[place, core, tile] = outs[
                    core * BLOCK : (core + 1) * BLOCK, tile * LANES : (tile + 1) * LANES
                ]
        return carry

    lax.fori_loop(0, 4, down_rows, 0)
    down_copied = keep(kv.at[:, pl.ds(0, 2), pl.ds(0, 12)], down_terms)
    feeds.relay()

    grad_mid = grad_rows.total()
    rms = jnp.sqrt(jnp.mean(middle[...] * middle[...], axis=1, keepdims=True) + EPSILON)
    scaled = middle[...] / rms
    gain_terms[...] = jnp.sum(grad_mid * scaled, axis=0, keepdims=True)
    weighted = grad_mid * gains[1:2]
    back = (weighted - scaled * jnp.mean(weighted * scaled, axis=1, keepdims=True)) / rms
    grad_middle[...] = cot_all[z, c].astype(F32) + back
    branch_grad = grad_middle[...].astype(BF16)

    def spread(step, carry):
        weights = w_out_all[step].reshape(4 * LANES, D)
        grads = lax.dot_general(branch_grad, weights, across, preferred_element_type=F32).astype(BF16)
        for part in range(2):
            grads_out[step * 2 + part] = grads[:, part * 256 : (part + 1) * 256]
        return carry

    lax.fori_loop(0, 4, spread, 0)
    kept = keep(grads_out.at[j], grads_in.at[j])
    dealt = [
        wire.send(grads_out.at[(j + k) % MEMBERS], grads_in.at[j], group[k - 1]) for k in (4, 5, 3, 2, 6, 7, 1)
    ]
    def out_weights(step, carry):
        cols = pl.ds(pl.multiple_of(step * 512, 512), 512)
        total = lax.dot_general(att_pad[:, cols], branch_grad, down_first, preferred_element_type=F32)
        w_out_all[step] = total.astype(BF16).reshape(4, LANES, D)
        return carry

    lax.fori_loop(0, 4, out_weights, 0)
    out_copied = keep(w_out_all.at[:, :, pl.ds(0, 96)], out_terms)

    wides.add_first()
    wides.second()
    feeds.add_first()
    feeds.second()
    feeds.arrive()
    for half in range(2):
        wide_tall[pl.ds(half * 48, 48), :1024] = feeds.total(half)
    split_rows(wide_tall, feed_dealt)
    feed_in[j] = feed_dealt[j]
    feed_dealt_copies = [
        wire.send(feed_dealt.at[(j + k) % MEMBERS], feed_in.at[j], group[k - 1]) for k in range(1, MEMBERS)
    ]
    wides.arrive()
    for half in range(2):
        down_grad[pl.ds(half * 16, 16)] = wides.total(half)
    for copy in feed_dealt_copies:
        copy.wait_recv()
    for grad, first in ((gate_grad, 0), (up_grad, 4)):
        for tile in range(32):
            line = tile // 2
            cols = slice((first + line // 4) * LANES, (first + line // 4 + 1) * LANES)
            parts = [(feed_in[4 * (tile % 2) + i, :, cols].astype(F32), line % 4) for i in range(4)]
            grad[:, tile * LANES : (tile + 1) * LANES] = mix_groups(parts)[:12]
    for copy in dealt:
        copy.wait_recv()
    for copy in (kept, down_copied, out_copied, att_copied):
        copy.wait()
    wire.close()
    grad_rows.close()


def start(
    parent, table, stream, w_query, w_key, w_value, w_gate, w_up, w_out, small_rows, live_row, cotangent, own_down
):
    shape, vmem = jax.ShapeDtypeStruct, pltpu.VMEM
    smem = pl.BlockSpec(memory_space=pltpu.SMEM)
    return communicate(
        start_kernel,
        (
            shape((MEMBERS, DEPTH), jnp.int32),
            shape((MEMBERS, 1, LANES), F32),
            shape((8, D), F32),
            shape((MEMBERS, 2 * BLOCK, LANES), BF16),
            shape((4, 2, BLOCK, D), BF16),
            shape((4, 4, 96, 512), BF16),
            shape((4, 4, 16, BLOCK, LANES), BF16),
            shape((BLOCK, D), F32),
            shape((1, LANES), F32),
            shape((BLOCK, D), F32),
            shape((MEMBERS, BLOCK, 2 * LANES), BF16),
            shape((4, 2, 12, BLOCK, LANES), BF16),
            shape((12, FF), F32),
            shape((12, FF), F32),
            shape((32, D), F32),
            shape((4, 4, 96, D), BF16),
            shape((1, D), F32),
            shape((MEMBERS, BLOCK, 2 * LANES), BF16),
            shape((MEMBERS, 8, 2 * BLOCK), F32),
        ),
        [smem] + [INVMEM] * 10 + [ANY] * 2,
        (smem,) + (INVMEM,) * 3 + (ANY,) * 3 + (INVMEM,) * 3 + (ANY,) * 2 + (INVMEM,) * 3 + (ANY, INVMEM, ANY, INVMEM),
        [
            vmem((MEMBERS, 16, 1536), BF16),
            vmem((16, 1536), BF16),
            vmem((16, LANES), BF16),
            vmem((16, FF), F32),
            vmem((MEMBERS, 16, 1536), BF16),
            vmem((MEMBERS, 16, 768), BF16),
            vmem((MEMBERS, 16, LANES), BF16),
            vmem((104, 1536), F32),
            vmem((96, 1536), BF16),
            vmem((96, 768), BF16),
            vmem((16, LANES), BF16),
            vmem((4, 4, 16, LANES), BF16),
            vmem((4, 4, 96, 512), BF16),
            vmem((12, BLOCK, LANES), BF16),
            vmem((4, 4, 16, BLOCK, LANES), BF16),
            vmem((4, 4, LANES, D), BF16),
            vmem((4, 4, 96, 1024), BF16),
            vmem((4, 4, 32, D), BF16),
            vmem((4, 2, BLOCK, D), BF16),
            vmem((4, 2, BLOCK, D), BF16),
        ]
        + chip_scatter_scratch()
        + [
            vmem((MEMBERS, BLOCK, 2 * LANES), BF16),
            vmem((MEMBERS, BLOCK, 2 * LANES), BF16),
            vmem((BLOCK, 2048), BF16),
            vmem((MEMBERS, BLOCK, 2 * LANES), BF16),
            vmem((MEMBERS, 16, 1024), BF16),
            vmem((MEMBERS, 16, 1024), BF16),
        ]
        + scatter_scratch(Rows(96, 1024))
        + scatter_scratch(Rows(32, D))
        + wire_scratch(242)
        + [pltpu.SemaphoreType.DMA((20,))],
        2,
        "start",
        63 * 2**20,
    )(parent, table, stream, w_query, w_key, w_value, w_gate, w_up, w_out, small_rows, live_row, cotangent, own_down)


def split_rows(tall, dealt):
    width = dealt.shape[2]
    for member in range(MEMBERS):
        dealt[member] = tall[pl.ds(member * 12, 16), :width].astype(BF16)


def attend_back_kernel(
    lineage, query, live, grad, attended, log_rows, kv_in, grad_query, grad_kv, kv, sums, packed, sems
):
    loaded = pltpu.make_async_copy(kv_in, kv, sems.at[16])
    loaded.start()

    def clear(step, carry):
        sums[step] = jnp.zeros((BLOCK, LANES), F32)
        return carry

    lax.fori_loop(0, 256, clear, 0)
    loaded.wait()

    def one(block, carry):
        attend_back_block(block, lineage, query, live, grad, attended, log_rows, grad_query, kv, sums)
        return carry

    lax.fori_loop(0, MEMBERS, one, 0)

    def stored(line):
        rows = pl.ds(line * 12, 12)
        return pltpu.make_async_copy(packed.at[rows], grad_kv.at[rows], sems.at[line])

    def store(line, carry):
        for tile in range(12):
            total = pack_tile(sums[line * 16 + tile], sums[line * 16 + 12 + tile // 3], tile % 3)
            packed[line * 12 + tile] = total.astype(BF16)
        stored(line).start()
        return carry

    lax.fori_loop(0, 16, store, 0)
    for line in range(16):
        stored(line).wait()


def attend_back_block(block, lineage, query, live, grad, attended, log_rows, grad_query, kv, sums):
    across, down_first = (((1,), (1,)), ((), ())), (((0,), (0,)), ((), ()))
    queries = query[block]
    grads = jnp.concatenate([grad[block, :, :LANES], grad[block, :, LANES:]], axis=0)
    outs = jnp.concatenate([attended[block, :, :LANES], attended[block, :, LANES:]], axis=0)
    product = grads.astype(F32) * outs.astype(F32)
    high = product.astype(BF16)
    low = (product - high.astype(F32)).astype(BF16)
    ones = jnp.ones((8, LANES), BF16)
    inner = lax.dot_general(ones, high, across, preferred_element_type=F32)
    inner = (inner + lax.dot_general(ones, low, across, preferred_element_type=F32))[:1]
    logs = log_rows[block, :1]
    limit = count_ancestors(lineage, block)
    u = lax.broadcasted_iota(jnp.int32, (BLOCK, 2 * BLOCK), 0)
    t = lax.broadcasted_iota(jnp.int32, (BLOCK, 2 * BLOCK), 1) % BLOCK
    alive = jnp.transpose(jnp.broadcast_to(live[block], (BLOCK, BLOCK)))
    alive = jnp.concatenate([alive, alive], axis=1)
    own = jnp.logical_and(u <= t, jnp.logical_or(alive > 0.5, u == t))
    turned = jnp.zeros((LANES, 2 * BLOCK), F32)
    for step in range(0, DEPTH, 2):
        units = []
        for node in (lineage[block, step], lineage[block, step + 1]):
            safe = jnp.maximum(node, 0)
            at, member = lax.div(safe, 8) * 16, lax.rem(safe, 8)
            units.append((node, at + key_unit(member), at + value_unit(member)))
        keys = jnp.concatenate([kv[unit[1]] for unit in units], axis=0)
        values = jnp.concatenate([kv[unit[2]] for unit in units], axis=0)
        scores = lax.dot_general(keys, queries, across, preferred_element_type=F32) * SCALE
        near, far = scores[:BLOCK], scores[BLOCK:]
        if step == 0:
            near = jnp.where(own, jnp.exp(jnp.where(own, near - logs, NEGATIVE)), 0.0)
        else:
            near = jnp.exp(near + (jnp.where(step < limit, 0.0, NEGATIVE) - logs))
        far = jnp.exp(far + (jnp.where(step + 1 < limit, 0.0, NEGATIVE) - logs))
        chances = jnp.concatenate([near, far], axis=0)
        grad_chances = lax.dot_general(values, grads, across, preferred_element_type=F32)
        grad_scores = (chances * (grad_chances - inner)).astype(BF16)
        grad_keys = jnp.dot(grad_scores, queries, preferred_element_type=F32) * SCALE
        grad_values = jnp.dot(chances.astype(BF16), grads, preferred_element_type=F32)
        for part, (node, at_key, at_value) in enumerate(units):
            rows = slice(part * BLOCK, (part + 1) * BLOCK)
            sums[jnp.where(node >= 0, at_key, 256)] += grad_keys[rows]
            sums[jnp.where(node >= 0, at_value, 256)] += grad_values[rows]
        turned = turned + lax.dot_general(keys, grad_scores, down_first, preferred_element_type=F32)
    grad_query[block] = jnp.transpose(turned) * SCALE


def attend_back(lineage, query, kv, live, grad, attended, log_rows):
    vmem = pltpu.VMEM
    return pl.pallas_call(
        attend_back_kernel,
        in_specs=[pl.BlockSpec(memory_space=pltpu.SMEM)] + [INVMEM] * 5 + [ANY],
        out_specs=(INVMEM, ANY),
        out_shape=(
            jax.ShapeDtypeStruct((MEMBERS, 2 * BLOCK, LANES), F32),
            jax.ShapeDtypeStruct((192, BLOCK, LANES), BF16),
        ),
        scratch_shapes=[
            vmem((256, BLOCK, LANES), BF16),
            vmem((257, BLOCK, LANES), F32),
            vmem((192, BLOCK, LANES), BF16),
            pltpu.SemaphoreType.DMA((17,)),
        ],
        compiler_params=pltpu.CompilerParams(vmem_limit_bytes=VMEM_BYTES),
        name="attend_back",
    )(lineage, query, live, grad, attended, log_rows, kv)


def gain_tiles(rows):
    lane = lane_of((8, LANES))
    tiles = [rows[:, tile * LANES : (tile + 1) * LANES] for tile in range(12)]
    pieces = []
    for piece in range(16):
        tile, skip = divmod(piece * 96, LANES)
        low = pltpu.roll(tiles[tile], (LANES - skip) % LANES, 1)
        high = pltpu.roll(tiles[min(tile + 1, 11)], (LANES - skip) % LANES, 1)
        pieces.append(jnp.where(lane < LANES - skip, low, high))
    return pieces


def ending_kernel(
    lineage, grad_query, table, stream_all, w_attn, gain, gain_two, stream, middle, grad_middle,
    kv_terms, down_terms, out_terms,
    mixed_out, stream_grad, query_grad, key_grad, value_grad, out_grad, gain_one, gain_two_out, rms_out,
    attn_grad, out_in, normed, raw, units, grad_terms, crossed_in, near_in, far_in, query_terms, pair_terms, attn_tall, attn_dealt,
    out_tall, out_dealt, out_mine, out_crossed, gain_terms, gain_in, gain_line, gain_in_two, gain_in_three,
    *scratch,
):
    xyzc = x, y, z, c = spot()
    j = z * 2 + c
    down_scratch, kv_scratch, query_scratch, pair_scratch, out_scratch = (
        scratch[:5], scratch[5:13], scratch[13:18], scratch[18:23], scratch[23:28]
    )
    send_sems, recv_sems, local_sem = scratch[28:]
    wire = Wire(send_sems, recv_sems)
    group = [group_peer(x, y, z, c, k) for k in range(1, MEMBERS)]
    peers = group + axis_peers(x, y, z, c, True)
    announce(peers)
    await_peers(peers)
    sibling = device_of(x, y, z, 1 - c)
    pairs = PlaneScatter(wire, kv_terms, Units(), kv_scratch, xyzc)
    pairs.first()
    attn_tall[96:] = jnp.zeros((8, 512), F32)
    out_tall[96:] = jnp.zeros((8, 768), F32)

    def norm_rows(step, carry):
        rows = pl.ds(pl.multiple_of(step * BLOCK, BLOCK), BLOCK)
        wide = stream_all[rows].astype(F32)
        rms = jnp.sqrt(jnp.mean(wide * wide, axis=1, keepdims=True) + EPSILON)
        normed[rows] = (wide * (1.0 / rms) * gain[0:1]).astype(BF16)
        return carry

    lax.fori_loop(0, MEMBERS, norm_rows, 0)

    def turn(block, v):
        depth = count_ancestors(lineage, block) - 1
        cos, sin = turning(table[depth])
        return (v * cos - swap_halves(v) * sin).astype(BF16)

    def query_rows(block, carry):
        rows = pl.ds(pl.multiple_of(block * BLOCK, BLOCK), BLOCK)
        raw[rows, :128] = turn(block, grad_query[block, :BLOCK])
        raw[rows, 128:256] = turn(block, grad_query[block, BLOCK:])
        return carry

    lax.fori_loop(0, MEMBERS, query_rows, 0)
    pairs.relay()
    downs = GroupScatter(wire, down_terms, *down_scratch, xyzc)
    downs.begin()
    own_half = pl.ds(pl.multiple_of(c * 768, 768), 768)
    other_half = pl.ds(pl.multiple_of((1 - c) * 768, 768), 768)
    crossed = wire.send(out_terms.at[:, :, :, other_half], out_crossed, sibling)
    local = pltpu.make_async_copy(out_terms.at[:, :, :, own_half], out_mine, local_sem)
    local.start()

    def weights_back(terms, first):
        def some(step, carry):
            cols = pl.ds(pl.multiple_of(step * 384, 384), 384)
            total = lax.dot_general(
                normed[:, cols], raw[:, first : first + 256], (((0,), (0,)), ((), ())), preferred_element_type=F32
            )
            terms[step] = total.astype(BF16).reshape(4, 96, 256)
            return carry

        lax.fori_loop(0, 4, some, 0)

    weights_back(query_terms, 0)
    query_sums = PlaneScatter(wire, query_terms, Rows(96, 256), query_scratch, xyzc)
    pair_sums = PlaneScatter(wire, pair_terms, Rows(96, 256), pair_scratch, xyzc)
    local.wait()
    crossed.wait_recv()

    def add_halves(step, carry):
        a, b = step // 4, step % 4
        total = out_mine[a, b].astype(F32) + out_crossed[a, b].astype(F32)
        out_mine[a, b] = total.astype(BF16)
        return carry

    lax.fori_loop(0, 16, add_halves, 0)
    outs = PlaneScatter(wire, out_mine, Rows(96, 768), out_scratch, xyzc)
    downs.turn()
    pairs.add_first()
    pairs.second()
    downs.finish(stream_grad)
    mixed_out[...] = (middle[...] + stream_grad[...]).astype(BF16)
    pairs.arrive()
    outs.first()
    query_sums.first()
    for half in range(2):
        units[pl.ds(half * 6, 6)] = pairs.total(half)
    for extra in range(4):
        units[12 + extra] = unpack_extra([units[extra * 3 + k] for k in range(3)])

    def pair_rows(block, carry):
        rows = pl.ds(pl.multiple_of(block * BLOCK, BLOCK), BLOCK)
        raw[rows, 256:384] = turn(block, units[key_unit(block)])
        value = units[value_unit(block)]
        raw[rows, 384:] = jnp.where(lane_of((BLOCK, LANES)) < HEAD_DIM, value, 0.0).astype(BF16)
        return carry

    lax.fori_loop(0, MEMBERS, pair_rows, 0)

    grad_rows = RingScatter(wire, grad_terms, crossed_in, near_in, far_in, xyzc)
    gain_terms[...] = jnp.zeros((1, D), F32)

    def rows_back(step):
        rows = pl.ds(pl.multiple_of(grad_rows.place(step) * 256, 256), 256)
        grads = lax.dot_general(raw[rows], w_attn[...], (((1,), (1,)), ((), ())), preferred_element_type=F32)
        grad_rows.put(step, grads.astype(BF16))
        wide = stream_all[rows].astype(F32)
        rms = jnp.sqrt(jnp.mean(wide * wide, axis=1, keepdims=True) + EPSILON)
        gain_terms[...] += jnp.sum(grads * (wide * (1.0 / rms)), axis=0, keepdims=True)

    rows_back(2)
    rows_back(1)
    grad_rows.turn(2)
    rows_back(3)
    grad_rows.turn(1)
    rows_back(0)
    grad_rows.turn(3)
    outs.relay()
    query_sums.relay()
    grad_rows.pass_on(1)
    grad_rows.pass_on(3)
    rows = jnp.concatenate([gain_terms[...], gain_two[...], jnp.zeros((6, D), F32)], axis=0)
    for piece, part in enumerate(gain_tiles(rows)):
        gain_in[piece // 4, piece % 4] = part
    gains = [
        wire.send(gain_in.at[(x + k) % 4], gain_line.at[k], device_of(x + k, y, z, c)) for k in range(1, 4)
    ]

    weights_back(pair_terms, 256)
    pair_sums.first()
    for copy in gains:
        copy.wait_recv()
    gain_line[0] = gain_in[x] + gain_line[1] + gain_line[2] + gain_line[3]
    gains = [
        wire.send(gain_line.at[0, (y + k) % 4], gain_in_two.at[k], device_of(x, y + k, z, c)) for k in range(1, 4)
    ]
    outs.add_first()
    outs.second()
    query_sums.add_first()
    query_sums.second()
    pair_sums.relay()

    wide = stream[...].astype(F32)
    rms = jnp.sqrt(jnp.mean(wide * wide, axis=1, keepdims=True) + EPSILON)
    rms_out[...] = jnp.transpose(jnp.broadcast_to(rms, (BLOCK, LANES)))[:1]
    scaled = wide / rms
    weighted = grad_rows.total() * gain[0:1]
    back = (weighted - scaled * jnp.mean(weighted * scaled, axis=1, keepdims=True)) / rms
    stream_grad[...] = grad_middle[...] + back

    for copy in gains:
        copy.wait_recv()
    gain_in_three[j] = gain_line[0, y] + gain_in_two[1] + gain_in_two[2] + gain_in_two[3]
    gains = [
        wire.send(gain_in_three.at[j], gain_in_three.at[j], group[k - 1]) for k in range(1, MEMBERS)
    ]
    pair_sums.add_first()
    pair_sums.second()
    outs.arrive()
    for half in range(2):
        out_tall[pl.ds(half * 48, 48)] = outs.total(half)
    split_rows(out_tall, out_dealt)
    out_in[j] = out_dealt[j]
    dealt = [
        wire.send(out_dealt.at[(j + k) % MEMBERS], out_in.at[j], group[k - 1]) for k in range(1, MEMBERS)
    ]
    query_sums.arrive()
    pair_sums.arrive()
    for half in range(2):
        attn_tall[pl.ds(half * 48, 48), :256] = query_sums.total(half)
        attn_tall[pl.ds(half * 48, 48), 256:] = pair_sums.total(half)
    split_rows(attn_tall, attn_dealt)
    attn_grad[j] = attn_dealt[j]
    dealt += [
        wire.send(attn_dealt.at[(j + k) % MEMBERS], attn_grad.at[j], group[k - 1]) for k in range(1, MEMBERS)
    ]
    for copy in gains:
        copy.wait_recv()
    total = gain_in_three[0]
    for member in range(1, MEMBERS):
        total = total + gain_in_three[member]
    own = pltpu.roll(total, (LANES - 12 * j) % LANES, 1)
    gain_one[...] = own[:1, :12]
    gain_two_out[...] = own[1:2, :12]
    for copy in dealt:
        copy.wait_recv()
    for core in range(2):
        total = out_in[core].astype(F32)
        for place in range(1, 4):
            total = total + out_in[place * 2 + core].astype(F32)
        out_grad[:, core * 768 : (core + 1) * 768] = total[:12]

    def tile_of(member, tile):
        return attn_grad[member, :, tile * LANES : (tile + 1) * LANES].astype(F32)

    for grad, pieces in (
        (query_grad, [tile_of(head // 2, head % 2) for head in range(HEADS)]),
        (key_grad, [tile_of(member, 2) for member in range(MEMBERS)]),
        (value_grad, [tile_of(member, 3) for member in range(MEMBERS)]),
    ):
        for tile, value in enumerate(join_heads(pieces)):
            grad[:, tile * LANES : (tile + 1) * LANES] = value[:12]
    wire.close()
    grad_rows.close()


def ending(
    lineage, grad_query, table, stream_all, w_attn, gain, gain_two, stream, middle, grad_middle,
    kv_terms, down_terms, out_terms,
):
    shape, vmem = jax.ShapeDtypeStruct, pltpu.VMEM
    smem = pl.BlockSpec(memory_space=pltpu.SMEM)
    return communicate(
        ending_kernel,
        (
            shape((BLOCK, D), BF16),
            shape((BLOCK, D), F32),
            shape((12, D), F32),
            shape((12, 768), F32),
            shape((12, 768), F32),
            shape((12, D), F32),
            shape((1, 12), F32),
            shape((1, 12), F32),
            shape((1, LANES), F32),
        ),
        [smem] + [INVMEM] * 9 + [ANY] * 3,
        (INVMEM,) * 9,
        [
            vmem((MEMBERS, 16, 512), BF16),
            vmem((MEMBERS, 16, 768), BF16),
            vmem((MEMBERS * BLOCK, D), BF16),
            vmem((MEMBERS * BLOCK, 512), BF16),
            vmem((16, BLOCK, LANES), F32),
            vmem((4, 2, 12, BLOCK, LANES), BF16),
        ]
        + [
            vmem((4, 12, BLOCK, LANES), BF16),
            vmem((2, 12, BLOCK, LANES), BF16),
            vmem((2, 6, BLOCK, LANES), BF16),
        ]
        + [
            vmem((4, 4, 96, 256), BF16),
            vmem((4, 4, 96, 256), BF16),
            vmem((104, 512), F32),
            vmem((MEMBERS, 16, 512), BF16),
            vmem((104, 768), F32),
            vmem((MEMBERS, 16, 768), BF16),
            vmem((4, 4, 96, 768), BF16),
            vmem((4, 4, 96, 768), BF16),
            vmem((1, D), F32),
            vmem((4, 4, 8, LANES), F32),
            vmem((4, 4, 8, LANES), F32),
            vmem((4, 8, LANES), F32),
            vmem((MEMBERS, 8, LANES), F32),
        ]
        + group_scatter_scratch()
        + scatter_scratch(Units(), room=True)
        + scatter_scratch(Rows(96, 256))
        + scatter_scratch(Rows(96, 256))
        + scatter_scratch(Rows(96, 768))
        + wire_scratch(120)
        + [pltpu.SemaphoreType.DMA],
        7,
        "ending",
        62 * 2**20,
    )(
        lineage, grad_query, table, stream_all, w_attn, gain, gain_two, stream, middle, grad_middle,
        kv_terms, down_terms, out_terms,
    )


def hand_over_kernel(*refs):
    count = len(refs) // 2
    for source, target in zip(refs[:count], refs[count:]):
        target[...] = source[...]


def hand_over(*arrays):
    return pl.pallas_call(
        hand_over_kernel,
        out_shape=tuple(jax.ShapeDtypeStruct(array.shape, array.dtype) for array in arrays),
        in_specs=[INVMEM] * len(arrays),
        out_specs=(INVMEM,) * len(arrays),
        compiler_params=pltpu.CompilerParams(vmem_limit_bytes=VMEM_BYTES),
        name="hand_over",
    )(*arrays)


def shards(
    stream, attn_gain, w_query, w_key, w_value, w_out, mlp_gain, w_gate, w_up, w_down, parent, live_mask, cotangent
):
    table = rope_table()
    small_rows = jnp.pad(jnp.stack([attn_gain, mlp_gain]).astype(F32), ((0, 6), (0, LANES - attn_gain.shape[0])))
    (
        lineage, live, gains, query, stream_all, w_attn, context, middle, branch_rms, grad_middle, grad_heads,
        down_terms, gate_grad, up_grad, down_grad, out_terms, gain_two_terms, attended, log_rows,
    ) = start(
        parent, table, stream, w_query, w_key, w_value, w_gate, w_up, w_out, small_rows,
        live_mask.reshape(1, BLOCK), cotangent, w_down,
    )
    grad_query, context_terms = attend_back(
        lineage, query, context.reshape(256, BLOCK, LANES), live, grad_heads, attended, log_rows
    )
    mixed_out, stream_grad, query_grad, key_grad, value_grad, out_grad, gain_one, gain_two, stream_rms = ending(
        lineage, grad_query, table, stream_all.reshape(MEMBERS * BLOCK, D), w_attn.reshape(D, 512), gains,
        gain_two_terms, stream, middle, grad_middle,
        context_terms.reshape(4, 4, 12, BLOCK, LANES), down_terms, out_terms,
    )
    (
        mixed_out, stream_grad, gain_one, query_grad, key_grad, value_grad, out_grad, gain_two,
        gate_grad, up_grad, down_grad, stream_rms, branch_rms,
    ) = hand_over(
        mixed_out, stream_grad, gain_one, query_grad, key_grad, value_grad, out_grad, gain_two,
        gate_grad, up_grad, down_grad, stream_rms, branch_rms,
    )
    return (
        mixed_out, stream_grad, gain_one[0], query_grad, key_grad, value_grad, out_grad, gain_two[0],
        gate_grad, up_grad, down_grad, stream_rms[0], branch_rms[0],
    )


def solution(mesh):
    rows, line = P("dev", None), P("dev")
    return jax.shard_map(
        shards,
        mesh=mesh,
        in_specs=(rows, line, rows, rows, rows, rows, line, rows, rows, rows, P(), line, rows),
        out_specs=(rows, rows, line, rows, rows, rows, rows, line, rows, rows, rows, line, line),
        check_vma=False,
    )
```

```python
import functools

import jax
import jax.numpy as jnp
import numpy as np
from jax import lax
from jax.experimental import pallas as pl
from jax.experimental.pallas import tpu as pltpu
from jax.sharding import PartitionSpec as P

HEADS = 16
KV_HEADS = 8
HEAD_DIM = 96
BLOCK = 128
DEPTH = 10
D = 1536
FF = 4096
MEMBERS = 8
LANES = 128

EPSILON = 1e-05
ROPE_BASE = 100000.0
NEGATIVE = -1e30
SCALE = HEAD_DIM ** (-0.5)
MESH = pl.DeviceIdType.MESH
BF16 = jnp.bfloat16
F32 = jnp.float32
VMEM_BYTES = 56 * 2**20


def spot():
    me = lax.axis_index("dev")
    return me // 32, (me // 8) % 4, (me // 2) % 4, me % 2


def device_of(x, y, z, c):
    return ((x % 4) * 4 + (y % 4)) * 8 + (z % 4) * 2 + c


def announce(peers):
    barrier = pltpu.get_barrier_semaphore()
    for peer in peers:
        pl.semaphore_signal(barrier, inc=1, device_id=(peer,), device_id_type=MESH)


def await_peers(peers):
    pl.semaphore_wait(pltpu.get_barrier_semaphore(), len(peers))


def axis_peers(x, y, z, c, far):
    steps = (1, 2, 3) if far else (1, 3)
    return [device_of(x + k, y, z, c) for k in steps] + [device_of(x, y + k, z, c) for k in steps]


def group_peer(x, y, z, c, k):
    member = (z * 2 + c + k) % MEMBERS
    return (x * 4 + y) * MEMBERS + member


class Wire:
    def __init__(self, send_sems, recv_sems):
        self.send_sems = send_sems
        self.recv_sems = recv_sems
        self.used = 0
        self.open = []

    def reserve(self, count):
        self.used += count
        return self.used - count

    def make(self, slot, source, target, peer):
        return pltpu.make_async_remote_copy(
            src_ref=source,
            dst_ref=target,
            send_sem=self.send_sems.at[slot],
            recv_sem=self.recv_sems.at[slot],
            device_id=(peer,),
            device_id_type=MESH,
        )

    def send(self, source, target, peer):
        copy = self.make(self.reserve(1), source, target, peer)
        copy.start()
        self.open.append(copy)
        return copy

    def close(self):
        for copy in self.open:
            copy.wait_send()
        self.open = []


class Ring:
    def __init__(self, wire, own, part, place, up, down):
        self.wire, self.own, self.part = wire, own, part
        self.place, self.up, self.down = place, up, down

    def begin(self):
        send, part, place = self.wire.send, self.part, self.place
        self.low_up = send(self.own(0), part(place, 0), self.up)
        self.high_down = send(self.own(1), part(place, 1), self.down)
        self.high_up = send(self.own(1), part(place, 1), self.up)
        self.low_down = send(self.own(0), part(place, 0), self.down)

    def relay(self):
        before, after = (self.place + 3) % 4, (self.place + 1) % 4
        self.low_up.wait_recv()
        self.far_up = self.wire.send(self.part(before, 0), self.part(before, 0), self.up)
        self.high_down.wait_recv()
        self.far_down = self.wire.send(self.part(after, 1), self.part(after, 1), self.down)

    def near(self):
        self.high_up.wait_recv()
        self.low_down.wait_recv()

    def far(self):
        self.far_up.wait_recv()
        self.far_down.wait_recv()


class PlaneGather:
    def __init__(self, wire, own, out, cut, xyzc):
        self.wire, self.own, self.out, self.cut = wire, own, out, cut
        x, y, z, c = xyzc
        self.x, self.y = x, y
        self.x_up, self.x_down = device_of(x + 1, y, z, c), device_of(x + 3, y, z, c)
        self.y_up, self.y_down = device_of(x, y + 1, z, c), device_of(x, y + 3, z, c)

    def pair(self, one_own, one_part, two_own, two_part, one_on_x):
        on_x = (self.x, self.x_up, self.x_down)
        on_y = (self.y, self.y_up, self.y_down)
        cut = self.cut.quarter
        self.one = Ring(
            self.wire,
            lambda side: one_own(cut(0, side)),
            lambda place, side: one_part(place, cut(0, side)),
            *(on_x if one_on_x else on_y),
        )
        self.two = Ring(
            self.wire,
            lambda side: two_own(cut(1, side)),
            lambda place, side: two_part(place, cut(1, side)),
            *(on_y if one_on_x else on_x),
        )
        self.one.begin()
        self.two.begin()

    def first(self):
        own, out, x, y = self.own, self.out, self.x, self.y
        self.pair(
            lambda q: own.at[q],
            lambda place, q: out.at[(place, y) + q],
            lambda q: own.at[q],
            lambda place, q: out.at[(x, place) + q],
            True,
        )

    def relay(self):
        self.one.relay()
        self.two.relay()

    def near(self):
        self.one.near()
        self.two.near()

    def far(self):
        self.one.far()
        self.two.far()

    def settle(self):
        self.near()
        self.far()

    def second(self):
        out, x, y = self.out, self.x, self.y
        every = slice(None)
        self.pair(
            lambda q: out.at[(every, y) + q],
            lambda place, q: out.at[(every, place) + q],
            lambda q: out.at[(x, every) + q],
            lambda place, q: out.at[(place, every) + q],
            False,
        )


class Rows:
    def __init__(self, rows, cols, start=0):
        self.rows, self.cols, self.start = rows // 2, cols // 2, start

    def half(self, half):
        return (pl.ds(half * self.rows, self.rows),)

    def side(self, side):
        return (slice(None), pl.ds(side * self.cols, self.cols))

    def quarter(self, half, side):
        first = self.start + side * self.cols
        if not isinstance(first, int):
            first = pl.multiple_of(first, LANES)
        return self.half(half) + (pl.ds(first, self.cols),)

    def shapes(self):
        return (self.rows, 2 * self.cols), (self.rows, self.cols)


class Units:
    def half(self, half):
        return (pl.ds(half * 6, 6),)

    def side(self, side):
        return (pl.ds(side * 3, 3),)

    def quarter(self, half, side):
        return (pl.ds(half * 6 + side * 3, 3),)

    def shapes(self):
        return (6, BLOCK, LANES), (3, BLOCK, LANES)


class GroupGather:
    def __init__(self, wire, own, out, xyzc):
        self.wire, self.own, self.out = wire, own, out
        x, y, z, c = xyzc
        self.z, self.c = z, c
        self.sibling = device_of(x, y, z, 1 - c)
        half = out.shape[2] // 2
        self.ring = Ring(
            wire,
            lambda side: own.at[pl.ds(side * half, half)],
            lambda place, side: out.at[place, c, pl.ds(side * half, half)],
            z, device_of(x, y, z + 1, c), device_of(x, y, z + 3, c),
        )
        self.crossed = []

    def begin(self):
        self.ring.begin()
        self.crossed.append(self.wire.send(self.own, self.out.at[self.z, self.c], self.sibling))

    def cross(self, k):
        piece = self.out.at[(self.z + k) % 4, self.c]
        self.crossed.append(self.wire.send(piece, piece, self.sibling))

    def relay(self):
        self.ring.relay()

    def near(self):
        self.ring.near()
        self.cross(1)
        self.cross(3)

    def far(self):
        self.ring.far()
        self.cross(2)

    def finish(self, after=0):
        for copy in self.crossed[after:]:
            copy.wait_recv()


class PlaneScatter:
    def __init__(self, wire, terms, cut, scratch, xyzc):
        self.wire, self.terms, self.cut = wire, terms, cut
        *room, self.near_in, self.far_in, self.passed, self.summed, self.second_in = scratch
        self.room = room
        self.x, self.y, self.z, self.c = xyzc

    def peer(self, along_x, k):
        if along_x:
            return device_of(self.x + k, self.y, self.z, self.c)
        return device_of(self.x, self.y + k, self.z, self.c)

    def place(self, half, k):
        return ((self.x, self.y)[half] + k) % 4

    def lead(self, half, k, line=slice(None)):
        place = self.place(half, k)
        return (place, line) if half == 0 else (line, place)

    def part(self, half, k, side):
        return self.terms.at[self.lead(half, k) + self.cut.quarter(half, side)]

    def own(self, half, line):
        if self.room:
            return self.room[0][half, line]
        return self.terms[self.lead(half, 0, line) + self.cut.half(half)]

    def edge(self, half, way, line):
        if self.room:
            return self.room[1][half, way, line]
        return self.terms[self.lead(half, (1, 3)[way], line) + self.cut.quarter(half, way)]

    def first(self):
        send = self.wire.send
        self.far, self.plain, self.locals = [], [], []
        if self.room:
            sems = self.room[2]
            for half in range(2):
                pairs = [(self.terms.at[self.lead(half, 0) + self.cut.half(half)], self.room[0].at[half])]
                pairs += [(self.part(half, (1, 3)[way], way), self.room[1].at[half, way]) for way in range(2)]
                for slot, (source, target) in enumerate(pairs):
                    copy = pltpu.make_async_copy(source, target, sems.at[half, slot])
                    copy.start()
                    self.locals.append(copy)
        for half in range(2):
            for way in range(2):
                self.far.append(
                    send(self.part(half, 2, way), self.far_in.at[half, way], self.peer(half == 0, (1, 3)[way]))
                )
        for half in range(2):
            for way in range(2):
                k = (1, 3)[way]
                landing = self.near_in.at[(half, way, slice(None)) + self.cut.side(1 - way)]
                self.plain.append(send(self.part(half, k, 1 - way), landing, self.peer(half == 0, k)))

    def relay(self):
        for copy in self.locals:
            copy.wait()
        self.relayed = []
        for half in range(2):
            for way in range(2):
                self.far[half * 2 + way].wait_recv()

                def add(line, carry):
                    total = self.edge(half, way, line).astype(F32) + self.far_in[half, way, line].astype(F32)
                    self.passed[half, way, line] = total.astype(BF16)
                    return carry

                lax.fori_loop(0, 4, add, 0)
                landing = self.near_in.at[(half, way, slice(None)) + self.cut.side(way)]
                self.relayed.append(
                    self.wire.send(self.passed.at[half, way], landing, self.peer(half == 0, (1, 3)[way]))
                )

    def add_first(self):
        for copy in self.plain + self.relayed:
            copy.wait_recv()
        for half in range(2):

            def body(line, carry):
                total = self.own(half, line).astype(F32)
                for way in range(2):
                    total = total + self.near_in[half, way, line].astype(F32)
                self.summed[half, line] = total.astype(BF16)
                return carry

            lax.fori_loop(0, 4, body, 0)

    def second(self):
        self.copies = []
        for k in (2, 1, 3):
            for half in range(2):
                self.copies.append(
                    self.wire.send(
                        self.summed.at[half, self.place(1 - half, k)],
                        self.second_in.at[half, k - 1],
                        self.peer(half == 1, k),
                    )
                )

    def total(self, half):
        total = self.summed[half, self.place(1 - half, 0)].astype(F32)
        for k in range(3):
            total = total + self.second_in[half, k].astype(F32)
        return total

    def arrive(self):
        for copy in self.copies:
            copy.wait_recv()


def scatter_scratch(cut, room=False):
    half, part = cut.shapes()
    vmem = pltpu.VMEM
    held = [vmem((2, 4) + half, BF16), vmem((2, 2, 4) + part, BF16), pltpu.SemaphoreType.DMA((2, 3))]
    return (held if room else []) + [
        vmem((2, 2, 4) + half, BF16),
        vmem((2, 2, 4) + part, BF16),
        vmem((2, 2, 4) + part, BF16),
        vmem((2, 4) + half, BF16),
        vmem((2, 3) + half, BF16),
    ]


class GroupScatter:
    def __init__(self, wire, terms, mine, crossed_in, summed, ring_in, local_sem, xyzc):
        self.wire, self.terms = wire, terms
        self.mine, self.crossed_in, self.summed, self.ring_in = mine, crossed_in, summed, ring_in
        self.x, self.y, self.z, self.c = xyzc
        self.local_sem = local_sem

    def begin(self):
        self.local = pltpu.make_async_copy(self.terms.at[:, self.c], self.mine, self.local_sem)
        self.local.start()
        sibling = device_of(self.x, self.y, self.z, 1 - self.c)
        self.crossed = {}
        for k in (2, 1, 3, 0):
            place = (self.z + k) % 4
            self.crossed[k] = self.wire.send(
                self.terms.at[place, 1 - self.c], self.crossed_in.at[place], sibling
            )

    def turn(self):
        self.local.wait()
        self.copies = []
        for k in (2, 1, 3):
            place = (self.z + k) % 4
            self.crossed[k].wait_recv()

            def body(tile, carry):
                total = self.mine[place, tile].astype(F32) + self.crossed_in[place, tile].astype(F32)
                self.summed[place, tile] = total.astype(BF16)
                return carry

            lax.fori_loop(0, 12, body, 0)
            self.copies.append(
                self.wire.send(
                    self.summed.at[place],
                    self.ring_in.at[k - 1],
                    device_of(self.x, self.y, self.z + k, self.c),
                )
            )

    def finish(self, out):
        self.crossed[0].wait_recv()
        for copy in self.copies:
            copy.wait_recv()
        for tile in range(12):
            total = self.mine[self.z, tile].astype(F32) + self.crossed_in[self.z, tile].astype(F32)
            for k in range(3):
                total = total + self.ring_in[k, tile].astype(F32)
            out[:, tile * LANES : (tile + 1) * LANES] = total


class ChipScatter:
    def __init__(self, wire, terms, at, crossed_in, ring_in, xyzc):
        self.wire, self.terms, self.at = wire, terms, at
        self.crossed_in, self.ring_in = crossed_in, ring_in
        self.x, self.y, self.z, self.c = xyzc
        self.crossed_slot, self.ring_slot = wire.reserve(4), wire.reserve(3)
        self.all_tiles = pl.ds(0, 12)

    def place(self, step):
        return (self.z + step) % 4

    def crossed(self, step):
        place = self.place(step)
        return self.wire.make(
            self.crossed_slot + step,
            self.terms.at[place, self.at + 1 - self.c, self.all_tiles],
            self.crossed_in.at[place],
            device_of(self.x, self.y, self.z, 1 - self.c),
        )

    def ring(self, step):
        return self.wire.make(
            self.ring_slot + step - 1,
            self.terms.at[self.place(step), self.at + self.c, self.all_tiles],
            self.ring_in.at[step - 1],
            device_of(self.x, self.y, self.z + step, self.c),
        )

    def put(self, step, grads):
        place = self.place(step)
        for core in range(2):
            for tile in range(12):
                self.terms[place, self.at + core, tile] = grads[
                    core * BLOCK : (core + 1) * BLOCK, tile * LANES : (tile + 1) * LANES
                ]
        self.crossed(step).start()

    def turn(self, step):
        place, line = self.place(step), self.at + self.c
        self.crossed(step).wait_recv()

        def add(tile, carry):
            total = self.terms[place, line, tile].astype(F32) + self.crossed_in[place, tile].astype(F32)
            self.terms[place, line, tile] = total.astype(BF16)
            return carry

        lax.fori_loop(0, 12, add, 0)
        self.ring(step).start()

    def total(self):
        self.crossed(0).wait_recv()
        for step in range(1, 4):
            self.ring(step).wait_recv()
        tiles = []
        for tile in range(12):
            total = self.terms[self.z, self.at + self.c, tile].astype(F32)
            total = total + self.crossed_in[self.z, tile].astype(F32)
            for step in range(3):
                total = total + self.ring_in[step, tile].astype(F32)
            tiles.append(total)
        return jnp.concatenate(tiles, axis=1)

    def close(self):
        for step in range(4):
            self.crossed(step).wait_send()
        for step in range(1, 4):
            self.ring(step).wait_send()


class RingScatter(ChipScatter):
    def __init__(self, wire, terms, crossed_in, near_in, far_in, xyzc):
        super().__init__(wire, terms, 0, crossed_in, None, xyzc)
        self.near_in, self.far_in = near_in, far_in
        self.moved = []

    def sum_tiles(self, place, tiles, extra=None):
        def add(tile, carry):
            total = self.terms[place, self.c, tile].astype(F32)
            if extra is None:
                total = total + self.crossed_in[place, tile].astype(F32)
            else:
                total = total + self.far_in[extra, tile - extra * 6].astype(F32)
            self.terms[place, self.c, tile] = total.astype(BF16)
            return carry

        lax.fori_loop(*tiles, add, 0)

    def move(self, place, first, landing, k):
        source = self.terms.at[place, self.c, pl.ds(first, 6)]
        copy = self.wire.send(source, landing, device_of(self.x, self.y, self.z + k, self.c))
        self.moved.append(copy)
        return copy

    def turn(self, step):
        place = self.place(step)
        self.crossed(step).wait_recv()
        self.sum_tiles(place, (0, 12))
        if step == 2:
            self.far = [self.move(place, 6 * way, self.far_in.at[way], (1, 3)[way]) for way in range(2)]
        else:
            way = (1, 3).index(step)
            plain = 6 * (1 - way)
            self.move(place, plain, self.near_in.at[way, pl.ds(plain, 6)], step)

    def pass_on(self, step):
        way = (1, 3).index(step)
        place = self.place(step)
        self.far[way].wait_recv()
        self.sum_tiles(place, (6 * way, 6 * way + 6), way)
        self.move(place, 6 * way, self.near_in.at[way, pl.ds(6 * way, 6)], step)

    def total(self):
        self.crossed(0).wait_recv()
        for copy in self.moved[2:]:
            copy.wait_recv()
        tiles = []
        for tile in range(12):
            total = self.terms[self.z, self.c, tile].astype(F32) + self.crossed_in[self.z, tile].astype(F32)
            for way in range(2):
                total = total + self.near_in[way, tile].astype(F32)
            tiles.append(total)
        return jnp.concatenate(tiles, axis=1)

    def close(self):
        for step in range(4):
            self.crossed(step).wait_send()


def group_scatter_scratch():
    return [
        pltpu.VMEM((4, 12, BLOCK, LANES), BF16),
        pltpu.VMEM((4, 12, BLOCK, LANES), BF16),
        pltpu.VMEM((4, 12, BLOCK, LANES), BF16),
        pltpu.VMEM((3, 12, BLOCK, LANES), BF16),
        pltpu.SemaphoreType.DMA,
    ]


def chip_scatter_scratch():
    return [pltpu.VMEM((4, 12, BLOCK, LANES), BF16), pltpu.VMEM((3, 12, BLOCK, LANES), BF16)]


def wire_scratch(count):
    return [pltpu.SemaphoreType.DMA((count,)), pltpu.SemaphoreType.DMA((count,))]


ANY = pl.BlockSpec(memory_space=pl.ANY)
INVMEM = pl.BlockSpec(memory_space=pltpu.VMEM)


def communicate(kernel, out_shapes, in_specs, out_specs, scratch, ident, name, vmem=VMEM_BYTES):
    return pl.pallas_call(
        kernel,
        out_shape=out_shapes,
        in_specs=in_specs,
        out_specs=out_specs,
        scratch_shapes=scratch,
        compiler_params=pltpu.CompilerParams(
            collective_id=ident, has_side_effects=True, vmem_limit_bytes=vmem
        ),
        name=name,
    )


def key_unit(member):
    return member + jnp.where(member >= 6, 6, 0) + jnp.where(member >= 7, 1, 0)


def value_unit(member):
    return member + 6 + jnp.where(member >= 6, 1, 0) + jnp.where(member >= 7, 1, 0)


def gain_rows(pieces):
    return jnp.concatenate(join_heads(pieces), axis=1)


def head_window(tiles, head):
    tile, skip = divmod(head * HEAD_DIM, LANES)
    lane = lane_of(tiles[0].shape)
    window = pltpu.roll(tiles[tile], (LANES - skip) % LANES, 1)
    if skip + HEAD_DIM > LANES:
        window = jnp.where(lane < LANES - skip, window, pltpu.roll(tiles[tile + 1], LANES - skip, 1))
    return jnp.where(lane < HEAD_DIM, window, 0.0)


def join_heads(pieces):
    lane = lane_of(pieces[0].shape)
    tiles = []
    for tile in range(len(pieces) * 3 // 4):
        piece, skip = divmod(tile * LANES, HEAD_DIM)
        low = pltpu.roll(pieces[piece], (LANES - skip) % LANES, 1)
        high = pltpu.roll(pieces[piece + 1], HEAD_DIM - skip, 1)
        tiles.append(jnp.where(lane < HEAD_DIM - skip, low, high))
    return tiles


def mix_groups(parts):
    group = lane_of(parts[0][0].shape) // 32
    mixed = None
    for i, (tile, g) in enumerate(parts):
        turned = pltpu.roll(tile, (32 * (i - g)) % LANES, 1)
        mixed = turned if mixed is None else jnp.where(group == i, turned, mixed)
    return mixed


def lane_of(shape):
    return lax.broadcasted_iota(jnp.int32, shape, len(shape) - 1)


def pack_tile(unit, extra, place):
    return jnp.where(lane_of(unit.shape) < HEAD_DIM, unit, pltpu.roll(extra, (96 - 32 * place) % LANES, 1))


def unpack_extra(tiles):
    lane = lane_of(tiles[0].shape)
    extra = jnp.where(lane < 32, pltpu.roll(tiles[0], 32, 1), 0.0)
    extra = jnp.where(jnp.logical_and(lane >= 32, lane < 64), pltpu.roll(tiles[1], 64, 1), extra)
    return jnp.where(jnp.logical_and(lane >= 64, lane < 96), pltpu.roll(tiles[2], 96, 1), extra)


def swap_halves(rows):
    lane = lane_of(rows.shape)
    return jnp.where(lane < HEAD_DIM // 2, pltpu.roll(rows, LANES - 48, 1), pltpu.roll(rows, 48, 1))


def rope_table():
    half = HEAD_DIM // 2
    frequency = ROPE_BASE ** (-2.0 * np.arange(half, dtype=np.float64) / HEAD_DIM)
    frequency = frequency.astype(np.float32)
    places = np.arange(DEPTH * BLOCK, dtype=np.float32)
    angles = (places[:, None] * frequency[None, :]).astype(np.float64)
    table = np.zeros((DEPTH * BLOCK, LANES), np.float32)
    table[:, :half] = np.cos(angles)
    table[:, half:HEAD_DIM] = np.sin(angles)
    return jnp.asarray(table.reshape(DEPTH, BLOCK, LANES))


def turning(table):
    lane = lane_of(table.shape)
    cosine = jnp.where(lane < 48, table, pltpu.roll(table, 48, 1))
    sine = jnp.where(lane < 48, -pltpu.roll(table, LANES - 48, 1), jnp.where(lane < HEAD_DIM, table, 0.0))
    return cosine, sine


def count_ancestors(lineage, block):
    count = jnp.int32(0)
    for step in range(DEPTH):
        count = count + jnp.where(lineage[block, step] >= 0, 1, 0)
    return count


def write_lineage(parent, first, lineage):
    def one(block, carry):
        def hop(step, node):
            lineage[block, step] = node
            above = parent[jnp.maximum(node, 0)]
            return jnp.where(node >= 0, above, -1)

        lax.fori_loop(0, DEPTH, hop, first + block)
        return carry

    lax.fori_loop(0, MEMBERS, one, 0)


def attend_block(lineage, block, queries, alive, load, scores):
    limit = count_ancestors(lineage, block)
    t = lax.broadcasted_iota(jnp.int32, (2 * BLOCK, BLOCK), 0) % BLOCK
    u = lax.broadcasted_iota(jnp.int32, (2 * BLOCK, BLOCK), 1)
    own = jnp.logical_and(u <= t, jnp.logical_or(alive > 0.5, u == t))
    nodes = [jnp.maximum(lineage[block, step], 0) for step in range(DEPTH)]
    pairs = range(0, DEPTH, 2)
    highest = None
    for step in pairs:
        keys = jnp.concatenate([load(node, key_unit(lax.rem(node, 8))) for node in nodes[step : step + 2]], axis=0)
        part = lax.dot_general(queries, keys, (((1,), (1,)), ((), ())), preferred_element_type=F32) * SCALE
        near = part[:, :BLOCK]
        if step == 0:
            near = jnp.where(own, near, NEGATIVE)
        else:
            near = near + jnp.where(step < limit, 0.0, NEGATIVE)
        far = part[:, BLOCK:] + jnp.where(step + 1 < limit, 0.0, NEGATIVE)
        scores[step] = near
        scores[step + 1] = far
        both = jnp.maximum(near, far)
        highest = both if step == 0 else jnp.maximum(highest, both)
    largest = jnp.max(highest, axis=1, keepdims=True)
    totals = jnp.zeros((2 * BLOCK, BLOCK), F32)
    attended = jnp.zeros((2 * BLOCK, LANES), F32)
    for step in pairs:
        near, far = jnp.exp(scores[step] - largest), jnp.exp(scores[step + 1] - largest)
        totals = totals + near + far
        values = jnp.concatenate(
            [load(node, value_unit(lax.rem(node, 8))) for node in nodes[step : step + 2]], axis=0
        )
        terms = jnp.concatenate([near.astype(BF16), far.astype(BF16)], axis=1)
        attended = attended + jnp.dot(terms, values, preferred_element_type=F32)
    total = jnp.sum(totals, axis=1, keepdims=True)
    return (attended / total).astype(BF16), largest + jnp.log(total)


def start_kernel(
    parent, table, stream, w_query, w_key, w_value, w_gate, w_up, w_out, small_rows, live_row, cotangent, own_down,
    lineage, live, gains, query, stream_all, attn_all,
    kv_out, middle, rms_out, grad_middle, grads_in, down_terms, gate_grad, up_grad, down_grad, out_terms, gain_terms,
    attended_out, log_rows,
    packed, out_low, small, stage, packed_in, out_in, small_in, wide_tall, wide_own, out_own, gain_own, gains_all,
    w_attn, own_kv, kv, w_out_all, w_feed, w_down, mid_all, cot_all, crossed_in, ring_in,
    att_out, att_in, att_pad, grads_out, feed_dealt, feed_in, *scratch,
):
    feed_scratch, wide_scratch = scratch[:5], scratch[5:10]
    send_sems, recv_sems, local_sems = scratch[10:]
    xyzc = x, y, z, c = spot()
    j = z * 2 + c
    base = (x * 4 + y) * MEMBERS
    sibling = device_of(x, y, z, 1 - c)
    wire = Wire(send_sems, recv_sems)
    group = [group_peer(x, y, z, c, k) for k in range(1, MEMBERS)]
    across, down_first = (((1,), (1,)), ((), ())), (((0,), (0,)), ((), ()))
    locals_ = []

    peers = group + axis_peers(x, y, z, c, True)
    announce(peers)

    stage[...] = jnp.zeros((16, FF), F32)
    wide_tall[96:] = jnp.zeros((8, 1536), F32)

    def staged(weights):
        width = weights.shape[1]
        stage[:12, :width] = weights[...].astype(F32)
        return [stage[:, tile * LANES : (tile + 1) * LANES] for tile in range(width // LANES)]

    def put_packed(member, tile, value):
        packed[member, :, tile * LANES : (tile + 1) * LANES] = value.astype(BF16)

    tiles = staged(w_query)
    for head in range(HEADS):
        put_packed(head // 2, head % 2, head_window(tiles, head))
    for place, weights in ((2, w_key), (3, w_value)):
        tiles = staged(weights)
        for member in range(MEMBERS):
            put_packed(member, place, head_window(tiles, member))
    for place, weights in ((4, w_gate), (8, w_up)):
        tiles = staged(weights)
        for member in range(MEMBERS):
            for tile in range(4):
                parts = [(tiles[2 * (4 * tile + i) + member // 4], member % 4) for i in range(4)]
                put_packed(member, place + tile, mix_groups(parts))
    out_low[...] = jnp.concatenate(staged(w_out), axis=1).astype(BF16)
    rows = pltpu.roll(small_rows[...], 12 * j, 1)
    live_rows = jnp.broadcast_to(live_row[...].astype(F32), (8, LANES))
    rows = jnp.where(lax.broadcasted_iota(jnp.int32, (8, LANES), 0) == 2, live_rows, rows)
    small[...] = jnp.concatenate([rows, jnp.zeros((8, LANES), F32)], axis=0).astype(BF16)
    await_peers(peers)

    def keep(source, target):
        copy = pltpu.make_async_copy(source, target, local_sems.at[len(locals_)])
        copy.start()
        locals_.append(copy)
        return copy

    def to_members(source, target):
        return [wire.send(source((j + k) % MEMBERS), target.at[j], group[k - 1]) for k in range(1, MEMBERS)]

    def half_of(member):
        return pl.ds(pl.multiple_of((member % 2) * 768, 768), 768)

    own_half = half_of(c)
    packed_dealt = to_members(lambda member: packed.at[member], packed_in)
    small_dealt = to_members(lambda member: small, small_in)
    first_kept = (keep(packed.at[j], packed_in.at[j]), keep(small, small_in.at[j]))
    out_kept = keep(out_low.at[:, own_half], out_in.at[j])
    streams = GroupGather(wire, stream, mid_all, xyzc)
    streams.begin()
    stream_kept = keep(stream, mid_all.at[z, c])
    write_lineage(parent, base, lineage)
    for line in range(16):
        w_out_all[line // 4, line % 4, 96:] = jnp.zeros((32, D), BF16)

    for copy in packed_dealt + small_dealt:
        copy.wait_recv()
    out_dealt = to_members(lambda member: out_low.at[:, half_of(member)], out_in)
    for copy in first_kept:
        copy.wait()
    for member in range(MEMBERS):
        wide_tall[pl.ds(member * 12, 12)] = packed_in[member].astype(F32)[:12]
    wide_own[...] = wide_tall[:96].astype(BF16)
    gain = small_in[0].astype(F32)
    for member in range(MEMBERS):
        row = small_in[member].astype(F32)
        live[member] = row[2:3]
        if member:
            gain = gain + row
    gain_own[...] = gain.astype(BF16)
    own_attn, own_feed = wide_own.at[:, pl.ds(0, 512)], wide_own.at[:, pl.ds(512, 1024)]
    attn = PlaneGather(wire, own_attn, w_attn, Rows(96, 512), xyzc)
    attn.first()
    tiny = [wire.send(gain_own, gains_all.at[x, y], device_of(x + k, y, z, c)) for k in range(1, 4)]
    attn_kept = keep(own_attn, w_attn.at[x, y])
    gain_kept = keep(gain_own, gains_all.at[x, y])
    feed_kept = keep(own_feed, w_feed.at[x, y])
    down_kept = keep(own_down, w_down.at[x, y])

    attn.relay()
    streams.relay()
    gain_kept.wait()
    for copy in tiny:
        copy.wait_recv()
    line = gains_all.at[:, y]
    tiny = [wire.send(line, line, device_of(x, y + k, z, c)) for k in range(1, 4)]
    attn_kept.wait()
    attn.settle()
    attn.second()
    for copy in out_dealt:
        copy.wait_recv()
    out_kept.wait()
    for member in range(MEMBERS):
        wide_tall[pl.ds(member * 12, 12), :768] = out_in[member].astype(F32)[:12]
    out_own[...] = wide_tall[:96, :768].astype(BF16)
    out_kept = keep(out_own, w_out_all.at[x, y, pl.ds(0, 96), own_half])
    out_kept.wait()
    outs = PlaneGather(wire, w_out_all.at[x, y], w_out_all, Rows(96, 768, c * 768), xyzc)
    outs.first()
    streams.near()
    streams.far()
    attn.relay()
    outs.relay()
    for copy in tiny:
        copy.wait_recv()
    pieces = [gains_all[piece // 4, piece % 4].astype(F32)[:8] for piece in range(16)]
    gains[...] = gain_rows(pieces)
    attn.settle()
    stream_kept.wait()
    streams.finish()
    attn_copied = keep(w_attn, attn_all)
    stream_copied = keep(mid_all, stream_all)

    def project(step, carry):
        wide = mid_all[step].reshape(2 * BLOCK, D).astype(F32)
        rms = jnp.sqrt(jnp.mean(wide * wide, axis=1, keepdims=True) + EPSILON)
        rows = (wide * (1.0 / rms) * gains[0:1]).astype(BF16)
        raw = jnp.dot(rows, w_attn[...].reshape(D, 512), preferred_element_type=F32)
        for part in range(2):
            block = step * 2 + part
            depth = count_ancestors(lineage, block) - 1
            cos, sin = turning(table[depth])

            def turn(head):
                v = raw[part * BLOCK : (part + 1) * BLOCK, head * LANES : (head + 1) * LANES]
                return (v * cos + swap_halves(v) * sin).astype(BF16)

            query[block, :BLOCK] = turn(0)
            query[block, BLOCK:] = turn(1)
            kv[x, y, key_unit(block)] = turn(2)
            kv[x, y, value_unit(block)] = raw[part * BLOCK : (part + 1) * BLOCK, 3 * LANES :].astype(BF16)
        return carry

    lax.fori_loop(0, 2, project, 0)
    outs.settle()
    outs.second()
    lax.fori_loop(2, 4, project, 0)
    for tile in range(12):
        extra = kv[x, y, 12 + tile // 3].astype(F32)
        own_kv[tile] = pack_tile(kv[x, y, tile].astype(F32), extra, tile % 3).astype(BF16)

    pairs = PlaneGather(wire, own_kv, kv, Units(), xyzc)
    pairs.first()
    outs.relay()
    kept = keep(own_kv, kv.at[x, y, pl.ds(0, 12)])
    cotangents = GroupGather(wire, cotangent, cot_all, xyzc)
    cotangents.begin()
    cot_kept = keep(cotangent, cot_all.at[z, c])
    pairs.relay()
    kept.wait()
    outs.settle()
    swap_part = w_out_all.at[:, :, pl.ds(0, 96), own_half]
    swapped = wire.send(swap_part, swap_part, sibling)
    pairs.settle()
    pairs.second()

    def unpack(half, k):
        def one(other, carry):
            piece = (other, (y + k) % 4) if half == 0 else ((x + k) % 4, other)
            for extra in (2 * half, 2 * half + 1):
                tiles = [kv[piece + (extra * 3 + part,)].astype(F32) for part in range(3)]
                kv[piece + (12 + extra,)] = unpack_extra(tiles).astype(BF16)
            return carry

        lax.fori_loop(0, 4, one, 0)

    unpack(0, 0)
    unpack(1, 0)
    cotangents.relay()
    cotangents.near()
    cotangents.far()
    pairs.relay()
    early, wire.open = wire.open, []
    feed = PlaneGather(wire, own_feed, w_feed, Rows(96, 1024), xyzc)
    down = PlaneGather(wire, own_down, w_down, Rows(32, D), xyzc)
    feed.first()
    down.first()
    pairs.near()
    for k in (1, 3):
        unpack(0, k)
        unpack(1, k)
    pairs.far()
    unpack(0, 2)
    unpack(1, 2)
    for copy in early:
        copy.wait_send()
    stream_copied.wait()
    attn_copied.wait()

    kv_copied = keep(kv, kv_out)

    att_slot = wire.reserve(MEMBERS - 1)

    def load(node, unit):
        return kv[lax.div(node, 32), lax.rem(lax.div(node, 8), 4), unit]

    def att_copy(k):
        block = (j + 1 + k) % MEMBERS
        return wire.make(att_slot + k, att_out.at[block], att_in.at[j], base + block)

    def attend_one(k, scores):
        block = (j + 1 + k) % MEMBERS
        attended, logs = attend_block(lineage, block, query[block], live[block], load, scores)
        log_rows[block] = jnp.transpose(jnp.broadcast_to(logs, (2 * BLOCK, LANES)))[:8]
        att_out[block, :, :LANES] = attended[:BLOCK]
        att_out[block, :, LANES:] = attended[BLOCK:]

    def attend_pair(pair):
        def both(one, two):
            attend_one(2 * pair, one)
            attend_one(2 * pair + 1, two)

        room = pltpu.VMEM((DEPTH, 2 * BLOCK, LANES), F32)
        pl.run_scoped(both, room, room)

        def give(k, carry):
            att_copy(k).start()
            return carry

        lax.fori_loop(2 * pair, min(2 * pair + 2, MEMBERS - 1), give, 0)

    attend_pair(0)
    feed.relay()
    down.relay()
    attend_pair(1)
    feed_kept.wait()
    down_kept.wait()
    feed.settle()
    feed.second()
    down.settle()
    down.second()
    attend_pair(2)
    attend_pair(3)
    feed.relay()
    down.relay()
    att_in[j] = att_out[j]
    att_copied = keep(att_out, attended_out)
    att_recv = [att_copy(k) for k in range(MEMBERS - 1)]

    for copy in att_recv:
        copy.wait_recv()
    for member in range(MEMBERS):
        att_pad[:, member * 256 : (member + 1) * 256] = att_in[member]
    swapped.wait_recv()

    def project_out(step, carry):
        cols = pl.ds(pl.multiple_of(step * 512, 512), 512)
        weights = w_out_all[:, :, :, cols].reshape(16 * LANES, 512)
        branch = jnp.dot(att_pad[...], weights, preferred_element_type=F32)
        middle[:, cols] = stream[:, cols].astype(F32) + branch
        return carry

    lax.fori_loop(0, 3, project_out, 0)
    rms = jnp.sqrt(jnp.mean(middle[...] * middle[...], axis=1, keepdims=True) + EPSILON)
    rms_out[...] = jnp.transpose(jnp.broadcast_to(rms, (BLOCK, LANES)))[:1]
    mid_all[z, c] = (middle[...] / rms * gains[1:2]).astype(BF16)
    mids = GroupGather(wire, mid_all.at[z, c], mid_all, xyzc)
    mids.begin()
    mids.relay()
    feed.settle()
    down.settle()
    kv_copied.wait()
    cot_kept.wait()
    cotangents.finish()
    for k in range(MEMBERS - 1):
        att_copy(k).wait_send()

    grad_rows = ChipScatter(wire, kv, 2, crossed_in, ring_in, xyzc)

    def rest(acts, grad_feed, feed_terms, wide_terms):
        feed_back_half(
            xyzc, wire, group, keep, mids, grad_rows, mid_all, cot_all, w_feed, w_down, w_out_all, kv, middle, gains,
            att_pad, att_copied, grads_out, feed_dealt, feed_in, wide_tall, feed_scratch, wide_scratch,
            acts, grad_feed, feed_terms, wide_terms,
            grad_middle, grads_in, down_terms, gate_grad, up_grad, down_grad, out_terms, gain_terms,
        )

    pl.run_scoped(
        rest,
        pltpu.VMEM((4, 2 * BLOCK, 512), BF16),
        pltpu.VMEM((4, 2 * BLOCK, 1024), BF16),
        pltpu.VMEM((4, 4, 96, 1024), BF16),
        pltpu.VMEM((4, 4, 32, D), BF16),
    )


def feed_back_half(
    xyzc, wire, group, keep, mids, grad_rows, mid_all, cot_all, w_feed, w_down, w_out_all, kv, middle, gains,
    att_pad, att_copied, grads_out, feed_dealt, feed_in, wide_tall, feed_scratch, wide_scratch,
    acts, grad_feed, feed_terms, wide_terms,
    grad_middle, grads_in, down_terms, gate_grad, up_grad, down_grad, out_terms, gain_terms,
):
    x, y, z, c = xyzc
    j = z * 2 + c
    across, down_first = (((1,), (1,)), ((), ())), (((0,), (0,)), ((), ()))

    def feed_forward(step):
        place = grad_rows.place(step)
        rows = mid_all[place].reshape(2 * BLOCK, D)
        weights = w_feed[...].reshape(D, 1024)
        both = jnp.dot(rows, weights, preferred_element_type=F32)
        gate, up = both[:, :512], both[:, 512:]
        sigmoid = 0.5 * jnp.tanh(0.5 * gate) + 0.5
        silu = gate * sigmoid
        acts[place] = (silu * up).astype(BF16)
        cot = cot_all[place].reshape(2 * BLOCK, D)
        grad_act = lax.dot_general(cot, w_down[...].reshape(512, D), across, preferred_element_type=F32)
        grad_gate = grad_act * up * sigmoid * (1.0 + gate * (1.0 - sigmoid))
        grad_feed[place, :, :512] = grad_gate.astype(BF16)
        grad_feed[place, :, 512:] = (grad_act * silu).astype(BF16)

    def feed_back(step):
        place = grad_rows.place(step)
        weights = w_feed[...].reshape(D, 1024)
        grads = lax.dot_general(grad_feed[place], weights, across, preferred_element_type=F32)
        grad_rows.put(step, grads.astype(BF16))

    mids.crossed[0].wait_recv()
    feed_forward(0)
    feed_back(0)
    mids.near()
    mids.crossed[1].wait_recv()
    feed_forward(1)
    feed_back(1)
    mids.far()
    mids.crossed[2].wait_recv()
    grad_rows.turn(1)
    feed_forward(3)
    feed_back(3)
    mids.crossed[3].wait_recv()
    grad_rows.turn(3)
    feed_forward(2)

    def down_weights(step, carry):
        cols = pl.ds(pl.multiple_of(step * 128, 128), 128)
        left = acts[:, :, cols].reshape(MEMBERS * BLOCK, 128)
        right = cot_all[...].reshape(MEMBERS * BLOCK, D)
        total = lax.dot_general(left, right, down_first, preferred_element_type=F32)
        wide_terms[step] = total.astype(BF16).reshape(4, 32, D)
        return carry

    lax.fori_loop(0, 4, down_weights, 0)
    wides = PlaneScatter(wire, wide_terms, Rows(32, D), wide_scratch, xyzc)
    wides.first()
    feed_back(2)

    def feed_weights(step, carry):
        cols = pl.ds(pl.multiple_of(step * 384, 384), 384)
        left = mid_all[:, :, :, cols].reshape(MEMBERS * BLOCK, 384)
        right = grad_feed[...].reshape(MEMBERS * BLOCK, 1024)
        total = lax.dot_general(left, right, down_first, preferred_element_type=F32)
        feed_terms[step] = total.astype(BF16).reshape(4, 96, 1024)
        return carry

    lax.fori_loop(0, 2, feed_weights, 0)
    grad_rows.turn(2)
    lax.fori_loop(2, 4, feed_weights, 0)
    feeds = PlaneScatter(wire, feed_terms, Rows(96, 1024), feed_scratch, xyzc)
    feeds.first()
    wides.relay()

    def down_rows(place, carry):
        outs = jnp.dot(acts[place], w_down[...].reshape(512, D), preferred_element_type=F32).astype(BF16)
        for core in range(2):
            for tile in range(12):
                kv[place, core, tile] = outs[
                    core * BLOCK : (core + 1) * BLOCK, tile * LANES : (tile + 1) * LANES
                ]
        return carry

    lax.fori_loop(0, 4, down_rows, 0)
    down_copied = keep(kv.at[:, pl.ds(0, 2), pl.ds(0, 12)], down_terms)
    grad_mid = grad_rows.total()
    rms = jnp.sqrt(jnp.mean(middle[...] * middle[...], axis=1, keepdims=True) + EPSILON)
    scaled = middle[...] / rms
    gain_terms[...] = jnp.sum(grad_mid * scaled, axis=0, keepdims=True)
    weighted = grad_mid * gains[1:2]
    back = (weighted - scaled * jnp.mean(weighted * scaled, axis=1, keepdims=True)) / rms
    grad_middle[...] = cot_all[z, c].astype(F32) + back
    branch_grad = grad_middle[...].astype(BF16)

    def spread(step, carry):
        weights = w_out_all[step].reshape(4 * LANES, D)
        grads = lax.dot_general(branch_grad, weights, across, preferred_element_type=F32).astype(BF16)
        for part in range(2):
            grads_out[step * 2 + part] = grads[:, part * 256 : (part + 1) * 256]
        return carry

    lax.fori_loop(0, 4, spread, 0)
    kept = keep(grads_out.at[j], grads_in.at[j])
    dealt = [
        wire.send(grads_out.at[(j + k) % MEMBERS], grads_in.at[j], group[k - 1]) for k in (4, 5, 3, 2, 6, 7, 1)
    ]
    feeds.relay()

    def out_weights(step, carry):
        cols = pl.ds(pl.multiple_of(step * 512, 512), 512)
        total = lax.dot_general(att_pad[:, cols], branch_grad, down_first, preferred_element_type=F32)
        w_out_all[step] = total.astype(BF16).reshape(4, LANES, D)
        return carry

    lax.fori_loop(0, 4, out_weights, 0)
    out_copied = keep(w_out_all.at[:, :, pl.ds(0, 96)], out_terms)

    wides.add_first()
    wides.second()
    feeds.add_first()
    feeds.second()
    feeds.arrive()
    for half in range(2):
        wide_tall[pl.ds(half * 48, 48), :1024] = feeds.total(half)
    split_rows(wide_tall, feed_dealt)
    feed_in[j] = feed_dealt[j]
    feed_dealt_copies = [
        wire.send(feed_dealt.at[(j + k) % MEMBERS], feed_in.at[j], group[k - 1]) for k in range(1, MEMBERS)
    ]
    wides.arrive()
    for half in range(2):
        down_grad[pl.ds(half * 16, 16)] = wides.total(half)
    for copy in feed_dealt_copies:
        copy.wait_recv()
    for grad, first in ((gate_grad, 0), (up_grad, 4)):
        for tile in range(32):
            line = tile // 2
            cols = slice((first + line // 4) * LANES, (first + line // 4 + 1) * LANES)
            parts = [(feed_in[4 * (tile % 2) + i, :, cols].astype(F32), line % 4) for i in range(4)]
            grad[:, tile * LANES : (tile + 1) * LANES] = mix_groups(parts)[:12]
    for copy in dealt:
        copy.wait_recv()
    for copy in (kept, down_copied, out_copied, att_copied):
        copy.wait()
    wire.close()
    grad_rows.close()


def start(
    parent, table, stream, w_query, w_key, w_value, w_gate, w_up, w_out, small_rows, live_row, cotangent, own_down
):
    shape, vmem = jax.ShapeDtypeStruct, pltpu.VMEM
    smem = pl.BlockSpec(memory_space=pltpu.SMEM)
    return communicate(
        start_kernel,
        (
            shape((MEMBERS, DEPTH), jnp.int32),
            shape((MEMBERS, 1, LANES), F32),
            shape((8, D), F32),
            shape((MEMBERS, 2 * BLOCK, LANES), BF16),
            shape((4, 2, BLOCK, D), BF16),
            shape((4, 4, 96, 512), BF16),
            shape((4, 4, 16, BLOCK, LANES), BF16),
            shape((BLOCK, D), F32),
            shape((1, LANES), F32),
            shape((BLOCK, D), F32),
            shape((MEMBERS, BLOCK, 2 * LANES), BF16),
            shape((4, 2, 12, BLOCK, LANES), BF16),
            shape((12, FF), F32),
            shape((12, FF), F32),
            shape((32, D), F32),
            shape((4, 4, 96, D), BF16),
            shape((1, D), F32),
            shape((MEMBERS, BLOCK, 2 * LANES), BF16),
            shape((MEMBERS, 8, 2 * BLOCK), F32),
        ),
        [smem] + [INVMEM] * 10 + [ANY] * 2,
        (smem,) + (INVMEM,) * 3 + (ANY,) * 3 + (INVMEM,) * 3 + (ANY,) * 2 + (INVMEM,) * 3 + (ANY, INVMEM, ANY, INVMEM),
        [
            vmem((MEMBERS, 16, 1536), BF16),
            vmem((16, 1536), BF16),
            vmem((16, LANES), BF16),
            vmem((16, FF), F32),
            vmem((MEMBERS, 16, 1536), BF16),
            vmem((MEMBERS, 16, 768), BF16),
            vmem((MEMBERS, 16, LANES), BF16),
            vmem((104, 1536), F32),
            vmem((96, 1536), BF16),
            vmem((96, 768), BF16),
            vmem((16, LANES), BF16),
            vmem((4, 4, 16, LANES), BF16),
            vmem((4, 4, 96, 512), BF16),
            vmem((12, BLOCK, LANES), BF16),
            vmem((4, 4, 16, BLOCK, LANES), BF16),
            vmem((4, 4, LANES, D), BF16),
            vmem((4, 4, 96, 1024), BF16),
            vmem((4, 4, 32, D), BF16),
            vmem((4, 2, BLOCK, D), BF16),
            vmem((4, 2, BLOCK, D), BF16),
        ]
        + chip_scatter_scratch()
        + [
            vmem((MEMBERS, BLOCK, 2 * LANES), BF16),
            vmem((MEMBERS, BLOCK, 2 * LANES), BF16),
            vmem((BLOCK, 2048), BF16),
            vmem((MEMBERS, BLOCK, 2 * LANES), BF16),
            vmem((MEMBERS, 16, 1024), BF16),
            vmem((MEMBERS, 16, 1024), BF16),
        ]
        + scatter_scratch(Rows(96, 1024))
        + scatter_scratch(Rows(32, D))
        + wire_scratch(242)
        + [pltpu.SemaphoreType.DMA((20,))],
        2,
        "start",
        63 * 2**20,
    )(parent, table, stream, w_query, w_key, w_value, w_gate, w_up, w_out, small_rows, live_row, cotangent, own_down)


def split_rows(tall, dealt):
    width = dealt.shape[2]
    for member in range(MEMBERS):
        dealt[member] = tall[pl.ds(member * 12, 16), :width].astype(BF16)


def attend_back_kernel(
    lineage, query, live, grad, attended, log_rows, kv_in, grad_query, grad_kv, kv, sums, packed, sems
):
    loaded = pltpu.make_async_copy(kv_in, kv, sems.at[16])
    loaded.start()

    def clear(step, carry):
        sums[step] = jnp.zeros((BLOCK, LANES), F32)
        return carry

    lax.fori_loop(0, 256, clear, 0)
    loaded.wait()

    def two(pair, carry):
        for block in (2 * pair, 2 * pair + 1):
            attend_back_block(block, lineage, query, live, grad, attended, log_rows, grad_query, kv, sums)
        return carry

    lax.fori_loop(0, MEMBERS // 2, two, 0)

    def stored(line):
        rows = pl.ds(line * 12, 12)
        return pltpu.make_async_copy(packed.at[rows], grad_kv.at[rows], sems.at[line])

    def store(line, carry):
        for tile in range(12):
            total = pack_tile(sums[line * 16 + tile], sums[line * 16 + 12 + tile // 3], tile % 3)
            packed[line * 12 + tile] = total.astype(BF16)
        stored(line).start()
        return carry

    lax.fori_loop(0, 16, store, 0)
    for line in range(16):
        stored(line).wait()


def attend_back_block(block, lineage, query, live, grad, attended, log_rows, grad_query, kv, sums):
    across, down_first = (((1,), (1,)), ((), ())), (((0,), (0,)), ((), ()))
    queries = query[block]
    grads = jnp.concatenate([grad[block, :, :LANES], grad[block, :, LANES:]], axis=0)
    outs = jnp.concatenate([attended[block, :, :LANES], attended[block, :, LANES:]], axis=0)
    product = grads.astype(F32) * outs.astype(F32)
    high = product.astype(BF16)
    low = (product - high.astype(F32)).astype(BF16)
    ones = jnp.ones((8, LANES), BF16)
    inner = lax.dot_general(ones, high, across, preferred_element_type=F32)
    inner = (inner + lax.dot_general(ones, low, across, preferred_element_type=F32))[:1]
    logs = log_rows[block, :1]
    limit = count_ancestors(lineage, block)
    u = lax.broadcasted_iota(jnp.int32, (BLOCK, 2 * BLOCK), 0)
    t = lax.broadcasted_iota(jnp.int32, (BLOCK, 2 * BLOCK), 1) % BLOCK
    alive = jnp.transpose(jnp.broadcast_to(live[block], (BLOCK, BLOCK)))
    alive = jnp.concatenate([alive, alive], axis=1)
    own = jnp.logical_and(u <= t, jnp.logical_or(alive > 0.5, u == t))
    turned = jnp.zeros((LANES, 2 * BLOCK), F32)
    for step in range(0, DEPTH, 2):
        units = []
        for node in (lineage[block, step], lineage[block, step + 1]):
            safe = jnp.maximum(node, 0)
            at, member = lax.div(safe, 8) * 16, lax.rem(safe, 8)
            units.append((node, at + key_unit(member), at + value_unit(member)))
        keys = jnp.concatenate([kv[unit[1]] for unit in units], axis=0)
        values = jnp.concatenate([kv[unit[2]] for unit in units], axis=0)
        scores = lax.dot_general(keys, queries, across, preferred_element_type=F32) * SCALE
        near, far = scores[:BLOCK], scores[BLOCK:]
        if step == 0:
            near = jnp.where(own, jnp.exp(jnp.where(own, near - logs, NEGATIVE)), 0.0)
        else:
            near = jnp.exp(near + (jnp.where(step < limit, 0.0, NEGATIVE) - logs))
        far = jnp.exp(far + (jnp.where(step + 1 < limit, 0.0, NEGATIVE) - logs))
        chances = jnp.concatenate([near, far], axis=0)
        grad_chances = lax.dot_general(values, grads, across, preferred_element_type=F32)
        grad_scores = (chances * (grad_chances - inner)).astype(BF16)
        grad_keys = jnp.dot(grad_scores, queries, preferred_element_type=F32) * SCALE
        grad_values = jnp.dot(chances.astype(BF16), grads, preferred_element_type=F32)
        for part, (node, at_key, at_value) in enumerate(units):
            rows = slice(part * BLOCK, (part + 1) * BLOCK)
            sums[jnp.where(node >= 0, at_key, 256)] += grad_keys[rows]
            sums[jnp.where(node >= 0, at_value, 256)] += grad_values[rows]
        turned = turned + lax.dot_general(keys, grad_scores, down_first, preferred_element_type=F32)
    grad_query[block] = jnp.transpose(turned) * SCALE


def attend_back(lineage, query, kv, live, grad, attended, log_rows):
    vmem = pltpu.VMEM
    return pl.pallas_call(
        attend_back_kernel,
        in_specs=[pl.BlockSpec(memory_space=pltpu.SMEM)] + [INVMEM] * 5 + [ANY],
        out_specs=(INVMEM, ANY),
        out_shape=(
            jax.ShapeDtypeStruct((MEMBERS, 2 * BLOCK, LANES), F32),
            jax.ShapeDtypeStruct((192, BLOCK, LANES), BF16),
        ),
        scratch_shapes=[
            vmem((256, BLOCK, LANES), BF16),
            vmem((257, BLOCK, LANES), F32),
            vmem((192, BLOCK, LANES), BF16),
            pltpu.SemaphoreType.DMA((17,)),
        ],
        compiler_params=pltpu.CompilerParams(vmem_limit_bytes=VMEM_BYTES),
        name="attend_back",
    )(lineage, query, live, grad, attended, log_rows, kv)


def gain_tiles(rows):
    lane = lane_of((8, LANES))
    tiles = [rows[:, tile * LANES : (tile + 1) * LANES] for tile in range(12)]
    pieces = []
    for piece in range(16):
        tile, skip = divmod(piece * 96, LANES)
        low = pltpu.roll(tiles[tile], (LANES - skip) % LANES, 1)
        high = pltpu.roll(tiles[min(tile + 1, 11)], (LANES - skip) % LANES, 1)
        pieces.append(jnp.where(lane < LANES - skip, low, high))
    return pieces


def ending_kernel(
    lineage, grad_query, table, stream_all, w_attn, gain, gain_two, stream, middle, grad_middle,
    kv_terms, down_terms, out_terms,
    mixed_out, stream_grad, query_grad, key_grad, value_grad, out_grad, gain_one, gain_two_out, rms_out,
    attn_grad, out_in, normed, raw, units, grad_terms, crossed_in, near_in, far_in, query_terms, pair_terms, attn_tall, attn_dealt,
    out_tall, out_dealt, out_mine, out_crossed, gain_terms, gain_in, gain_line, gain_in_two, gain_in_three,
    *scratch,
):
    xyzc = x, y, z, c = spot()
    j = z * 2 + c
    down_scratch, kv_scratch, query_scratch, pair_scratch, out_scratch = (
        scratch[:5], scratch[5:13], scratch[13:18], scratch[18:23], scratch[23:28]
    )
    send_sems, recv_sems, local_sem = scratch[28:]
    wire = Wire(send_sems, recv_sems)
    group = [group_peer(x, y, z, c, k) for k in range(1, MEMBERS)]
    peers = group + axis_peers(x, y, z, c, True)
    announce(peers)
    await_peers(peers)
    sibling = device_of(x, y, z, 1 - c)
    pairs = PlaneScatter(wire, kv_terms, Units(), kv_scratch, xyzc)
    pairs.first()
    attn_tall[96:] = jnp.zeros((8, 512), F32)
    out_tall[96:] = jnp.zeros((8, 768), F32)

    def norm_rows(step, carry):
        rows = pl.ds(pl.multiple_of(step * BLOCK, BLOCK), BLOCK)
        wide = stream_all[rows].astype(F32)
        rms = jnp.sqrt(jnp.mean(wide * wide, axis=1, keepdims=True) + EPSILON)
        normed[rows] = (wide * (1.0 / rms) * gain[0:1]).astype(BF16)
        return carry

    lax.fori_loop(0, MEMBERS, norm_rows, 0)

    def turn(block, v):
        depth = count_ancestors(lineage, block) - 1
        cos, sin = turning(table[depth])
        return (v * cos - swap_halves(v) * sin).astype(BF16)

    def query_rows(block, carry):
        rows = pl.ds(pl.multiple_of(block * BLOCK, BLOCK), BLOCK)
        raw[rows, :128] = turn(block, grad_query[block, :BLOCK])
        raw[rows, 128:256] = turn(block, grad_query[block, BLOCK:])
        return carry

    lax.fori_loop(0, MEMBERS, query_rows, 0)
    pairs.relay()
    downs = GroupScatter(wire, down_terms, *down_scratch, xyzc)
    downs.begin()
    own_half = pl.ds(pl.multiple_of(c * 768, 768), 768)
    other_half = pl.ds(pl.multiple_of((1 - c) * 768, 768), 768)
    crossed = wire.send(out_terms.at[:, :, :, other_half], out_crossed, sibling)
    local = pltpu.make_async_copy(out_terms.at[:, :, :, own_half], out_mine, local_sem)
    local.start()

    def weights_back(terms, first):
        def some(step, carry):
            cols = pl.ds(pl.multiple_of(step * 384, 384), 384)
            total = lax.dot_general(
                normed[:, cols], raw[:, first : first + 256], (((0,), (0,)), ((), ())), preferred_element_type=F32
            )
            terms[step] = total.astype(BF16).reshape(4, 96, 256)
            return carry

        lax.fori_loop(0, 4, some, 0)

    weights_back(query_terms, 0)
    query_sums = PlaneScatter(wire, query_terms, Rows(96, 256), query_scratch, xyzc)
    pair_sums = PlaneScatter(wire, pair_terms, Rows(96, 256), pair_scratch, xyzc)
    local.wait()
    crossed.wait_recv()

    def add_halves(step, carry):
        a, b = step // 4, step % 4
        total = out_mine[a, b].astype(F32) + out_crossed[a, b].astype(F32)
        out_mine[a, b] = total.astype(BF16)
        return carry

    lax.fori_loop(0, 16, add_halves, 0)
    outs = PlaneScatter(wire, out_mine, Rows(96, 768), out_scratch, xyzc)
    downs.turn()
    pairs.add_first()
    pairs.second()
    downs.finish(stream_grad)
    mixed_out[...] = (middle[...] + stream_grad[...]).astype(BF16)
    pairs.arrive()
    outs.first()
    query_sums.first()
    for half in range(2):
        units[pl.ds(half * 6, 6)] = pairs.total(half)
    for extra in range(4):
        units[12 + extra] = unpack_extra([units[extra * 3 + k] for k in range(3)])

    def pair_rows(block, carry):
        rows = pl.ds(pl.multiple_of(block * BLOCK, BLOCK), BLOCK)
        raw[rows, 256:384] = turn(block, units[key_unit(block)])
        value = units[value_unit(block)]
        raw[rows, 384:] = jnp.where(lane_of((BLOCK, LANES)) < HEAD_DIM, value, 0.0).astype(BF16)
        return carry

    lax.fori_loop(0, MEMBERS, pair_rows, 0)

    grad_rows = RingScatter(wire, grad_terms, crossed_in, near_in, far_in, xyzc)
    gain_terms[...] = jnp.zeros((1, D), F32)

    def rows_back(step):
        rows = pl.ds(pl.multiple_of(grad_rows.place(step) * 256, 256), 256)
        grads = lax.dot_general(raw[rows], w_attn[...], (((1,), (1,)), ((), ())), preferred_element_type=F32)
        grad_rows.put(step, grads.astype(BF16))
        wide = stream_all[rows].astype(F32)
        rms = jnp.sqrt(jnp.mean(wide * wide, axis=1, keepdims=True) + EPSILON)
        gain_terms[...] += jnp.sum(grads * (wide * (1.0 / rms)), axis=0, keepdims=True)

    rows_back(2)
    rows_back(1)
    grad_rows.turn(2)
    rows_back(3)
    grad_rows.turn(1)
    rows_back(0)
    grad_rows.turn(3)
    outs.relay()
    query_sums.relay()
    grad_rows.pass_on(1)
    grad_rows.pass_on(3)
    rows = jnp.concatenate([gain_terms[...], gain_two[...], jnp.zeros((6, D), F32)], axis=0)
    for piece, part in enumerate(gain_tiles(rows)):
        gain_in[piece // 4, piece % 4] = part
    gains = [
        wire.send(gain_in.at[(x + k) % 4], gain_line.at[k], device_of(x + k, y, z, c)) for k in range(1, 4)
    ]

    weights_back(pair_terms, 256)
    pair_sums.first()
    for copy in gains:
        copy.wait_recv()
    gain_line[0] = gain_in[x] + gain_line[1] + gain_line[2] + gain_line[3]
    gains = [
        wire.send(gain_line.at[0, (y + k) % 4], gain_in_two.at[k], device_of(x, y + k, z, c)) for k in range(1, 4)
    ]
    outs.add_first()
    outs.second()
    query_sums.add_first()
    query_sums.second()
    pair_sums.relay()
    outs.arrive()
    for half in range(2):
        out_tall[pl.ds(half * 48, 48)] = outs.total(half)
    split_rows(out_tall, out_dealt)
    out_in[j] = out_dealt[j]
    dealt = [
        wire.send(out_dealt.at[(j + k) % MEMBERS], out_in.at[j], group[k - 1]) for k in range(1, MEMBERS)
    ]
    pair_sums.add_first()
    pair_sums.second()

    wide = stream[...].astype(F32)
    rms = jnp.sqrt(jnp.mean(wide * wide, axis=1, keepdims=True) + EPSILON)
    rms_out[...] = jnp.transpose(jnp.broadcast_to(rms, (BLOCK, LANES)))[:1]
    scaled = wide / rms
    weighted = grad_rows.total() * gain[0:1]
    back = (weighted - scaled * jnp.mean(weighted * scaled, axis=1, keepdims=True)) / rms
    stream_grad[...] = grad_middle[...] + back

    for copy in gains:
        copy.wait_recv()
    gain_in_three[j] = gain_line[0, y] + gain_in_two[1] + gain_in_two[2] + gain_in_two[3]
    gains = [
        wire.send(gain_in_three.at[j], gain_in_three.at[j], group[k - 1]) for k in range(1, MEMBERS)
    ]
    query_sums.arrive()
    pair_sums.arrive()
    for half in range(2):
        attn_tall[pl.ds(half * 48, 48), :256] = query_sums.total(half)
        attn_tall[pl.ds(half * 48, 48), 256:] = pair_sums.total(half)
    split_rows(attn_tall, attn_dealt)
    attn_grad[j] = attn_dealt[j]
    dealt += [
        wire.send(attn_dealt.at[(j + k) % MEMBERS], attn_grad.at[j], group[k - 1]) for k in range(1, MEMBERS)
    ]
    for copy in gains:
        copy.wait_recv()
    total = gain_in_three[0]
    for member in range(1, MEMBERS):
        total = total + gain_in_three[member]
    own = pltpu.roll(total, (LANES - 12 * j) % LANES, 1)
    gain_one[...] = own[:1, :12]
    gain_two_out[...] = own[1:2, :12]
    for copy in dealt:
        copy.wait_recv()
    for core in range(2):
        total = out_in[core].astype(F32)
        for place in range(1, 4):
            total = total + out_in[place * 2 + core].astype(F32)
        out_grad[:, core * 768 : (core + 1) * 768] = total[:12]

    def tile_of(member, tile):
        return attn_grad[member, :, tile * LANES : (tile + 1) * LANES].astype(F32)

    for grad, pieces in (
        (query_grad, [tile_of(head // 2, head % 2) for head in range(HEADS)]),
        (key_grad, [tile_of(member, 2) for member in range(MEMBERS)]),
        (value_grad, [tile_of(member, 3) for member in range(MEMBERS)]),
    ):
        for tile, value in enumerate(join_heads(pieces)):
            grad[:, tile * LANES : (tile + 1) * LANES] = value[:12]
    wire.close()
    grad_rows.close()


def ending(
    lineage, grad_query, table, stream_all, w_attn, gain, gain_two, stream, middle, grad_middle,
    kv_terms, down_terms, out_terms,
):
    shape, vmem = jax.ShapeDtypeStruct, pltpu.VMEM
    smem = pl.BlockSpec(memory_space=pltpu.SMEM)
    return communicate(
        ending_kernel,
        (
            shape((BLOCK, D), BF16),
            shape((BLOCK, D), F32),
            shape((12, D), F32),
            shape((12, 768), F32),
            shape((12, 768), F32),
            shape((12, D), F32),
            shape((1, 12), F32),
            shape((1, 12), F32),
            shape((1, LANES), F32),
        ),
        [smem] + [INVMEM] * 9 + [ANY] * 3,
        (INVMEM,) * 9,
        [
            vmem((MEMBERS, 16, 512), BF16),
            vmem((MEMBERS, 16, 768), BF16),
            vmem((MEMBERS * BLOCK, D), BF16),
            vmem((MEMBERS * BLOCK, 512), BF16),
            vmem((16, BLOCK, LANES), F32),
            vmem((4, 2, 12, BLOCK, LANES), BF16),
        ]
        + [
            vmem((4, 12, BLOCK, LANES), BF16),
            vmem((2, 12, BLOCK, LANES), BF16),
            vmem((2, 6, BLOCK, LANES), BF16),
        ]
        + [
            vmem((4, 4, 96, 256), BF16),
            vmem((4, 4, 96, 256), BF16),
            vmem((104, 512), F32),
            vmem((MEMBERS, 16, 512), BF16),
            vmem((104, 768), F32),
            vmem((MEMBERS, 16, 768), BF16),
            vmem((4, 4, 96, 768), BF16),
            vmem((4, 4, 96, 768), BF16),
            vmem((1, D), F32),
            vmem((4, 4, 8, LANES), F32),
            vmem((4, 4, 8, LANES), F32),
            vmem((4, 8, LANES), F32),
            vmem((MEMBERS, 8, LANES), F32),
        ]
        + group_scatter_scratch()
        + scatter_scratch(Units(), room=True)
        + scatter_scratch(Rows(96, 256))
        + scatter_scratch(Rows(96, 256))
        + scatter_scratch(Rows(96, 768))
        + wire_scratch(120)
        + [pltpu.SemaphoreType.DMA],
        7,
        "ending",
        62 * 2**20,
    )(
        lineage, grad_query, table, stream_all, w_attn, gain, gain_two, stream, middle, grad_middle,
        kv_terms, down_terms, out_terms,
    )


def hand_over_kernel(*refs):
    count = len(refs) // 2
    for source, target in zip(refs[:count], refs[count:]):
        target[...] = source[...]


def hand_over(*arrays):
    return pl.pallas_call(
        hand_over_kernel,
        out_shape=tuple(jax.ShapeDtypeStruct(array.shape, array.dtype) for array in arrays),
        in_specs=[INVMEM] * len(arrays),
        out_specs=(INVMEM,) * len(arrays),
        compiler_params=pltpu.CompilerParams(vmem_limit_bytes=VMEM_BYTES),
        name="hand_over",
    )(*arrays)


def shards(
    stream, attn_gain, w_query, w_key, w_value, w_out, mlp_gain, w_gate, w_up, w_down, parent, live_mask, cotangent
):
    table = rope_table()
    small_rows = jnp.pad(jnp.stack([attn_gain, mlp_gain]).astype(F32), ((0, 6), (0, LANES - attn_gain.shape[0])))
    (
        lineage, live, gains, query, stream_all, w_attn, context, middle, branch_rms, grad_middle, grad_heads,
        down_terms, gate_grad, up_grad, down_grad, out_terms, gain_two_terms, attended, log_rows,
    ) = start(
        parent, table, stream, w_query, w_key, w_value, w_gate, w_up, w_out, small_rows,
        live_mask.reshape(1, BLOCK), cotangent, w_down,
    )
    grad_query, context_terms = attend_back(
        lineage, query, context.reshape(256, BLOCK, LANES), live, grad_heads, attended, log_rows
    )
    mixed_out, stream_grad, query_grad, key_grad, value_grad, out_grad, gain_one, gain_two, stream_rms = ending(
        lineage, grad_query, table, stream_all.reshape(MEMBERS * BLOCK, D), w_attn.reshape(D, 512), gains,
        gain_two_terms, stream, middle, grad_middle,
        context_terms.reshape(4, 4, 12, BLOCK, LANES), down_terms, out_terms,
    )
    (
        mixed_out, stream_grad, gain_one, query_grad, key_grad, value_grad, out_grad, gain_two,
        gate_grad, up_grad, down_grad, stream_rms, branch_rms,
    ) = hand_over(
        mixed_out, stream_grad, gain_one, query_grad, key_grad, value_grad, out_grad, gain_two,
        gate_grad, up_grad, down_grad, stream_rms, branch_rms,
    )
    return (
        mixed_out, stream_grad, gain_one[0], query_grad, key_grad, value_grad, out_grad, gain_two[0],
        gate_grad, up_grad, down_grad, stream_rms[0], branch_rms[0],
    )


def solution(mesh):
    rows, line = P("dev", None), P("dev")
    return jax.shard_map(
        shards,
        mesh=mesh,
        in_specs=(rows, line, rows, rows, rows, rows, line, rows, rows, rows, P(), line, rows),
        out_specs=(rows, rows, line, rows, rows, rows, rows, line, rows, rows, rows, line, line),
        check_vma=False,
    )
```

```python
import functools

import jax
import jax.numpy as jnp
import numpy as np
from jax import lax
from jax.experimental import pallas as pl
from jax.experimental.pallas import tpu as pltpu
from jax.sharding import PartitionSpec as P

HEADS = 16
KV_HEADS = 8
HEAD_DIM = 96
BLOCK = 128
DEPTH = 10
D = 1536
FF = 4096
MEMBERS = 8
LANES = 128

EPSILON = 1e-05
ROPE_BASE = 100000.0
NEGATIVE = -1e30
SCALE = HEAD_DIM ** (-0.5)
MESH = pl.DeviceIdType.MESH
BF16 = jnp.bfloat16
F32 = jnp.float32
VMEM_BYTES = 56 * 2**20


def spot():
    me = lax.axis_index("dev")
    return me // 32, (me // 8) % 4, (me // 2) % 4, me % 2


def device_of(x, y, z, c):
    return ((x % 4) * 4 + (y % 4)) * 8 + (z % 4) * 2 + c


def announce(peers):
    barrier = pltpu.get_barrier_semaphore()
    for peer in peers:
        pl.semaphore_signal(barrier, inc=1, device_id=(peer,), device_id_type=MESH)


def await_peers(peers):
    pl.semaphore_wait(pltpu.get_barrier_semaphore(), len(peers))


def axis_peers(x, y, z, c, far):
    steps = (1, 2, 3) if far else (1, 3)
    return [device_of(x + k, y, z, c) for k in steps] + [device_of(x, y + k, z, c) for k in steps]


def group_peer(x, y, z, c, k):
    member = (z * 2 + c + k) % MEMBERS
    return (x * 4 + y) * MEMBERS + member


class Wire:
    def __init__(self, send_sems, recv_sems):
        self.send_sems = send_sems
        self.recv_sems = recv_sems
        self.used = 0
        self.open = []

    def reserve(self, count):
        self.used += count
        return self.used - count

    def make(self, slot, source, target, peer):
        return pltpu.make_async_remote_copy(
            src_ref=source,
            dst_ref=target,
            send_sem=self.send_sems.at[slot],
            recv_sem=self.recv_sems.at[slot],
            device_id=(peer,),
            device_id_type=MESH,
        )

    def send(self, source, target, peer):
        copy = self.make(self.reserve(1), source, target, peer)
        copy.start()
        self.open.append(copy)
        return copy

    def close(self):
        for copy in self.open:
            copy.wait_send()
        self.open = []


class Ring:
    def __init__(self, wire, own, part, place, up, down):
        self.wire, self.own, self.part = wire, own, part
        self.place, self.up, self.down = place, up, down

    def begin(self):
        send, part, place = self.wire.send, self.part, self.place
        self.low_up = send(self.own(0), part(place, 0), self.up)
        self.high_down = send(self.own(1), part(place, 1), self.down)
        self.high_up = send(self.own(1), part(place, 1), self.up)
        self.low_down = send(self.own(0), part(place, 0), self.down)

    def relay(self):
        before, after = (self.place + 3) % 4, (self.place + 1) % 4
        self.low_up.wait_recv()
        self.far_up = self.wire.send(self.part(before, 0), self.part(before, 0), self.up)
        self.high_down.wait_recv()
        self.far_down = self.wire.send(self.part(after, 1), self.part(after, 1), self.down)

    def near(self):
        self.high_up.wait_recv()
        self.low_down.wait_recv()

    def far(self):
        self.far_up.wait_recv()
        self.far_down.wait_recv()


class PlaneGather:
    def __init__(self, wire, own, out, cut, xyzc):
        self.wire, self.own, self.out, self.cut = wire, own, out, cut
        x, y, z, c = xyzc
        self.x, self.y = x, y
        self.x_up, self.x_down = device_of(x + 1, y, z, c), device_of(x + 3, y, z, c)
        self.y_up, self.y_down = device_of(x, y + 1, z, c), device_of(x, y + 3, z, c)

    def pair(self, one_own, one_part, two_own, two_part, one_on_x):
        on_x = (self.x, self.x_up, self.x_down)
        on_y = (self.y, self.y_up, self.y_down)
        cut = self.cut.quarter
        self.one = Ring(
            self.wire,
            lambda side: one_own(cut(0, side)),
            lambda place, side: one_part(place, cut(0, side)),
            *(on_x if one_on_x else on_y),
        )
        self.two = Ring(
            self.wire,
            lambda side: two_own(cut(1, side)),
            lambda place, side: two_part(place, cut(1, side)),
            *(on_y if one_on_x else on_x),
        )
        self.one.begin()
        self.two.begin()

    def first(self):
        own, out, x, y = self.own, self.out, self.x, self.y
        self.pair(
            lambda q: own.at[q],
            lambda place, q: out.at[(place, y) + q],
            lambda q: own.at[q],
            lambda place, q: out.at[(x, place) + q],
            True,
        )

    def relay(self):
        self.one.relay()
        self.two.relay()

    def near(self):
        self.one.near()
        self.two.near()

    def far(self):
        self.one.far()
        self.two.far()

    def settle(self):
        self.near()
        self.far()

    def second(self):
        out, x, y = self.out, self.x, self.y
        every = slice(None)
        self.pair(
            lambda q: out.at[(every, y) + q],
            lambda place, q: out.at[(every, place) + q],
            lambda q: out.at[(x, every) + q],
            lambda place, q: out.at[(place, every) + q],
            False,
        )


class Rows:
    def __init__(self, rows, cols, start=0):
        self.rows, self.cols, self.start = rows // 2, cols // 2, start

    def half(self, half):
        return (pl.ds(half * self.rows, self.rows),)

    def side(self, side):
        return (slice(None), pl.ds(side * self.cols, self.cols))

    def quarter(self, half, side):
        first = self.start + side * self.cols
        if not isinstance(first, int):
            first = pl.multiple_of(first, LANES)
        return self.half(half) + (pl.ds(first, self.cols),)

    def shapes(self):
        return (self.rows, 2 * self.cols), (self.rows, self.cols)


class Units:
    def half(self, half):
        return (pl.ds(half * 6, 6),)

    def side(self, side):
        return (pl.ds(side * 3, 3),)

    def quarter(self, half, side):
        return (pl.ds(half * 6 + side * 3, 3),)

    def shapes(self):
        return (6, BLOCK, LANES), (3, BLOCK, LANES)


class GroupGather:
    def __init__(self, wire, own, out, xyzc):
        self.wire, self.own, self.out = wire, own, out
        x, y, z, c = xyzc
        self.z, self.c = z, c
        self.sibling = device_of(x, y, z, 1 - c)
        half = out.shape[2] // 2
        self.ring = Ring(
            wire,
            lambda side: own.at[pl.ds(side * half, half)],
            lambda place, side: out.at[place, c, pl.ds(side * half, half)],
            z, device_of(x, y, z + 1, c), device_of(x, y, z + 3, c),
        )
        self.crossed = []

    def begin(self):
        self.ring.begin()
        self.crossed.append(self.wire.send(self.own, self.out.at[self.z, self.c], self.sibling))

    def cross(self, k):
        piece = self.out.at[(self.z + k) % 4, self.c]
        self.crossed.append(self.wire.send(piece, piece, self.sibling))

    def relay(self):
        self.ring.relay()

    def near(self):
        self.ring.near()
        self.cross(1)
        self.cross(3)

    def far(self):
        self.ring.far()
        self.cross(2)

    def finish(self, after=0):
        for copy in self.crossed[after:]:
            copy.wait_recv()


class SecondRound:
    def __init__(self, wire, summed, second_in, xyzc):
        self.wire, self.summed, self.second_in = wire, summed, second_in
        self.x, self.y, self.z, self.c = xyzc

    def peer(self, along_x, k):
        if along_x:
            return device_of(self.x + k, self.y, self.z, self.c)
        return device_of(self.x, self.y + k, self.z, self.c)

    def place(self, half, k):
        return ((self.x, self.y)[half] + k) % 4

    def second(self):
        self.copies = []
        for k in (2, 1, 3):
            for half in range(2):
                self.copies.append(
                    self.wire.send(
                        self.summed.at[half, self.place(1 - half, k)],
                        self.second_in.at[half, k - 1],
                        self.peer(half == 1, k),
                    )
                )

    def total(self, half):
        total = self.summed[half, self.place(1 - half, 0)].astype(F32)
        for k in range(3):
            total = total + self.second_in[half, k].astype(F32)
        return total

    def arrive(self):
        for copy in self.copies:
            copy.wait_recv()


class PlaneScatter(SecondRound):
    def __init__(self, wire, terms, cut, scratch, xyzc):
        *room, self.near_in, self.far_in, self.passed, summed, second_in = scratch
        super().__init__(wire, summed, second_in, xyzc)
        self.terms, self.cut, self.room = terms, cut, room

    def lead(self, half, k, line=slice(None)):
        place = self.place(half, k)
        return (place, line) if half == 0 else (line, place)

    def part(self, half, k, side):
        return self.terms.at[self.lead(half, k) + self.cut.quarter(half, side)]

    def own(self, half, line):
        if self.room:
            return self.room[0][half, line]
        return self.terms[self.lead(half, 0, line) + self.cut.half(half)]

    def edge(self, half, way, line):
        if self.room:
            return self.room[1][half, way, line]
        return self.terms[self.lead(half, (1, 3)[way], line) + self.cut.quarter(half, way)]

    def first(self):
        send = self.wire.send
        self.far, self.plain, self.locals = [], [], []
        if self.room:
            sems = self.room[2]
            for half in range(2):
                pairs = [(self.terms.at[self.lead(half, 0) + self.cut.half(half)], self.room[0].at[half])]
                pairs += [(self.part(half, (1, 3)[way], way), self.room[1].at[half, way]) for way in range(2)]
                for slot, (source, target) in enumerate(pairs):
                    copy = pltpu.make_async_copy(source, target, sems.at[half, slot])
                    copy.start()
                    self.locals.append(copy)
        for half in range(2):
            for way in range(2):
                self.far.append(
                    send(self.part(half, 2, way), self.far_in.at[half, way], self.peer(half == 0, (1, 3)[way]))
                )
        for half in range(2):
            for way in range(2):
                k = (1, 3)[way]
                landing = self.near_in.at[(half, way, slice(None)) + self.cut.side(1 - way)]
                self.plain.append(send(self.part(half, k, 1 - way), landing, self.peer(half == 0, k)))

    def relay(self):
        for copy in self.locals:
            copy.wait()
        self.relayed = []
        for half in range(2):
            for way in range(2):
                self.far[half * 2 + way].wait_recv()

                def add(line, carry):
                    total = self.edge(half, way, line).astype(F32) + self.far_in[half, way, line].astype(F32)
                    self.passed[half, way, line] = total.astype(BF16)
                    return carry

                lax.fori_loop(0, 4, add, 0)
                landing = self.near_in.at[(half, way, slice(None)) + self.cut.side(way)]
                self.relayed.append(
                    self.wire.send(self.passed.at[half, way], landing, self.peer(half == 0, (1, 3)[way]))
                )

    def add_first(self):
        for copy in self.plain + self.relayed:
            copy.wait_recv()
        for half in range(2):

            def body(line, carry):
                total = self.own(half, line).astype(F32)
                for way in range(2):
                    total = total + self.near_in[half, way, line].astype(F32)
                self.summed[half, line] = total.astype(BF16)
                return carry

            lax.fori_loop(0, 4, body, 0)


def scatter_scratch(cut, room=False):
    half, part = cut.shapes()
    vmem = pltpu.VMEM
    held = [vmem((2, 4) + half, BF16), vmem((2, 2, 4) + part, BF16), pltpu.SemaphoreType.DMA((2, 3))]
    return (held if room else []) + [
        vmem((2, 2, 4) + half, BF16),
        vmem((2, 2, 4) + part, BF16),
        vmem((2, 2, 4) + part, BF16),
        vmem((2, 4) + half, BF16),
        vmem((2, 3) + half, BF16),
    ]


class GroupScatter:
    def __init__(self, wire, terms, mine, crossed_in, summed, ring_in, local_sem, xyzc):
        self.wire, self.terms = wire, terms
        self.mine, self.crossed_in, self.summed, self.ring_in = mine, crossed_in, summed, ring_in
        self.x, self.y, self.z, self.c = xyzc
        self.local_sem = local_sem

    def begin(self):
        self.local = pltpu.make_async_copy(self.terms.at[:, self.c], self.mine, self.local_sem)
        self.local.start()
        sibling = device_of(self.x, self.y, self.z, 1 - self.c)
        self.crossed = {}
        for k in (2, 1, 3, 0):
            place = (self.z + k) % 4
            self.crossed[k] = self.wire.send(
                self.terms.at[place, 1 - self.c], self.crossed_in.at[place], sibling
            )

    def turn(self):
        self.local.wait()
        self.copies = []
        for k in (2, 1, 3):
            place = (self.z + k) % 4
            self.crossed[k].wait_recv()

            def body(tile, carry):
                total = self.mine[place, tile].astype(F32) + self.crossed_in[place, tile].astype(F32)
                self.summed[place, tile] = total.astype(BF16)
                return carry

            lax.fori_loop(0, 12, body, 0)
            self.copies.append(
                self.wire.send(
                    self.summed.at[place],
                    self.ring_in.at[k - 1],
                    device_of(self.x, self.y, self.z + k, self.c),
                )
            )

    def finish(self, out):
        self.crossed[0].wait_recv()
        for copy in self.copies:
            copy.wait_recv()
        for tile in range(12):
            total = self.mine[self.z, tile].astype(F32) + self.crossed_in[self.z, tile].astype(F32)
            for k in range(3):
                total = total + self.ring_in[k, tile].astype(F32)
            out[:, tile * LANES : (tile + 1) * LANES] = total


class ChipScatter:
    def __init__(self, wire, terms, at, crossed_in, ring_in, xyzc):
        self.wire, self.terms, self.at = wire, terms, at
        self.crossed_in, self.ring_in = crossed_in, ring_in
        self.x, self.y, self.z, self.c = xyzc
        self.crossed_slot, self.ring_slot = wire.reserve(4), wire.reserve(3)
        self.all_tiles = pl.ds(0, 12)

    def place(self, step):
        return (self.z + step) % 4

    def crossed(self, step):
        place = self.place(step)
        return self.wire.make(
            self.crossed_slot + step,
            self.terms.at[place, self.at + 1 - self.c, self.all_tiles],
            self.crossed_in.at[place],
            device_of(self.x, self.y, self.z, 1 - self.c),
        )

    def ring(self, step):
        return self.wire.make(
            self.ring_slot + step - 1,
            self.terms.at[self.place(step), self.at + self.c, self.all_tiles],
            self.ring_in.at[step - 1],
            device_of(self.x, self.y, self.z + step, self.c),
        )

    def put(self, step, grads):
        place = self.place(step)
        for core in range(2):
            for tile in range(12):
                self.terms[place, self.at + core, tile] = grads[
                    core * BLOCK : (core + 1) * BLOCK, tile * LANES : (tile + 1) * LANES
                ]
        self.crossed(step).start()

    def turn(self, step):
        place, line = self.place(step), self.at + self.c
        self.crossed(step).wait_recv()

        def add(tile, carry):
            total = self.terms[place, line, tile].astype(F32) + self.crossed_in[place, tile].astype(F32)
            self.terms[place, line, tile] = total.astype(BF16)
            return carry

        lax.fori_loop(0, 12, add, 0)
        self.ring(step).start()

    def total(self):
        self.crossed(0).wait_recv()
        for step in range(1, 4):
            self.ring(step).wait_recv()
        tiles = []
        for tile in range(12):
            total = self.terms[self.z, self.at + self.c, tile].astype(F32)
            total = total + self.crossed_in[self.z, tile].astype(F32)
            for step in range(3):
                total = total + self.ring_in[step, tile].astype(F32)
            tiles.append(total)
        return jnp.concatenate(tiles, axis=1)

    def close(self):
        for step in range(4):
            self.crossed(step).wait_send()
        for step in range(1, 4):
            self.ring(step).wait_send()


class RingScatter(ChipScatter):
    def __init__(self, wire, terms, crossed_in, near_in, far_in, xyzc):
        super().__init__(wire, terms, 0, crossed_in, None, xyzc)
        self.near_in, self.far_in = near_in, far_in
        self.moved = []

    def sum_tiles(self, place, tiles, extra=None):
        def add(tile, carry):
            total = self.terms[place, self.c, tile].astype(F32)
            if extra is None:
                total = total + self.crossed_in[place, tile].astype(F32)
            else:
                total = total + self.far_in[extra, tile - extra * 6].astype(F32)
            self.terms[place, self.c, tile] = total.astype(BF16)
            return carry

        lax.fori_loop(*tiles, add, 0)

    def move(self, place, first, landing, k):
        source = self.terms.at[place, self.c, pl.ds(first, 6)]
        copy = self.wire.send(source, landing, device_of(self.x, self.y, self.z + k, self.c))
        self.moved.append(copy)
        return copy

    def turn(self, step):
        place = self.place(step)
        self.crossed(step).wait_recv()
        self.sum_tiles(place, (0, 12))
        if step == 2:
            self.far = [self.move(place, 6 * way, self.far_in.at[way], (1, 3)[way]) for way in range(2)]
        else:
            way = (1, 3).index(step)
            plain = 6 * (1 - way)
            self.move(place, plain, self.near_in.at[way, pl.ds(plain, 6)], step)

    def pass_on(self, step):
        way = (1, 3).index(step)
        place = self.place(step)
        self.far[way].wait_recv()
        self.sum_tiles(place, (6 * way, 6 * way + 6), way)
        self.move(place, 6 * way, self.near_in.at[way, pl.ds(6 * way, 6)], step)

    def total(self):
        self.crossed(0).wait_recv()
        for copy in self.moved[2:]:
            copy.wait_recv()
        tiles = []
        for tile in range(12):
            total = self.terms[self.z, self.c, tile].astype(F32) + self.crossed_in[self.z, tile].astype(F32)
            for way in range(2):
                total = total + self.near_in[way, tile].astype(F32)
            tiles.append(total)
        return jnp.concatenate(tiles, axis=1)

    def close(self):
        for step in range(4):
            self.crossed(step).wait_send()


def group_scatter_scratch():
    return [
        pltpu.VMEM((4, 12, BLOCK, LANES), BF16),
        pltpu.VMEM((4, 12, BLOCK, LANES), BF16),
        pltpu.VMEM((4, 12, BLOCK, LANES), BF16),
        pltpu.VMEM((3, 12, BLOCK, LANES), BF16),
        pltpu.SemaphoreType.DMA,
    ]


def chip_scatter_scratch():
    return [pltpu.VMEM((4, 12, BLOCK, LANES), BF16), pltpu.VMEM((3, 12, BLOCK, LANES), BF16)]


def wire_scratch(count):
    return [pltpu.SemaphoreType.DMA((count,)), pltpu.SemaphoreType.DMA((count,))]


ANY = pl.BlockSpec(memory_space=pl.ANY)
INVMEM = pl.BlockSpec(memory_space=pltpu.VMEM)


def communicate(kernel, out_shapes, in_specs, out_specs, scratch, ident, name, vmem=VMEM_BYTES):
    return pl.pallas_call(
        kernel,
        out_shape=out_shapes,
        in_specs=in_specs,
        out_specs=out_specs,
        scratch_shapes=scratch,
        compiler_params=pltpu.CompilerParams(
            collective_id=ident, has_side_effects=True, vmem_limit_bytes=vmem
        ),
        name=name,
    )


def key_unit(member):
    return member + jnp.where(member >= 6, 6, 0) + jnp.where(member >= 7, 1, 0)


def value_unit(member):
    return member + 6 + jnp.where(member >= 6, 1, 0) + jnp.where(member >= 7, 1, 0)


def gain_rows(pieces):
    return jnp.concatenate(join_heads(pieces), axis=1)


def head_window(tiles, head):
    tile, skip = divmod(head * HEAD_DIM, LANES)
    lane = lane_of(tiles[0].shape)
    window = pltpu.roll(tiles[tile], (LANES - skip) % LANES, 1)
    if skip + HEAD_DIM > LANES:
        window = jnp.where(lane < LANES - skip, window, pltpu.roll(tiles[tile + 1], LANES - skip, 1))
    return jnp.where(lane < HEAD_DIM, window, 0.0)


def join_heads(pieces):
    lane = lane_of(pieces[0].shape)
    tiles = []
    for tile in range(len(pieces) * 3 // 4):
        piece, skip = divmod(tile * LANES, HEAD_DIM)
        low = pltpu.roll(pieces[piece], (LANES - skip) % LANES, 1)
        high = pltpu.roll(pieces[piece + 1], HEAD_DIM - skip, 1)
        tiles.append(jnp.where(lane < HEAD_DIM - skip, low, high))
    return tiles


def mix_groups(parts):
    group = lane_of(parts[0][0].shape) // 32
    mixed = None
    for i, (tile, g) in enumerate(parts):
        turned = pltpu.roll(tile, (32 * (i - g)) % LANES, 1)
        mixed = turned if mixed is None else jnp.where(group == i, turned, mixed)
    return mixed


def lane_of(shape):
    return lax.broadcasted_iota(jnp.int32, shape, len(shape) - 1)


def pack_tile(unit, extra, place):
    return jnp.where(lane_of(unit.shape) < HEAD_DIM, unit, pltpu.roll(extra, (96 - 32 * place) % LANES, 1))


def unpack_extra(tiles):
    lane = lane_of(tiles[0].shape)
    extra = jnp.where(lane < 32, pltpu.roll(tiles[0], 32, 1), 0.0)
    extra = jnp.where(jnp.logical_and(lane >= 32, lane < 64), pltpu.roll(tiles[1], 64, 1), extra)
    return jnp.where(jnp.logical_and(lane >= 64, lane < 96), pltpu.roll(tiles[2], 96, 1), extra)


def swap_halves(rows):
    lane = lane_of(rows.shape)
    return jnp.where(lane < HEAD_DIM // 2, pltpu.roll(rows, LANES - 48, 1), pltpu.roll(rows, 48, 1))


def rope_table():
    half = HEAD_DIM // 2
    frequency = ROPE_BASE ** (-2.0 * np.arange(half, dtype=np.float64) / HEAD_DIM)
    frequency = frequency.astype(np.float32)
    places = np.arange(DEPTH * BLOCK, dtype=np.float32)
    angles = (places[:, None] * frequency[None, :]).astype(np.float64)
    table = np.zeros((DEPTH * BLOCK, LANES), np.float32)
    table[:, :half] = np.cos(angles)
    table[:, half:HEAD_DIM] = np.sin(angles)
    return jnp.asarray(table.reshape(DEPTH, BLOCK, LANES))


def turning(table):
    lane = lane_of(table.shape)
    cosine = jnp.where(lane < 48, table, pltpu.roll(table, 48, 1))
    sine = jnp.where(lane < 48, -pltpu.roll(table, LANES - 48, 1), jnp.where(lane < HEAD_DIM, table, 0.0))
    return cosine, sine


def count_ancestors(lineage, block):
    count = jnp.int32(0)
    for step in range(DEPTH):
        count = count + jnp.where(lineage[block, step] >= 0, 1, 0)
    return count


def write_lineage(parent, first, lineage):
    def one(block, carry):
        def hop(step, node):
            lineage[block, step] = node
            above = parent[jnp.maximum(node, 0)]
            return jnp.where(node >= 0, above, -1)

        lax.fori_loop(0, DEPTH, hop, first + block)
        return carry

    lax.fori_loop(0, MEMBERS, one, 0)


def attend_block(lineage, block, queries, alive, load, scores):
    limit = count_ancestors(lineage, block)
    t = lax.broadcasted_iota(jnp.int32, (2 * BLOCK, BLOCK), 0) % BLOCK
    u = lax.broadcasted_iota(jnp.int32, (2 * BLOCK, BLOCK), 1)
    own = jnp.logical_and(u <= t, jnp.logical_or(alive > 0.5, u == t))
    nodes = [jnp.maximum(lineage[block, step], 0) for step in range(DEPTH)]
    pairs = range(0, DEPTH, 2)
    highest = None
    for step in pairs:
        keys = jnp.concatenate([load(node, key_unit(lax.rem(node, 8))) for node in nodes[step : step + 2]], axis=0)
        part = lax.dot_general(queries, keys, (((1,), (1,)), ((), ())), preferred_element_type=F32) * SCALE
        near = part[:, :BLOCK]
        if step == 0:
            near = jnp.where(own, near, NEGATIVE)
        else:
            near = near + jnp.where(step < limit, 0.0, NEGATIVE)
        far = part[:, BLOCK:] + jnp.where(step + 1 < limit, 0.0, NEGATIVE)
        scores[step] = near
        scores[step + 1] = far
        both = jnp.maximum(near, far)
        highest = both if step == 0 else jnp.maximum(highest, both)
    largest = jnp.max(highest, axis=1, keepdims=True)
    totals = jnp.zeros((2 * BLOCK, BLOCK), F32)
    attended = jnp.zeros((2 * BLOCK, LANES), F32)
    for step in pairs:
        near, far = jnp.exp(scores[step] - largest), jnp.exp(scores[step + 1] - largest)
        totals = totals + near + far
        values = jnp.concatenate(
            [load(node, value_unit(lax.rem(node, 8))) for node in nodes[step : step + 2]], axis=0
        )
        terms = jnp.concatenate([near.astype(BF16), far.astype(BF16)], axis=1)
        attended = attended + jnp.dot(terms, values, preferred_element_type=F32)
    total = jnp.sum(totals, axis=1, keepdims=True)
    return (attended / total).astype(BF16), largest + jnp.log(total)


def start_kernel(
    parent, table, stream, w_query, w_key, w_value, w_gate, w_up, w_out, small_rows, live_row, cotangent, own_down,
    lineage, live, gains, query, stream_all, attn_all,
    kv_out, middle, rms_out, grad_middle, grads_in, down_terms, feed_lines, wide_lines, out_terms, gain_terms,
    attended_out, log_rows,
    packed, out_low, small, stage, packed_in, out_in, small_in, wide_tall, wide_own, out_own, gain_own, gains_all,
    w_attn, own_kv, kv, w_out_all, w_feed, w_down, mid_all, cot_all, crossed_in, ring_in,
    att_out, att_in, att_pad, grads_out, *scratch,
):
    feed_scratch, wide_scratch = scratch[:5], scratch[5:10]
    send_sems, recv_sems, local_sems = scratch[10:]
    xyzc = x, y, z, c = spot()
    j = z * 2 + c
    base = (x * 4 + y) * MEMBERS
    sibling = device_of(x, y, z, 1 - c)
    wire = Wire(send_sems, recv_sems)
    group = [group_peer(x, y, z, c, k) for k in range(1, MEMBERS)]
    across, down_first = (((1,), (1,)), ((), ())), (((0,), (0,)), ((), ()))
    locals_ = []

    peers = group + axis_peers(x, y, z, c, True)
    announce(peers)

    stage[...] = jnp.zeros((16, FF), F32)
    wide_tall[96:] = jnp.zeros((8, 1536), F32)

    def staged(weights):
        width = weights.shape[1]
        stage[:12, :width] = weights[...].astype(F32)
        return [stage[:, tile * LANES : (tile + 1) * LANES] for tile in range(width // LANES)]

    def put_packed(member, tile, value):
        packed[member, :, tile * LANES : (tile + 1) * LANES] = value.astype(BF16)

    tiles = staged(w_query)
    for head in range(HEADS):
        put_packed(head // 2, head % 2, head_window(tiles, head))
    for place, weights in ((2, w_key), (3, w_value)):
        tiles = staged(weights)
        for member in range(MEMBERS):
            put_packed(member, place, head_window(tiles, member))
    for place, weights in ((4, w_gate), (8, w_up)):
        tiles = staged(weights)
        for member in range(MEMBERS):
            for tile in range(4):
                parts = [(tiles[2 * (4 * tile + i) + member // 4], member % 4) for i in range(4)]
                put_packed(member, place + tile, mix_groups(parts))
    out_low[...] = jnp.concatenate(staged(w_out), axis=1).astype(BF16)
    rows = pltpu.roll(small_rows[...], 12 * j, 1)
    live_rows = jnp.broadcast_to(live_row[...].astype(F32), (8, LANES))
    rows = jnp.where(lax.broadcasted_iota(jnp.int32, (8, LANES), 0) == 2, live_rows, rows)
    small[...] = jnp.concatenate([rows, jnp.zeros((8, LANES), F32)], axis=0).astype(BF16)
    await_peers(peers)

    def keep(source, target):
        copy = pltpu.make_async_copy(source, target, local_sems.at[len(locals_)])
        copy.start()
        locals_.append(copy)
        return copy

    def to_members(source, target):
        return [wire.send(source((j + k) % MEMBERS), target.at[j], group[k - 1]) for k in range(1, MEMBERS)]

    def half_of(member):
        return pl.ds(pl.multiple_of((member % 2) * 768, 768), 768)

    own_half = half_of(c)
    attn_part, feed_part = pl.ds(0, 512), pl.ds(512, 1024)
    attn_dealt = to_members(lambda member: packed.at[member, :, attn_part], packed_in.at[:, :, attn_part])
    small_dealt = to_members(lambda member: small, small_in)
    streams = GroupGather(wire, stream, mid_all, xyzc)
    streams.begin()
    first_kept = (keep(packed.at[j], packed_in.at[j]), keep(small, small_in.at[j]))
    out_kept = keep(out_low.at[:, own_half], out_in.at[j])
    stream_kept = keep(stream, mid_all.at[z, c])
    write_lineage(parent, base, lineage)
    for line in range(16):
        w_out_all[line // 4, line % 4, 96:] = jnp.zeros((32, D), BF16)

    for copy in attn_dealt + small_dealt:
        copy.wait_recv()
    out_dealt = to_members(lambda member: out_low.at[:, half_of(member)], out_in)
    feed_dealt_in = to_members(lambda member: packed.at[member, :, feed_part], packed_in.at[:, :, feed_part])
    for copy in first_kept:
        copy.wait()
    for member in range(MEMBERS):
        wide_tall[pl.ds(member * 12, 12), :512] = packed_in[member, :, :512].astype(F32)[:12]
    wide_own[:, :512] = wide_tall[:96, :512].astype(BF16)
    gain = small_in[0].astype(F32)
    for member in range(MEMBERS):
        row = small_in[member].astype(F32)
        live[member] = row[2:3]
        if member:
            gain = gain + row
    gain_own[...] = gain.astype(BF16)
    own_attn, own_feed = wide_own.at[:, pl.ds(0, 512)], wide_own.at[:, pl.ds(512, 1024)]
    attn = PlaneGather(wire, own_attn, w_attn, Rows(96, 512), xyzc)
    attn.first()
    tiny = [wire.send(gain_own, gains_all.at[x, y], device_of(x + k, y, z, c)) for k in range(1, 4)]
    attn_kept = keep(own_attn, w_attn.at[x, y])
    gain_kept = keep(gain_own, gains_all.at[x, y])
    down_kept = keep(own_down, w_down.at[x, y])

    attn.relay()
    streams.relay()
    gain_kept.wait()
    for copy in tiny:
        copy.wait_recv()
    line = gains_all.at[:, y]
    tiny = [wire.send(line, line, device_of(x, y + k, z, c)) for k in range(1, 4)]
    attn_kept.wait()
    attn.settle()
    attn.second()
    for copy in out_dealt:
        copy.wait_recv()
    out_kept.wait()
    for member in range(MEMBERS):
        wide_tall[pl.ds(member * 12, 12), :768] = out_in[member].astype(F32)[:12]
    out_own[...] = wide_tall[:96, :768].astype(BF16)
    out_kept = keep(out_own, w_out_all.at[x, y, pl.ds(0, 96), own_half])
    out_kept.wait()
    outs = PlaneGather(wire, w_out_all.at[x, y], w_out_all, Rows(96, 768, c * 768), xyzc)
    outs.first()
    for copy in feed_dealt_in:
        copy.wait_recv()
    for member in range(MEMBERS):
        wide_tall[pl.ds(member * 12, 12), 512:] = packed_in[member, :, 512:].astype(F32)[:12]
    wide_own[:, 512:] = wide_tall[:96, 512:].astype(BF16)
    feed_kept = keep(own_feed, w_feed.at[x, y])
    streams.near()
    streams.far()
    attn.relay()
    outs.relay()
    for copy in tiny:
        copy.wait_recv()
    pieces = [gains_all[piece // 4, piece % 4].astype(F32)[:8] for piece in range(16)]
    gains[...] = gain_rows(pieces)
    attn.settle()
    stream_kept.wait()
    streams.finish()
    attn_copied = keep(w_attn, attn_all)
    stream_copied = keep(mid_all, stream_all)

    def project(step, carry):
        wide = mid_all[step].reshape(2 * BLOCK, D).astype(F32)
        rms = jnp.sqrt(jnp.mean(wide * wide, axis=1, keepdims=True) + EPSILON)
        rows = (wide * (1.0 / rms) * gains[0:1]).astype(BF16)
        raw = jnp.dot(rows, w_attn[...].reshape(D, 512), preferred_element_type=F32)
        for part in range(2):
            block = step * 2 + part
            depth = count_ancestors(lineage, block) - 1
            cos, sin = turning(table[depth])

            def turn(head):
                v = raw[part * BLOCK : (part + 1) * BLOCK, head * LANES : (head + 1) * LANES]
                return (v * cos + swap_halves(v) * sin).astype(BF16)

            query[block, :BLOCK] = turn(0)
            query[block, BLOCK:] = turn(1)
            kv[x, y, key_unit(block)] = turn(2)
            kv[x, y, value_unit(block)] = raw[part * BLOCK : (part + 1) * BLOCK, 3 * LANES :].astype(BF16)
        return carry

    lax.fori_loop(0, 2, project, 0)
    outs.settle()
    outs.second()
    lax.fori_loop(2, 4, project, 0)
    for tile in range(12):
        extra = kv[x, y, 12 + tile // 3].astype(F32)
        own_kv[tile] = pack_tile(kv[x, y, tile].astype(F32), extra, tile % 3).astype(BF16)

    pairs = PlaneGather(wire, own_kv, kv, Units(), xyzc)
    pairs.first()
    outs.relay()
    kept = keep(own_kv, kv.at[x, y, pl.ds(0, 12)])
    cotangents = GroupGather(wire, cotangent, cot_all, xyzc)
    cotangents.begin()
    cot_kept = keep(cotangent, cot_all.at[z, c])
    pairs.relay()
    kept.wait()
    outs.settle()
    swap_part = w_out_all.at[:, :, pl.ds(0, 96), own_half]
    swapped = wire.send(swap_part, swap_part, sibling)
    pairs.settle()
    pairs.second()

    def unpack(half, k):
        def one(other, carry):
            piece = (other, (y + k) % 4) if half == 0 else ((x + k) % 4, other)
            for extra in (2 * half, 2 * half + 1):
                tiles = [kv[piece + (extra * 3 + part,)].astype(F32) for part in range(3)]
                kv[piece + (12 + extra,)] = unpack_extra(tiles).astype(BF16)
            return carry

        lax.fori_loop(0, 4, one, 0)

    unpack(0, 0)
    unpack(1, 0)
    cotangents.relay()
    cotangents.near()
    cotangents.far()
    pairs.relay()
    early, wire.open = wire.open, []
    feed = PlaneGather(wire, own_feed, w_feed, Rows(96, 1024), xyzc)
    down = PlaneGather(wire, own_down, w_down, Rows(32, D), xyzc)
    feed.first()
    down.first()
    pairs.near()
    for k in (1, 3):
        unpack(0, k)
        unpack(1, k)
    pairs.far()
    unpack(0, 2)
    unpack(1, 2)
    for copy in early:
        copy.wait_send()
    stream_copied.wait()
    attn_copied.wait()

    kv_copied = keep(kv, kv_out)

    att_slot = wire.reserve(MEMBERS - 1)

    def load(node, unit):
        return kv[lax.div(node, 32), lax.rem(lax.div(node, 8), 4), unit]

    def att_copy(k):
        block = (j + 1 + k) % MEMBERS
        return wire.make(att_slot + k, att_out.at[block], att_in.at[j], base + block)

    def attend_one(k, scores):
        block = (j + 1 + k) % MEMBERS
        attended, logs = attend_block(lineage, block, query[block], live[block], load, scores)
        log_rows[block] = jnp.transpose(jnp.broadcast_to(logs, (2 * BLOCK, LANES)))[:8]
        att_out[block, :, :LANES] = attended[:BLOCK]
        att_out[block, :, LANES:] = attended[BLOCK:]

    def attend_pair(pair):
        def both(one, two):
            attend_one(2 * pair, one)
            attend_one(2 * pair + 1, two)

        room = pltpu.VMEM((DEPTH, 2 * BLOCK, LANES), F32)
        pl.run_scoped(both, room, room)

        def give(k, carry):
            att_copy(k).start()
            return carry

        lax.fori_loop(2 * pair, min(2 * pair + 2, MEMBERS - 1), give, 0)

    attend_pair(0)
    feed.relay()
    down.relay()
    attend_pair(1)
    feed_kept.wait()
    down_kept.wait()
    feed.settle()
    feed.second()
    down.settle()
    down.second()
    attend_pair(2)
    attend_pair(3)
    feed.relay()
    down.relay()
    att_in[j] = att_out[j]
    att_copied = keep(att_out, attended_out)
    att_recv = [att_copy(k) for k in range(MEMBERS - 1)]

    for copy in att_recv:
        copy.wait_recv()
    for member in range(MEMBERS):
        att_pad[:, member * 256 : (member + 1) * 256] = att_in[member]
    swapped.wait_recv()

    def project_out(step, carry):
        cols = pl.ds(pl.multiple_of(step * 512, 512), 512)
        weights = w_out_all[:, :, :, cols].reshape(16 * LANES, 512)
        branch = jnp.dot(att_pad[...], weights, preferred_element_type=F32)
        middle[:, cols] = stream[:, cols].astype(F32) + branch
        return carry

    lax.fori_loop(0, 3, project_out, 0)
    rms = jnp.sqrt(jnp.mean(middle[...] * middle[...], axis=1, keepdims=True) + EPSILON)
    rms_out[...] = jnp.transpose(jnp.broadcast_to(rms, (BLOCK, LANES)))[:1]
    mid_all[z, c] = (middle[...] / rms * gains[1:2]).astype(BF16)
    mids = GroupGather(wire, mid_all.at[z, c], mid_all, xyzc)
    mids.begin()
    mids.relay()
    feed.settle()
    down.settle()
    kv_copied.wait()
    cot_kept.wait()
    cotangents.finish()
    for k in range(MEMBERS - 1):
        att_copy(k).wait_send()

    grad_rows = ChipScatter(wire, kv, 2, crossed_in, ring_in, xyzc)

    def rest(acts, grad_feed, feed_terms, wide_terms):
        feed_back_half(
            xyzc, wire, group, keep, mids, grad_rows, mid_all, cot_all, w_feed, w_down, w_out_all, kv, middle, gains,
            att_pad, att_copied, grads_out, feed_scratch, wide_scratch,
            acts, grad_feed, feed_terms, wide_terms,
            grad_middle, grads_in, down_terms, feed_lines, wide_lines, out_terms, gain_terms,
        )

    pl.run_scoped(
        rest,
        pltpu.VMEM((4, 2 * BLOCK, 512), BF16),
        pltpu.VMEM((4, 2 * BLOCK, 1024), BF16),
        pltpu.VMEM((4, 4, 96, 1024), BF16),
        pltpu.VMEM((4, 4, 32, D), BF16),
    )


def feed_back_half(
    xyzc, wire, group, keep, mids, grad_rows, mid_all, cot_all, w_feed, w_down, w_out_all, kv, middle, gains,
    att_pad, att_copied, grads_out, feed_scratch, wide_scratch,
    acts, grad_feed, feed_terms, wide_terms,
    grad_middle, grads_in, down_terms, feed_lines, wide_lines, out_terms, gain_terms,
):
    x, y, z, c = xyzc
    j = z * 2 + c
    across, down_first = (((1,), (1,)), ((), ())), (((0,), (0,)), ((), ()))

    def feed_forward(step):
        place = grad_rows.place(step)
        rows = mid_all[place].reshape(2 * BLOCK, D)
        weights = w_feed[...].reshape(D, 1024)
        both = jnp.dot(rows, weights, preferred_element_type=F32)
        gate, up = both[:, :512], both[:, 512:]
        sigmoid = 0.5 * jnp.tanh(0.5 * gate) + 0.5
        silu = gate * sigmoid
        acts[place] = (silu * up).astype(BF16)
        cot = cot_all[place].reshape(2 * BLOCK, D)
        grad_act = lax.dot_general(cot, w_down[...].reshape(512, D), across, preferred_element_type=F32)
        grad_gate = grad_act * up * sigmoid * (1.0 + gate * (1.0 - sigmoid))
        grad_feed[place, :, :512] = grad_gate.astype(BF16)
        grad_feed[place, :, 512:] = (grad_act * silu).astype(BF16)

    def feed_back(step):
        place = grad_rows.place(step)
        weights = w_feed[...].reshape(D, 1024)
        grads = lax.dot_general(grad_feed[place], weights, across, preferred_element_type=F32)
        grad_rows.put(step, grads.astype(BF16))

    mids.crossed[0].wait_recv()
    feed_forward(0)
    feed_back(0)
    mids.near()
    mids.crossed[1].wait_recv()
    feed_forward(1)
    feed_back(1)
    mids.far()
    mids.crossed[2].wait_recv()
    grad_rows.turn(1)
    feed_forward(3)
    feed_back(3)
    mids.crossed[3].wait_recv()
    grad_rows.turn(3)
    feed_forward(2)

    def down_weights(step, carry):
        cols = pl.ds(pl.multiple_of(step * 128, 128), 128)
        left = acts[:, :, cols].reshape(MEMBERS * BLOCK, 128)
        right = cot_all[...].reshape(MEMBERS * BLOCK, D)
        total = lax.dot_general(left, right, down_first, preferred_element_type=F32)
        wide_terms[step] = total.astype(BF16).reshape(4, 32, D)
        return carry

    lax.fori_loop(0, 4, down_weights, 0)
    wides = PlaneScatter(wire, wide_terms, Rows(32, D), wide_scratch, xyzc)
    wides.first()
    feed_back(2)

    def feed_weights(step, carry):
        cols = pl.ds(pl.multiple_of(step * 384, 384), 384)
        left = mid_all[:, :, :, cols].reshape(MEMBERS * BLOCK, 384)
        right = grad_feed[...].reshape(MEMBERS * BLOCK, 1024)
        total = lax.dot_general(left, right, down_first, preferred_element_type=F32)
        feed_terms[step] = total.astype(BF16).reshape(4, 96, 1024)
        return carry

    lax.fori_loop(0, 2, feed_weights, 0)
    grad_rows.turn(2)
    lax.fori_loop(2, 4, feed_weights, 0)
    feeds = PlaneScatter(wire, feed_terms, Rows(96, 1024), feed_scratch, xyzc)
    feeds.first()
    wides.relay()

    def down_rows(place, carry):
        outs = jnp.dot(acts[place], w_down[...].reshape(512, D), preferred_element_type=F32).astype(BF16)
        for core in range(2):
            for tile in range(12):
                kv[place, core, tile] = outs[
                    core * BLOCK : (core + 1) * BLOCK, tile * LANES : (tile + 1) * LANES
                ]
        return carry

    lax.fori_loop(0, 4, down_rows, 0)
    down_copied = keep(kv.at[:, pl.ds(0, 2), pl.ds(0, 12)], down_terms)
    grad_mid = grad_rows.total()
    rms = jnp.sqrt(jnp.mean(middle[...] * middle[...], axis=1, keepdims=True) + EPSILON)
    scaled = middle[...] / rms
    gain_terms[...] = jnp.sum(grad_mid * scaled, axis=0, keepdims=True)
    weighted = grad_mid * gains[1:2]
    back = (weighted - scaled * jnp.mean(weighted * scaled, axis=1, keepdims=True)) / rms
    grad_middle[...] = cot_all[z, c].astype(F32) + back
    branch_grad = grad_middle[...].astype(BF16)

    def spread(step, carry):
        weights = w_out_all[step].reshape(4 * LANES, D)
        grads = lax.dot_general(branch_grad, weights, across, preferred_element_type=F32).astype(BF16)
        for part in range(2):
            grads_out[step * 2 + part] = grads[:, part * 256 : (part + 1) * 256]
        return carry

    lax.fori_loop(0, 4, spread, 0)
    kept = keep(grads_out.at[j], grads_in.at[j])
    dealt = [
        wire.send(grads_out.at[(j + k) % MEMBERS], grads_in.at[j], group[k - 1]) for k in (4, 5, 3, 2, 6, 7, 1)
    ]
    feeds.relay()

    def out_weights(step, carry):
        cols = pl.ds(pl.multiple_of(step * 512, 512), 512)
        total = lax.dot_general(att_pad[:, cols], branch_grad, down_first, preferred_element_type=F32)
        w_out_all[step] = total.astype(BF16).reshape(4, LANES, D)
        return carry

    lax.fori_loop(0, 4, out_weights, 0)
    out_copied = keep(w_out_all.at[:, :, pl.ds(0, 96)], out_terms)

    wides.add_first()
    wide_copied = keep(wides.summed, wide_lines)
    feeds.add_first()
    feed_copied = keep(feeds.summed, feed_lines)
    for copy in dealt:
        copy.wait_recv()
    for copy in (kept, down_copied, out_copied, att_copied, wide_copied, feed_copied):
        copy.wait()
    wire.close()
    grad_rows.close()


def start(
    parent, table, stream, w_query, w_key, w_value, w_gate, w_up, w_out, small_rows, live_row, cotangent, own_down
):
    shape, vmem = jax.ShapeDtypeStruct, pltpu.VMEM
    smem = pl.BlockSpec(memory_space=pltpu.SMEM)
    return communicate(
        start_kernel,
        (
            shape((MEMBERS, DEPTH), jnp.int32),
            shape((MEMBERS, 1, LANES), F32),
            shape((8, D), F32),
            shape((MEMBERS, 2 * BLOCK, LANES), BF16),
            shape((4, 2, BLOCK, D), BF16),
            shape((4, 4, 96, 512), BF16),
            shape((4, 4, 16, BLOCK, LANES), BF16),
            shape((BLOCK, D), F32),
            shape((1, LANES), F32),
            shape((BLOCK, D), F32),
            shape((MEMBERS, BLOCK, 2 * LANES), BF16),
            shape((4, 2, 12, BLOCK, LANES), BF16),
            shape((2, 4, 48, 1024), BF16),
            shape((2, 4, 16, D), BF16),
            shape((4, 4, 96, D), BF16),
            shape((1, D), F32),
            shape((MEMBERS, BLOCK, 2 * LANES), BF16),
            shape((MEMBERS, 8, 2 * BLOCK), F32),
        ),
        [smem] + [INVMEM] * 10 + [ANY] * 2,
        (smem,) + (INVMEM,) * 3 + (ANY,) * 3 + (INVMEM,) * 3 + (ANY,) * 5 + (INVMEM, ANY, INVMEM),
        [
            vmem((MEMBERS, 16, 1536), BF16),
            vmem((16, 1536), BF16),
            vmem((16, LANES), BF16),
            vmem((16, FF), F32),
            vmem((MEMBERS, 16, 1536), BF16),
            vmem((MEMBERS, 16, 768), BF16),
            vmem((MEMBERS, 16, LANES), BF16),
            vmem((104, 1536), F32),
            vmem((96, 1536), BF16),
            vmem((96, 768), BF16),
            vmem((16, LANES), BF16),
            vmem((4, 4, 16, LANES), BF16),
            vmem((4, 4, 96, 512), BF16),
            vmem((12, BLOCK, LANES), BF16),
            vmem((4, 4, 16, BLOCK, LANES), BF16),
            vmem((4, 4, LANES, D), BF16),
            vmem((4, 4, 96, 1024), BF16),
            vmem((4, 4, 32, D), BF16),
            vmem((4, 2, BLOCK, D), BF16),
            vmem((4, 2, BLOCK, D), BF16),
        ]
        + chip_scatter_scratch()
        + [
            vmem((MEMBERS, BLOCK, 2 * LANES), BF16),
            vmem((MEMBERS, BLOCK, 2 * LANES), BF16),
            vmem((BLOCK, 2048), BF16),
            vmem((MEMBERS, BLOCK, 2 * LANES), BF16),
        ]
        + scatter_scratch(Rows(96, 1024))
        + scatter_scratch(Rows(32, D))
        + wire_scratch(250)
        + [pltpu.SemaphoreType.DMA((20,))],
        2,
        "start",
        63 * 2**20,
    )(parent, table, stream, w_query, w_key, w_value, w_gate, w_up, w_out, small_rows, live_row, cotangent, own_down)


def split_rows(tall, dealt):
    width = dealt.shape[2]
    for member in range(MEMBERS):
        dealt[member] = tall[pl.ds(member * 12, 16), :width].astype(BF16)


def attend_back_kernel(
    lineage, query, live, grad, attended, log_rows, kv_in, grad_query, grad_kv, kv, sums, packed, sems
):
    loaded = pltpu.make_async_copy(kv_in, kv, sems.at[16])
    loaded.start()

    def clear(step, carry):
        sums[step] = jnp.zeros((BLOCK, LANES), F32)
        return carry

    lax.fori_loop(0, 256, clear, 0)
    loaded.wait()

    def two(pair, carry):
        for block in (2 * pair, 2 * pair + 1):
            attend_back_block(block, lineage, query, live, grad, attended, log_rows, grad_query, kv, sums)
        return carry

    lax.fori_loop(0, MEMBERS // 2, two, 0)

    def stored(line):
        rows = pl.ds(line * 12, 12)
        return pltpu.make_async_copy(packed.at[rows], grad_kv.at[rows], sems.at[line])

    def store(line, carry):
        for tile in range(12):
            total = pack_tile(sums[line * 16 + tile], sums[line * 16 + 12 + tile // 3], tile % 3)
            packed[line * 12 + tile] = total.astype(BF16)
        stored(line).start()
        return carry

    lax.fori_loop(0, 16, store, 0)
    for line in range(16):
        stored(line).wait()


def attend_back_block(block, lineage, query, live, grad, attended, log_rows, grad_query, kv, sums):
    across, down_first = (((1,), (1,)), ((), ())), (((0,), (0,)), ((), ()))
    queries = query[block]
    grads = jnp.concatenate([grad[block, :, :LANES], grad[block, :, LANES:]], axis=0)
    outs = jnp.concatenate([attended[block, :, :LANES], attended[block, :, LANES:]], axis=0)
    product = grads.astype(F32) * outs.astype(F32)
    high = product.astype(BF16)
    low = (product - high.astype(F32)).astype(BF16)
    ones = jnp.ones((8, LANES), BF16)
    inner = lax.dot_general(ones, high, across, preferred_element_type=F32)
    inner = (inner + lax.dot_general(ones, low, across, preferred_element_type=F32))[:1]
    logs = log_rows[block, :1]
    limit = count_ancestors(lineage, block)
    u = lax.broadcasted_iota(jnp.int32, (BLOCK, 2 * BLOCK), 0)
    t = lax.broadcasted_iota(jnp.int32, (BLOCK, 2 * BLOCK), 1) % BLOCK
    alive = jnp.transpose(jnp.broadcast_to(live[block], (BLOCK, BLOCK)))
    alive = jnp.concatenate([alive, alive], axis=1)
    own = jnp.logical_and(u <= t, jnp.logical_or(alive > 0.5, u == t))
    turned = jnp.zeros((LANES, 2 * BLOCK), F32)
    for step in range(0, DEPTH, 2):
        units = []
        for node in (lineage[block, step], lineage[block, step + 1]):
            safe = jnp.maximum(node, 0)
            at, member = lax.div(safe, 8) * 16, lax.rem(safe, 8)
            units.append((node, at + key_unit(member), at + value_unit(member)))
        keys = jnp.concatenate([kv[unit[1]] for unit in units], axis=0)
        values = jnp.concatenate([kv[unit[2]] for unit in units], axis=0)
        scores = lax.dot_general(keys, queries, across, preferred_element_type=F32) * SCALE
        near, far = scores[:BLOCK], scores[BLOCK:]
        if step == 0:
            near = jnp.where(own, jnp.exp(jnp.where(own, near - logs, NEGATIVE)), 0.0)
        else:
            near = jnp.exp(near + (jnp.where(step < limit, 0.0, NEGATIVE) - logs))
        far = jnp.exp(far + (jnp.where(step + 1 < limit, 0.0, NEGATIVE) - logs))
        chances = jnp.concatenate([near, far], axis=0)
        grad_chances = lax.dot_general(values, grads, across, preferred_element_type=F32)
        grad_scores = (chances * (grad_chances - inner)).astype(BF16)
        grad_keys = jnp.dot(grad_scores, queries, preferred_element_type=F32) * SCALE
        grad_values = jnp.dot(chances.astype(BF16), grads, preferred_element_type=F32)
        for part, (node, at_key, at_value) in enumerate(units):
            rows = slice(part * BLOCK, (part + 1) * BLOCK)
            sums[jnp.where(node >= 0, at_key, 256)] += grad_keys[rows]
            sums[jnp.where(node >= 0, at_value, 256)] += grad_values[rows]
        turned = turned + lax.dot_general(keys, grad_scores, down_first, preferred_element_type=F32)
    grad_query[block] = jnp.transpose(turned) * SCALE


def attend_back(lineage, query, kv, live, grad, attended, log_rows):
    vmem = pltpu.VMEM
    return pl.pallas_call(
        attend_back_kernel,
        in_specs=[pl.BlockSpec(memory_space=pltpu.SMEM)] + [INVMEM] * 5 + [ANY],
        out_specs=(INVMEM, ANY),
        out_shape=(
            jax.ShapeDtypeStruct((MEMBERS, 2 * BLOCK, LANES), F32),
            jax.ShapeDtypeStruct((192, BLOCK, LANES), BF16),
        ),
        scratch_shapes=[
            vmem((256, BLOCK, LANES), BF16),
            vmem((257, BLOCK, LANES), F32),
            vmem((192, BLOCK, LANES), BF16),
            pltpu.SemaphoreType.DMA((17,)),
        ],
        compiler_params=pltpu.CompilerParams(vmem_limit_bytes=VMEM_BYTES),
        name="attend_back",
    )(lineage, query, live, grad, attended, log_rows, kv)


def gain_tiles(rows):
    lane = lane_of((8, LANES))
    tiles = [rows[:, tile * LANES : (tile + 1) * LANES] for tile in range(12)]
    pieces = []
    for piece in range(16):
        tile, skip = divmod(piece * 96, LANES)
        low = pltpu.roll(tiles[tile], (LANES - skip) % LANES, 1)
        high = pltpu.roll(tiles[min(tile + 1, 11)], (LANES - skip) % LANES, 1)
        pieces.append(jnp.where(lane < LANES - skip, low, high))
    return pieces


def ending_kernel(
    lineage, grad_query, table, stream_all, w_attn, gain, gain_two, stream, middle, grad_middle,
    feed_lines, wide_lines, kv_terms, down_terms, out_terms,
    mixed_out, stream_grad, query_grad, key_grad, value_grad, out_grad, gain_one, gain_two_out, rms_out,
    gate_grad, up_grad, down_grad,
    feed_second, wide_second, feed_tall, feed_dealt, feed_in, attn_grad, out_in, normed, raw, units, grad_terms, crossed_in, near_in, far_in, query_terms, pair_terms, attn_tall, attn_dealt,
    out_tall, out_dealt, out_mine, out_crossed, gain_terms, gain_in, gain_line, gain_in_two, gain_in_three,
    *scratch,
):
    xyzc = x, y, z, c = spot()
    j = z * 2 + c
    down_scratch, kv_scratch, query_scratch, pair_scratch, out_scratch = (
        scratch[:5], scratch[5:13], scratch[13:18], scratch[18:23], scratch[23:28]
    )
    send_sems, recv_sems, local_sem = scratch[28:]
    wire = Wire(send_sems, recv_sems)
    group = [group_peer(x, y, z, c, k) for k in range(1, MEMBERS)]
    peers = group + axis_peers(x, y, z, c, True)
    announce(peers)
    await_peers(peers)
    sibling = device_of(x, y, z, 1 - c)
    pairs = PlaneScatter(wire, kv_terms, Units(), kv_scratch, xyzc)
    pairs.first()
    attn_tall[96:] = jnp.zeros((8, 512), F32)
    feed_tall[96:] = jnp.zeros((8, 1024), F32)
    out_tall[96:] = jnp.zeros((8, 768), F32)

    def norm_rows(step, carry):
        rows = pl.ds(pl.multiple_of(step * BLOCK, BLOCK), BLOCK)
        wide = stream_all[rows].astype(F32)
        rms = jnp.sqrt(jnp.mean(wide * wide, axis=1, keepdims=True) + EPSILON)
        normed[rows] = (wide * (1.0 / rms) * gain[0:1]).astype(BF16)
        return carry

    lax.fori_loop(0, MEMBERS, norm_rows, 0)

    def turn(block, v):
        depth = count_ancestors(lineage, block) - 1
        cos, sin = turning(table[depth])
        return (v * cos - swap_halves(v) * sin).astype(BF16)

    def query_rows(block, carry):
        rows = pl.ds(pl.multiple_of(block * BLOCK, BLOCK), BLOCK)
        raw[rows, :128] = turn(block, grad_query[block, :BLOCK])
        raw[rows, 128:256] = turn(block, grad_query[block, BLOCK:])
        return carry

    lax.fori_loop(0, MEMBERS, query_rows, 0)
    pairs.relay()
    downs = GroupScatter(wire, down_terms, *down_scratch, xyzc)
    downs.begin()
    own_half = pl.ds(pl.multiple_of(c * 768, 768), 768)
    other_half = pl.ds(pl.multiple_of((1 - c) * 768, 768), 768)
    crossed = wire.send(out_terms.at[:, :, :, other_half], out_crossed, sibling)
    local = pltpu.make_async_copy(out_terms.at[:, :, :, own_half], out_mine, local_sem)
    local.start()

    def weights_back(terms, first):
        def some(step, carry):
            cols = pl.ds(pl.multiple_of(step * 384, 384), 384)
            total = lax.dot_general(
                normed[:, cols], raw[:, first : first + 256], (((0,), (0,)), ((), ())), preferred_element_type=F32
            )
            terms[step] = total.astype(BF16).reshape(4, 96, 256)
            return carry

        lax.fori_loop(0, 4, some, 0)

    weights_back(query_terms, 0)
    query_sums = PlaneScatter(wire, query_terms, Rows(96, 256), query_scratch, xyzc)
    pair_sums = PlaneScatter(wire, pair_terms, Rows(96, 256), pair_scratch, xyzc)
    local.wait()
    crossed.wait_recv()

    def add_halves(step, carry):
        a, b = step // 4, step % 4
        total = out_mine[a, b].astype(F32) + out_crossed[a, b].astype(F32)
        out_mine[a, b] = total.astype(BF16)
        return carry

    lax.fori_loop(0, 16, add_halves, 0)
    outs = PlaneScatter(wire, out_mine, Rows(96, 768), out_scratch, xyzc)
    downs.turn()
    pairs.add_first()
    pairs.second()
    downs.finish(stream_grad)
    mixed_out[...] = (middle[...] + stream_grad[...]).astype(BF16)
    pairs.arrive()
    outs.first()
    query_sums.first()
    for half in range(2):
        units[pl.ds(half * 6, 6)] = pairs.total(half)
    for extra in range(4):
        units[12 + extra] = unpack_extra([units[extra * 3 + k] for k in range(3)])

    def pair_rows(block, carry):
        rows = pl.ds(pl.multiple_of(block * BLOCK, BLOCK), BLOCK)
        raw[rows, 256:384] = turn(block, units[key_unit(block)])
        value = units[value_unit(block)]
        raw[rows, 384:] = jnp.where(lane_of((BLOCK, LANES)) < HEAD_DIM, value, 0.0).astype(BF16)
        return carry

    lax.fori_loop(0, MEMBERS, pair_rows, 0)

    grad_rows = RingScatter(wire, grad_terms, crossed_in, near_in, far_in, xyzc)
    gain_terms[...] = jnp.zeros((1, D), F32)

    def rows_back(step):
        rows = pl.ds(pl.multiple_of(grad_rows.place(step) * 256, 256), 256)
        grads = lax.dot_general(raw[rows], w_attn[...], (((1,), (1,)), ((), ())), preferred_element_type=F32)
        grad_rows.put(step, grads.astype(BF16))
        wide = stream_all[rows].astype(F32)
        rms = jnp.sqrt(jnp.mean(wide * wide, axis=1, keepdims=True) + EPSILON)
        gain_terms[...] += jnp.sum(grads * (wide * (1.0 / rms)), axis=0, keepdims=True)

    rows_back(2)
    rows_back(1)
    grad_rows.turn(2)
    rows_back(3)
    grad_rows.turn(1)
    rows_back(0)
    grad_rows.turn(3)
    outs.relay()
    query_sums.relay()
    grad_rows.pass_on(1)
    grad_rows.pass_on(3)
    rows = jnp.concatenate([gain_terms[...], gain_two[...], jnp.zeros((6, D), F32)], axis=0)
    for piece, part in enumerate(gain_tiles(rows)):
        gain_in[piece // 4, piece % 4] = part
    gains = [
        wire.send(gain_in.at[(x + k) % 4], gain_line.at[k], device_of(x + k, y, z, c)) for k in range(1, 4)
    ]

    weights_back(pair_terms, 256)
    pair_sums.first()
    for copy in gains:
        copy.wait_recv()
    gain_line[0] = gain_in[x] + gain_line[1] + gain_line[2] + gain_line[3]
    gains = [
        wire.send(gain_line.at[0, (y + k) % 4], gain_in_two.at[k], device_of(x, y + k, z, c)) for k in range(1, 4)
    ]
    outs.add_first()
    outs.second()
    query_sums.add_first()
    query_sums.second()
    pair_sums.relay()
    outs.arrive()
    for half in range(2):
        out_tall[pl.ds(half * 48, 48)] = outs.total(half)
    split_rows(out_tall, out_dealt)
    out_in[j] = out_dealt[j]
    dealt = [
        wire.send(out_dealt.at[(j + k) % MEMBERS], out_in.at[j], group[k - 1]) for k in range(1, MEMBERS)
    ]
    pair_sums.add_first()
    pair_sums.second()
    feeds = SecondRound(wire, feed_lines, feed_second, xyzc)
    wides = SecondRound(wire, wide_lines, wide_second, xyzc)
    feeds.second()
    wides.second()

    wide = stream[...].astype(F32)
    rms = jnp.sqrt(jnp.mean(wide * wide, axis=1, keepdims=True) + EPSILON)
    rms_out[...] = jnp.transpose(jnp.broadcast_to(rms, (BLOCK, LANES)))[:1]
    scaled = wide / rms
    weighted = grad_rows.total() * gain[0:1]
    back = (weighted - scaled * jnp.mean(weighted * scaled, axis=1, keepdims=True)) / rms
    stream_grad[...] = grad_middle[...] + back

    for copy in gains:
        copy.wait_recv()
    gain_in_three[j] = gain_line[0, y] + gain_in_two[1] + gain_in_two[2] + gain_in_two[3]
    gains = [
        wire.send(gain_in_three.at[j], gain_in_three.at[j], group[k - 1]) for k in range(1, MEMBERS)
    ]
    query_sums.arrive()
    pair_sums.arrive()
    for half in range(2):
        attn_tall[pl.ds(half * 48, 48), :256] = query_sums.total(half)
        attn_tall[pl.ds(half * 48, 48), 256:] = pair_sums.total(half)
    split_rows(attn_tall, attn_dealt)
    attn_grad[j] = attn_dealt[j]
    dealt += [
        wire.send(attn_dealt.at[(j + k) % MEMBERS], attn_grad.at[j], group[k - 1]) for k in range(1, MEMBERS)
    ]
    feeds.arrive()
    for half in range(2):
        feed_tall[pl.ds(half * 48, 48)] = feeds.total(half)
    split_rows(feed_tall, feed_dealt)
    feed_in[j] = feed_dealt[j]
    feed_copies = [
        wire.send(feed_dealt.at[(j + k) % MEMBERS], feed_in.at[j], group[k - 1]) for k in range(1, MEMBERS)
    ]
    wides.arrive()
    for half in range(2):
        down_grad[pl.ds(half * 16, 16)] = wides.total(half)
    for copy in gains:
        copy.wait_recv()
    total = gain_in_three[0]
    for member in range(1, MEMBERS):
        total = total + gain_in_three[member]
    own = pltpu.roll(total, (LANES - 12 * j) % LANES, 1)
    gain_one[...] = own[:1, :12]
    gain_two_out[...] = own[1:2, :12]
    for copy in dealt:
        copy.wait_recv()
    for core in range(2):
        total = out_in[core].astype(F32)
        for place in range(1, 4):
            total = total + out_in[place * 2 + core].astype(F32)
        out_grad[:, core * 768 : (core + 1) * 768] = total[:12]

    def tile_of(member, tile):
        return attn_grad[member, :, tile * LANES : (tile + 1) * LANES].astype(F32)

    for grad, pieces in (
        (query_grad, [tile_of(head // 2, head % 2) for head in range(HEADS)]),
        (key_grad, [tile_of(member, 2) for member in range(MEMBERS)]),
        (value_grad, [tile_of(member, 3) for member in range(MEMBERS)]),
    ):
        for tile, value in enumerate(join_heads(pieces)):
            grad[:, tile * LANES : (tile + 1) * LANES] = value[:12]
    for copy in feed_copies:
        copy.wait_recv()
    for grad, first in ((gate_grad, 0), (up_grad, 4)):
        for tile in range(32):
            line = tile // 2
            cols = slice((first + line // 4) * LANES, (first + line // 4 + 1) * LANES)
            parts = [(feed_in[4 * (tile % 2) + i, :, cols].astype(F32), line % 4) for i in range(4)]
            grad[:, tile * LANES : (tile + 1) * LANES] = mix_groups(parts)[:12]
    wire.close()
    grad_rows.close()


def ending(
    lineage, grad_query, table, stream_all, w_attn, gain, gain_two, stream, middle, grad_middle,
    feed_lines, wide_lines, kv_terms, down_terms, out_terms,
):
    shape, vmem = jax.ShapeDtypeStruct, pltpu.VMEM
    smem = pl.BlockSpec(memory_space=pltpu.SMEM)
    return communicate(
        ending_kernel,
        (
            shape((BLOCK, D), BF16),
            shape((BLOCK, D), F32),
            shape((12, D), F32),
            shape((12, 768), F32),
            shape((12, 768), F32),
            shape((12, D), F32),
            shape((1, 12), F32),
            shape((1, 12), F32),
            shape((1, LANES), F32),
            shape((12, FF), F32),
            shape((12, FF), F32),
            shape((32, D), F32),
        ),
        [smem] + [INVMEM] * 11 + [ANY] * 3,
        (INVMEM,) * 12,
        [
            vmem((2, 3, 48, 1024), BF16),
            vmem((2, 3, 16, D), BF16),
            vmem((104, 1024), F32),
            vmem((MEMBERS, 16, 1024), BF16),
            vmem((MEMBERS, 16, 1024), BF16),
            vmem((MEMBERS, 16, 512), BF16),
            vmem((MEMBERS, 16, 768), BF16),
            vmem((MEMBERS * BLOCK, D), BF16),
            vmem((MEMBERS * BLOCK, 512), BF16),
            vmem((16, BLOCK, LANES), F32),
            vmem((4, 2, 12, BLOCK, LANES), BF16),
        ]
        + [
            vmem((4, 12, BLOCK, LANES), BF16),
            vmem((2, 12, BLOCK, LANES), BF16),
            vmem((2, 6, BLOCK, LANES), BF16),
        ]
        + [
            vmem((4, 4, 96, 256), BF16),
            vmem((4, 4, 96, 256), BF16),
            vmem((104, 512), F32),
            vmem((MEMBERS, 16, 512), BF16),
            vmem((104, 768), F32),
            vmem((MEMBERS, 16, 768), BF16),
            vmem((4, 4, 96, 768), BF16),
            vmem((4, 4, 96, 768), BF16),
            vmem((1, D), F32),
            vmem((4, 4, 8, LANES), F32),
            vmem((4, 4, 8, LANES), F32),
            vmem((4, 8, LANES), F32),
            vmem((MEMBERS, 8, LANES), F32),
        ]
        + group_scatter_scratch()
        + scatter_scratch(Units(), room=True)
        + scatter_scratch(Rows(96, 256))
        + scatter_scratch(Rows(96, 256))
        + scatter_scratch(Rows(96, 768))
        + wire_scratch(140)
        + [pltpu.SemaphoreType.DMA],
        7,
        "ending",
        62 * 2**20,
    )(
        lineage, grad_query, table, stream_all, w_attn, gain, gain_two, stream, middle, grad_middle,
        feed_lines, wide_lines, kv_terms, down_terms, out_terms,
    )


def hand_over_kernel(*refs):
    count = len(refs) // 2
    for source, target in zip(refs[:count], refs[count:]):
        target[...] = source[...]


def hand_over(*arrays):
    return pl.pallas_call(
        hand_over_kernel,
        out_shape=tuple(jax.ShapeDtypeStruct(array.shape, array.dtype) for array in arrays),
        in_specs=[INVMEM] * len(arrays),
        out_specs=(INVMEM,) * len(arrays),
        compiler_params=pltpu.CompilerParams(vmem_limit_bytes=VMEM_BYTES),
        name="hand_over",
    )(*arrays)


def shards(
    stream, attn_gain, w_query, w_key, w_value, w_out, mlp_gain, w_gate, w_up, w_down, parent, live_mask, cotangent
):
    table = rope_table()
    small_rows = jnp.pad(jnp.stack([attn_gain, mlp_gain]).astype(F32), ((0, 6), (0, LANES - attn_gain.shape[0])))
    (
        lineage, live, gains, query, stream_all, w_attn, context, middle, branch_rms, grad_middle, grad_heads,
        down_terms, feed_lines, wide_lines, out_terms, gain_two_terms, attended, log_rows,
    ) = start(
        parent, table, stream, w_query, w_key, w_value, w_gate, w_up, w_out, small_rows,
        live_mask.reshape(1, BLOCK), cotangent, w_down,
    )
    grad_query, context_terms = attend_back(
        lineage, query, context.reshape(256, BLOCK, LANES), live, grad_heads, attended, log_rows
    )
    (
        mixed_out, stream_grad, query_grad, key_grad, value_grad, out_grad, gain_one, gain_two, stream_rms,
        gate_grad, up_grad, down_grad,
    ) = ending(
        lineage, grad_query, table, stream_all.reshape(MEMBERS * BLOCK, D), w_attn.reshape(D, 512), gains,
        gain_two_terms, stream, middle, grad_middle, feed_lines, wide_lines,
        context_terms.reshape(4, 4, 12, BLOCK, LANES), down_terms, out_terms,
    )
    (
        mixed_out, stream_grad, gain_one, query_grad, key_grad, value_grad, out_grad, gain_two,
        gate_grad, up_grad, down_grad, stream_rms, branch_rms,
    ) = hand_over(
        mixed_out, stream_grad, gain_one, query_grad, key_grad, value_grad, out_grad, gain_two,
        gate_grad, up_grad, down_grad, stream_rms, branch_rms,
    )
    return (
        mixed_out, stream_grad, gain_one[0], query_grad, key_grad, value_grad, out_grad, gain_two[0],
        gate_grad, up_grad, down_grad, stream_rms[0], branch_rms[0],
    )


def solution(mesh):
    rows, line = P("dev", None), P("dev")
    return jax.shard_map(
        shards,
        mesh=mesh,
        in_specs=(rows, line, rows, rows, rows, rows, line, rows, rows, rows, P(), line, rows),
        out_specs=(rows, rows, line, rows, rows, rows, rows, line, rows, rows, rows, line, line),
        check_vma=False,
    )
```

```python
import functools

import jax
import jax.numpy as jnp
import numpy as np
from jax import lax
from jax.experimental import pallas as pl
from jax.experimental.pallas import tpu as pltpu
from jax.sharding import PartitionSpec as P

HEADS = 16
KV_HEADS = 8
HEAD_DIM = 96
BLOCK = 128
DEPTH = 10
D = 1536
FF = 4096
MEMBERS = 8
LANES = 128

EPSILON = 1e-05
ROPE_BASE = 100000.0
NEGATIVE = -1e30
SCALE = HEAD_DIM ** (-0.5)
MESH = pl.DeviceIdType.MESH
BF16 = jnp.bfloat16
F32 = jnp.float32
VMEM_BYTES = 56 * 2**20


def spot():
    me = lax.axis_index("dev")
    return me // 32, (me // 8) % 4, (me // 2) % 4, me % 2


def device_of(x, y, z, c):
    return ((x % 4) * 4 + (y % 4)) * 8 + (z % 4) * 2 + c


def announce(peers):
    barrier = pltpu.get_barrier_semaphore()
    for peer in peers:
        pl.semaphore_signal(barrier, inc=1, device_id=(peer,), device_id_type=MESH)


def await_peers(peers):
    pl.semaphore_wait(pltpu.get_barrier_semaphore(), len(peers))


def axis_peers(x, y, z, c, far):
    steps = (1, 2, 3) if far else (1, 3)
    return [device_of(x + k, y, z, c) for k in steps] + [device_of(x, y + k, z, c) for k in steps]


def group_peer(x, y, z, c, k):
    member = (z * 2 + c + k) % MEMBERS
    return (x * 4 + y) * MEMBERS + member


class Wire:
    def __init__(self, send_sems, recv_sems):
        self.send_sems = send_sems
        self.recv_sems = recv_sems
        self.used = 0
        self.open = []

    def reserve(self, count):
        self.used += count
        return self.used - count

    def make(self, slot, source, target, peer):
        return pltpu.make_async_remote_copy(
            src_ref=source,
            dst_ref=target,
            send_sem=self.send_sems.at[slot],
            recv_sem=self.recv_sems.at[slot],
            device_id=(peer,),
            device_id_type=MESH,
        )

    def send(self, source, target, peer):
        copy = self.make(self.reserve(1), source, target, peer)
        copy.start()
        self.open.append(copy)
        return copy

    def close(self):
        for copy in self.open:
            copy.wait_send()
        self.open = []


class Ring:
    def __init__(self, wire, own, part, place, up, down):
        self.wire, self.own, self.part = wire, own, part
        self.place, self.up, self.down = place, up, down

    def begin(self):
        send, part, place = self.wire.send, self.part, self.place
        self.low_up = send(self.own(0), part(place, 0), self.up)
        self.high_down = send(self.own(1), part(place, 1), self.down)
        self.high_up = send(self.own(1), part(place, 1), self.up)
        self.low_down = send(self.own(0), part(place, 0), self.down)

    def relay(self):
        before, after = (self.place + 3) % 4, (self.place + 1) % 4
        self.low_up.wait_recv()
        self.far_up = self.wire.send(self.part(before, 0), self.part(before, 0), self.up)
        self.high_down.wait_recv()
        self.far_down = self.wire.send(self.part(after, 1), self.part(after, 1), self.down)

    def near(self):
        self.high_up.wait_recv()
        self.low_down.wait_recv()

    def far(self):
        self.far_up.wait_recv()
        self.far_down.wait_recv()


class PlaneGather:
    def __init__(self, wire, own, out, cut, xyzc):
        self.wire, self.own, self.out, self.cut = wire, own, out, cut
        x, y, z, c = xyzc
        self.x, self.y = x, y
        self.x_up, self.x_down = device_of(x + 1, y, z, c), device_of(x + 3, y, z, c)
        self.y_up, self.y_down = device_of(x, y + 1, z, c), device_of(x, y + 3, z, c)

    def pair(self, one_own, one_part, two_own, two_part, one_on_x):
        on_x = (self.x, self.x_up, self.x_down)
        on_y = (self.y, self.y_up, self.y_down)
        cut = self.cut.quarter
        self.one = Ring(
            self.wire,
            lambda side: one_own(cut(0, side)),
            lambda place, side: one_part(place, cut(0, side)),
            *(on_x if one_on_x else on_y),
        )
        self.two = Ring(
            self.wire,
            lambda side: two_own(cut(1, side)),
            lambda place, side: two_part(place, cut(1, side)),
            *(on_y if one_on_x else on_x),
        )
        self.one.begin()
        self.two.begin()

    def first(self):
        own, out, x, y = self.own, self.out, self.x, self.y
        self.pair(
            lambda q: own.at[q],
            lambda place, q: out.at[(place, y) + q],
            lambda q: own.at[q],
            lambda place, q: out.at[(x, place) + q],
            True,
        )

    def relay(self):
        self.one.relay()
        self.two.relay()

    def near(self):
        self.one.near()
        self.two.near()

    def far(self):
        self.one.far()
        self.two.far()

    def settle(self):
        self.near()
        self.far()

    def second(self):
        out, x, y = self.out, self.x, self.y
        every = slice(None)
        self.pair(
            lambda q: out.at[(every, y) + q],
            lambda place, q: out.at[(every, place) + q],
            lambda q: out.at[(x, every) + q],
            lambda place, q: out.at[(place, every) + q],
            False,
        )


class Rows:
    def __init__(self, rows, cols, start=0):
        self.rows, self.cols, self.start = rows // 2, cols // 2, start

    def half(self, half):
        return (pl.ds(half * self.rows, self.rows),)

    def side(self, side):
        return (slice(None), pl.ds(side * self.cols, self.cols))

    def quarter(self, half, side):
        first = self.start + side * self.cols
        if not isinstance(first, int):
            first = pl.multiple_of(first, LANES)
        return self.half(half) + (pl.ds(first, self.cols),)

    def shapes(self):
        return (self.rows, 2 * self.cols), (self.rows, self.cols)


class Units:
    def half(self, half):
        return (pl.ds(half * 6, 6),)

    def side(self, side):
        return (pl.ds(side * 3, 3),)

    def quarter(self, half, side):
        return (pl.ds(half * 6 + side * 3, 3),)

    def shapes(self):
        return (6, BLOCK, LANES), (3, BLOCK, LANES)


class GroupGather:
    def __init__(self, wire, own, out, xyzc):
        self.wire, self.own, self.out = wire, own, out
        x, y, z, c = xyzc
        self.z, self.c = z, c
        self.sibling = device_of(x, y, z, 1 - c)
        half = out.shape[2] // 2
        self.ring = Ring(
            wire,
            lambda side: own.at[pl.ds(side * half, half)],
            lambda place, side: out.at[place, c, pl.ds(side * half, half)],
            z, device_of(x, y, z + 1, c), device_of(x, y, z + 3, c),
        )
        self.crossed = []

    def begin(self):
        self.ring.begin()
        self.crossed.append(self.wire.send(self.own, self.out.at[self.z, self.c], self.sibling))

    def cross(self, k):
        piece = self.out.at[(self.z + k) % 4, self.c]
        self.crossed.append(self.wire.send(piece, piece, self.sibling))

    def relay(self):
        self.ring.relay()

    def near(self):
        self.ring.near()
        self.cross(1)
        self.cross(3)

    def far(self):
        self.ring.far()
        self.cross(2)

    def finish(self, after=0):
        for copy in self.crossed[after:]:
            copy.wait_recv()


class SecondRound:
    def __init__(self, wire, summed, second_in, xyzc):
        self.wire, self.summed, self.second_in = wire, summed, second_in
        self.x, self.y, self.z, self.c = xyzc

    def peer(self, along_x, k):
        if along_x:
            return device_of(self.x + k, self.y, self.z, self.c)
        return device_of(self.x, self.y + k, self.z, self.c)

    def place(self, half, k):
        return ((self.x, self.y)[half] + k) % 4

    def second(self):
        self.copies = []
        for k in (2, 1, 3):
            for half in range(2):
                self.copies.append(
                    self.wire.send(
                        self.summed.at[half, self.place(1 - half, k)],
                        self.second_in.at[half, k - 1],
                        self.peer(half == 1, k),
                    )
                )

    def total(self, half):
        total = self.summed[half, self.place(1 - half, 0)].astype(F32)
        for k in range(3):
            total = total + self.second_in[half, k].astype(F32)
        return total

    def arrive(self):
        for copy in self.copies:
            copy.wait_recv()


class PlaneScatter(SecondRound):
    def __init__(self, wire, terms, cut, scratch, xyzc):
        *room, self.near_in, self.far_in, self.passed, summed, second_in = scratch
        super().__init__(wire, summed, second_in, xyzc)
        self.terms, self.cut, self.room = terms, cut, room

    def lead(self, half, k, line=slice(None)):
        place = self.place(half, k)
        return (place, line) if half == 0 else (line, place)

    def part(self, half, k, side):
        return self.terms.at[self.lead(half, k) + self.cut.quarter(half, side)]

    def own(self, half, line):
        if self.room:
            return self.room[0][half, line]
        return self.terms[self.lead(half, 0, line) + self.cut.half(half)]

    def edge(self, half, way, line):
        if self.room:
            return self.room[1][half, way, line]
        return self.terms[self.lead(half, (1, 3)[way], line) + self.cut.quarter(half, way)]

    def first(self):
        send = self.wire.send
        self.far, self.plain, self.locals = [], [], []
        if self.room:
            sems = self.room[2]
            for half in range(2):
                pairs = [(self.terms.at[self.lead(half, 0) + self.cut.half(half)], self.room[0].at[half])]
                pairs += [(self.part(half, (1, 3)[way], way), self.room[1].at[half, way]) for way in range(2)]
                for slot, (source, target) in enumerate(pairs):
                    copy = pltpu.make_async_copy(source, target, sems.at[half, slot])
                    copy.start()
                    self.locals.append(copy)
        for half in range(2):
            for way in range(2):
                self.far.append(
                    send(self.part(half, 2, way), self.far_in.at[half, way], self.peer(half == 0, (1, 3)[way]))
                )
        for half in range(2):
            for way in range(2):
                k = (1, 3)[way]
                landing = self.near_in.at[(half, way, slice(None)) + self.cut.side(1 - way)]
                self.plain.append(send(self.part(half, k, 1 - way), landing, self.peer(half == 0, k)))

    def relay(self):
        for copy in self.locals:
            copy.wait()
        self.relayed = []
        for half in range(2):
            for way in range(2):
                self.far[half * 2 + way].wait_recv()

                def add(line, carry):
                    total = self.edge(half, way, line).astype(F32) + self.far_in[half, way, line].astype(F32)
                    self.passed[half, way, line] = total.astype(BF16)
                    return carry

                lax.fori_loop(0, 4, add, 0)
                landing = self.near_in.at[(half, way, slice(None)) + self.cut.side(way)]
                self.relayed.append(
                    self.wire.send(self.passed.at[half, way], landing, self.peer(half == 0, (1, 3)[way]))
                )

    def add_first(self):
        for copy in self.plain + self.relayed:
            copy.wait_recv()
        for half in range(2):

            def body(line, carry):
                total = self.own(half, line).astype(F32)
                for way in range(2):
                    total = total + self.near_in[half, way, line].astype(F32)
                self.summed[half, line] = total.astype(BF16)
                return carry

            lax.fori_loop(0, 4, body, 0)


def scatter_scratch(cut, room=False):
    half, part = cut.shapes()
    vmem = pltpu.VMEM
    held = [vmem((2, 4) + half, BF16), vmem((2, 2, 4) + part, BF16), pltpu.SemaphoreType.DMA((2, 3))]
    return (held if room else []) + [
        vmem((2, 2, 4) + half, BF16),
        vmem((2, 2, 4) + part, BF16),
        vmem((2, 2, 4) + part, BF16),
        vmem((2, 4) + half, BF16),
        vmem((2, 3) + half, BF16),
    ]


class GroupScatter:
    def __init__(self, wire, terms, mine, crossed_in, summed, ring_in, local_sem, xyzc):
        self.wire, self.terms = wire, terms
        self.mine, self.crossed_in, self.summed, self.ring_in = mine, crossed_in, summed, ring_in
        self.x, self.y, self.z, self.c = xyzc
        self.local_sem = local_sem

    def begin(self):
        self.local = pltpu.make_async_copy(self.terms.at[:, self.c], self.mine, self.local_sem)
        self.local.start()
        sibling = device_of(self.x, self.y, self.z, 1 - self.c)
        self.crossed = {}
        for k in (2, 1, 3, 0):
            place = (self.z + k) % 4
            self.crossed[k] = self.wire.send(
                self.terms.at[place, 1 - self.c], self.crossed_in.at[place], sibling
            )

    def turn(self):
        self.local.wait()
        self.copies = []
        for k in (2, 1, 3):
            place = (self.z + k) % 4
            self.crossed[k].wait_recv()

            def body(tile, carry):
                total = self.mine[place, tile].astype(F32) + self.crossed_in[place, tile].astype(F32)
                self.summed[place, tile] = total.astype(BF16)
                return carry

            lax.fori_loop(0, 12, body, 0)
            self.copies.append(
                self.wire.send(
                    self.summed.at[place],
                    self.ring_in.at[k - 1],
                    device_of(self.x, self.y, self.z + k, self.c),
                )
            )

    def finish(self, out):
        self.crossed[0].wait_recv()
        for copy in self.copies:
            copy.wait_recv()
        for tile in range(12):
            total = self.mine[self.z, tile].astype(F32) + self.crossed_in[self.z, tile].astype(F32)
            for k in range(3):
                total = total + self.ring_in[k, tile].astype(F32)
            out[:, tile * LANES : (tile + 1) * LANES] = total


class ChipScatter:
    def __init__(self, wire, terms, at, crossed_in, ring_in, xyzc):
        self.wire, self.terms, self.at = wire, terms, at
        self.crossed_in, self.ring_in = crossed_in, ring_in
        self.x, self.y, self.z, self.c = xyzc
        self.crossed_slot, self.ring_slot = wire.reserve(4), wire.reserve(3)
        self.all_tiles = pl.ds(0, 12)

    def place(self, step):
        return (self.z + step) % 4

    def crossed(self, step):
        place = self.place(step)
        return self.wire.make(
            self.crossed_slot + step,
            self.terms.at[place, self.at + 1 - self.c, self.all_tiles],
            self.crossed_in.at[place],
            device_of(self.x, self.y, self.z, 1 - self.c),
        )

    def ring(self, step):
        return self.wire.make(
            self.ring_slot + step - 1,
            self.terms.at[self.place(step), self.at + self.c, self.all_tiles],
            self.ring_in.at[step - 1],
            device_of(self.x, self.y, self.z + step, self.c),
        )

    def put(self, step, grads):
        place = self.place(step)
        for core in range(2):
            for tile in range(12):
                self.terms[place, self.at + core, tile] = grads[
                    core * BLOCK : (core + 1) * BLOCK, tile * LANES : (tile + 1) * LANES
                ]
        self.crossed(step).start()

    def turn(self, step):
        place, line = self.place(step), self.at + self.c
        self.crossed(step).wait_recv()

        def add(tile, carry):
            total = self.terms[place, line, tile].astype(F32) + self.crossed_in[place, tile].astype(F32)
            self.terms[place, line, tile] = total.astype(BF16)
            return carry

        lax.fori_loop(0, 12, add, 0)
        self.ring(step).start()

    def total(self):
        self.crossed(0).wait_recv()
        for step in range(1, 4):
            self.ring(step).wait_recv()
        tiles = []
        for tile in range(12):
            total = self.terms[self.z, self.at + self.c, tile].astype(F32)
            total = total + self.crossed_in[self.z, tile].astype(F32)
            for step in range(3):
                total = total + self.ring_in[step, tile].astype(F32)
            tiles.append(total)
        return jnp.concatenate(tiles, axis=1)

    def close(self):
        for step in range(4):
            self.crossed(step).wait_send()
        for step in range(1, 4):
            self.ring(step).wait_send()


class RingScatter(ChipScatter):
    def __init__(self, wire, terms, crossed_in, near_in, far_in, xyzc):
        super().__init__(wire, terms, 0, crossed_in, None, xyzc)
        self.near_in, self.far_in = near_in, far_in
        self.moved = []

    def sum_tiles(self, place, tiles, extra=None):
        def add(tile, carry):
            total = self.terms[place, self.c, tile].astype(F32)
            if extra is None:
                total = total + self.crossed_in[place, tile].astype(F32)
            else:
                total = total + self.far_in[extra, tile - extra * 6].astype(F32)
            self.terms[place, self.c, tile] = total.astype(BF16)
            return carry

        lax.fori_loop(*tiles, add, 0)

    def move(self, place, first, landing, k):
        source = self.terms.at[place, self.c, pl.ds(first, 6)]
        copy = self.wire.send(source, landing, device_of(self.x, self.y, self.z + k, self.c))
        self.moved.append(copy)
        return copy

    def turn(self, step):
        place = self.place(step)
        self.crossed(step).wait_recv()
        self.sum_tiles(place, (0, 12))
        if step == 2:
            self.far = [self.move(place, 6 * way, self.far_in.at[way], (1, 3)[way]) for way in range(2)]
        else:
            way = (1, 3).index(step)
            plain = 6 * (1 - way)
            self.move(place, plain, self.near_in.at[way, pl.ds(plain, 6)], step)

    def pass_on(self, step):
        way = (1, 3).index(step)
        place = self.place(step)
        self.far[way].wait_recv()
        self.sum_tiles(place, (6 * way, 6 * way + 6), way)
        self.move(place, 6 * way, self.near_in.at[way, pl.ds(6 * way, 6)], step)

    def total(self):
        self.crossed(0).wait_recv()
        for copy in self.moved[2:]:
            copy.wait_recv()
        tiles = []
        for tile in range(12):
            total = self.terms[self.z, self.c, tile].astype(F32) + self.crossed_in[self.z, tile].astype(F32)
            for way in range(2):
                total = total + self.near_in[way, tile].astype(F32)
            tiles.append(total)
        return jnp.concatenate(tiles, axis=1)

    def close(self):
        for step in range(4):
            self.crossed(step).wait_send()


def group_scatter_scratch():
    return [
        pltpu.VMEM((4, 12, BLOCK, LANES), BF16),
        pltpu.VMEM((4, 12, BLOCK, LANES), BF16),
        pltpu.VMEM((4, 12, BLOCK, LANES), BF16),
        pltpu.VMEM((3, 12, BLOCK, LANES), BF16),
        pltpu.SemaphoreType.DMA,
    ]


def chip_scatter_scratch():
    return [pltpu.VMEM((4, 12, BLOCK, LANES), BF16), pltpu.VMEM((3, 12, BLOCK, LANES), BF16)]


def wire_scratch(count):
    return [pltpu.SemaphoreType.DMA((count,)), pltpu.SemaphoreType.DMA((count,))]


ANY = pl.BlockSpec(memory_space=pl.ANY)
INVMEM = pl.BlockSpec(memory_space=pltpu.VMEM)


def communicate(kernel, out_shapes, in_specs, out_specs, scratch, ident, name, vmem=VMEM_BYTES):
    return pl.pallas_call(
        kernel,
        out_shape=out_shapes,
        in_specs=in_specs,
        out_specs=out_specs,
        scratch_shapes=scratch,
        compiler_params=pltpu.CompilerParams(
            collective_id=ident, has_side_effects=True, vmem_limit_bytes=vmem
        ),
        name=name,
    )


def key_unit(member):
    return member + jnp.where(member >= 6, 6, 0) + jnp.where(member >= 7, 1, 0)


def value_unit(member):
    return member + 6 + jnp.where(member >= 6, 1, 0) + jnp.where(member >= 7, 1, 0)


def gain_rows(pieces):
    return jnp.concatenate(join_heads(pieces), axis=1)


def head_window(tiles, head):
    tile, skip = divmod(head * HEAD_DIM, LANES)
    lane = lane_of(tiles[0].shape)
    window = pltpu.roll(tiles[tile], (LANES - skip) % LANES, 1)
    if skip + HEAD_DIM > LANES:
        window = jnp.where(lane < LANES - skip, window, pltpu.roll(tiles[tile + 1], LANES - skip, 1))
    return jnp.where(lane < HEAD_DIM, window, 0.0)


def join_heads(pieces):
    lane = lane_of(pieces[0].shape)
    tiles = []
    for tile in range(len(pieces) * 3 // 4):
        piece, skip = divmod(tile * LANES, HEAD_DIM)
        low = pltpu.roll(pieces[piece], (LANES - skip) % LANES, 1)
        high = pltpu.roll(pieces[piece + 1], HEAD_DIM - skip, 1)
        tiles.append(jnp.where(lane < HEAD_DIM - skip, low, high))
    return tiles


def mix_groups(parts):
    group = lane_of(parts[0][0].shape) // 32
    mixed = None
    for i, (tile, g) in enumerate(parts):
        turned = pltpu.roll(tile, (32 * (i - g)) % LANES, 1)
        mixed = turned if mixed is None else jnp.where(group == i, turned, mixed)
    return mixed


def lane_of(shape):
    return lax.broadcasted_iota(jnp.int32, shape, len(shape) - 1)


def pack_tile(unit, extra, place):
    return jnp.where(lane_of(unit.shape) < HEAD_DIM, unit, pltpu.roll(extra, (96 - 32 * place) % LANES, 1))


def unpack_extra(tiles):
    lane = lane_of(tiles[0].shape)
    extra = jnp.where(lane < 32, pltpu.roll(tiles[0], 32, 1), 0.0)
    extra = jnp.where(jnp.logical_and(lane >= 32, lane < 64), pltpu.roll(tiles[1], 64, 1), extra)
    return jnp.where(jnp.logical_and(lane >= 64, lane < 96), pltpu.roll(tiles[2], 96, 1), extra)


def swap_halves(rows):
    lane = lane_of(rows.shape)
    return jnp.where(lane < HEAD_DIM // 2, pltpu.roll(rows, LANES - 48, 1), pltpu.roll(rows, 48, 1))


def rope_table():
    half = HEAD_DIM // 2
    frequency = ROPE_BASE ** (-2.0 * np.arange(half, dtype=np.float64) / HEAD_DIM)
    frequency = frequency.astype(np.float32)
    places = np.arange(DEPTH * BLOCK, dtype=np.float32)
    angles = (places[:, None] * frequency[None, :]).astype(np.float64)
    table = np.zeros((DEPTH * BLOCK, LANES), np.float32)
    table[:, :half] = np.cos(angles)
    table[:, half:HEAD_DIM] = np.sin(angles)
    return jnp.asarray(table.reshape(DEPTH, BLOCK, LANES))


def turning(table):
    lane = lane_of(table.shape)
    cosine = jnp.where(lane < 48, table, pltpu.roll(table, 48, 1))
    sine = jnp.where(lane < 48, -pltpu.roll(table, LANES - 48, 1), jnp.where(lane < HEAD_DIM, table, 0.0))
    return cosine, sine


def count_ancestors(lineage, block):
    count = jnp.int32(0)
    for step in range(DEPTH):
        count = count + jnp.where(lineage[block, step] >= 0, 1, 0)
    return count


def write_lineage(parent, first, lineage):
    def one(block, carry):
        def hop(step, node):
            lineage[block, step] = node
            above = parent[jnp.maximum(node, 0)]
            return jnp.where(node >= 0, above, -1)

        lax.fori_loop(0, DEPTH, hop, first + block)
        return carry

    lax.fori_loop(0, MEMBERS, one, 0)


def attend_block(lineage, block, queries, alive, load, scores):
    limit = count_ancestors(lineage, block)
    t = lax.broadcasted_iota(jnp.int32, (2 * BLOCK, BLOCK), 0) % BLOCK
    u = lax.broadcasted_iota(jnp.int32, (2 * BLOCK, BLOCK), 1)
    own = jnp.logical_and(u <= t, jnp.logical_or(alive > 0.5, u == t))
    nodes = [jnp.maximum(lineage[block, step], 0) for step in range(DEPTH)]
    pairs = range(0, DEPTH, 2)
    highest = None
    for step in pairs:
        keys = jnp.concatenate([load(node, key_unit(lax.rem(node, 8))) for node in nodes[step : step + 2]], axis=0)
        part = lax.dot_general(queries, keys, (((1,), (1,)), ((), ())), preferred_element_type=F32) * SCALE
        near = part[:, :BLOCK]
        if step == 0:
            near = jnp.where(own, near, NEGATIVE)
        else:
            near = near + jnp.where(step < limit, 0.0, NEGATIVE)
        far = part[:, BLOCK:] + jnp.where(step + 1 < limit, 0.0, NEGATIVE)
        scores[step] = near
        scores[step + 1] = far
        both = jnp.maximum(near, far)
        highest = both if step == 0 else jnp.maximum(highest, both)
    largest = jnp.max(highest, axis=1, keepdims=True)
    totals = jnp.zeros((2 * BLOCK, BLOCK), F32)
    attended = jnp.zeros((2 * BLOCK, LANES), F32)
    for step in pairs:
        near, far = jnp.exp(scores[step] - largest), jnp.exp(scores[step + 1] - largest)
        totals = totals + near + far
        values = jnp.concatenate(
            [load(node, value_unit(lax.rem(node, 8))) for node in nodes[step : step + 2]], axis=0
        )
        terms = jnp.concatenate([near.astype(BF16), far.astype(BF16)], axis=1)
        attended = attended + jnp.dot(terms, values, preferred_element_type=F32)
    total = jnp.sum(totals, axis=1, keepdims=True)
    return (attended / total).astype(BF16), largest + jnp.log(total)


def start_kernel(
    parent, table, stream, w_query, w_key, w_value, w_gate, w_up, w_out, small_rows, live_row, cotangent, own_down,
    lineage, live, gains, query, stream_all, attn_all,
    kv_out, middle, rms_out, grad_middle, grads_in, down_terms, feed_lines, wide_lines, out_terms, gain_terms,
    attended_out, log_rows,
    packed, out_low, small, stage, packed_in, out_in, small_in, wide_tall, wide_own, out_own, gain_own, gains_all,
    w_attn, own_kv, kv, w_out_all, w_feed, w_down, mid_all, cot_all, crossed_in, ring_in,
    att_out, att_in, att_pad, grads_out, *scratch,
):
    feed_scratch, wide_scratch = scratch[:5], scratch[5:10]
    send_sems, recv_sems, local_sems = scratch[10:]
    xyzc = x, y, z, c = spot()
    j = z * 2 + c
    base = (x * 4 + y) * MEMBERS
    sibling = device_of(x, y, z, 1 - c)
    wire = Wire(send_sems, recv_sems)
    group = [group_peer(x, y, z, c, k) for k in range(1, MEMBERS)]
    across, down_first = (((1,), (1,)), ((), ())), (((0,), (0,)), ((), ()))
    locals_ = []

    peers = group + axis_peers(x, y, z, c, True)
    announce(peers)

    stage[...] = jnp.zeros((16, FF), F32)
    wide_tall[96:] = jnp.zeros((8, 1536), F32)

    def staged(weights):
        width = weights.shape[1]
        stage[:12, :width] = weights[...].astype(F32)
        return [stage[:, tile * LANES : (tile + 1) * LANES] for tile in range(width // LANES)]

    def put_packed(member, tile, value):
        packed[member, :, tile * LANES : (tile + 1) * LANES] = value.astype(BF16)

    tiles = staged(w_query)
    for head in range(HEADS):
        put_packed(head // 2, head % 2, head_window(tiles, head))
    for place, weights in ((2, w_key), (3, w_value)):
        tiles = staged(weights)
        for member in range(MEMBERS):
            put_packed(member, place, head_window(tiles, member))
    for place, weights in ((4, w_gate), (8, w_up)):
        tiles = staged(weights)
        for member in range(MEMBERS):
            for tile in range(4):
                parts = [(tiles[2 * (4 * tile + i) + member // 4], member % 4) for i in range(4)]
                put_packed(member, place + tile, mix_groups(parts))
    out_low[...] = jnp.concatenate(staged(w_out), axis=1).astype(BF16)
    rows = pltpu.roll(small_rows[...], 12 * j, 1)
    live_rows = jnp.broadcast_to(live_row[...].astype(F32), (8, LANES))
    rows = jnp.where(lax.broadcasted_iota(jnp.int32, (8, LANES), 0) == 2, live_rows, rows)
    small[...] = jnp.concatenate([rows, jnp.zeros((8, LANES), F32)], axis=0).astype(BF16)
    await_peers(peers)

    def keep(source, target):
        copy = pltpu.make_async_copy(source, target, local_sems.at[len(locals_)])
        copy.start()
        locals_.append(copy)
        return copy

    def to_members(source, target):
        return [wire.send(source((j + k) % MEMBERS), target.at[j], group[k - 1]) for k in range(1, MEMBERS)]

    def half_of(member):
        return pl.ds(pl.multiple_of((member % 2) * 768, 768), 768)

    own_half = half_of(c)
    attn_part, feed_part = pl.ds(0, 512), pl.ds(512, 1024)
    attn_dealt = to_members(lambda member: packed.at[member, :, attn_part], packed_in.at[:, :, attn_part])
    small_dealt = to_members(lambda member: small, small_in)
    streams = GroupGather(wire, stream, mid_all, xyzc)
    streams.begin()
    first_kept = (keep(packed.at[j], packed_in.at[j]), keep(small, small_in.at[j]))
    out_kept = keep(out_low.at[:, own_half], out_in.at[j])
    stream_kept = keep(stream, mid_all.at[z, c])
    write_lineage(parent, base, lineage)
    for line in range(16):
        w_out_all[line // 4, line % 4, 96:] = jnp.zeros((32, D), BF16)

    for copy in attn_dealt + small_dealt:
        copy.wait_recv()
    out_dealt = to_members(lambda member: out_low.at[:, half_of(member)], out_in)
    feed_dealt_in = to_members(lambda member: packed.at[member, :, feed_part], packed_in.at[:, :, feed_part])
    for copy in first_kept:
        copy.wait()
    for member in range(MEMBERS):
        wide_tall[pl.ds(member * 12, 12), :512] = packed_in[member, :, :512].astype(F32)[:12]
    wide_own[:, :512] = wide_tall[:96, :512].astype(BF16)
    gain = small_in[0].astype(F32)
    for member in range(MEMBERS):
        row = small_in[member].astype(F32)
        live[member] = row[2:3]
        if member:
            gain = gain + row
    gain_own[...] = gain.astype(BF16)
    own_attn, own_feed = wide_own.at[:, pl.ds(0, 512)], wide_own.at[:, pl.ds(512, 1024)]
    attn = PlaneGather(wire, own_attn, w_attn, Rows(96, 512), xyzc)
    attn.first()
    tiny = [wire.send(gain_own, gains_all.at[x, y], device_of(x + k, y, z, c)) for k in range(1, 4)]
    attn_kept = keep(own_attn, w_attn.at[x, y])
    gain_kept = keep(gain_own, gains_all.at[x, y])
    down_kept = keep(own_down, w_down.at[x, y])

    attn.relay()
    streams.relay()
    gain_kept.wait()
    for copy in tiny:
        copy.wait_recv()
    line = gains_all.at[:, y]
    tiny = [wire.send(line, line, device_of(x, y + k, z, c)) for k in range(1, 4)]
    attn_kept.wait()
    attn.settle()
    attn.second()
    for copy in out_dealt:
        copy.wait_recv()
    out_kept.wait()
    for member in range(MEMBERS):
        wide_tall[pl.ds(member * 12, 12), :768] = out_in[member].astype(F32)[:12]
    out_own[...] = wide_tall[:96, :768].astype(BF16)
    out_kept = keep(out_own, w_out_all.at[x, y, pl.ds(0, 96), own_half])
    out_kept.wait()
    outs = PlaneGather(wire, w_out_all.at[x, y], w_out_all, Rows(96, 768, c * 768), xyzc)
    outs.first()
    for copy in feed_dealt_in:
        copy.wait_recv()
    for member in range(MEMBERS):
        wide_tall[pl.ds(member * 12, 12), 512:] = packed_in[member, :, 512:].astype(F32)[:12]
    wide_own[:, 512:] = wide_tall[:96, 512:].astype(BF16)
    feed_kept = keep(own_feed, w_feed.at[x, y])
    streams.near()
    streams.far()
    attn.relay()
    outs.relay()
    for copy in tiny:
        copy.wait_recv()
    pieces = [gains_all[piece // 4, piece % 4].astype(F32)[:8] for piece in range(16)]
    gains[...] = gain_rows(pieces)
    attn.settle()
    stream_kept.wait()
    streams.finish()
    attn_copied = keep(w_attn, attn_all)
    stream_copied = keep(mid_all, stream_all)

    def project(step, carry):
        wide = mid_all[step].reshape(2 * BLOCK, D).astype(F32)
        rms = jnp.sqrt(jnp.mean(wide * wide, axis=1, keepdims=True) + EPSILON)
        rows = (wide * (1.0 / rms) * gains[0:1]).astype(BF16)
        raw = jnp.dot(rows, w_attn[...].reshape(D, 512), preferred_element_type=F32)
        for part in range(2):
            block = step * 2 + part
            depth = count_ancestors(lineage, block) - 1
            cos, sin = turning(table[depth])

            def turn(head):
                v = raw[part * BLOCK : (part + 1) * BLOCK, head * LANES : (head + 1) * LANES]
                return (v * cos + swap_halves(v) * sin).astype(BF16)

            query[block, :BLOCK] = turn(0)
            query[block, BLOCK:] = turn(1)
            kv[x, y, key_unit(block)] = turn(2)
            kv[x, y, value_unit(block)] = raw[part * BLOCK : (part + 1) * BLOCK, 3 * LANES :].astype(BF16)
        return carry

    lax.fori_loop(0, 2, project, 0)
    outs.settle()
    outs.second()
    lax.fori_loop(2, 4, project, 0)
    for tile in range(12):
        extra = kv[x, y, 12 + tile // 3].astype(F32)
        own_kv[tile] = pack_tile(kv[x, y, tile].astype(F32), extra, tile % 3).astype(BF16)

    pairs = PlaneGather(wire, own_kv, kv, Units(), xyzc)
    pairs.first()
    outs.relay()
    kept = keep(own_kv, kv.at[x, y, pl.ds(0, 12)])
    cotangents = GroupGather(wire, cotangent, cot_all, xyzc)
    cotangents.begin()
    cot_kept = keep(cotangent, cot_all.at[z, c])
    pairs.relay()
    kept.wait()
    outs.settle()
    swap_part = w_out_all.at[:, :, pl.ds(0, 96), own_half]
    swapped = wire.send(swap_part, swap_part, sibling)
    pairs.settle()
    pairs.second()

    def unpack(index, carry):
        k, half, other, extra = index // 16, (index // 8) % 2, (index // 2) % 4, index % 2
        a = half * ((x + k) % 4) + (1 - half) * other
        b = half * other + (1 - half) * ((y + k) % 4)
        extra = extra + 2 * half
        tiles = [kv[a, b, extra * 3 + part].astype(F32) for part in range(3)]
        kv[a, b, 12 + extra] = unpack_extra(tiles).astype(BF16)
        return carry

    lax.fori_loop(0, 16, unpack, 0)
    cotangents.relay()
    cotangents.near()
    cotangents.far()
    pairs.relay()
    early, wire.open = wire.open, []
    feed = PlaneGather(wire, own_feed, w_feed, Rows(96, 1024), xyzc)
    down = PlaneGather(wire, own_down, w_down, Rows(32, D), xyzc)
    feed.first()
    down.first()
    pairs.near()
    lax.fori_loop(16, 32, unpack, 0)
    lax.fori_loop(48, 64, unpack, 0)
    pairs.far()
    lax.fori_loop(32, 48, unpack, 0)
    for copy in early:
        copy.wait_send()
    stream_copied.wait()
    attn_copied.wait()

    kv_copied = keep(kv, kv_out)

    att_slot = wire.reserve(MEMBERS - 1)

    def load(node, unit):
        return kv[lax.div(node, 32), lax.rem(lax.div(node, 8), 4), unit]

    def att_copy(k):
        block = (j + 1 + k) % MEMBERS
        return wire.make(att_slot + k, att_out.at[block], att_in.at[j], base + block)

    def attend_one(k, scores):
        block = (j + 1 + k) % MEMBERS
        attended, logs = attend_block(lineage, block, query[block], live[block], load, scores)
        log_rows[block] = jnp.transpose(jnp.broadcast_to(logs, (2 * BLOCK, LANES)))[:8]
        att_out[block, :, :LANES] = attended[:BLOCK]
        att_out[block, :, LANES:] = attended[BLOCK:]

    def attend_pairs(first, last):
        def both(one, two):
            def each(pair, carry):
                attend_one(2 * pair, one)
                attend_one(2 * pair + 1, two)
                return carry

            lax.fori_loop(first, last, each, 0)

        room = pltpu.VMEM((DEPTH, 2 * BLOCK, LANES), F32)
        pl.run_scoped(both, room, room)

        def give(k, carry):
            att_copy(k).start()
            return carry

        lax.fori_loop(2 * first, min(2 * last, MEMBERS - 1), give, 0)

    attend_pairs(0, 1)
    feed.relay()
    down.relay()
    attend_pairs(1, 2)
    feed_kept.wait()
    down_kept.wait()
    feed.settle()
    feed.second()
    down.settle()
    down.second()
    attend_pairs(2, 4)
    feed.relay()
    down.relay()
    att_in[j] = att_out[j]
    att_copied = keep(att_out, attended_out)
    att_recv = [att_copy(k) for k in range(MEMBERS - 1)]

    for copy in att_recv:
        copy.wait_recv()
    for member in range(MEMBERS):
        att_pad[:, member * 256 : (member + 1) * 256] = att_in[member]
    swapped.wait_recv()

    def project_out(step, carry):
        cols = pl.ds(pl.multiple_of(step * 512, 512), 512)
        weights = w_out_all[:, :, :, cols].reshape(16 * LANES, 512)
        branch = jnp.dot(att_pad[...], weights, preferred_element_type=F32)
        middle[:, cols] = stream[:, cols].astype(F32) + branch
        return carry

    lax.fori_loop(0, 3, project_out, 0)
    rms = jnp.sqrt(jnp.mean(middle[...] * middle[...], axis=1, keepdims=True) + EPSILON)
    rms_out[...] = jnp.transpose(jnp.broadcast_to(rms, (BLOCK, LANES)))[:1]
    mid_all[z, c] = (middle[...] / rms * gains[1:2]).astype(BF16)
    mids = GroupGather(wire, mid_all.at[z, c], mid_all, xyzc)
    mids.begin()
    mids.relay()
    feed.settle()
    down.settle()
    kv_copied.wait()
    cot_kept.wait()
    cotangents.finish()
    for k in range(MEMBERS - 1):
        att_copy(k).wait_send()

    grad_rows = ChipScatter(wire, kv, 2, crossed_in, ring_in, xyzc)

    def rest(acts, grad_feed, feed_terms, wide_terms):
        feed_back_half(
            xyzc, wire, group, keep, mids, grad_rows, mid_all, cot_all, w_feed, w_down, w_out_all, kv, middle, gains,
            att_pad, att_copied, grads_out, feed_scratch, wide_scratch,
            acts, grad_feed, feed_terms, wide_terms,
            grad_middle, grads_in, down_terms, feed_lines, wide_lines, out_terms, gain_terms,
        )

    pl.run_scoped(
        rest,
        pltpu.VMEM((4, 2 * BLOCK, 512), BF16),
        pltpu.VMEM((4, 2 * BLOCK, 1024), BF16),
        pltpu.VMEM((4, 4, 96, 1024), BF16),
        pltpu.VMEM((4, 4, 32, D), BF16),
    )


def feed_back_half(
    xyzc, wire, group, keep, mids, grad_rows, mid_all, cot_all, w_feed, w_down, w_out_all, kv, middle, gains,
    att_pad, att_copied, grads_out, feed_scratch, wide_scratch,
    acts, grad_feed, feed_terms, wide_terms,
    grad_middle, grads_in, down_terms, feed_lines, wide_lines, out_terms, gain_terms,
):
    x, y, z, c = xyzc
    j = z * 2 + c
    across, down_first = (((1,), (1,)), ((), ())), (((0,), (0,)), ((), ()))

    def feed_forward(step):
        place = grad_rows.place(step)
        rows = mid_all[place].reshape(2 * BLOCK, D)
        weights = w_feed[...].reshape(D, 1024)
        both = jnp.dot(rows, weights, preferred_element_type=F32)
        gate, up = both[:, :512], both[:, 512:]
        sigmoid = 0.5 * jnp.tanh(0.5 * gate) + 0.5
        silu = gate * sigmoid
        acts[place] = (silu * up).astype(BF16)
        cot = cot_all[place].reshape(2 * BLOCK, D)
        grad_act = lax.dot_general(cot, w_down[...].reshape(512, D), across, preferred_element_type=F32)
        grad_gate = grad_act * up * sigmoid * (1.0 + gate * (1.0 - sigmoid))
        grad_feed[place, :, :512] = grad_gate.astype(BF16)
        grad_feed[place, :, 512:] = (grad_act * silu).astype(BF16)

    def feed_back(step):
        place = grad_rows.place(step)
        weights = w_feed[...].reshape(D, 1024)
        grads = lax.dot_general(grad_feed[place], weights, across, preferred_element_type=F32)
        grad_rows.put(step, grads.astype(BF16))

    mids.crossed[0].wait_recv()
    feed_forward(0)
    feed_back(0)
    mids.near()
    mids.crossed[1].wait_recv()
    mids.crossed[2].wait_recv()

    def near_chunk(index, carry):
        step = 1 + 2 * index
        feed_forward(step)
        feed_back(step)

        @pl.when(index > 0)
        def _():
            grad_rows.turn(1)

        return carry

    lax.fori_loop(0, 2, near_chunk, 0)
    mids.far()
    mids.crossed[3].wait_recv()
    grad_rows.turn(3)
    feed_forward(2)

    def down_weights(step, carry):
        cols = pl.ds(pl.multiple_of(step * 128, 128), 128)
        left = acts[:, :, cols].reshape(MEMBERS * BLOCK, 128)
        right = cot_all[...].reshape(MEMBERS * BLOCK, D)
        total = lax.dot_general(left, right, down_first, preferred_element_type=F32)
        wide_terms[step] = total.astype(BF16).reshape(4, 32, D)
        return carry

    lax.fori_loop(0, 4, down_weights, 0)
    wides = PlaneScatter(wire, wide_terms, Rows(32, D), wide_scratch, xyzc)
    wides.first()
    feed_back(2)

    def feed_weights(step, carry):
        cols = pl.ds(pl.multiple_of(step * 384, 384), 384)
        left = mid_all[:, :, :, cols].reshape(MEMBERS * BLOCK, 384)
        right = grad_feed[...].reshape(MEMBERS * BLOCK, 1024)
        total = lax.dot_general(left, right, down_first, preferred_element_type=F32)
        feed_terms[step] = total.astype(BF16).reshape(4, 96, 1024)
        return carry

    lax.fori_loop(0, 2, feed_weights, 0)
    grad_rows.turn(2)
    lax.fori_loop(2, 4, feed_weights, 0)
    feeds = PlaneScatter(wire, feed_terms, Rows(96, 1024), feed_scratch, xyzc)
    feeds.first()
    wides.relay()

    def down_rows(place, carry):
        outs = jnp.dot(acts[place], w_down[...].reshape(512, D), preferred_element_type=F32).astype(BF16)
        for core in range(2):
            for tile in range(12):
                kv[place, core, tile] = outs[
                    core * BLOCK : (core + 1) * BLOCK, tile * LANES : (tile + 1) * LANES
                ]
        return carry

    lax.fori_loop(0, 4, down_rows, 0)
    down_copied = keep(kv.at[:, pl.ds(0, 2), pl.ds(0, 12)], down_terms)
    grad_mid = grad_rows.total()
    rms = jnp.sqrt(jnp.mean(middle[...] * middle[...], axis=1, keepdims=True) + EPSILON)
    scaled = middle[...] / rms
    gain_terms[...] = jnp.sum(grad_mid * scaled, axis=0, keepdims=True)
    weighted = grad_mid * gains[1:2]
    back = (weighted - scaled * jnp.mean(weighted * scaled, axis=1, keepdims=True)) / rms
    grad_middle[...] = cot_all[z, c].astype(F32) + back
    branch_grad = grad_middle[...].astype(BF16)

    def spread(step, carry):
        weights = w_out_all[step].reshape(4 * LANES, D)
        grads = lax.dot_general(branch_grad, weights, across, preferred_element_type=F32).astype(BF16)
        for part in range(2):
            grads_out[step * 2 + part] = grads[:, part * 256 : (part + 1) * 256]
        return carry

    lax.fori_loop(0, 4, spread, 0)
    kept = keep(grads_out.at[j], grads_in.at[j])
    dealt = [
        wire.send(grads_out.at[(j + k) % MEMBERS], grads_in.at[j], group[k - 1]) for k in (4, 5, 3, 2, 6, 7, 1)
    ]
    feeds.relay()

    def out_weights(step, carry):
        cols = pl.ds(pl.multiple_of(step * 512, 512), 512)
        total = lax.dot_general(att_pad[:, cols], branch_grad, down_first, preferred_element_type=F32)
        w_out_all[step] = total.astype(BF16).reshape(4, LANES, D)
        return carry

    lax.fori_loop(0, 4, out_weights, 0)
    out_copied = keep(w_out_all.at[:, :, pl.ds(0, 96)], out_terms)

    wides.add_first()
    wide_copied = keep(wides.summed, wide_lines)
    feeds.add_first()
    feed_copied = keep(feeds.summed, feed_lines)
    for copy in dealt:
        copy.wait_recv()
    for copy in (kept, down_copied, out_copied, att_copied, wide_copied, feed_copied):
        copy.wait()
    wire.close()
    grad_rows.close()


def start(
    parent, table, stream, w_query, w_key, w_value, w_gate, w_up, w_out, small_rows, live_row, cotangent, own_down
):
    shape, vmem = jax.ShapeDtypeStruct, pltpu.VMEM
    smem = pl.BlockSpec(memory_space=pltpu.SMEM)
    return communicate(
        start_kernel,
        (
            shape((MEMBERS, DEPTH), jnp.int32),
            shape((MEMBERS, 1, LANES), F32),
            shape((8, D), F32),
            shape((MEMBERS, 2 * BLOCK, LANES), BF16),
            shape((4, 2, BLOCK, D), BF16),
            shape((4, 4, 96, 512), BF16),
            shape((4, 4, 16, BLOCK, LANES), BF16),
            shape((BLOCK, D), F32),
            shape((1, LANES), F32),
            shape((BLOCK, D), F32),
            shape((MEMBERS, BLOCK, 2 * LANES), BF16),
            shape((4, 2, 12, BLOCK, LANES), BF16),
            shape((2, 4, 48, 1024), BF16),
            shape((2, 4, 16, D), BF16),
            shape((4, 4, 96, D), BF16),
            shape((1, D), F32),
            shape((MEMBERS, BLOCK, 2 * LANES), BF16),
            shape((MEMBERS, 8, 2 * BLOCK), F32),
        ),
        [smem] + [INVMEM] * 10 + [ANY] * 2,
        (smem,) + (INVMEM,) * 3 + (ANY,) * 3 + (INVMEM,) * 3 + (ANY,) * 5 + (INVMEM, ANY, INVMEM),
        [
            vmem((MEMBERS, 16, 1536), BF16),
            vmem((16, 1536), BF16),
            vmem((16, LANES), BF16),
            vmem((16, FF), F32),
            vmem((MEMBERS, 16, 1536), BF16),
            vmem((MEMBERS, 16, 768), BF16),
            vmem((MEMBERS, 16, LANES), BF16),
            vmem((104, 1536), F32),
            vmem((96, 1536), BF16),
            vmem((96, 768), BF16),
            vmem((16, LANES), BF16),
            vmem((4, 4, 16, LANES), BF16),
            vmem((4, 4, 96, 512), BF16),
            vmem((12, BLOCK, LANES), BF16),
            vmem((4, 4, 16, BLOCK, LANES), BF16),
            vmem((4, 4, LANES, D), BF16),
            vmem((4, 4, 96, 1024), BF16),
            vmem((4, 4, 32, D), BF16),
            vmem((4, 2, BLOCK, D), BF16),
            vmem((4, 2, BLOCK, D), BF16),
        ]
        + chip_scatter_scratch()
        + [
            vmem((MEMBERS, BLOCK, 2 * LANES), BF16),
            vmem((MEMBERS, BLOCK, 2 * LANES), BF16),
            vmem((BLOCK, 2048), BF16),
            vmem((MEMBERS, BLOCK, 2 * LANES), BF16),
        ]
        + scatter_scratch(Rows(96, 1024))
        + scatter_scratch(Rows(32, D))
        + wire_scratch(250)
        + [pltpu.SemaphoreType.DMA((20,))],
        2,
        "start",
        63 * 2**20,
    )(parent, table, stream, w_query, w_key, w_value, w_gate, w_up, w_out, small_rows, live_row, cotangent, own_down)


def split_rows(tall, dealt):
    width = dealt.shape[2]
    for member in range(MEMBERS):
        dealt[member] = tall[pl.ds(member * 12, 16), :width].astype(BF16)


def attend_back_kernel(
    lineage, query, live, grad, attended, log_rows, kv_in, grad_query, grad_kv, kv, sums, packed, sems
):
    loaded = pltpu.make_async_copy(kv_in, kv, sems.at[16])
    loaded.start()

    def clear(step, carry):
        sums[step] = jnp.zeros((BLOCK, LANES), F32)
        return carry

    lax.fori_loop(0, 256, clear, 0)
    loaded.wait()

    def two(pair, carry):
        for block in (2 * pair, 2 * pair + 1):
            attend_back_block(block, lineage, query, live, grad, attended, log_rows, grad_query, kv, sums)
        return carry

    lax.fori_loop(0, MEMBERS // 2, two, 0)

    def stored(line):
        rows = pl.ds(line * 12, 12)
        return pltpu.make_async_copy(packed.at[rows], grad_kv.at[rows], sems.at[line])

    def store(line, carry):
        for tile in range(12):
            total = pack_tile(sums[line * 16 + tile], sums[line * 16 + 12 + tile // 3], tile % 3)
            packed[line * 12 + tile] = total.astype(BF16)
        stored(line).start()
        return carry

    lax.fori_loop(0, 16, store, 0)
    for line in range(16):
        stored(line).wait()


def attend_back_block(block, lineage, query, live, grad, attended, log_rows, grad_query, kv, sums):
    across, down_first = (((1,), (1,)), ((), ())), (((0,), (0,)), ((), ()))
    queries = query[block]
    grads = jnp.concatenate([grad[block, :, :LANES], grad[block, :, LANES:]], axis=0)
    outs = jnp.concatenate([attended[block, :, :LANES], attended[block, :, LANES:]], axis=0)
    product = grads.astype(F32) * outs.astype(F32)
    high = product.astype(BF16)
    low = (product - high.astype(F32)).astype(BF16)
    ones = jnp.ones((8, LANES), BF16)
    inner = lax.dot_general(ones, high, across, preferred_element_type=F32)
    inner = (inner + lax.dot_general(ones, low, across, preferred_element_type=F32))[:1]
    logs = log_rows[block, :1]
    limit = count_ancestors(lineage, block)
    u = lax.broadcasted_iota(jnp.int32, (BLOCK, 2 * BLOCK), 0)
    t = lax.broadcasted_iota(jnp.int32, (BLOCK, 2 * BLOCK), 1) % BLOCK
    alive = jnp.transpose(jnp.broadcast_to(live[block], (BLOCK, BLOCK)))
    alive = jnp.concatenate([alive, alive], axis=1)
    own = jnp.logical_and(u <= t, jnp.logical_or(alive > 0.5, u == t))
    turned = jnp.zeros((LANES, 2 * BLOCK), F32)
    for step in range(0, DEPTH, 2):
        units = []
        for node in (lineage[block, step], lineage[block, step + 1]):
            safe = jnp.maximum(node, 0)
            at, member = lax.div(safe, 8) * 16, lax.rem(safe, 8)
            units.append((node, at + key_unit(member), at + value_unit(member)))
        keys = jnp.concatenate([kv[unit[1]] for unit in units], axis=0)
        values = jnp.concatenate([kv[unit[2]] for unit in units], axis=0)
        scores = lax.dot_general(keys, queries, across, preferred_element_type=F32) * SCALE
        near, far = scores[:BLOCK], scores[BLOCK:]
        if step == 0:
            near = jnp.where(own, jnp.exp(jnp.where(own, near - logs, NEGATIVE)), 0.0)
        else:
            near = jnp.exp(near + (jnp.where(step < limit, 0.0, NEGATIVE) - logs))
        far = jnp.exp(far + (jnp.where(step + 1 < limit, 0.0, NEGATIVE) - logs))
        chances = jnp.concatenate([near, far], axis=0)
        grad_chances = lax.dot_general(values, grads, across, preferred_element_type=F32)
        grad_scores = (chances * (grad_chances - inner)).astype(BF16)
        grad_keys = jnp.dot(grad_scores, queries, preferred_element_type=F32) * SCALE
        grad_values = jnp.dot(chances.astype(BF16), grads, preferred_element_type=F32)
        for part, (node, at_key, at_value) in enumerate(units):
            rows = slice(part * BLOCK, (part + 1) * BLOCK)
            sums[jnp.where(node >= 0, at_key, 256)] += grad_keys[rows]
            sums[jnp.where(node >= 0, at_value, 256)] += grad_values[rows]
        turned = turned + lax.dot_general(keys, grad_scores, down_first, preferred_element_type=F32)
    grad_query[block] = jnp.transpose(turned) * SCALE


def attend_back(lineage, query, kv, live, grad, attended, log_rows):
    vmem = pltpu.VMEM
    return pl.pallas_call(
        attend_back_kernel,
        in_specs=[pl.BlockSpec(memory_space=pltpu.SMEM)] + [INVMEM] * 5 + [ANY],
        out_specs=(INVMEM, ANY),
        out_shape=(
            jax.ShapeDtypeStruct((MEMBERS, 2 * BLOCK, LANES), F32),
            jax.ShapeDtypeStruct((192, BLOCK, LANES), BF16),
        ),
        scratch_shapes=[
            vmem((256, BLOCK, LANES), BF16),
            vmem((257, BLOCK, LANES), F32),
            vmem((192, BLOCK, LANES), BF16),
            pltpu.SemaphoreType.DMA((17,)),
        ],
        compiler_params=pltpu.CompilerParams(vmem_limit_bytes=VMEM_BYTES),
        name="attend_back",
    )(lineage, query, live, grad, attended, log_rows, kv)


def gain_tiles(rows):
    lane = lane_of((8, LANES))
    tiles = [rows[:, tile * LANES : (tile + 1) * LANES] for tile in range(12)]
    pieces = []
    for piece in range(16):
        tile, skip = divmod(piece * 96, LANES)
        low = pltpu.roll(tiles[tile], (LANES - skip) % LANES, 1)
        high = pltpu.roll(tiles[min(tile + 1, 11)], (LANES - skip) % LANES, 1)
        pieces.append(jnp.where(lane < LANES - skip, low, high))
    return pieces


def ending_kernel(
    lineage, grad_query, table, stream_all, w_attn, gain, gain_two, stream, middle, grad_middle,
    feed_lines, wide_lines, kv_terms, down_terms, out_terms,
    mixed_out, stream_grad, query_grad, key_grad, value_grad, out_grad, gain_one, gain_two_out, rms_out,
    gate_grad, up_grad, down_grad,
    feed_second, wide_second, feed_tall, feed_dealt, feed_in, attn_grad, out_in, normed, raw, units, grad_terms, crossed_in, near_in, far_in, query_terms, pair_terms, attn_tall, attn_dealt,
    out_tall, out_dealt, out_mine, out_crossed, gain_terms, gain_in, gain_line, gain_in_two, gain_in_three,
    *scratch,
):
    xyzc = x, y, z, c = spot()
    j = z * 2 + c
    down_scratch, kv_scratch, query_scratch, pair_scratch, out_scratch = (
        scratch[:5], scratch[5:13], scratch[13:18], scratch[18:23], scratch[23:28]
    )
    send_sems, recv_sems, local_sem = scratch[28:]
    wire = Wire(send_sems, recv_sems)
    group = [group_peer(x, y, z, c, k) for k in range(1, MEMBERS)]
    peers = group + axis_peers(x, y, z, c, True)
    announce(peers)
    await_peers(peers)
    sibling = device_of(x, y, z, 1 - c)
    pairs = PlaneScatter(wire, kv_terms, Units(), kv_scratch, xyzc)
    pairs.first()
    attn_tall[96:] = jnp.zeros((8, 512), F32)
    feed_tall[96:] = jnp.zeros((8, 1024), F32)
    out_tall[96:] = jnp.zeros((8, 768), F32)

    def norm_rows(step, carry):
        rows = pl.ds(pl.multiple_of(step * BLOCK, BLOCK), BLOCK)
        wide = stream_all[rows].astype(F32)
        rms = jnp.sqrt(jnp.mean(wide * wide, axis=1, keepdims=True) + EPSILON)
        normed[rows] = (wide * (1.0 / rms) * gain[0:1]).astype(BF16)
        return carry

    lax.fori_loop(0, MEMBERS, norm_rows, 0)

    def turn(block, v):
        depth = count_ancestors(lineage, block) - 1
        cos, sin = turning(table[depth])
        return (v * cos - swap_halves(v) * sin).astype(BF16)

    def query_rows(block, carry):
        rows = pl.ds(pl.multiple_of(block * BLOCK, BLOCK), BLOCK)
        raw[rows, :128] = turn(block, grad_query[block, :BLOCK])
        raw[rows, 128:256] = turn(block, grad_query[block, BLOCK:])
        return carry

    lax.fori_loop(0, MEMBERS, query_rows, 0)
    pairs.relay()
    downs = GroupScatter(wire, down_terms, *down_scratch, xyzc)
    downs.begin()
    own_half = pl.ds(pl.multiple_of(c * 768, 768), 768)
    other_half = pl.ds(pl.multiple_of((1 - c) * 768, 768), 768)
    crossed = wire.send(out_terms.at[:, :, :, other_half], out_crossed, sibling)
    local = pltpu.make_async_copy(out_terms.at[:, :, :, own_half], out_mine, local_sem)
    local.start()

    def weights_back(terms, first):
        def some(step, carry):
            cols = pl.ds(pl.multiple_of(step * 384, 384), 384)
            total = lax.dot_general(
                normed[:, cols], raw[:, first : first + 256], (((0,), (0,)), ((), ())), preferred_element_type=F32
            )
            terms[step] = total.astype(BF16).reshape(4, 96, 256)
            return carry

        lax.fori_loop(0, 4, some, 0)

    weights_back(query_terms, 0)
    query_sums = PlaneScatter(wire, query_terms, Rows(96, 256), query_scratch, xyzc)
    pair_sums = PlaneScatter(wire, pair_terms, Rows(96, 256), pair_scratch, xyzc)
    local.wait()
    crossed.wait_recv()

    def add_halves(step, carry):
        a, b = step // 4, step % 4
        total = out_mine[a, b].astype(F32) + out_crossed[a, b].astype(F32)
        out_mine[a, b] = total.astype(BF16)
        return carry

    lax.fori_loop(0, 16, add_halves, 0)
    outs = PlaneScatter(wire, out_mine, Rows(96, 768), out_scratch, xyzc)
    downs.turn()
    pairs.add_first()
    pairs.second()
    downs.finish(stream_grad)
    mixed_out[...] = (middle[...] + stream_grad[...]).astype(BF16)
    pairs.arrive()
    outs.first()
    query_sums.first()
    for half in range(2):
        units[pl.ds(half * 6, 6)] = pairs.total(half)
    for extra in range(4):
        units[12 + extra] = unpack_extra([units[extra * 3 + k] for k in range(3)])

    def pair_rows(block, carry):
        rows = pl.ds(pl.multiple_of(block * BLOCK, BLOCK), BLOCK)
        raw[rows, 256:384] = turn(block, units[key_unit(block)])
        value = units[value_unit(block)]
        raw[rows, 384:] = jnp.where(lane_of((BLOCK, LANES)) < HEAD_DIM, value, 0.0).astype(BF16)
        return carry

    lax.fori_loop(0, MEMBERS, pair_rows, 0)

    grad_rows = RingScatter(wire, grad_terms, crossed_in, near_in, far_in, xyzc)
    gain_terms[...] = jnp.zeros((1, D), F32)

    def rows_back(step):
        rows = pl.ds(pl.multiple_of(grad_rows.place(step) * 256, 256), 256)
        grads = lax.dot_general(raw[rows], w_attn[...], (((1,), (1,)), ((), ())), preferred_element_type=F32)
        grad_rows.put(step, grads.astype(BF16))
        wide = stream_all[rows].astype(F32)
        rms = jnp.sqrt(jnp.mean(wide * wide, axis=1, keepdims=True) + EPSILON)
        gain_terms[...] += jnp.sum(grads * (wide * (1.0 / rms)), axis=0, keepdims=True)

    rows_back(2)
    rows_back(1)
    grad_rows.turn(2)
    rows_back(3)
    grad_rows.turn(1)
    rows_back(0)
    grad_rows.turn(3)
    outs.relay()
    query_sums.relay()
    grad_rows.pass_on(1)
    grad_rows.pass_on(3)
    rows = jnp.concatenate([gain_terms[...], gain_two[...], jnp.zeros((6, D), F32)], axis=0)
    for piece, part in enumerate(gain_tiles(rows)):
        gain_in[piece // 4, piece % 4] = part
    gains = [
        wire.send(gain_in.at[(x + k) % 4], gain_line.at[k], device_of(x + k, y, z, c)) for k in range(1, 4)
    ]

    weights_back(pair_terms, 256)
    pair_sums.first()
    for copy in gains:
        copy.wait_recv()
    gain_line[0] = gain_in[x] + gain_line[1] + gain_line[2] + gain_line[3]
    gains = [
        wire.send(gain_line.at[0, (y + k) % 4], gain_in_two.at[k], device_of(x, y + k, z, c)) for k in range(1, 4)
    ]
    outs.add_first()
    outs.second()
    query_sums.add_first()
    query_sums.second()
    pair_sums.relay()
    outs.arrive()
    for half in range(2):
        out_tall[pl.ds(half * 48, 48)] = outs.total(half)
    split_rows(out_tall, out_dealt)
    out_in[j] = out_dealt[j]
    dealt = [
        wire.send(out_dealt.at[(j + k) % MEMBERS], out_in.at[j], group[k - 1]) for k in range(1, MEMBERS)
    ]
    pair_sums.add_first()
    pair_sums.second()
    feeds = SecondRound(wire, feed_lines, feed_second, xyzc)
    wides = SecondRound(wire, wide_lines, wide_second, xyzc)
    feeds.second()
    wides.second()

    wide = stream[...].astype(F32)
    rms = jnp.sqrt(jnp.mean(wide * wide, axis=1, keepdims=True) + EPSILON)
    rms_out[...] = jnp.transpose(jnp.broadcast_to(rms, (BLOCK, LANES)))[:1]
    scaled = wide / rms
    weighted = grad_rows.total() * gain[0:1]
    back = (weighted - scaled * jnp.mean(weighted * scaled, axis=1, keepdims=True)) / rms
    stream_grad[...] = grad_middle[...] + back

    for copy in gains:
        copy.wait_recv()
    gain_in_three[j] = gain_line[0, y] + gain_in_two[1] + gain_in_two[2] + gain_in_two[3]
    gains = [
        wire.send(gain_in_three.at[j], gain_in_three.at[j], group[k - 1]) for k in range(1, MEMBERS)
    ]
    query_sums.arrive()
    pair_sums.arrive()
    for half in range(2):
        attn_tall[pl.ds(half * 48, 48), :256] = query_sums.total(half)
        attn_tall[pl.ds(half * 48, 48), 256:] = pair_sums.total(half)
    split_rows(attn_tall, attn_dealt)
    attn_grad[j] = attn_dealt[j]
    dealt += [
        wire.send(attn_dealt.at[(j + k) % MEMBERS], attn_grad.at[j], group[k - 1]) for k in range(1, MEMBERS)
    ]
    feeds.arrive()
    for half in range(2):
        feed_tall[pl.ds(half * 48, 48)] = feeds.total(half)
    split_rows(feed_tall, feed_dealt)
    feed_in[j] = feed_dealt[j]
    feed_copies = [
        wire.send(feed_dealt.at[(j + k) % MEMBERS], feed_in.at[j], group[k - 1]) for k in range(1, MEMBERS)
    ]
    wides.arrive()
    for half in range(2):
        down_grad[pl.ds(half * 16, 16)] = wides.total(half)
    for copy in gains:
        copy.wait_recv()
    total = gain_in_three[0]
    for member in range(1, MEMBERS):
        total = total + gain_in_three[member]
    own = pltpu.roll(total, (LANES - 12 * j) % LANES, 1)
    gain_one[...] = own[:1, :12]
    gain_two_out[...] = own[1:2, :12]
    for copy in dealt:
        copy.wait_recv()
    for core in range(2):
        total = out_in[core].astype(F32)
        for place in range(1, 4):
            total = total + out_in[place * 2 + core].astype(F32)
        out_grad[:, core * 768 : (core + 1) * 768] = total[:12]

    def tile_of(member, tile):
        return attn_grad[member, :, tile * LANES : (tile + 1) * LANES].astype(F32)

    for grad, pieces in (
        (query_grad, [tile_of(head // 2, head % 2) for head in range(HEADS)]),
        (key_grad, [tile_of(member, 2) for member in range(MEMBERS)]),
        (value_grad, [tile_of(member, 3) for member in range(MEMBERS)]),
    ):
        for tile, value in enumerate(join_heads(pieces)):
            grad[:, tile * LANES : (tile + 1) * LANES] = value[:12]
    for copy in feed_copies:
        copy.wait_recv()
    for grad, first in ((gate_grad, 0), (up_grad, 4)):
        for tile in range(32):
            line = tile // 2
            cols = slice((first + line // 4) * LANES, (first + line // 4 + 1) * LANES)
            parts = [(feed_in[4 * (tile % 2) + i, :, cols].astype(F32), line % 4) for i in range(4)]
            grad[:, tile * LANES : (tile + 1) * LANES] = mix_groups(parts)[:12]
    wire.close()
    grad_rows.close()


def ending(
    lineage, grad_query, table, stream_all, w_attn, gain, gain_two, stream, middle, grad_middle,
    feed_lines, wide_lines, kv_terms, down_terms, out_terms,
):
    shape, vmem = jax.ShapeDtypeStruct, pltpu.VMEM
    smem = pl.BlockSpec(memory_space=pltpu.SMEM)
    return communicate(
        ending_kernel,
        (
            shape((BLOCK, D), BF16),
            shape((BLOCK, D), F32),
            shape((12, D), F32),
            shape((12, 768), F32),
            shape((12, 768), F32),
            shape((12, D), F32),
            shape((1, 12), F32),
            shape((1, 12), F32),
            shape((1, LANES), F32),
            shape((12, FF), F32),
            shape((12, FF), F32),
            shape((32, D), F32),
        ),
        [smem] + [INVMEM] * 11 + [ANY] * 3,
        (INVMEM,) * 12,
        [
            vmem((2, 3, 48, 1024), BF16),
            vmem((2, 3, 16, D), BF16),
            vmem((104, 1024), F32),
            vmem((MEMBERS, 16, 1024), BF16),
            vmem((MEMBERS, 16, 1024), BF16),
            vmem((MEMBERS, 16, 512), BF16),
            vmem((MEMBERS, 16, 768), BF16),
            vmem((MEMBERS * BLOCK, D), BF16),
            vmem((MEMBERS * BLOCK, 512), BF16),
            vmem((16, BLOCK, LANES), F32),
            vmem((4, 2, 12, BLOCK, LANES), BF16),
        ]
        + [
            vmem((4, 12, BLOCK, LANES), BF16),
            vmem((2, 12, BLOCK, LANES), BF16),
            vmem((2, 6, BLOCK, LANES), BF16),
        ]
        + [
            vmem((4, 4, 96, 256), BF16),
            vmem((4, 4, 96, 256), BF16),
            vmem((104, 512), F32),
            vmem((MEMBERS, 16, 512), BF16),
            vmem((104, 768), F32),
            vmem((MEMBERS, 16, 768), BF16),
            vmem((4, 4, 96, 768), BF16),
            vmem((4, 4, 96, 768), BF16),
            vmem((1, D), F32),
            vmem((4, 4, 8, LANES), F32),
            vmem((4, 4, 8, LANES), F32),
            vmem((4, 8, LANES), F32),
            vmem((MEMBERS, 8, LANES), F32),
        ]
        + group_scatter_scratch()
        + scatter_scratch(Units(), room=True)
        + scatter_scratch(Rows(96, 256))
        + scatter_scratch(Rows(96, 256))
        + scatter_scratch(Rows(96, 768))
        + wire_scratch(140)
        + [pltpu.SemaphoreType.DMA],
        7,
        "ending",
        62 * 2**20,
    )(
        lineage, grad_query, table, stream_all, w_attn, gain, gain_two, stream, middle, grad_middle,
        feed_lines, wide_lines, kv_terms, down_terms, out_terms,
    )


def hand_over_kernel(*refs):
    count = len(refs) // 2
    for source, target in zip(refs[:count], refs[count:]):
        target[...] = source[...]


def hand_over(*arrays):
    return pl.pallas_call(
        hand_over_kernel,
        out_shape=tuple(jax.ShapeDtypeStruct(array.shape, array.dtype) for array in arrays),
        in_specs=[INVMEM] * len(arrays),
        out_specs=(INVMEM,) * len(arrays),
        compiler_params=pltpu.CompilerParams(vmem_limit_bytes=VMEM_BYTES),
        name="hand_over",
    )(*arrays)


def shards(
    stream, attn_gain, w_query, w_key, w_value, w_out, mlp_gain, w_gate, w_up, w_down, parent, live_mask, cotangent
):
    table = rope_table()
    small_rows = jnp.pad(jnp.stack([attn_gain, mlp_gain]).astype(F32), ((0, 6), (0, LANES - attn_gain.shape[0])))
    (
        lineage, live, gains, query, stream_all, w_attn, context, middle, branch_rms, grad_middle, grad_heads,
        down_terms, feed_lines, wide_lines, out_terms, gain_two_terms, attended, log_rows,
    ) = start(
        parent, table, stream, w_query, w_key, w_value, w_gate, w_up, w_out, small_rows,
        live_mask.reshape(1, BLOCK), cotangent, w_down,
    )
    grad_query, context_terms = attend_back(
        lineage, query, context.reshape(256, BLOCK, LANES), live, grad_heads, attended, log_rows
    )
    (
        mixed_out, stream_grad, query_grad, key_grad, value_grad, out_grad, gain_one, gain_two, stream_rms,
        gate_grad, up_grad, down_grad,
    ) = ending(
        lineage, grad_query, table, stream_all.reshape(MEMBERS * BLOCK, D), w_attn.reshape(D, 512), gains,
        gain_two_terms, stream, middle, grad_middle, feed_lines, wide_lines,
        context_terms.reshape(4, 4, 12, BLOCK, LANES), down_terms, out_terms,
    )
    (
        mixed_out, stream_grad, gain_one, query_grad, key_grad, value_grad, out_grad, gain_two,
        gate_grad, up_grad, down_grad, stream_rms, branch_rms,
    ) = hand_over(
        mixed_out, stream_grad, gain_one, query_grad, key_grad, value_grad, out_grad, gain_two,
        gate_grad, up_grad, down_grad, stream_rms, branch_rms,
    )
    return (
        mixed_out, stream_grad, gain_one[0], query_grad, key_grad, value_grad, out_grad, gain_two[0],
        gate_grad, up_grad, down_grad, stream_rms[0], branch_rms[0],
    )


def solution(mesh):
    rows, line = P("dev", None), P("dev")
    return jax.shard_map(
        shards,
        mesh=mesh,
        in_specs=(rows, line, rows, rows, rows, rows, line, rows, rows, rows, P(), line, rows),
        out_specs=(rows, rows, line, rows, rows, rows, rows, line, rows, rows, rows, line, line),
        check_vma=False,
    )
```

```python
import functools

import jax
import jax.numpy as jnp
import numpy as np
from jax import lax
from jax.experimental import pallas as pl
from jax.experimental.pallas import tpu as pltpu
from jax.sharding import PartitionSpec as P

HEADS = 16
KV_HEADS = 8
HEAD_DIM = 96
BLOCK = 128
DEPTH = 10
D = 1536
FF = 4096
MEMBERS = 8
LANES = 128

EPSILON = 1e-05
ROPE_BASE = 100000.0
NEGATIVE = -1e30
SCALE = HEAD_DIM ** (-0.5)
MESH = pl.DeviceIdType.MESH
BF16 = jnp.bfloat16
F32 = jnp.float32
VMEM_BYTES = 56 * 2**20


def spot():
    me = lax.axis_index("dev")
    return me // 32, (me // 8) % 4, (me // 2) % 4, me % 2


def device_of(x, y, z, c):
    return ((x % 4) * 4 + (y % 4)) * 8 + (z % 4) * 2 + c


def announce(peers):
    barrier = pltpu.get_barrier_semaphore()
    for peer in peers:
        pl.semaphore_signal(barrier, inc=1, device_id=(peer,), device_id_type=MESH)


def await_peers(peers):
    pl.semaphore_wait(pltpu.get_barrier_semaphore(), len(peers))


def axis_peers(x, y, z, c, far):
    steps = (1, 2, 3) if far else (1, 3)
    return [device_of(x + k, y, z, c) for k in steps] + [device_of(x, y + k, z, c) for k in steps]


def group_peer(x, y, z, c, k):
    member = (z * 2 + c + k) % MEMBERS
    return (x * 4 + y) * MEMBERS + member


class Wire:
    def __init__(self, send_sems, recv_sems):
        self.send_sems = send_sems
        self.recv_sems = recv_sems
        self.used = 0
        self.open = []

    def reserve(self, count):
        self.used += count
        return self.used - count

    def make(self, slot, source, target, peer):
        return pltpu.make_async_remote_copy(
            src_ref=source,
            dst_ref=target,
            send_sem=self.send_sems.at[slot],
            recv_sem=self.recv_sems.at[slot],
            device_id=(peer,),
            device_id_type=MESH,
        )

    def send(self, source, target, peer):
        copy = self.make(self.reserve(1), source, target, peer)
        copy.start()
        self.open.append(copy)
        return copy

    def close(self):
        for copy in self.open:
            copy.wait_send()
        self.open = []


class Ring:
    def __init__(self, wire, own, part, place, up, down):
        self.wire, self.own, self.part = wire, own, part
        self.place, self.up, self.down = place, up, down

    def begin(self):
        send, part, place = self.wire.send, self.part, self.place
        self.low_up = send(self.own(0), part(place, 0), self.up)
        self.high_down = send(self.own(1), part(place, 1), self.down)
        self.high_up = send(self.own(1), part(place, 1), self.up)
        self.low_down = send(self.own(0), part(place, 0), self.down)

    def relay(self):
        before, after = (self.place + 3) % 4, (self.place + 1) % 4
        self.low_up.wait_recv()
        self.far_up = self.wire.send(self.part(before, 0), self.part(before, 0), self.up)
        self.high_down.wait_recv()
        self.far_down = self.wire.send(self.part(after, 1), self.part(after, 1), self.down)

    def near(self):
        self.high_up.wait_recv()
        self.low_down.wait_recv()

    def far(self):
        self.far_up.wait_recv()
        self.far_down.wait_recv()


class PlaneGather:
    def __init__(self, wire, own, out, cut, xyzc):
        self.wire, self.own, self.out, self.cut = wire, own, out, cut
        x, y, z, c = xyzc
        self.x, self.y = x, y
        self.x_up, self.x_down = device_of(x + 1, y, z, c), device_of(x + 3, y, z, c)
        self.y_up, self.y_down = device_of(x, y + 1, z, c), device_of(x, y + 3, z, c)

    def pair(self, one_own, one_part, two_own, two_part, one_on_x):
        on_x = (self.x, self.x_up, self.x_down)
        on_y = (self.y, self.y_up, self.y_down)
        cut = self.cut.quarter
        self.one = Ring(
            self.wire,
            lambda side: one_own(cut(0, side)),
            lambda place, side: one_part(place, cut(0, side)),
            *(on_x if one_on_x else on_y),
        )
        self.two = Ring(
            self.wire,
            lambda side: two_own(cut(1, side)),
            lambda place, side: two_part(place, cut(1, side)),
            *(on_y if one_on_x else on_x),
        )
        self.one.begin()
        self.two.begin()

    def first(self):
        own, out, x, y = self.own, self.out, self.x, self.y
        self.pair(
            lambda q: own.at[q],
            lambda place, q: out.at[(place, y) + q],
            lambda q: own.at[q],
            lambda place, q: out.at[(x, place) + q],
            True,
        )

    def relay(self):
        self.one.relay()
        self.two.relay()

    def near(self):
        self.one.near()
        self.two.near()

    def far(self):
        self.one.far()
        self.two.far()

    def settle(self):
        self.near()
        self.far()

    def second(self):
        out, x, y = self.out, self.x, self.y
        every = slice(None)
        self.pair(
            lambda q: out.at[(every, y) + q],
            lambda place, q: out.at[(every, place) + q],
            lambda q: out.at[(x, every) + q],
            lambda place, q: out.at[(place, every) + q],
            False,
        )


class Rows:
    def __init__(self, rows, cols, start=0):
        self.rows, self.cols, self.start = rows // 2, cols // 2, start

    def half(self, half):
        return (pl.ds(half * self.rows, self.rows),)

    def side(self, side):
        return (slice(None), pl.ds(side * self.cols, self.cols))

    def quarter(self, half, side):
        first = self.start + side * self.cols
        if not isinstance(first, int):
            first = pl.multiple_of(first, LANES)
        return self.half(half) + (pl.ds(first, self.cols),)

    def shapes(self):
        return (self.rows, 2 * self.cols), (self.rows, self.cols)


class Units:
    def half(self, half):
        return (pl.ds(half * 6, 6),)

    def side(self, side):
        return (pl.ds(side * 3, 3),)

    def quarter(self, half, side):
        return (pl.ds(half * 6 + side * 3, 3),)

    def shapes(self):
        return (6, BLOCK, LANES), (3, BLOCK, LANES)


class GroupGather:
    def __init__(self, wire, own, out, xyzc):
        self.wire, self.own, self.out = wire, own, out
        x, y, z, c = xyzc
        self.z, self.c = z, c
        self.sibling = device_of(x, y, z, 1 - c)
        half = out.shape[2] // 2
        self.ring = Ring(
            wire,
            lambda side: own.at[pl.ds(side * half, half)],
            lambda place, side: out.at[place, c, pl.ds(side * half, half)],
            z, device_of(x, y, z + 1, c), device_of(x, y, z + 3, c),
        )
        self.crossed = []

    def begin(self):
        self.ring.begin()
        self.crossed.append(self.wire.send(self.own, self.out.at[self.z, self.c], self.sibling))

    def cross(self, k):
        piece = self.out.at[(self.z + k) % 4, self.c]
        self.crossed.append(self.wire.send(piece, piece, self.sibling))

    def relay(self):
        self.ring.relay()

    def near(self):
        self.ring.near()
        self.cross(1)
        self.cross(3)

    def far(self):
        self.ring.far()
        self.cross(2)

    def finish(self, after=0):
        for copy in self.crossed[after:]:
            copy.wait_recv()


class SecondRound:
    def __init__(self, wire, summed, second_in, xyzc):
        self.wire, self.summed, self.second_in = wire, summed, second_in
        self.x, self.y, self.z, self.c = xyzc

    def peer(self, along_x, k):
        if along_x:
            return device_of(self.x + k, self.y, self.z, self.c)
        return device_of(self.x, self.y + k, self.z, self.c)

    def place(self, half, k):
        return ((self.x, self.y)[half] + k) % 4

    def second(self):
        self.copies = []
        for k in (2, 1, 3):
            for half in range(2):
                self.copies.append(
                    self.wire.send(
                        self.summed.at[half, self.place(1 - half, k)],
                        self.second_in.at[half, k - 1],
                        self.peer(half == 1, k),
                    )
                )

    def total(self, half):
        total = self.summed[half, self.place(1 - half, 0)].astype(F32)
        for k in range(3):
            total = total + self.second_in[half, k].astype(F32)
        return total

    def arrive(self):
        for copy in self.copies:
            copy.wait_recv()


class PlaneScatter(SecondRound):
    def __init__(self, wire, terms, cut, scratch, xyzc):
        *room, self.near_in, self.far_in, self.passed, summed, second_in = scratch
        super().__init__(wire, summed, second_in, xyzc)
        self.terms, self.cut, self.room = terms, cut, room

    def lead(self, half, k, line=slice(None)):
        place = self.place(half, k)
        return (place, line) if half == 0 else (line, place)

    def part(self, half, k, side):
        return self.terms.at[self.lead(half, k) + self.cut.quarter(half, side)]

    def own(self, half, line):
        if self.room:
            return self.room[0][half, line]
        return self.terms[self.lead(half, 0, line) + self.cut.half(half)]

    def edge(self, half, way, line):
        if self.room:
            return self.room[1][half, way, line]
        return self.terms[self.lead(half, (1, 3)[way], line) + self.cut.quarter(half, way)]

    def first(self):
        send = self.wire.send
        self.far, self.plain, self.locals = [], [], []
        if self.room:
            sems = self.room[2]
            for half in range(2):
                pairs = [(self.terms.at[self.lead(half, 0) + self.cut.half(half)], self.room[0].at[half])]
                pairs += [(self.part(half, (1, 3)[way], way), self.room[1].at[half, way]) for way in range(2)]
                for slot, (source, target) in enumerate(pairs):
                    copy = pltpu.make_async_copy(source, target, sems.at[half, slot])
                    copy.start()
                    self.locals.append(copy)
        for half in range(2):
            for way in range(2):
                self.far.append(
                    send(self.part(half, 2, way), self.far_in.at[half, way], self.peer(half == 0, (1, 3)[way]))
                )
        for half in range(2):
            for way in range(2):
                k = (1, 3)[way]
                landing = self.near_in.at[(half, way, slice(None)) + self.cut.side(1 - way)]
                self.plain.append(send(self.part(half, k, 1 - way), landing, self.peer(half == 0, k)))

    def relay(self):
        for copy in self.locals:
            copy.wait()
        self.relayed = []
        for half in range(2):
            for way in range(2):
                self.far[half * 2 + way].wait_recv()

                def add(line, carry):
                    total = self.edge(half, way, line).astype(F32) + self.far_in[half, way, line].astype(F32)
                    self.passed[half, way, line] = total.astype(BF16)
                    return carry

                lax.fori_loop(0, 4, add, 0)
                landing = self.near_in.at[(half, way, slice(None)) + self.cut.side(way)]
                self.relayed.append(
                    self.wire.send(self.passed.at[half, way], landing, self.peer(half == 0, (1, 3)[way]))
                )

    def add_first(self):
        for copy in self.plain + self.relayed:
            copy.wait_recv()
        for half in range(2):

            def body(line, carry):
                total = self.own(half, line).astype(F32)
                for way in range(2):
                    total = total + self.near_in[half, way, line].astype(F32)
                self.summed[half, line] = total.astype(BF16)
                return carry

            lax.fori_loop(0, 4, body, 0)


def scatter_scratch(cut, room=False):
    half, part = cut.shapes()
    vmem = pltpu.VMEM
    held = [vmem((2, 4) + half, BF16), vmem((2, 2, 4) + part, BF16), pltpu.SemaphoreType.DMA((2, 3))]
    return (held if room else []) + [
        vmem((2, 2, 4) + half, BF16),
        vmem((2, 2, 4) + part, BF16),
        vmem((2, 2, 4) + part, BF16),
        vmem((2, 4) + half, BF16),
        vmem((2, 3) + half, BF16),
    ]


class GroupScatter:
    def __init__(self, wire, terms, mine, crossed_in, summed, ring_in, local_sem, xyzc):
        self.wire, self.terms = wire, terms
        self.mine, self.crossed_in, self.summed, self.ring_in = mine, crossed_in, summed, ring_in
        self.x, self.y, self.z, self.c = xyzc
        self.local_sem = local_sem

    def begin(self):
        self.local = pltpu.make_async_copy(self.terms.at[:, self.c], self.mine, self.local_sem)
        self.local.start()
        sibling = device_of(self.x, self.y, self.z, 1 - self.c)
        self.crossed = {}
        for k in (2, 1, 3, 0):
            place = (self.z + k) % 4
            self.crossed[k] = self.wire.send(
                self.terms.at[place, 1 - self.c], self.crossed_in.at[place], sibling
            )

    def turn(self):
        self.local.wait()
        self.copies = []
        for k in (2, 1, 3):
            place = (self.z + k) % 4
            self.crossed[k].wait_recv()

            def body(tile, carry):
                total = self.mine[place, tile].astype(F32) + self.crossed_in[place, tile].astype(F32)
                self.summed[place, tile] = total.astype(BF16)
                return carry

            lax.fori_loop(0, 12, body, 0)
            self.copies.append(
                self.wire.send(
                    self.summed.at[place],
                    self.ring_in.at[k - 1],
                    device_of(self.x, self.y, self.z + k, self.c),
                )
            )

    def finish(self, out):
        self.crossed[0].wait_recv()
        for copy in self.copies:
            copy.wait_recv()
        for tile in range(12):
            total = self.mine[self.z, tile].astype(F32) + self.crossed_in[self.z, tile].astype(F32)
            for k in range(3):
                total = total + self.ring_in[k, tile].astype(F32)
            out[:, tile * LANES : (tile + 1) * LANES] = total


class ChipScatter:
    def __init__(self, wire, terms, at, crossed_in, ring_in, xyzc):
        self.wire, self.terms, self.at = wire, terms, at
        self.crossed_in, self.ring_in = crossed_in, ring_in
        self.x, self.y, self.z, self.c = xyzc
        self.crossed_slot, self.ring_slot = wire.reserve(4), wire.reserve(3)
        self.all_tiles = pl.ds(0, 12)

    def place(self, step):
        return (self.z + step) % 4

    def crossed(self, step):
        place = self.place(step)
        return self.wire.make(
            self.crossed_slot + step,
            self.terms.at[place, self.at + 1 - self.c, self.all_tiles],
            self.crossed_in.at[place],
            device_of(self.x, self.y, self.z, 1 - self.c),
        )

    def ring(self, step):
        return self.wire.make(
            self.ring_slot + step - 1,
            self.terms.at[self.place(step), self.at + self.c, self.all_tiles],
            self.ring_in.at[step - 1],
            device_of(self.x, self.y, self.z + step, self.c),
        )

    def put(self, step, grads):
        place = self.place(step)
        for core in range(2):
            for tile in range(12):
                self.terms[place, self.at + core, tile] = grads[
                    core * BLOCK : (core + 1) * BLOCK, tile * LANES : (tile + 1) * LANES
                ]
        self.crossed(step).start()

    def turn(self, step):
        place, line = self.place(step), self.at + self.c
        self.crossed(step).wait_recv()

        def add(tile, carry):
            total = self.terms[place, line, tile].astype(F32) + self.crossed_in[place, tile].astype(F32)
            self.terms[place, line, tile] = total.astype(BF16)
            return carry

        lax.fori_loop(0, 12, add, 0)
        self.ring(step).start()

    def total(self):
        self.crossed(0).wait_recv()
        for step in range(1, 4):
            self.ring(step).wait_recv()
        tiles = []
        for tile in range(12):
            total = self.terms[self.z, self.at + self.c, tile].astype(F32)
            total = total + self.crossed_in[self.z, tile].astype(F32)
            for step in range(3):
                total = total + self.ring_in[step, tile].astype(F32)
            tiles.append(total)
        return jnp.concatenate(tiles, axis=1)

    def close(self):
        for step in range(4):
            self.crossed(step).wait_send()
        for step in range(1, 4):
            self.ring(step).wait_send()


class RingScatter(ChipScatter):
    def __init__(self, wire, terms, crossed_in, near_in, far_in, xyzc):
        super().__init__(wire, terms, 0, crossed_in, None, xyzc)
        self.near_in, self.far_in = near_in, far_in
        self.moved = []

    def sum_tiles(self, place, tiles, extra=None):
        def add(tile, carry):
            total = self.terms[place, self.c, tile].astype(F32)
            if extra is None:
                total = total + self.crossed_in[place, tile].astype(F32)
            else:
                total = total + self.far_in[extra, tile - extra * 6].astype(F32)
            self.terms[place, self.c, tile] = total.astype(BF16)
            return carry

        lax.fori_loop(*tiles, add, 0)

    def move(self, place, first, landing, k):
        source = self.terms.at[place, self.c, pl.ds(first, 6)]
        copy = self.wire.send(source, landing, device_of(self.x, self.y, self.z + k, self.c))
        self.moved.append(copy)
        return copy

    def turn(self, step):
        place = self.place(step)
        self.crossed(step).wait_recv()
        self.sum_tiles(place, (0, 12))
        if step == 2:
            self.far = [self.move(place, 6 * way, self.far_in.at[way], (1, 3)[way]) for way in range(2)]
        else:
            way = (1, 3).index(step)
            plain = 6 * (1 - way)
            self.move(place, plain, self.near_in.at[way, pl.ds(plain, 6)], step)

    def pass_on(self, step):
        way = (1, 3).index(step)
        place = self.place(step)
        self.far[way].wait_recv()
        self.sum_tiles(place, (6 * way, 6 * way + 6), way)
        self.move(place, 6 * way, self.near_in.at[way, pl.ds(6 * way, 6)], step)

    def total(self):
        self.crossed(0).wait_recv()
        for copy in self.moved[2:]:
            copy.wait_recv()
        tiles = []
        for tile in range(12):
            total = self.terms[self.z, self.c, tile].astype(F32) + self.crossed_in[self.z, tile].astype(F32)
            for way in range(2):
                total = total + self.near_in[way, tile].astype(F32)
            tiles.append(total)
        return jnp.concatenate(tiles, axis=1)

    def close(self):
        for step in range(4):
            self.crossed(step).wait_send()


def group_scatter_scratch():
    return [
        pltpu.VMEM((4, 12, BLOCK, LANES), BF16),
        pltpu.VMEM((4, 12, BLOCK, LANES), BF16),
        pltpu.VMEM((4, 12, BLOCK, LANES), BF16),
        pltpu.VMEM((3, 12, BLOCK, LANES), BF16),
        pltpu.SemaphoreType.DMA,
    ]


def chip_scatter_scratch():
    return [pltpu.VMEM((4, 12, BLOCK, LANES), BF16), pltpu.VMEM((3, 12, BLOCK, LANES), BF16)]


def wire_scratch(count):
    return [pltpu.SemaphoreType.DMA((count,)), pltpu.SemaphoreType.DMA((count,))]


ANY = pl.BlockSpec(memory_space=pl.ANY)
INVMEM = pl.BlockSpec(memory_space=pltpu.VMEM)


def communicate(kernel, out_shapes, in_specs, out_specs, scratch, ident, name, vmem=VMEM_BYTES):
    return pl.pallas_call(
        kernel,
        out_shape=out_shapes,
        in_specs=in_specs,
        out_specs=out_specs,
        scratch_shapes=scratch,
        compiler_params=pltpu.CompilerParams(
            collective_id=ident, has_side_effects=True, vmem_limit_bytes=vmem
        ),
        name=name,
    )


def key_unit(member):
    return member + jnp.where(member >= 6, 6, 0) + jnp.where(member >= 7, 1, 0)


def value_unit(member):
    return member + 6 + jnp.where(member >= 6, 1, 0) + jnp.where(member >= 7, 1, 0)


def gain_rows(pieces):
    return jnp.concatenate(join_heads(pieces), axis=1)


def head_window(tiles, head):
    tile, skip = divmod(head * HEAD_DIM, LANES)
    lane = lane_of(tiles[0].shape)
    window = pltpu.roll(tiles[tile], (LANES - skip) % LANES, 1)
    if skip + HEAD_DIM > LANES:
        window = jnp.where(lane < LANES - skip, window, pltpu.roll(tiles[tile + 1], LANES - skip, 1))
    return jnp.where(lane < HEAD_DIM, window, 0.0)


def join_heads(pieces):
    lane = lane_of(pieces[0].shape)
    tiles = []
    for tile in range(len(pieces) * 3 // 4):
        piece, skip = divmod(tile * LANES, HEAD_DIM)
        low = pltpu.roll(pieces[piece], (LANES - skip) % LANES, 1)
        high = pltpu.roll(pieces[piece + 1], HEAD_DIM - skip, 1)
        tiles.append(jnp.where(lane < HEAD_DIM - skip, low, high))
    return tiles


def mix_groups(parts):
    group = lane_of(parts[0][0].shape) // 32
    mixed = None
    for i, (tile, g) in enumerate(parts):
        turned = pltpu.roll(tile, (32 * (i - g)) % LANES, 1)
        mixed = turned if mixed is None else jnp.where(group == i, turned, mixed)
    return mixed


def lane_of(shape):
    return lax.broadcasted_iota(jnp.int32, shape, len(shape) - 1)


def pack_tile(unit, extra, place):
    return jnp.where(lane_of(unit.shape) < HEAD_DIM, unit, pltpu.roll(extra, (96 - 32 * place) % LANES, 1))


def unpack_extra(tiles):
    lane = lane_of(tiles[0].shape)
    extra = jnp.where(lane < 32, pltpu.roll(tiles[0], 32, 1), 0.0)
    extra = jnp.where(jnp.logical_and(lane >= 32, lane < 64), pltpu.roll(tiles[1], 64, 1), extra)
    return jnp.where(jnp.logical_and(lane >= 64, lane < 96), pltpu.roll(tiles[2], 96, 1), extra)


def swap_halves(rows):
    lane = lane_of(rows.shape)
    return jnp.where(lane < HEAD_DIM // 2, pltpu.roll(rows, LANES - 48, 1), pltpu.roll(rows, 48, 1))


def rope_table():
    half = HEAD_DIM // 2
    frequency = ROPE_BASE ** (-2.0 * np.arange(half, dtype=np.float64) / HEAD_DIM)
    frequency = frequency.astype(np.float32)
    places = np.arange(DEPTH * BLOCK, dtype=np.float32)
    angles = (places[:, None] * frequency[None, :]).astype(np.float64)
    table = np.zeros((DEPTH * BLOCK, LANES), np.float32)
    table[:, :half] = np.cos(angles)
    table[:, half:HEAD_DIM] = np.sin(angles)
    return jnp.asarray(table.reshape(DEPTH, BLOCK, LANES))


def turning(table):
    lane = lane_of(table.shape)
    cosine = jnp.where(lane < 48, table, pltpu.roll(table, 48, 1))
    sine = jnp.where(lane < 48, -pltpu.roll(table, LANES - 48, 1), jnp.where(lane < HEAD_DIM, table, 0.0))
    return cosine, sine


def count_ancestors(lineage, block):
    count = jnp.int32(0)
    for step in range(DEPTH):
        count = count + jnp.where(lineage[block, step] >= 0, 1, 0)
    return count


def write_lineage(parent, first, lineage):
    def one(block, carry):
        def hop(step, node):
            lineage[block, step] = node
            above = parent[jnp.maximum(node, 0)]
            return jnp.where(node >= 0, above, -1)

        lax.fori_loop(0, DEPTH, hop, first + block)
        return carry

    lax.fori_loop(0, MEMBERS, one, 0)


def attend_block(lineage, block, queries, alive, load, scores):
    limit = count_ancestors(lineage, block)
    t = lax.broadcasted_iota(jnp.int32, (2 * BLOCK, BLOCK), 0) % BLOCK
    u = lax.broadcasted_iota(jnp.int32, (2 * BLOCK, BLOCK), 1)
    own = jnp.logical_and(u <= t, jnp.logical_or(alive > 0.5, u == t))
    nodes = [jnp.maximum(lineage[block, step], 0) for step in range(DEPTH)]
    pairs = range(0, DEPTH, 2)
    highest = None
    for step in pairs:
        keys = jnp.concatenate([load(node, key_unit(lax.rem(node, 8))) for node in nodes[step : step + 2]], axis=0)
        part = lax.dot_general(queries, keys, (((1,), (1,)), ((), ())), preferred_element_type=F32) * SCALE
        near = part[:, :BLOCK]
        if step == 0:
            near = jnp.where(own, near, NEGATIVE)
        else:
            near = near + jnp.where(step < limit, 0.0, NEGATIVE)
        far = part[:, BLOCK:] + jnp.where(step + 1 < limit, 0.0, NEGATIVE)
        scores[step] = near
        scores[step + 1] = far
        both = jnp.maximum(near, far)
        highest = both if step == 0 else jnp.maximum(highest, both)
    largest = jnp.max(highest, axis=1, keepdims=True)
    totals = jnp.zeros((2 * BLOCK, BLOCK), F32)
    attended = jnp.zeros((2 * BLOCK, LANES), F32)
    for step in pairs:
        near, far = jnp.exp(scores[step] - largest), jnp.exp(scores[step + 1] - largest)
        totals = totals + near + far
        values = jnp.concatenate(
            [load(node, value_unit(lax.rem(node, 8))) for node in nodes[step : step + 2]], axis=0
        )
        terms = jnp.concatenate([near.astype(BF16), far.astype(BF16)], axis=1)
        attended = attended + jnp.dot(terms, values, preferred_element_type=F32)
    total = jnp.sum(totals, axis=1, keepdims=True)
    return (attended / total).astype(BF16), largest + jnp.log(total)


def start_kernel(
    parent, table, stream, w_query, w_key, w_value, w_gate, w_up, w_out, small_rows, live_row, cotangent, own_down,
    lineage, live, gains, query, stream_all, attn_all,
    kv_out, middle, rms_out, grad_middle, grads_in, down_terms, feed_lines, wide_lines, out_terms, gain_terms,
    attended_out, log_rows,
    packed, out_low, small, stage, packed_in, out_in, small_in, wide_tall, wide_own, out_own, gain_own, gains_all,
    w_attn, own_kv, kv, w_out_all, w_feed, w_down, mid_all, cot_all, crossed_in, ring_in,
    att_out, att_in, att_pad, grads_out, *scratch,
):
    feed_scratch, wide_scratch = scratch[:5], scratch[5:10]
    send_sems, recv_sems, local_sems = scratch[10:]
    xyzc = x, y, z, c = spot()
    j = z * 2 + c
    base = (x * 4 + y) * MEMBERS
    sibling = device_of(x, y, z, 1 - c)
    wire = Wire(send_sems, recv_sems)
    group = [group_peer(x, y, z, c, k) for k in range(1, MEMBERS)]
    across, down_first = (((1,), (1,)), ((), ())), (((0,), (0,)), ((), ()))
    locals_ = []

    peers = group + axis_peers(x, y, z, c, True)
    announce(peers)

    stage[...] = jnp.zeros((16, FF), F32)
    wide_tall[96:] = jnp.zeros((8, 1536), F32)

    def staged(weights):
        width = weights.shape[1]
        stage[:12, :width] = weights[...].astype(F32)
        return [stage[:, tile * LANES : (tile + 1) * LANES] for tile in range(width // LANES)]

    def put_packed(member, tile, value):
        packed[member, :, tile * LANES : (tile + 1) * LANES] = value.astype(BF16)

    tiles = staged(w_query)
    for head in range(HEADS):
        put_packed(head // 2, head % 2, head_window(tiles, head))
    for place, weights in ((2, w_key), (3, w_value)):
        tiles = staged(weights)
        for member in range(MEMBERS):
            put_packed(member, place, head_window(tiles, member))
    for place, weights in ((4, w_gate), (8, w_up)):
        tiles = staged(weights)
        for member in range(MEMBERS):
            for tile in range(4):
                parts = [(tiles[2 * (4 * tile + i) + member // 4], member % 4) for i in range(4)]
                put_packed(member, place + tile, mix_groups(parts))
    out_low[...] = jnp.concatenate(staged(w_out), axis=1).astype(BF16)
    rows = pltpu.roll(small_rows[...], 12 * j, 1)
    live_rows = jnp.broadcast_to(live_row[...].astype(F32), (8, LANES))
    rows = jnp.where(lax.broadcasted_iota(jnp.int32, (8, LANES), 0) == 2, live_rows, rows)
    small[...] = jnp.concatenate([rows, jnp.zeros((8, LANES), F32)], axis=0).astype(BF16)
    await_peers(peers)

    def keep(source, target):
        copy = pltpu.make_async_copy(source, target, local_sems.at[len(locals_)])
        copy.start()
        locals_.append(copy)
        return copy

    def to_members(source, target):
        return [wire.send(source((j + k) % MEMBERS), target.at[j], group[k - 1]) for k in range(1, MEMBERS)]

    def half_of(member):
        return pl.ds(pl.multiple_of((member % 2) * 768, 768), 768)

    own_half = half_of(c)
    attn_part, feed_part = pl.ds(0, 512), pl.ds(512, 1024)
    attn_dealt = to_members(lambda member: packed.at[member, :, attn_part], packed_in.at[:, :, attn_part])
    small_dealt = to_members(lambda member: small, small_in)
    streams = GroupGather(wire, stream, mid_all, xyzc)
    streams.begin()
    first_kept = (keep(packed.at[j], packed_in.at[j]), keep(small, small_in.at[j]))
    out_kept = keep(out_low.at[:, own_half], out_in.at[j])
    stream_kept = keep(stream, mid_all.at[z, c])
    write_lineage(parent, base, lineage)
    for line in range(16):
        w_out_all[line // 4, line % 4, 96:] = jnp.zeros((32, D), BF16)

    for copy in attn_dealt + small_dealt:
        copy.wait_recv()
    out_dealt = to_members(lambda member: out_low.at[:, half_of(member)], out_in)
    feed_dealt_in = to_members(lambda member: packed.at[member, :, feed_part], packed_in.at[:, :, feed_part])
    for copy in first_kept:
        copy.wait()
    for member in range(MEMBERS):
        wide_tall[pl.ds(member * 12, 12), :512] = packed_in[member, :, :512].astype(F32)[:12]
    wide_own[:, :512] = wide_tall[:96, :512].astype(BF16)
    gain = small_in[0].astype(F32)
    for member in range(MEMBERS):
        row = small_in[member].astype(F32)
        live[member] = row[2:3]
        if member:
            gain = gain + row
    gain_own[...] = gain.astype(BF16)
    own_attn, own_feed = wide_own.at[:, pl.ds(0, 512)], wide_own.at[:, pl.ds(512, 1024)]
    attn = PlaneGather(wire, own_attn, w_attn, Rows(96, 512), xyzc)
    attn.first()
    tiny = [wire.send(gain_own, gains_all.at[x, y], device_of(x + k, y, z, c)) for k in range(1, 4)]
    attn_kept = keep(own_attn, w_attn.at[x, y])
    gain_kept = keep(gain_own, gains_all.at[x, y])
    down_kept = keep(own_down, w_down.at[x, y])

    attn.relay()
    streams.relay()
    gain_kept.wait()
    for copy in tiny:
        copy.wait_recv()
    line = gains_all.at[:, y]
    tiny = [wire.send(line, line, device_of(x, y + k, z, c)) for k in range(1, 4)]
    attn_kept.wait()
    attn.settle()
    attn.second()
    for copy in out_dealt:
        copy.wait_recv()
    out_kept.wait()
    for member in range(MEMBERS):
        wide_tall[pl.ds(member * 12, 12), :768] = out_in[member].astype(F32)[:12]
    out_own[...] = wide_tall[:96, :768].astype(BF16)
    out_kept = keep(out_own, w_out_all.at[x, y, pl.ds(0, 96), own_half])
    out_kept.wait()
    outs = PlaneGather(wire, w_out_all.at[x, y], w_out_all, Rows(96, 768, c * 768), xyzc)
    outs.first()
    for copy in feed_dealt_in:
        copy.wait_recv()
    for member in range(MEMBERS):
        wide_tall[pl.ds(member * 12, 12), 512:] = packed_in[member, :, 512:].astype(F32)[:12]
    wide_own[:, 512:] = wide_tall[:96, 512:].astype(BF16)
    feed_kept = keep(own_feed, w_feed.at[x, y])
    streams.near()
    streams.far()
    attn.relay()
    outs.relay()
    for copy in tiny:
        copy.wait_recv()
    pieces = [gains_all[piece // 4, piece % 4].astype(F32)[:8] for piece in range(16)]
    gains[...] = gain_rows(pieces)
    attn.settle()
    stream_kept.wait()
    streams.finish()
    attn_copied = keep(w_attn, attn_all)
    stream_copied = keep(mid_all, stream_all)

    def project(step, carry):
        wide = mid_all[step].reshape(2 * BLOCK, D).astype(F32)
        rms = jnp.sqrt(jnp.mean(wide * wide, axis=1, keepdims=True) + EPSILON)
        rows = (wide * (1.0 / rms) * gains[0:1]).astype(BF16)
        raw = jnp.dot(rows, w_attn[...].reshape(D, 512), preferred_element_type=F32)
        for part in range(2):
            block = step * 2 + part
            depth = count_ancestors(lineage, block) - 1
            cos, sin = turning(table[depth])

            def turn(head):
                v = raw[part * BLOCK : (part + 1) * BLOCK, head * LANES : (head + 1) * LANES]
                return (v * cos + swap_halves(v) * sin).astype(BF16)

            query[block, :BLOCK] = turn(0)
            query[block, BLOCK:] = turn(1)
            kv[x, y, key_unit(block)] = turn(2)
            kv[x, y, value_unit(block)] = raw[part * BLOCK : (part + 1) * BLOCK, 3 * LANES :].astype(BF16)
        return carry

    lax.fori_loop(0, 2, project, 0)
    outs.settle()
    outs.second()
    lax.fori_loop(2, 4, project, 0)
    for tile in range(12):
        extra = kv[x, y, 12 + tile // 3].astype(F32)
        own_kv[tile] = pack_tile(kv[x, y, tile].astype(F32), extra, tile % 3).astype(BF16)

    pairs = PlaneGather(wire, own_kv, kv, Units(), xyzc)
    pairs.first()
    outs.relay()
    kept = keep(own_kv, kv.at[x, y, pl.ds(0, 12)])
    cotangents = GroupGather(wire, cotangent, cot_all, xyzc)
    cotangents.begin()
    cot_kept = keep(cotangent, cot_all.at[z, c])
    pairs.relay()
    kept.wait()
    outs.settle()
    swap_part = w_out_all.at[:, :, pl.ds(0, 96), own_half]
    swapped = wire.send(swap_part, swap_part, sibling)
    pairs.settle()
    pairs.second()

    def unpack(index, carry):
        k, half, other, extra = index // 16, (index // 8) % 2, (index // 2) % 4, index % 2
        a = half * ((x + k) % 4) + (1 - half) * other
        b = half * other + (1 - half) * ((y + k) % 4)
        extra = extra + 2 * half
        tiles = [kv[a, b, extra * 3 + part].astype(F32) for part in range(3)]
        kv[a, b, 12 + extra] = unpack_extra(tiles).astype(BF16)
        return carry

    lax.fori_loop(0, 16, unpack, 0)
    cotangents.relay()
    cotangents.near()
    cotangents.far()
    pairs.relay()
    early, wire.open = wire.open, []
    feed = PlaneGather(wire, own_feed, w_feed, Rows(96, 1024), xyzc)
    down = PlaneGather(wire, own_down, w_down, Rows(32, D), xyzc)
    feed.first()
    down.first()
    pairs.near()
    lax.fori_loop(16, 32, unpack, 0)
    lax.fori_loop(48, 64, unpack, 0)
    pairs.far()
    lax.fori_loop(32, 48, unpack, 0)
    for copy in early:
        copy.wait_send()
    stream_copied.wait()
    attn_copied.wait()

    kv_copied = keep(kv, kv_out)

    att_slot = wire.reserve(MEMBERS - 1)

    def load(node, unit):
        return kv[lax.div(node, 32), lax.rem(lax.div(node, 8), 4), unit]

    def att_copy(k):
        block = (j + 1 + k) % MEMBERS
        return wire.make(att_slot + k, att_out.at[block], att_in.at[j], base + block)

    def attend_one(k, scores):
        block = (j + 1 + k) % MEMBERS
        attended, logs = attend_block(lineage, block, query[block], live[block], load, scores)
        log_rows[block] = jnp.transpose(jnp.broadcast_to(logs, (2 * BLOCK, LANES)))[:8]
        att_out[block, :, :LANES] = attended[:BLOCK]
        att_out[block, :, LANES:] = attended[BLOCK:]

    def attend_pairs(first, last):
        def both(one, two):
            def each(pair, carry):
                attend_one(2 * pair, one)
                attend_one(2 * pair + 1, two)
                return carry

            lax.fori_loop(first, last, each, 0)

        room = pltpu.VMEM((DEPTH, 2 * BLOCK, LANES), F32)
        pl.run_scoped(both, room, room)

        def give(k, carry):
            att_copy(k).start()
            return carry

        lax.fori_loop(2 * first, min(2 * last, MEMBERS - 1), give, 0)

    attend_pairs(0, 1)
    feed.relay()
    down.relay()
    attend_pairs(1, 2)
    feed_kept.wait()
    down_kept.wait()
    feed.settle()
    feed.second()
    down.settle()
    down.second()
    attend_pairs(2, 4)
    feed.relay()
    down.relay()
    att_in[j] = att_out[j]
    att_copied = keep(att_out, attended_out)
    att_recv = [att_copy(k) for k in range(MEMBERS - 1)]

    for copy in att_recv:
        copy.wait_recv()
    for member in range(MEMBERS):
        att_pad[:, member * 256 : (member + 1) * 256] = att_in[member]
    swapped.wait_recv()

    def project_out(step, carry):
        cols = pl.ds(pl.multiple_of(step * 512, 512), 512)
        weights = w_out_all[:, :, :, cols].reshape(16 * LANES, 512)
        branch = jnp.dot(att_pad[...], weights, preferred_element_type=F32)
        middle[:, cols] = stream[:, cols].astype(F32) + branch
        return carry

    lax.fori_loop(0, 3, project_out, 0)
    rms = jnp.sqrt(jnp.mean(middle[...] * middle[...], axis=1, keepdims=True) + EPSILON)
    rms_out[...] = jnp.transpose(jnp.broadcast_to(rms, (BLOCK, LANES)))[:1]
    mid_all[z, c] = (middle[...] / rms * gains[1:2]).astype(BF16)
    mids = GroupGather(wire, mid_all.at[z, c], mid_all, xyzc)
    mids.begin()
    mids.relay()
    feed.settle()
    down.settle()
    kv_copied.wait()
    cot_kept.wait()
    cotangents.finish()
    for k in range(MEMBERS - 1):
        att_copy(k).wait_send()

    grad_rows = ChipScatter(wire, kv, 2, crossed_in, ring_in, xyzc)

    def rest(acts, grad_feed, feed_terms, wide_terms):
        feed_back_half(
            xyzc, wire, group, keep, mids, grad_rows, mid_all, cot_all, w_feed, w_down, w_out_all, kv, middle, gains,
            att_pad, att_copied, grads_out, feed_scratch, wide_scratch,
            acts, grad_feed, feed_terms, wide_terms,
            grad_middle, grads_in, down_terms, feed_lines, wide_lines, out_terms, gain_terms,
        )

    pl.run_scoped(
        rest,
        pltpu.VMEM((4, 2 * BLOCK, 512), BF16),
        pltpu.VMEM((4, 2 * BLOCK, 1024), BF16),
        pltpu.VMEM((4, 4, 96, 1024), BF16),
        pltpu.VMEM((4, 4, 32, D), BF16),
    )


def feed_back_half(
    xyzc, wire, group, keep, mids, grad_rows, mid_all, cot_all, w_feed, w_down, w_out_all, kv, middle, gains,
    att_pad, att_copied, grads_out, feed_scratch, wide_scratch,
    acts, grad_feed, feed_terms, wide_terms,
    grad_middle, grads_in, down_terms, feed_lines, wide_lines, out_terms, gain_terms,
):
    x, y, z, c = xyzc
    j = z * 2 + c
    across, down_first = (((1,), (1,)), ((), ())), (((0,), (0,)), ((), ()))

    def feed_forward(step):
        place = grad_rows.place(step)
        rows = mid_all[place].reshape(2 * BLOCK, D)
        weights = w_feed[...].reshape(D, 1024)
        both = jnp.dot(rows, weights, preferred_element_type=F32)
        gate, up = both[:, :512], both[:, 512:]
        sigmoid = 0.5 * jnp.tanh(0.5 * gate) + 0.5
        silu = gate * sigmoid
        acts[place] = (silu * up).astype(BF16)
        cot = cot_all[place].reshape(2 * BLOCK, D)
        grad_act = lax.dot_general(cot, w_down[...].reshape(512, D), across, preferred_element_type=F32)
        grad_gate = grad_act * up * sigmoid * (1.0 + gate * (1.0 - sigmoid))
        grad_feed[place, :, :512] = grad_gate.astype(BF16)
        grad_feed[place, :, 512:] = (grad_act * silu).astype(BF16)

    def feed_back(step):
        place = grad_rows.place(step)
        weights = w_feed[...].reshape(D, 1024)
        grads = lax.dot_general(grad_feed[place], weights, across, preferred_element_type=F32)
        grad_rows.put(step, grads.astype(BF16))

    mids.crossed[0].wait_recv()
    feed_forward(0)
    feed_back(0)
    mids.near()
    mids.crossed[1].wait_recv()
    mids.crossed[2].wait_recv()

    def near_chunk(index, carry):
        step = 1 + 2 * index
        feed_forward(step)
        feed_back(step)

        @pl.when(index > 0)
        def _():
            grad_rows.turn(1)

        return carry

    lax.fori_loop(0, 2, near_chunk, 0)
    mids.far()
    mids.crossed[3].wait_recv()
    grad_rows.turn(3)
    feed_forward(2)

    def down_weights(step, carry):
        cols = pl.ds(pl.multiple_of(step * 128, 128), 128)
        left = acts[:, :, cols].reshape(MEMBERS * BLOCK, 128)
        right = cot_all[...].reshape(MEMBERS * BLOCK, D)
        total = lax.dot_general(left, right, down_first, preferred_element_type=F32)
        wide_terms[step] = total.astype(BF16).reshape(4, 32, D)
        return carry

    lax.fori_loop(0, 4, down_weights, 0)
    wides = PlaneScatter(wire, wide_terms, Rows(32, D), wide_scratch, xyzc)
    wides.first()
    feed_back(2)

    def feed_weights(step, carry):
        cols = pl.ds(pl.multiple_of(step * 384, 384), 384)
        left = mid_all[:, :, :, cols].reshape(MEMBERS * BLOCK, 384)
        right = grad_feed[...].reshape(MEMBERS * BLOCK, 1024)
        total = lax.dot_general(left, right, down_first, preferred_element_type=F32)
        feed_terms[step] = total.astype(BF16).reshape(4, 96, 1024)
        return carry

    lax.fori_loop(0, 2, feed_weights, 0)
    grad_rows.turn(2)
    lax.fori_loop(2, 4, feed_weights, 0)
    feeds = PlaneScatter(wire, feed_terms, Rows(96, 1024), feed_scratch, xyzc)
    feeds.first()
    wides.relay()

    def down_rows(place, carry):
        outs = jnp.dot(acts[place], w_down[...].reshape(512, D), preferred_element_type=F32).astype(BF16)
        for core in range(2):
            for tile in range(12):
                kv[place, core, tile] = outs[
                    core * BLOCK : (core + 1) * BLOCK, tile * LANES : (tile + 1) * LANES
                ]
        return carry

    lax.fori_loop(0, 4, down_rows, 0)
    down_copied = keep(kv.at[:, pl.ds(0, 2), pl.ds(0, 12)], down_terms)
    grad_mid = grad_rows.total()
    rms = jnp.sqrt(jnp.mean(middle[...] * middle[...], axis=1, keepdims=True) + EPSILON)
    scaled = middle[...] / rms
    gain_terms[...] = jnp.sum(grad_mid * scaled, axis=0, keepdims=True)
    weighted = grad_mid * gains[1:2]
    back = (weighted - scaled * jnp.mean(weighted * scaled, axis=1, keepdims=True)) / rms
    grad_middle[...] = cot_all[z, c].astype(F32) + back
    branch_grad = grad_middle[...].astype(BF16)

    def spread(step, carry):
        weights = w_out_all[step].reshape(4 * LANES, D)
        grads = lax.dot_general(branch_grad, weights, across, preferred_element_type=F32).astype(BF16)
        for part in range(2):
            grads_out[step * 2 + part] = grads[:, part * 256 : (part + 1) * 256]
        return carry

    lax.fori_loop(0, 4, spread, 0)
    kept = keep(grads_out.at[j], grads_in.at[j])
    dealt = [
        wire.send(grads_out.at[(j + k) % MEMBERS], grads_in.at[j], group[k - 1]) for k in (4, 5, 3, 2, 6, 7, 1)
    ]
    feeds.relay()

    def out_weights(step, carry):
        cols = pl.ds(pl.multiple_of(step * 512, 512), 512)
        total = lax.dot_general(att_pad[:, cols], branch_grad, down_first, preferred_element_type=F32)
        w_out_all[step] = total.astype(BF16).reshape(4, LANES, D)
        return carry

    lax.fori_loop(0, 4, out_weights, 0)
    out_copied = keep(w_out_all.at[:, :, pl.ds(0, 96)], out_terms)

    wides.add_first()
    wide_copied = keep(wides.summed, wide_lines)
    feeds.add_first()
    feed_copied = keep(feeds.summed, feed_lines)
    for copy in dealt:
        copy.wait_recv()
    for copy in (kept, down_copied, out_copied, att_copied, wide_copied, feed_copied):
        copy.wait()
    wire.close()
    grad_rows.close()


def start(
    parent, table, stream, w_query, w_key, w_value, w_gate, w_up, w_out, small_rows, live_row, cotangent, own_down
):
    shape, vmem = jax.ShapeDtypeStruct, pltpu.VMEM
    smem = pl.BlockSpec(memory_space=pltpu.SMEM)
    return communicate(
        start_kernel,
        (
            shape((MEMBERS, DEPTH), jnp.int32),
            shape((MEMBERS, 1, LANES), F32),
            shape((8, D), F32),
            shape((MEMBERS, 2 * BLOCK, LANES), BF16),
            shape((4, 2, BLOCK, D), BF16),
            shape((4, 4, 96, 512), BF16),
            shape((4, 4, 16, BLOCK, LANES), BF16),
            shape((BLOCK, D), F32),
            shape((1, LANES), F32),
            shape((BLOCK, D), F32),
            shape((MEMBERS, BLOCK, 2 * LANES), BF16),
            shape((4, 2, 12, BLOCK, LANES), BF16),
            shape((2, 4, 48, 1024), BF16),
            shape((2, 4, 16, D), BF16),
            shape((4, 4, 96, D), BF16),
            shape((1, D), F32),
            shape((MEMBERS, BLOCK, 2 * LANES), BF16),
            shape((MEMBERS, 8, 2 * BLOCK), F32),
        ),
        [smem] + [INVMEM] * 10 + [ANY] * 2,
        (smem,) + (INVMEM,) * 3 + (ANY,) * 3 + (INVMEM,) * 3 + (ANY,) * 5 + (INVMEM, ANY, INVMEM),
        [
            vmem((MEMBERS, 16, 1536), BF16),
            vmem((16, 1536), BF16),
            vmem((16, LANES), BF16),
            vmem((16, FF), F32),
            vmem((MEMBERS, 16, 1536), BF16),
            vmem((MEMBERS, 16, 768), BF16),
            vmem((MEMBERS, 16, LANES), BF16),
            vmem((104, 1536), F32),
            vmem((96, 1536), BF16),
            vmem((96, 768), BF16),
            vmem((16, LANES), BF16),
            vmem((4, 4, 16, LANES), BF16),
            vmem((4, 4, 96, 512), BF16),
            vmem((12, BLOCK, LANES), BF16),
            vmem((4, 4, 16, BLOCK, LANES), BF16),
            vmem((4, 4, LANES, D), BF16),
            vmem((4, 4, 96, 1024), BF16),
            vmem((4, 4, 32, D), BF16),
            vmem((4, 2, BLOCK, D), BF16),
            vmem((4, 2, BLOCK, D), BF16),
        ]
        + chip_scatter_scratch()
        + [
            vmem((MEMBERS, BLOCK, 2 * LANES), BF16),
            vmem((MEMBERS, BLOCK, 2 * LANES), BF16),
            vmem((BLOCK, 2048), BF16),
            vmem((MEMBERS, BLOCK, 2 * LANES), BF16),
        ]
        + scatter_scratch(Rows(96, 1024))
        + scatter_scratch(Rows(32, D))
        + wire_scratch(250)
        + [pltpu.SemaphoreType.DMA((20,))],
        2,
        "start",
        63 * 2**20,
    )(parent, table, stream, w_query, w_key, w_value, w_gate, w_up, w_out, small_rows, live_row, cotangent, own_down)


def split_rows(tall, dealt):
    width = dealt.shape[2]
    for member in range(MEMBERS):
        dealt[member] = tall[pl.ds(member * 12, 16), :width].astype(BF16)


def attend_back_kernel(
    lineage, query, live, grad, attended, log_rows, kv_in, grad_query, grad_kv, kv, sums, packed, sems
):
    loaded = pltpu.make_async_copy(kv_in, kv, sems.at[16])
    loaded.start()

    def clear(step, carry):
        sums[step] = jnp.zeros((BLOCK, LANES), F32)
        return carry

    lax.fori_loop(0, 256, clear, 0)
    loaded.wait()

    def two(pair, carry):
        for block in (2 * pair, 2 * pair + 1):
            attend_back_block(block, lineage, query, live, grad, attended, log_rows, grad_query, kv, sums)
        return carry

    lax.fori_loop(0, MEMBERS // 2, two, 0)

    def stored(line):
        rows = pl.ds(line * 12, 12)
        return pltpu.make_async_copy(packed.at[rows], grad_kv.at[rows], sems.at[line])

    def store(line, carry):
        for tile in range(12):
            total = pack_tile(sums[line * 16 + tile], sums[line * 16 + 12 + tile // 3], tile % 3)
            packed[line * 12 + tile] = total.astype(BF16)
        stored(line).start()
        return carry

    lax.fori_loop(0, 16, store, 0)
    for line in range(16):
        stored(line).wait()


def attend_back_block(block, lineage, query, live, grad, attended, log_rows, grad_query, kv, sums):
    across, down_first = (((1,), (1,)), ((), ())), (((0,), (0,)), ((), ()))
    queries = query[block]
    grads = jnp.concatenate([grad[block, :, :LANES], grad[block, :, LANES:]], axis=0)
    outs = jnp.concatenate([attended[block, :, :LANES], attended[block, :, LANES:]], axis=0)
    product = grads.astype(F32) * outs.astype(F32)
    high = product.astype(BF16)
    low = (product - high.astype(F32)).astype(BF16)
    ones = jnp.ones((8, LANES), BF16)
    inner = lax.dot_general(ones, high, across, preferred_element_type=F32)
    inner = (inner + lax.dot_general(ones, low, across, preferred_element_type=F32))[:1]
    logs = log_rows[block, :1]
    limit = count_ancestors(lineage, block)
    u = lax.broadcasted_iota(jnp.int32, (BLOCK, 2 * BLOCK), 0)
    t = lax.broadcasted_iota(jnp.int32, (BLOCK, 2 * BLOCK), 1) % BLOCK
    alive = jnp.transpose(jnp.broadcast_to(live[block], (BLOCK, BLOCK)))
    alive = jnp.concatenate([alive, alive], axis=1)
    own = jnp.logical_and(u <= t, jnp.logical_or(alive > 0.5, u == t))
    turned = jnp.zeros((LANES, 2 * BLOCK), F32)
    for step in range(0, DEPTH, 2):
        units = []
        for node in (lineage[block, step], lineage[block, step + 1]):
            safe = jnp.maximum(node, 0)
            at, member = lax.div(safe, 8) * 16, lax.rem(safe, 8)
            units.append((node, at + key_unit(member), at + value_unit(member)))
        keys = jnp.concatenate([kv[unit[1]] for unit in units], axis=0)
        values = jnp.concatenate([kv[unit[2]] for unit in units], axis=0)
        scores = lax.dot_general(keys, queries, across, preferred_element_type=F32) * SCALE
        near, far = scores[:BLOCK], scores[BLOCK:]
        if step == 0:
            near = jnp.where(own, jnp.exp(jnp.where(own, near - logs, NEGATIVE)), 0.0)
        else:
            near = jnp.exp(near + (jnp.where(step < limit, 0.0, NEGATIVE) - logs))
        far = jnp.exp(far + (jnp.where(step + 1 < limit, 0.0, NEGATIVE) - logs))
        chances = jnp.concatenate([near, far], axis=0)
        grad_chances = lax.dot_general(values, grads, across, preferred_element_type=F32)
        grad_scores = (chances * (grad_chances - inner)).astype(BF16)
        grad_keys = jnp.dot(grad_scores, queries, preferred_element_type=F32) * SCALE
        grad_values = jnp.dot(chances.astype(BF16), grads, preferred_element_type=F32)
        for part, (node, at_key, at_value) in enumerate(units):
            rows = slice(part * BLOCK, (part + 1) * BLOCK)
            sums[jnp.where(node >= 0, at_key, 256)] += grad_keys[rows]
            sums[jnp.where(node >= 0, at_value, 256)] += grad_values[rows]
        turned = turned + lax.dot_general(keys, grad_scores, down_first, preferred_element_type=F32)
    grad_query[block] = jnp.transpose(turned) * SCALE


def attend_back(lineage, query, kv, live, grad, attended, log_rows):
    vmem = pltpu.VMEM
    return pl.pallas_call(
        attend_back_kernel,
        in_specs=[pl.BlockSpec(memory_space=pltpu.SMEM)] + [INVMEM] * 5 + [ANY],
        out_specs=(INVMEM, ANY),
        out_shape=(
            jax.ShapeDtypeStruct((MEMBERS, 2 * BLOCK, LANES), F32),
            jax.ShapeDtypeStruct((192, BLOCK, LANES), BF16),
        ),
        scratch_shapes=[
            vmem((256, BLOCK, LANES), BF16),
            vmem((257, BLOCK, LANES), F32),
            vmem((192, BLOCK, LANES), BF16),
            pltpu.SemaphoreType.DMA((17,)),
        ],
        compiler_params=pltpu.CompilerParams(vmem_limit_bytes=VMEM_BYTES),
        name="attend_back",
    )(lineage, query, live, grad, attended, log_rows, kv)


def gain_tiles(rows):
    lane = lane_of((8, LANES))
    tiles = [rows[:, tile * LANES : (tile + 1) * LANES] for tile in range(12)]
    pieces = []
    for piece in range(16):
        tile, skip = divmod(piece * 96, LANES)
        low = pltpu.roll(tiles[tile], (LANES - skip) % LANES, 1)
        high = pltpu.roll(tiles[min(tile + 1, 11)], (LANES - skip) % LANES, 1)
        pieces.append(jnp.where(lane < LANES - skip, low, high))
    return pieces


def ending_kernel(
    lineage, grad_query, table, stream_all, w_attn, gain, gain_two, stream, middle, grad_middle,
    feed_lines, wide_lines, kv_terms, down_terms, out_terms,
    mixed_out, stream_grad, query_grad, key_grad, value_grad, out_grad, gain_one, gain_two_out, rms_out,
    gate_grad, up_grad, down_grad,
    feed_second, wide_second, feed_tall, feed_dealt, feed_in, attn_grad, out_in, normed, raw, units, grad_terms, crossed_in, near_in, far_in, query_terms, pair_terms, attn_tall, attn_dealt,
    out_tall, out_dealt, out_mine, out_crossed, gain_terms, gain_in, gain_line, gain_in_two, gain_in_three,
    *scratch,
):
    xyzc = x, y, z, c = spot()
    j = z * 2 + c
    down_scratch, kv_scratch, query_scratch, pair_scratch, out_scratch = (
        scratch[:5], scratch[5:13], scratch[13:18], scratch[18:23], scratch[23:28]
    )
    send_sems, recv_sems, local_sem = scratch[28:]
    wire = Wire(send_sems, recv_sems)
    group = [group_peer(x, y, z, c, k) for k in range(1, MEMBERS)]
    peers = group + axis_peers(x, y, z, c, True)
    announce(peers)
    await_peers(peers)
    sibling = device_of(x, y, z, 1 - c)
    pairs = PlaneScatter(wire, kv_terms, Units(), kv_scratch, xyzc)
    pairs.first()
    attn_tall[96:] = jnp.zeros((8, 512), F32)
    feed_tall[96:] = jnp.zeros((8, 1024), F32)
    out_tall[96:] = jnp.zeros((8, 768), F32)

    def norm_rows(step, carry):
        rows = pl.ds(pl.multiple_of(step * BLOCK, BLOCK), BLOCK)
        wide = stream_all[rows].astype(F32)
        rms = jnp.sqrt(jnp.mean(wide * wide, axis=1, keepdims=True) + EPSILON)
        normed[rows] = (wide * (1.0 / rms) * gain[0:1]).astype(BF16)
        return carry

    lax.fori_loop(0, MEMBERS, norm_rows, 0)

    def turn(block, v):
        depth = count_ancestors(lineage, block) - 1
        cos, sin = turning(table[depth])
        return (v * cos - swap_halves(v) * sin).astype(BF16)

    def query_rows(block, carry):
        rows = pl.ds(pl.multiple_of(block * BLOCK, BLOCK), BLOCK)
        raw[rows, :128] = turn(block, grad_query[block, :BLOCK])
        raw[rows, 128:256] = turn(block, grad_query[block, BLOCK:])
        return carry

    lax.fori_loop(0, MEMBERS, query_rows, 0)
    pairs.relay()
    downs = GroupScatter(wire, down_terms, *down_scratch, xyzc)
    downs.begin()
    own_half = pl.ds(pl.multiple_of(c * 768, 768), 768)
    other_half = pl.ds(pl.multiple_of((1 - c) * 768, 768), 768)
    crossed = wire.send(out_terms.at[:, :, :, other_half], out_crossed, sibling)
    local = pltpu.make_async_copy(out_terms.at[:, :, :, own_half], out_mine, local_sem)
    local.start()

    def weights_back(terms, first):
        def some(step, carry):
            cols = pl.ds(pl.multiple_of(step * 384, 384), 384)
            total = lax.dot_general(
                normed[:, cols], raw[:, first : first + 256], (((0,), (0,)), ((), ())), preferred_element_type=F32
            )
            terms[step] = total.astype(BF16).reshape(4, 96, 256)
            return carry

        lax.fori_loop(0, 4, some, 0)

    weights_back(query_terms, 0)
    query_sums = PlaneScatter(wire, query_terms, Rows(96, 256), query_scratch, xyzc)
    pair_sums = PlaneScatter(wire, pair_terms, Rows(96, 256), pair_scratch, xyzc)
    local.wait()
    crossed.wait_recv()

    def add_halves(step, carry):
        a, b = step // 4, step % 4
        total = out_mine[a, b].astype(F32) + out_crossed[a, b].astype(F32)
        out_mine[a, b] = total.astype(BF16)
        return carry

    lax.fori_loop(0, 16, add_halves, 0)
    outs = PlaneScatter(wire, out_mine, Rows(96, 768), out_scratch, xyzc)
    downs.turn()
    pairs.add_first()
    pairs.second()
    downs.finish(stream_grad)
    mixed_out[...] = (middle[...] + stream_grad[...]).astype(BF16)
    pairs.arrive()
    outs.first()
    query_sums.first()
    feeds = SecondRound(wire, feed_lines, feed_second, xyzc)
    wides = SecondRound(wire, wide_lines, wide_second, xyzc)
    feeds.second()
    wides.second()
    for half in range(2):
        units[pl.ds(half * 6, 6)] = pairs.total(half)
    for extra in range(4):
        units[12 + extra] = unpack_extra([units[extra * 3 + k] for k in range(3)])

    def pair_rows(block, carry):
        rows = pl.ds(pl.multiple_of(block * BLOCK, BLOCK), BLOCK)
        raw[rows, 256:384] = turn(block, units[key_unit(block)])
        value = units[value_unit(block)]
        raw[rows, 384:] = jnp.where(lane_of((BLOCK, LANES)) < HEAD_DIM, value, 0.0).astype(BF16)
        return carry

    lax.fori_loop(0, MEMBERS, pair_rows, 0)

    grad_rows = RingScatter(wire, grad_terms, crossed_in, near_in, far_in, xyzc)
    gain_terms[...] = jnp.zeros((1, D), F32)

    def rows_back(step):
        rows = pl.ds(pl.multiple_of(grad_rows.place(step) * 256, 256), 256)
        grads = lax.dot_general(raw[rows], w_attn[...], (((1,), (1,)), ((), ())), preferred_element_type=F32)
        grad_rows.put(step, grads.astype(BF16))
        wide = stream_all[rows].astype(F32)
        rms = jnp.sqrt(jnp.mean(wide * wide, axis=1, keepdims=True) + EPSILON)
        gain_terms[...] += jnp.sum(grads * (wide * (1.0 / rms)), axis=0, keepdims=True)

    rows_back(2)
    rows_back(1)
    grad_rows.turn(2)
    rows_back(3)
    grad_rows.turn(1)
    rows_back(0)
    grad_rows.turn(3)
    outs.relay()
    query_sums.relay()
    grad_rows.pass_on(1)
    grad_rows.pass_on(3)
    rows = jnp.concatenate([gain_terms[...], gain_two[...], jnp.zeros((6, D), F32)], axis=0)
    for piece, part in enumerate(gain_tiles(rows)):
        gain_in[piece // 4, piece % 4] = part
    gains = [
        wire.send(gain_in.at[(x + k) % 4], gain_line.at[k], device_of(x + k, y, z, c)) for k in range(1, 4)
    ]

    weights_back(pair_terms, 256)
    pair_sums.first()
    for copy in gains:
        copy.wait_recv()
    gain_line[0] = gain_in[x] + gain_line[1] + gain_line[2] + gain_line[3]
    gains = [
        wire.send(gain_line.at[0, (y + k) % 4], gain_in_two.at[k], device_of(x, y + k, z, c)) for k in range(1, 4)
    ]
    outs.add_first()
    outs.second()
    query_sums.add_first()
    query_sums.second()
    pair_sums.relay()
    outs.arrive()
    for half in range(2):
        out_tall[pl.ds(half * 48, 48)] = outs.total(half)
    split_rows(out_tall, out_dealt)
    out_in[j] = out_dealt[j]
    dealt = [
        wire.send(out_dealt.at[(j + k) % MEMBERS], out_in.at[j], group[k - 1]) for k in range(1, MEMBERS)
    ]
    feeds.arrive()
    for half in range(2):
        feed_tall[pl.ds(half * 48, 48)] = feeds.total(half)
    split_rows(feed_tall, feed_dealt)
    feed_in[j] = feed_dealt[j]
    feed_copies = [
        wire.send(feed_dealt.at[(j + k) % MEMBERS], feed_in.at[j], group[k - 1]) for k in range(1, MEMBERS)
    ]
    wides.arrive()
    for half in range(2):
        down_grad[pl.ds(half * 16, 16)] = wides.total(half)
    pair_sums.add_first()
    pair_sums.second()

    wide = stream[...].astype(F32)
    rms = jnp.sqrt(jnp.mean(wide * wide, axis=1, keepdims=True) + EPSILON)
    rms_out[...] = jnp.transpose(jnp.broadcast_to(rms, (BLOCK, LANES)))[:1]
    scaled = wide / rms
    weighted = grad_rows.total() * gain[0:1]
    back = (weighted - scaled * jnp.mean(weighted * scaled, axis=1, keepdims=True)) / rms
    stream_grad[...] = grad_middle[...] + back

    for copy in gains:
        copy.wait_recv()
    gain_in_three[j] = gain_line[0, y] + gain_in_two[1] + gain_in_two[2] + gain_in_two[3]
    gains = [
        wire.send(gain_in_three.at[j], gain_in_three.at[j], group[k - 1]) for k in range(1, MEMBERS)
    ]
    query_sums.arrive()
    pair_sums.arrive()
    for half in range(2):
        attn_tall[pl.ds(half * 48, 48), :256] = query_sums.total(half)
        attn_tall[pl.ds(half * 48, 48), 256:] = pair_sums.total(half)
    split_rows(attn_tall, attn_dealt)
    attn_grad[j] = attn_dealt[j]
    dealt += [
        wire.send(attn_dealt.at[(j + k) % MEMBERS], attn_grad.at[j], group[k - 1]) for k in range(1, MEMBERS)
    ]
    for copy in gains:
        copy.wait_recv()
    total = gain_in_three[0]
    for member in range(1, MEMBERS):
        total = total + gain_in_three[member]
    own = pltpu.roll(total, (LANES - 12 * j) % LANES, 1)
    gain_one[...] = own[:1, :12]
    gain_two_out[...] = own[1:2, :12]
    for copy in feed_copies:
        copy.wait_recv()
    for grad, first in ((gate_grad, 0), (up_grad, 4)):
        for tile in range(32):
            line = tile // 2
            cols = slice((first + line // 4) * LANES, (first + line // 4 + 1) * LANES)
            parts = [(feed_in[4 * (tile % 2) + i, :, cols].astype(F32), line % 4) for i in range(4)]
            grad[:, tile * LANES : (tile + 1) * LANES] = mix_groups(parts)[:12]
    for copy in dealt:
        copy.wait_recv()
    for core in range(2):
        total = out_in[core].astype(F32)
        for place in range(1, 4):
            total = total + out_in[place * 2 + core].astype(F32)
        out_grad[:, core * 768 : (core + 1) * 768] = total[:12]

    def tile_of(member, tile):
        return attn_grad[member, :, tile * LANES : (tile + 1) * LANES].astype(F32)

    for grad, pieces in (
        (query_grad, [tile_of(head // 2, head % 2) for head in range(HEADS)]),
        (key_grad, [tile_of(member, 2) for member in range(MEMBERS)]),
        (value_grad, [tile_of(member, 3) for member in range(MEMBERS)]),
    ):
        for tile, value in enumerate(join_heads(pieces)):
            grad[:, tile * LANES : (tile + 1) * LANES] = value[:12]
    wire.close()
    grad_rows.close()


def ending(
    lineage, grad_query, table, stream_all, w_attn, gain, gain_two, stream, middle, grad_middle,
    feed_lines, wide_lines, kv_terms, down_terms, out_terms,
):
    shape, vmem = jax.ShapeDtypeStruct, pltpu.VMEM
    smem = pl.BlockSpec(memory_space=pltpu.SMEM)
    return communicate(
        ending_kernel,
        (
            shape((BLOCK, D), BF16),
            shape((BLOCK, D), F32),
            shape((12, D), F32),
            shape((12, 768), F32),
            shape((12, 768), F32),
            shape((12, D), F32),
            shape((1, 12), F32),
            shape((1, 12), F32),
            shape((1, LANES), F32),
            shape((12, FF), F32),
            shape((12, FF), F32),
            shape((32, D), F32),
        ),
        [smem] + [INVMEM] * 11 + [ANY] * 3,
        (INVMEM,) * 12,
        [
            vmem((2, 3, 48, 1024), BF16),
            vmem((2, 3, 16, D), BF16),
            vmem((104, 1024), F32),
            vmem((MEMBERS, 16, 1024), BF16),
            vmem((MEMBERS, 16, 1024), BF16),
            vmem((MEMBERS, 16, 512), BF16),
            vmem((MEMBERS, 16, 768), BF16),
            vmem((MEMBERS * BLOCK, D), BF16),
            vmem((MEMBERS * BLOCK, 512), BF16),
            vmem((16, BLOCK, LANES), F32),
            vmem((4, 2, 12, BLOCK, LANES), BF16),
        ]
        + [
            vmem((4, 12, BLOCK, LANES), BF16),
            vmem((2, 12, BLOCK, LANES), BF16),
            vmem((2, 6, BLOCK, LANES), BF16),
        ]
        + [
            vmem((4, 4, 96, 256), BF16),
            vmem((4, 4, 96, 256), BF16),
            vmem((104, 512), F32),
            vmem((MEMBERS, 16, 512), BF16),
            vmem((104, 768), F32),
            vmem((MEMBERS, 16, 768), BF16),
            vmem((4, 4, 96, 768), BF16),
            vmem((4, 4, 96, 768), BF16),
            vmem((1, D), F32),
            vmem((4, 4, 8, LANES), F32),
            vmem((4, 4, 8, LANES), F32),
            vmem((4, 8, LANES), F32),
            vmem((MEMBERS, 8, LANES), F32),
        ]
        + group_scatter_scratch()
        + scatter_scratch(Units(), room=True)
        + scatter_scratch(Rows(96, 256))
        + scatter_scratch(Rows(96, 256))
        + scatter_scratch(Rows(96, 768))
        + wire_scratch(140)
        + [pltpu.SemaphoreType.DMA],
        7,
        "ending",
        62 * 2**20,
    )(
        lineage, grad_query, table, stream_all, w_attn, gain, gain_two, stream, middle, grad_middle,
        feed_lines, wide_lines, kv_terms, down_terms, out_terms,
    )


def hand_over_kernel(*refs):
    count = len(refs) // 2
    for source, target in zip(refs[:count], refs[count:]):
        target[...] = source[...]


def hand_over(*arrays):
    return pl.pallas_call(
        hand_over_kernel,
        out_shape=tuple(jax.ShapeDtypeStruct(array.shape, array.dtype) for array in arrays),
        in_specs=[INVMEM] * len(arrays),
        out_specs=(INVMEM,) * len(arrays),
        compiler_params=pltpu.CompilerParams(vmem_limit_bytes=VMEM_BYTES),
        name="hand_over",
    )(*arrays)


def shards(
    stream, attn_gain, w_query, w_key, w_value, w_out, mlp_gain, w_gate, w_up, w_down, parent, live_mask, cotangent
):
    table = rope_table()
    small_rows = jnp.pad(jnp.stack([attn_gain, mlp_gain]).astype(F32), ((0, 6), (0, LANES - attn_gain.shape[0])))
    (
        lineage, live, gains, query, stream_all, w_attn, context, middle, branch_rms, grad_middle, grad_heads,
        down_terms, feed_lines, wide_lines, out_terms, gain_two_terms, attended, log_rows,
    ) = start(
        parent, table, stream, w_query, w_key, w_value, w_gate, w_up, w_out, small_rows,
        live_mask.reshape(1, BLOCK), cotangent, w_down,
    )
    grad_query, context_terms = attend_back(
        lineage, query, context.reshape(256, BLOCK, LANES), live, grad_heads, attended, log_rows
    )
    (
        mixed_out, stream_grad, query_grad, key_grad, value_grad, out_grad, gain_one, gain_two, stream_rms,
        gate_grad, up_grad, down_grad,
    ) = ending(
        lineage, grad_query, table, stream_all.reshape(MEMBERS * BLOCK, D), w_attn.reshape(D, 512), gains,
        gain_two_terms, stream, middle, grad_middle, feed_lines, wide_lines,
        context_terms.reshape(4, 4, 12, BLOCK, LANES), down_terms, out_terms,
    )
    (
        mixed_out, stream_grad, gain_one, query_grad, key_grad, value_grad, out_grad, gain_two,
        gate_grad, up_grad, down_grad, stream_rms, branch_rms,
    ) = hand_over(
        mixed_out, stream_grad, gain_one, query_grad, key_grad, value_grad, out_grad, gain_two,
        gate_grad, up_grad, down_grad, stream_rms, branch_rms,
    )
    return (
        mixed_out, stream_grad, gain_one[0], query_grad, key_grad, value_grad, out_grad, gain_two[0],
        gate_grad, up_grad, down_grad, stream_rms[0], branch_rms[0],
    )


def solution(mesh):
    rows, line = P("dev", None), P("dev")
    return jax.shard_map(
        shards,
        mesh=mesh,
        in_specs=(rows, line, rows, rows, rows, rows, line, rows, rows, rows, P(), line, rows),
        out_specs=(rows, rows, line, rows, rows, rows, rows, line, rows, rows, rows, line, line),
        check_vma=False,
    )
```
